32 devices in a mesh: rep: 4 (over y, x), shard: 8 (over z, core).
Axes of the slice: x: 2, y: 2, z: 4, core: 2. Of those that a mesh axis runs over, the one named last changes fastest.
Arguments:
- tokens: bfloat16 [8192, 2048], P(('rep', 'shard')), may hold values from -6 to 6
- document_ends: int32 [32, 4], P(('rep', 'shard')), may hold values from 0 to 256, as said below
- projector: bfloat16 [2048, 6144], P('shard'), may hold values from -0.125 to 0.125
- projbias: bfloat16 [6144], P('shard'), may hold values from -3 to 3
- combiner: bfloat16 [2048, 2048], P('shard'), may hold values from -0.5 to 0.5
- combbias: bfloat16 [2048], P('shard'), may hold values from -2 to 2
- expander: bfloat16 [2048, 8192], P('shard'), may hold values from -0.125 to 0.125
- expbias: bfloat16 [8192], P('shard'), may hold values from -3 to 3
- contractor: bfloat16 [8192, 2048], P('shard'), may hold values from -0.0625 to 0.0625
- contbias: bfloat16 [2048], P('shard'), may hold values from -2 to 2
- attendgain: bfloat16 [2048], P('shard'), may hold values from 0.099609375 to 1.8984375
- attendshift: bfloat16 [2048], P('shard'), may hold values from -2 to 2
- feedgain: bfloat16 [2048], P('shard'), may hold values from 0.099609375 to 1.8984375
- feedshift: bfloat16 [2048], P('shard'), may hold values from -2 to 2
- cotangent: bfloat16 [8192, 2048], P(('rep', 'shard')), may hold values from -6 to 6
Outputs:
- block_output: bfloat16 [8192, 2048], P(('rep', 'shard'))
- input_gradient: bfloat16 [8192, 2048], P(('rep', 'shard'))
- projector_gradient: float32 [2048, 6144], P('shard')
- projbias_gradient: float32 [6144], P('shard')
- combiner_gradient: float32 [2048, 2048], P('shard')
- combbias_gradient: float32 [2048], P('shard')
- expander_gradient: float32 [2048, 8192], P('shard')
- expbias_gradient: float32 [8192], P('shard')
- contractor_gradient: float32 [8192, 2048], P('shard')
- contbias_gradient: float32 [2048], P('shard')
- attendgain_gradient: float32 [2048], P('shard')
- attendshift_gradient: float32 [2048], P('shard')
- feedgain_gradient: float32 [2048], P('shard')
- feedshift_gradient: float32 [2048], P('shard')
The draws below stay inside these ranges and needn't reach their ends.
Inputs may be any that keep to these rules, and one draw needn't show every extreme that they name: `document_ends`: each row never falls; a device's documents run from slot 0 to its last entry one after another, and slots from the last entry on are padding. The last entry is 128 or more, and 256 on some device.
All inputs are finite; a program needn't handle non-finite values.
Results may differ from the reference program's by a relative error of at most 0.015.
Values may be sent and summed in bfloat16 or wider, within the bound.
A program may use at most 512 MiB of HBM per device.

```python
import math
import jax
import jax.numpy as jnp
from jax import lax

D = 2048
FF = 8192
H = 8
ROT = 64
ROWS = 256
DOCS = 4
NDEV = 32
TOKENS = 8192


def draw_document_ends(key, part):
    key = jax.random.fold_in(key, 11)
    key_live, key_full, key_share = jax.random.split(key, 3)
    filled = jax.random.randint(key_live, (NDEV,), ROWS // 2, ROWS + 1)
    chosen = jax.random.randint(key_full, (), 0, NDEV)
    filled = jnp.where(jnp.arange(NDEV) == chosen, ROWS, filled)
    shares = jax.random.randint(key_share, (NDEV, DOCS), 1, 9)
    running = jnp.cumsum(shares, axis=1)
    return (running * filled[:, None] // running[:, -1:]).astype(jnp.int32)


def shard_levels(rng, dims, cuts, low, largest):
    def one(dim, shards_of):
        steps = jax.random.uniform(jax.random.fold_in(jax.random.fold_in(rng, 6), dim), (shards_of,), jnp.float32, low / len(cuts), largest / len(cuts))
        return jnp.repeat(jnp.exp(steps), dims[dim] // shards_of).reshape((-1,) + (1,) * (len(dims) - dim - 1))

    loudness = one(*cuts[0])
    for cut in cuts[1:]:
        loudness = loudness * one(*cut)
    return loudness


def scatter_about(own_key, extent, deviation, limit, cuts=(), held_as=jnp.bfloat16):
    level = shard_levels(own_key, extent, cuts, -0.22, 0.18) if cuts else 1.0
    values = jax.random.normal(own_key, extent, jnp.float32) * deviation * level
    return jnp.minimum(jnp.maximum(values, -limit), limit).astype(held_as)


def setup_inputs(seed: int = 0) -> dict:
    arg_keys = jax.random.split(jax.random.key(seed), 16)
    return {
        "tokens": scatter_about(arg_keys[0], (TOKENS, D), 1.0, 6.0, ((0, 32),)),
        "document_ends": draw_document_ends(jax.random.fold_in(arg_keys[15], 71), 0),
        "projector": scatter_about(arg_keys[2], (D, 3 * D), D ** -0.5, 0.125, ((0, 8),)),
        "projbias": scatter_about(arg_keys[3], (3 * D,), 0.5, 3.0, ((0, 8),)),
        "combiner": scatter_about(arg_keys[4], (D, D), (D // 16) ** -0.5, 0.5, ((0, 8),)),
        "combbias": scatter_about(arg_keys[5], (D,), 0.3, 2.0, ((0, 8),)),
        "expander": scatter_about(arg_keys[6], (D, FF), D ** -0.5, 0.125, ((0, 8),)),
        "expbias": scatter_about(arg_keys[7], (FF,), 0.5, 3.0, ((0, 8),)),
        "contractor": scatter_about(arg_keys[8], (FF, D), FF ** -0.5, 0.0625, ((0, 8),)),
        "contbias": scatter_about(arg_keys[9], (D,), 0.3, 2.0, ((0, 8),)),
        "attendgain": jnp.clip(1.0 + 0.18 * jax.random.normal(arg_keys[10], (D,), jnp.float32), 0.099609375, 1.8984375).astype(jnp.bfloat16),
        "attendshift": scatter_about(arg_keys[11], (D,), 0.3, 2.0, ((0, 8),)),
        "feedgain": jnp.clip(1.0 + 0.18 * jax.random.normal(arg_keys[12], (D,), jnp.float32), 0.099609375, 1.8984375).astype(jnp.bfloat16),
        "feedshift": scatter_about(arg_keys[13], (D,), 0.3, 2.0, ((0, 8),)),
        "cotangent": scatter_about(arg_keys[14], (TOKENS, D), 1.0, 6.0, ((0, 32),)),
    }


@jax.custom_vjp
def low(v):
    return lax.optimization_barrier(v.astype(jnp.bfloat16)).astype(jnp.float32)

@jax.custom_vjp
def low_back(v):
    return v

def low_keep(v):
    return (low(v), None)

def low_pass(kept, grad):
    return (grad,)

def back_keep(v):
    return (v, None)

def back_low(kept, grad):
    return (low(grad),)
low.defvjp(low_keep, low_pass)
low_back.defvjp(back_keep, back_low)
epsilon = 1e-05
masked_value = -1e+30
highest = lax.Precision.HIGHEST

def product(left, right):
    return jnp.dot(left, right, precision=highest)

def normalize(values):
    centre = lax.optimization_barrier(jnp.mean(values, axis=1, keepdims=True))
    centred = values - centre
    spread = lax.optimization_barrier(jnp.mean(centred * centred, axis=1, keepdims=True))
    inverse = lax.rsqrt(spread + epsilon)
    return (centred * inverse, inverse)

def layout(ends, count):
    index = jnp.arange(count, dtype=jnp.int32)
    passed = index[:, None] >= ends[None, :]
    document = lax.optimization_barrier(jnp.sum(passed.astype(jnp.int32), axis=1))
    begin = lax.optimization_barrier(jnp.max(jnp.where(passed, ends[None, :], 0), axis=1))
    position = (index - begin).astype(jnp.float32)
    allowed = (document[:, None] == document[None, :]) & (index[None, :] <= index[:, None])
    return (position, allowed, index < ends[-1])

def rotary_tables(position, rotary):
    half = rotary // 2
    freqs = jnp.exp(-jnp.arange(half, dtype=jnp.float32) * (2.0 / rotary) * math.log(10000.0))
    angles = position[:, None] * freqs[None, :]
    angles = jnp.concatenate([angles, angles], axis=1)
    return (jnp.cos(angles)[:, None, :], jnp.sin(angles)[:, None, :])

def rotate(values, cosine, sine, rotary):
    half = rotary // 2
    front = values[..., :rotary]
    turned = jnp.concatenate([-front[..., half:], front[..., :half]], axis=-1)
    return jnp.concatenate([front * cosine + turned * sine, values[..., rotary:]], axis=-1)

def device_forward(params, values, ends):
    projector, projbias, combiner, combbias, expander, expbias, contractor, contbias, attendgain, attendshift, feedgain, feedshift = params
    count, width = values.shape
    headsize = width // H
    position, allowed, live = layout(ends, count)
    cosine, sine = rotary_tables(position, ROT)
    normed, inverse = normalize(values)
    first_input = low(normed * attendgain + attendshift)
    second_input = low(normed * feedgain + feedshift)
    mixed = low_back(product(first_input, projector) + projbias)
    query = low(rotate(mixed[:, :width].reshape(count, H, headsize), cosine, sine, ROT))
    keys = low(rotate(mixed[:, width:2 * width].reshape(count, H, headsize), cosine, sine, ROT))
    vals = low(mixed[:, 2 * width:].reshape(count, H, headsize))
    scores = jnp.einsum('qhd,khd->hqk', query, keys, precision=highest) * (1.0 / math.sqrt(headsize))
    scores = low_back(jnp.where(allowed[None], scores, masked_value))
    peak = lax.optimization_barrier(jnp.max(scores, axis=2, keepdims=True))
    raised = jnp.exp(scores - peak)
    probs = raised / lax.optimization_barrier(jnp.sum(raised, axis=2, keepdims=True))
    context = jnp.einsum('hqk,khd->qhd', low(probs), vals, precision=highest).reshape(count, width)
    context = low(low_back(context))
    attended = product(context, combiner) + combbias
    hidden = low_back(product(second_input, expander) + expbias)
    active = low(jax.nn.gelu(hidden, approximate=False))
    feedout = product(active, contractor) + contbias
    return values + jnp.where(live[:, None], attended + feedout, 0.0)

def reference(tokens, document_ends, projector, projbias, combiner, combbias, expander, expbias, contractor, contbias, attendgain, attendshift, feedgain, feedshift, cotangent):
    params = tuple((item.astype(jnp.float32) for item in (projector, projbias, combiner, combbias, expander, expbias, contractor, contbias, attendgain, attendshift, feedgain, feedshift)))
    stacked = tokens.astype(jnp.float32).reshape(NDEV, ROWS, D)

    def forward(weights, inputs):

        def single(item):
            return device_forward(weights, item[0], item[1])
        return lax.map(jax.checkpoint(single), (inputs, document_ends))
    outputs, pullback = jax.vjp(forward, params, stacked)
    grads, input_grads = pullback(cotangent.astype(jnp.float32).reshape(NDEV, ROWS, D))
    block_output = outputs.reshape(TOKENS, D).astype(jnp.bfloat16)
    input_gradient = input_grads.reshape(TOKENS, D).astype(jnp.bfloat16)
    return (block_output, input_gradient, grads[0], grads[1], grads[2], grads[3], grads[4], grads[5], grads[6], grads[7], grads[8], grads[9], grads[10], grads[11])
```

```python
from functools import partial
import math

import jax
import jax.numpy as jnp
from jax import lax
from jax.sharding import PartitionSpec as P

H = 8
ROT = 64
BLOCK = 256

epsilon = 1e-05
masked_value = -1e30
f32 = jnp.float32
bf16 = jnp.bfloat16


def normalize(values):
    centre = jnp.mean(values, axis=1, keepdims=True)
    centred = values - centre
    spread = jnp.mean(centred * centred, axis=1, keepdims=True)
    inverse = lax.rsqrt(spread + epsilon)
    return (centred * inverse, inverse)


def layout(ends, count):
    index = jnp.arange(count, dtype=jnp.int32)
    passed = index[:, None] >= ends[None, :]
    document = jnp.sum(passed.astype(jnp.int32), axis=1)
    begin = jnp.max(jnp.where(passed, ends[None, :], 0), axis=1)
    position = (index - begin).astype(f32)
    allowed = (document[:, None] == document[None, :]) & (index[None, :] <= index[:, None])
    return (position, allowed, index < ends[-1])


def rotary_tables(position, rotary):
    half = rotary // 2
    freqs = jnp.exp(-jnp.arange(half, dtype=f32) * (2.0 / rotary) * math.log(10000.0))
    angles = position[..., None] * freqs
    angles = jnp.concatenate([angles, angles], axis=-1)
    return (jnp.cos(angles), jnp.sin(angles))


def rotate(values, cosine, sine, rotary):
    half = rotary // 2
    front = values[..., :rotary]
    turned = jnp.concatenate([-front[..., half:], front[..., :half]], axis=-1)
    return jnp.concatenate([front * cosine + turned * sine, values[..., rotary:]], axis=-1)


def unrotate(grads, cosine, sine, rotary):
    half = rotary // 2
    front = grads[..., :rotary]
    scaled = front * sine
    backward = jnp.concatenate([scaled[..., half:], -scaled[..., :half]], axis=-1)
    return jnp.concatenate([front * cosine + backward, grads[..., rotary:]], axis=-1)


def right_trans(left, right):
    return lax.dot_general(left, right, (((1,), (1,)), ((), ())), preferred_element_type=f32)


def left_trans(left, right):
    return lax.dot_general(left, right, (((0,), (0,)), ((), ())), preferred_element_type=f32)


def sharded_heads(
    tokens, document_ends, projector, projbias, combiner, combbias, expander, expbias,
    contractor, contbias, attendgain, attendshift, feedgain, feedshift, cotangent,
):
    count, width = tokens.shape
    n = lax.axis_size("shard")
    me = lax.axis_index("shard")
    head = width // H
    factor = 1.0 / math.sqrt(head)
    rows = width // n
    exp_cols = lax.all_to_all(expander, "shard", split_axis=1, concat_axis=0, tiled=True)
    proj_cols = lax.all_to_all(
        projector.reshape(rows, 3, n, head), "shard", split_axis=2, concat_axis=0, tiled=True
    ).reshape(width, 3 * head)
    vectors = jnp.concatenate(
        [projbias, combbias, contbias, attendgain, attendshift, feedgain, feedshift]
    )
    vectors = lax.all_gather(vectors, "shard", axis=0, tiled=False).astype(f32)
    wide = projbias.shape[0]
    full_projbias = vectors[:, :wide].reshape(3, n, head)
    my_projbias = lax.dynamic_index_in_dim(full_projbias, me, axis=1, keepdims=False).reshape(-1)
    gains = vectors[:, wide:].reshape(n, 6, rows).transpose(1, 0, 2).reshape(6, width)
    comb_b, cont_b, a_gain, a_shift, f_gain, f_shift = (gains[i] for i in range(6))
    ends = lax.all_gather(document_ends, "shard", axis=0, tiled=True)
    x = lax.all_gather(tokens, "shard", axis=0, tiled=True)
    position, allowed, live = jax.vmap(lambda e: layout(e, count))(ends)
    _, _, my_live = layout(document_ends[0], count)
    upstream = lax.all_gather(
        jnp.where(my_live[:, None], cotangent, jnp.zeros_like(cotangent)), "shard", axis=0, tiled=True
    )
    cosine, sine = rotary_tables(position, ROT)
    floated = x.astype(f32)
    normed, inverse = normalize(floated)
    first = (normed * a_gain + a_shift).astype(bf16)
    second = (normed * f_gain + f_shift).astype(bf16)
    mixed = jnp.dot(first, proj_cols, preferred_element_type=f32) + my_projbias
    mixed = mixed.reshape(n, count, 3, head)
    q = rotate(mixed[:, :, 0], cosine, sine, ROT).astype(bf16)
    k = rotate(mixed[:, :, 1], cosine, sine, ROT).astype(bf16)
    v = mixed[:, :, 2].astype(bf16)
    scores = jnp.einsum("bqd,bkd->bqk", q, k, preferred_element_type=f32) * factor
    scores = jnp.where(allowed, scores, masked_value)
    peak = jnp.max(scores, axis=2, keepdims=True)
    raised = jnp.exp(scores - peak)
    probs = raised / jnp.sum(raised, axis=2, keepdims=True)
    probs_low = probs.astype(bf16)
    context = jnp.einsum("bqk,bkd->bqd", probs_low, v, preferred_element_type=f32)
    context = context.reshape(n * count, head).astype(bf16)
    hidden = jnp.dot(second, exp_cols, preferred_element_type=f32) + expbias.astype(f32)
    activated, gelu_back = jax.vjp(partial(jax.nn.gelu, approximate=False), hidden)
    active = activated.astype(bf16)
    part = jnp.dot(context, combiner, preferred_element_type=f32) + jnp.dot(
        active, contractor, preferred_element_type=f32
    )
    summed = lax.psum_scatter(part.astype(bf16), "shard", scatter_dimension=0, tiled=True)
    block_output = tokens.astype(f32) + jnp.where(
        my_live[:, None], summed.astype(f32) + comb_b + cont_b, 0.0
    )
    block_output = block_output.astype(bf16)

    d_active = right_trans(upstream, contractor)
    d_hidden = gelu_back(d_active)[0].astype(bf16)
    contractor_part = left_trans(active, upstream).astype(bf16)
    combiner_part = left_trans(context, upstream).astype(bf16)
    expander_part = left_trans(second, d_hidden).astype(bf16)
    hidden_bias = jnp.sum(d_hidden, axis=0, dtype=f32)
    d_context = right_trans(upstream, combiner).astype(bf16).reshape(n, count, head)
    d_probs = jnp.einsum("bqd,bkd->bqk", d_context, v, preferred_element_type=f32)
    d_v = jnp.einsum("bqk,bqd->bkd", probs_low, d_context, preferred_element_type=f32)
    d_s = (probs * (d_probs - jnp.sum(d_probs * probs, axis=2, keepdims=True))).astype(bf16)
    d_q = jnp.einsum("bqk,bkd->bqd", d_s, k, preferred_element_type=f32) * factor
    d_k = jnp.einsum("bqk,bqd->bkd", d_s, q, preferred_element_type=f32) * factor
    d_mixed = jnp.concatenate(
        [unrotate(d_q, cosine, sine, ROT), unrotate(d_k, cosine, sine, ROT), d_v], axis=-1
    ).astype(bf16).reshape(n * count, 3 * head)
    projector_part = left_trans(first, d_mixed).astype(bf16)
    mixed_bias = jnp.sum(d_mixed, axis=0, dtype=f32)
    d_first = right_trans(d_mixed, proj_cols)
    d_second = right_trans(d_hidden, exp_cols)
    sums = jnp.stack(
        [
            jnp.sum(d_first * normed, axis=0),
            jnp.sum(d_first, axis=0),
            jnp.sum(d_second * normed, axis=0),
            jnp.sum(d_second, axis=0),
        ]
    )
    d_normed = lax.psum_scatter(
        (d_first * a_gain + d_second * f_gain).astype(bf16),
        "shard", scatter_dimension=0, tiled=True,
    ).astype(f32)
    own_normed, own_inverse = normalize(tokens.astype(f32))
    grad = cotangent.astype(f32) + own_inverse * (
        d_normed
        - jnp.mean(d_normed, axis=1, keepdims=True)
        - own_normed * jnp.mean(d_normed * own_normed, axis=1, keepdims=True)
    )
    input_gradient = grad.astype(bf16)

    expander_part = lax.all_to_all(expander_part, "shard", split_axis=0, concat_axis=1, tiled=True)
    projector_part = lax.all_to_all(
        projector_part.reshape(width, 3, 1, head), "shard", split_axis=0, concat_axis=2, tiled=True
    ).reshape(rows, 3 * width)
    out_bias = jnp.sum(upstream, axis=0, dtype=f32)
    mixed_full = jnp.zeros((3, n, head), f32)
    mixed_full = lax.dynamic_update_slice(mixed_full, mixed_bias.reshape(3, 1, head), (0, me, 0))
    vector = jnp.concatenate(
        [
            mixed_full.reshape(n, wide),
            sums.reshape(4, n, rows).transpose(1, 0, 2).reshape(n, 4 * rows),
        ],
        axis=1,
    )
    vector = lax.psum_scatter(vector, "shard", scatter_dimension=0, tiled=True)[0]
    own_out = lax.dynamic_slice(out_bias, (me * rows,), (rows,))
    vector = lax.psum(jnp.concatenate([vector, own_out, hidden_bias]), "rep")
    mixed_bias = vector[:wide]
    a, b, c, d, out_bias = (vector[wide + i * rows : wide + (i + 1) * rows] for i in range(5))
    hidden_bias = vector[wide + 5 * rows :]
    projector_part, combiner_part, expander_part, contractor_part = (
        item.astype(f32)
        for item in lax.psum(
            (projector_part, combiner_part, expander_part, contractor_part), "rep"
        )
    )
    return (
        block_output, input_gradient, projector_part, mixed_bias, combiner_part, out_bias,
        expander_part, hidden_bias, contractor_part, out_bias, a, b, c, d,
    )


def masked_scores(query_low, keys_low, allowed, factor):
    scores = (
        jnp.einsum("qhd,khd->hqk", query_low, keys_low, preferred_element_type=jnp.float32) * factor
    )
    return jnp.where(allowed[None], scores, masked_value)


def weight_sums(left, right):
    piece = lax.slice_in_dim(
        left, 0, left.shape[1] // lax.axis_size("shard") * lax.axis_size("shard"), axis=1
    )
    return lax.psum_scatter(
        left_trans(piece, right).astype(jnp.bfloat16), "shard", scatter_dimension=0, tiled=True
    ).astype(jnp.float32)


def local(
    tokens,
    document_ends,
    projector,
    projbias,
    combiner,
    combbias,
    expander,
    expbias,
    contractor,
    contbias,
    attendgain,
    attendshift,
    feedgain,
    feedshift,
    cotangent,
):
    count, width = tokens.shape
    headsize = width // H
    factor = 1.0 / math.sqrt(headsize)
    position, allowed, live = layout(document_ends[0], count)
    cosine, sine = rotary_tables(position, ROT)
    cosine, sine = cosine[:, None, :], sine[:, None, :]
    (
        full_projector,
        full_combiner,
        full_projbias,
        full_combbias,
        gain_attend,
        shift_attend,
        gain_feed,
        shift_feed,
    ) = (
        lax.all_gather(projector, "shard", axis=0, tiled=True),
        lax.all_gather(combiner, "shard", axis=0, tiled=True),
        lax.all_gather(projbias, "shard", axis=0, tiled=True),
        lax.all_gather(combbias, "shard", axis=0, tiled=True),
        lax.all_gather(attendgain, "shard", axis=0, tiled=True),
        lax.all_gather(attendshift, "shard", axis=0, tiled=True),
        lax.all_gather(feedgain, "shard", axis=0, tiled=True),
        lax.all_gather(feedshift, "shard", axis=0, tiled=True),
    )
    floated = tokens.astype(jnp.float32)
    normed, inverse = normalize(floated)
    first_input = (normed * gain_attend + shift_attend).astype(jnp.bfloat16)
    second_input = (normed * gain_feed + shift_feed).astype(jnp.bfloat16)
    mixed = jnp.dot(first_input, full_projector, preferred_element_type=jnp.float32) + full_projbias
    query_low = rotate(mixed[:, :width].reshape(count, H, headsize), cosine, sine, ROT).astype(
        jnp.bfloat16
    )
    keys_low = rotate(
        mixed[:, width : 2 * width].reshape(count, H, headsize), cosine, sine, ROT
    ).astype(jnp.bfloat16)
    values_low = mixed[:, 2 * width :].reshape(count, H, headsize).astype(jnp.bfloat16)
    scores = masked_scores(query_low, keys_low, allowed, factor)
    peak = jnp.max(scores, axis=2, keepdims=True)
    raised = jnp.exp(scores - peak)
    total = jnp.sum(raised, axis=2, keepdims=True)
    probs_low = (raised / total).astype(jnp.bfloat16)
    logsum = peak + jnp.log(total)
    context = jnp.einsum("hqk,khd->qhd", probs_low, values_low, preferred_element_type=jnp.float32)
    context = context.reshape(count, width).astype(jnp.bfloat16)
    attended = jnp.dot(context, full_combiner, preferred_element_type=jnp.float32) + full_combbias
    full_expander, full_contractor, full_expbias, full_contbias = (
        lax.all_gather(expander, "shard", axis=0, tiled=True),
        lax.all_gather(contractor, "shard", axis=0, tiled=True),
        lax.all_gather(expbias, "shard", axis=0, tiled=True),
        lax.all_gather(contbias, "shard", axis=0, tiled=True),
    )
    hidden = jnp.dot(second_input, full_expander, preferred_element_type=jnp.float32) + full_expbias
    activated, gelu_back = jax.vjp(partial(jax.nn.gelu, approximate=False), hidden)
    active_low = activated.astype(jnp.bfloat16)
    feedout = (
        jnp.dot(active_low, full_contractor, preferred_element_type=jnp.float32) + full_contbias
    )
    block_output = (floated + jnp.where(live[:, None], attended + feedout, 0.0)).astype(
        jnp.bfloat16
    )
    (
        back_projector,
        back_combiner,
        back_expander,
        back_contractor,
        back_gain_attend,
        back_gain_feed,
    ) = (
        lax.all_gather(projector, "shard", axis=0, tiled=True),
        lax.all_gather(combiner, "shard", axis=0, tiled=True),
        lax.all_gather(expander, "shard", axis=0, tiled=True),
        lax.all_gather(contractor, "shard", axis=0, tiled=True),
        lax.all_gather(attendgain, "shard", axis=0, tiled=True),
        lax.all_gather(feedgain, "shard", axis=0, tiled=True),
    )
    upstream = jnp.where(live[:, None], cotangent, jnp.zeros_like(cotangent))
    contractor_part = weight_sums(active_low, upstream)
    combiner_part = weight_sums(context, upstream)
    output_bias = jnp.sum(upstream, axis=0, dtype=jnp.float32)
    d_active = right_trans(upstream, back_contractor)
    d_hidden = gelu_back(d_active)[0].astype(jnp.bfloat16)
    expander_part = weight_sums(second_input, d_hidden)
    hidden_bias = jnp.sum(d_hidden, axis=0, dtype=jnp.float32)
    d_second = right_trans(d_hidden, back_expander)
    d_context = (
        right_trans(upstream, back_combiner).reshape(count, H, headsize).astype(jnp.bfloat16)
    )
    scores_again = masked_scores(query_low, keys_low, allowed, factor)
    probs = jnp.exp(scores_again - logsum)
    d_probs = jnp.einsum("qhd,khd->hqk", d_context, values_low, preferred_element_type=jnp.float32)
    d_values = jnp.einsum("hqk,qhd->khd", probs_low, d_context, preferred_element_type=jnp.float32)
    d_scores = (probs * (d_probs - jnp.sum(d_probs * probs, axis=2, keepdims=True))).astype(
        jnp.bfloat16
    )
    d_query = (
        jnp.einsum("hqk,khd->qhd", d_scores, keys_low, preferred_element_type=jnp.float32) * factor
    )
    d_keys = (
        jnp.einsum("hqk,qhd->khd", d_scores, query_low, preferred_element_type=jnp.float32) * factor
    )
    d_mixed = jnp.concatenate(
        [
            unrotate(d_query, cosine, sine, ROT).reshape(count, width),
            unrotate(d_keys, cosine, sine, ROT).reshape(count, width),
            d_values.reshape(count, width),
        ],
        axis=1,
    ).astype(jnp.bfloat16)
    projector_part = weight_sums(first_input, d_mixed)
    mixed_bias = jnp.sum(d_mixed, axis=0, dtype=jnp.float32)
    d_first = right_trans(d_mixed, back_projector)
    attend_scale = jnp.sum(d_first * normed, axis=0)
    attend_offset = jnp.sum(d_first, axis=0)
    feed_scale = jnp.sum(d_second * normed, axis=0)
    feed_offset = jnp.sum(d_second, axis=0)
    d_normed = d_first * back_gain_attend + d_second * back_gain_feed
    grad_float = cotangent.astype(jnp.float32) + inverse * (
        d_normed
        - jnp.mean(d_normed, axis=1, keepdims=True)
        - normed * jnp.mean(d_normed * normed, axis=1, keepdims=True)
    )
    input_gradient = grad_float.astype(jnp.bfloat16)
    mixed_bias, output_bias, hidden_bias, attend_scale, attend_offset, feed_scale, feed_offset = (
        lax.psum_scatter(
            mixed_bias.astype(jnp.bfloat16), "shard", scatter_dimension=0, tiled=True
        ).astype(jnp.float32),
        lax.psum_scatter(
            output_bias.astype(jnp.bfloat16), "shard", scatter_dimension=0, tiled=True
        ).astype(jnp.float32),
        lax.psum_scatter(
            hidden_bias.astype(jnp.bfloat16), "shard", scatter_dimension=0, tiled=True
        ).astype(jnp.float32),
        lax.psum_scatter(
            attend_scale.astype(jnp.bfloat16), "shard", scatter_dimension=0, tiled=True
        ).astype(jnp.float32),
        lax.psum_scatter(
            attend_offset.astype(jnp.bfloat16), "shard", scatter_dimension=0, tiled=True
        ).astype(jnp.float32),
        lax.psum_scatter(
            feed_scale.astype(jnp.bfloat16), "shard", scatter_dimension=0, tiled=True
        ).astype(jnp.float32),
        lax.psum_scatter(
            feed_offset.astype(jnp.bfloat16), "shard", scatter_dimension=0, tiled=True
        ).astype(jnp.float32),
    )
    (
        projector_part,
        mixed_bias,
        combiner_part,
        output_bias,
        expander_part,
        hidden_bias,
        contractor_part,
        attend_scale,
        attend_offset,
        feed_scale,
        feed_offset,
    ) = (
        lax.psum(projector_part.astype(jnp.bfloat16), "rep").astype(jnp.float32),
        lax.psum(mixed_bias.astype(jnp.bfloat16), "rep").astype(jnp.float32),
        lax.psum(combiner_part.astype(jnp.bfloat16), "rep").astype(jnp.float32),
        lax.psum(output_bias.astype(jnp.bfloat16), "rep").astype(jnp.float32),
        lax.psum(expander_part.astype(jnp.bfloat16), "rep").astype(jnp.float32),
        lax.psum(hidden_bias.astype(jnp.bfloat16), "rep").astype(jnp.float32),
        lax.psum(contractor_part.astype(jnp.bfloat16), "rep").astype(jnp.float32),
        lax.psum(attend_scale.astype(jnp.bfloat16), "rep").astype(jnp.float32),
        lax.psum(attend_offset.astype(jnp.bfloat16), "rep").astype(jnp.float32),
        lax.psum(feed_scale.astype(jnp.bfloat16), "rep").astype(jnp.float32),
        lax.psum(feed_offset.astype(jnp.bfloat16), "rep").astype(jnp.float32),
    )
    return (
        block_output,
        input_gradient,
        projector_part,
        mixed_bias,
        combiner_part,
        output_bias,
        expander_part,
        hidden_bias,
        contractor_part,
        output_bias,
        attend_scale,
        attend_offset,
        feed_scale,
        feed_offset,
    )


def solution(mesh):
    placed = (
        P(("rep", "shard"), None),
        P(("rep", "shard"), None),
        P("shard", None),
        P("shard"),
        P("shard", None),
        P("shard"),
        P("shard", None),
        P("shard"),
        P("shard", None),
        P("shard"),
        P("shard"),
        P("shard"),
        P("shard"),
        P("shard"),
        P(("rep", "shard"), None),
    )
    return jax.shard_map(
        sharded_heads if mesh.shape["shard"] == H else local,
        mesh=mesh,
        in_specs=placed,
        out_specs=(
            P(("rep", "shard"), None),
            P(("rep", "shard"), None),
            P("shard", None),
            P("shard"),
            P("shard", None),
            P("shard"),
            P("shard", None),
            P("shard"),
            P("shard", None),
            P("shard"),
            P("shard"),
            P("shard"),
            P("shard"),
            P("shard"),
        ),
        check_vma=False,
    )
```

```python
from functools import partial
import math

import jax
import jax.numpy as jnp
from jax import lax
from jax.experimental import pallas as pl
from jax.experimental.pallas import tpu as pltpu
from jax.sharding import PartitionSpec as P

H = 8
ROT = 64
DOCS = 4
LANES = 128
VMEM_LIMIT = 60 * 1024 * 1024

epsilon = 1e-05
masked_value = -1e30
f32 = jnp.float32
bf16 = jnp.bfloat16


def normalize(values):
    centre = jnp.mean(values, axis=1, keepdims=True)
    centred = values - centre
    spread = jnp.mean(centred * centred, axis=1, keepdims=True)
    inverse = lax.rsqrt(spread + epsilon)
    return (centred * inverse, inverse)


def layout(ends, count):
    index = jnp.arange(count, dtype=jnp.int32)
    passed = index[:, None] >= ends[None, :]
    document = jnp.sum(passed.astype(jnp.int32), axis=1)
    begin = jnp.max(jnp.where(passed, ends[None, :], 0), axis=1)
    position = (index - begin).astype(f32)
    allowed = (document[:, None] == document[None, :]) & (index[None, :] <= index[:, None])
    return (position, allowed, index < ends[-1])


def rotary_tables(position, rotary):
    half = rotary // 2
    freqs = jnp.exp(-jnp.arange(half, dtype=f32) * (2.0 / rotary) * math.log(10000.0))
    angles = position[..., None] * freqs
    angles = jnp.concatenate([angles, angles], axis=-1)
    return (jnp.cos(angles), jnp.sin(angles))


def rotate(values, cosine, sine, rotary):
    half = rotary // 2
    front = values[..., :rotary]
    turned = jnp.concatenate([-front[..., half:], front[..., :half]], axis=-1)
    return jnp.concatenate([front * cosine + turned * sine, values[..., rotary:]], axis=-1)


def unrotate(grads, cosine, sine, rotary):
    half = rotary // 2
    front = grads[..., :rotary]
    scaled = front * sine
    backward = jnp.concatenate([scaled[..., half:], -scaled[..., :half]], axis=-1)
    return jnp.concatenate([front * cosine + backward, grads[..., rotary:]], axis=-1)


def right_trans(left, right):
    return lax.dot_general(left, right, (((1,), (1,)), ((), ())), preferred_element_type=f32)


def left_trans(left, right):
    return lax.dot_general(left, right, (((0,), (0,)), ((), ())), preferred_element_type=f32)


def masked_scores(query_low, keys_low, allowed, factor):
    scores = (
        jnp.einsum("qhd,khd->hqk", query_low, keys_low, preferred_element_type=jnp.float32) * factor
    )
    return jnp.where(allowed[None], scores, masked_value)


def weight_sums(left, right):
    piece = lax.slice_in_dim(
        left, 0, left.shape[1] // lax.axis_size("shard") * lax.axis_size("shard"), axis=1
    )
    return lax.psum_scatter(
        left_trans(piece, right).astype(jnp.bfloat16), "shard", scatter_dimension=0, tiled=True
    ).astype(jnp.float32)


def local(
    tokens,
    document_ends,
    projector,
    projbias,
    combiner,
    combbias,
    expander,
    expbias,
    contractor,
    contbias,
    attendgain,
    attendshift,
    feedgain,
    feedshift,
    cotangent,
):
    count, width = tokens.shape
    headsize = width // H
    factor = 1.0 / math.sqrt(headsize)
    position, allowed, live = layout(document_ends[0], count)
    cosine, sine = rotary_tables(position, ROT)
    cosine, sine = cosine[:, None, :], sine[:, None, :]
    (
        full_projector,
        full_combiner,
        full_projbias,
        full_combbias,
        gain_attend,
        shift_attend,
        gain_feed,
        shift_feed,
    ) = (
        lax.all_gather(projector, "shard", axis=0, tiled=True),
        lax.all_gather(combiner, "shard", axis=0, tiled=True),
        lax.all_gather(projbias, "shard", axis=0, tiled=True),
        lax.all_gather(combbias, "shard", axis=0, tiled=True),
        lax.all_gather(attendgain, "shard", axis=0, tiled=True),
        lax.all_gather(attendshift, "shard", axis=0, tiled=True),
        lax.all_gather(feedgain, "shard", axis=0, tiled=True),
        lax.all_gather(feedshift, "shard", axis=0, tiled=True),
    )
    floated = tokens.astype(jnp.float32)
    normed, inverse = normalize(floated)
    first_input = (normed * gain_attend + shift_attend).astype(jnp.bfloat16)
    second_input = (normed * gain_feed + shift_feed).astype(jnp.bfloat16)
    mixed = jnp.dot(first_input, full_projector, preferred_element_type=jnp.float32) + full_projbias
    query_low = rotate(mixed[:, :width].reshape(count, H, headsize), cosine, sine, ROT).astype(
        jnp.bfloat16
    )
    keys_low = rotate(
        mixed[:, width : 2 * width].reshape(count, H, headsize), cosine, sine, ROT
    ).astype(jnp.bfloat16)
    values_low = mixed[:, 2 * width :].reshape(count, H, headsize).astype(jnp.bfloat16)
    scores = masked_scores(query_low, keys_low, allowed, factor)
    peak = jnp.max(scores, axis=2, keepdims=True)
    raised = jnp.exp(scores - peak)
    total = jnp.sum(raised, axis=2, keepdims=True)
    probs_low = (raised / total).astype(jnp.bfloat16)
    logsum = peak + jnp.log(total)
    context = jnp.einsum("hqk,khd->qhd", probs_low, values_low, preferred_element_type=jnp.float32)
    context = context.reshape(count, width).astype(jnp.bfloat16)
    attended = jnp.dot(context, full_combiner, preferred_element_type=jnp.float32) + full_combbias
    full_expander, full_contractor, full_expbias, full_contbias = (
        lax.all_gather(expander, "shard", axis=0, tiled=True),
        lax.all_gather(contractor, "shard", axis=0, tiled=True),
        lax.all_gather(expbias, "shard", axis=0, tiled=True),
        lax.all_gather(contbias, "shard", axis=0, tiled=True),
    )
    hidden = jnp.dot(second_input, full_expander, preferred_element_type=jnp.float32) + full_expbias
    activated, gelu_back = jax.vjp(partial(jax.nn.gelu, approximate=False), hidden)
    active_low = activated.astype(jnp.bfloat16)
    feedout = (
        jnp.dot(active_low, full_contractor, preferred_element_type=jnp.float32) + full_contbias
    )
    block_output = (floated + jnp.where(live[:, None], attended + feedout, 0.0)).astype(
        jnp.bfloat16
    )
    (
        back_projector,
        back_combiner,
        back_expander,
        back_contractor,
        back_gain_attend,
        back_gain_feed,
    ) = (
        lax.all_gather(projector, "shard", axis=0, tiled=True),
        lax.all_gather(combiner, "shard", axis=0, tiled=True),
        lax.all_gather(expander, "shard", axis=0, tiled=True),
        lax.all_gather(contractor, "shard", axis=0, tiled=True),
        lax.all_gather(attendgain, "shard", axis=0, tiled=True),
        lax.all_gather(feedgain, "shard", axis=0, tiled=True),
    )
    upstream = jnp.where(live[:, None], cotangent, jnp.zeros_like(cotangent))
    contractor_part = weight_sums(active_low, upstream)
    combiner_part = weight_sums(context, upstream)
    output_bias = jnp.sum(upstream, axis=0, dtype=jnp.float32)
    d_active = right_trans(upstream, back_contractor)
    d_hidden = gelu_back(d_active)[0].astype(jnp.bfloat16)
    expander_part = weight_sums(second_input, d_hidden)
    hidden_bias = jnp.sum(d_hidden, axis=0, dtype=jnp.float32)
    d_second = right_trans(d_hidden, back_expander)
    d_context = (
        right_trans(upstream, back_combiner).reshape(count, H, headsize).astype(jnp.bfloat16)
    )
    scores_again = masked_scores(query_low, keys_low, allowed, factor)
    probs = jnp.exp(scores_again - logsum)
    d_probs = jnp.einsum("qhd,khd->hqk", d_context, values_low, preferred_element_type=jnp.float32)
    d_values = jnp.einsum("hqk,qhd->khd", probs_low, d_context, preferred_element_type=jnp.float32)
    d_scores = (probs * (d_probs - jnp.sum(d_probs * probs, axis=2, keepdims=True))).astype(
        jnp.bfloat16
    )
    d_query = (
        jnp.einsum("hqk,khd->qhd", d_scores, keys_low, preferred_element_type=jnp.float32) * factor
    )
    d_keys = (
        jnp.einsum("hqk,qhd->khd", d_scores, query_low, preferred_element_type=jnp.float32) * factor
    )
    d_mixed = jnp.concatenate(
        [
            unrotate(d_query, cosine, sine, ROT).reshape(count, width),
            unrotate(d_keys, cosine, sine, ROT).reshape(count, width),
            d_values.reshape(count, width),
        ],
        axis=1,
    ).astype(jnp.bfloat16)
    projector_part = weight_sums(first_input, d_mixed)
    mixed_bias = jnp.sum(d_mixed, axis=0, dtype=jnp.float32)
    d_first = right_trans(d_mixed, back_projector)
    attend_scale = jnp.sum(d_first * normed, axis=0)
    attend_offset = jnp.sum(d_first, axis=0)
    feed_scale = jnp.sum(d_second * normed, axis=0)
    feed_offset = jnp.sum(d_second, axis=0)
    d_normed = d_first * back_gain_attend + d_second * back_gain_feed
    grad_float = cotangent.astype(jnp.float32) + inverse * (
        d_normed
        - jnp.mean(d_normed, axis=1, keepdims=True)
        - normed * jnp.mean(d_normed * normed, axis=1, keepdims=True)
    )
    input_gradient = grad_float.astype(jnp.bfloat16)
    mixed_bias, output_bias, hidden_bias, attend_scale, attend_offset, feed_scale, feed_offset = (
        lax.psum_scatter(
            mixed_bias.astype(jnp.bfloat16), "shard", scatter_dimension=0, tiled=True
        ).astype(jnp.float32),
        lax.psum_scatter(
            output_bias.astype(jnp.bfloat16), "shard", scatter_dimension=0, tiled=True
        ).astype(jnp.float32),
        lax.psum_scatter(
            hidden_bias.astype(jnp.bfloat16), "shard", scatter_dimension=0, tiled=True
        ).astype(jnp.float32),
        lax.psum_scatter(
            attend_scale.astype(jnp.bfloat16), "shard", scatter_dimension=0, tiled=True
        ).astype(jnp.float32),
        lax.psum_scatter(
            attend_offset.astype(jnp.bfloat16), "shard", scatter_dimension=0, tiled=True
        ).astype(jnp.float32),
        lax.psum_scatter(
            feed_scale.astype(jnp.bfloat16), "shard", scatter_dimension=0, tiled=True
        ).astype(jnp.float32),
        lax.psum_scatter(
            feed_offset.astype(jnp.bfloat16), "shard", scatter_dimension=0, tiled=True
        ).astype(jnp.float32),
    )
    (
        projector_part,
        mixed_bias,
        combiner_part,
        output_bias,
        expander_part,
        hidden_bias,
        contractor_part,
        attend_scale,
        attend_offset,
        feed_scale,
        feed_offset,
    ) = (
        lax.psum(projector_part.astype(jnp.bfloat16), "rep").astype(jnp.float32),
        lax.psum(mixed_bias.astype(jnp.bfloat16), "rep").astype(jnp.float32),
        lax.psum(combiner_part.astype(jnp.bfloat16), "rep").astype(jnp.float32),
        lax.psum(output_bias.astype(jnp.bfloat16), "rep").astype(jnp.float32),
        lax.psum(expander_part.astype(jnp.bfloat16), "rep").astype(jnp.float32),
        lax.psum(hidden_bias.astype(jnp.bfloat16), "rep").astype(jnp.float32),
        lax.psum(contractor_part.astype(jnp.bfloat16), "rep").astype(jnp.float32),
        lax.psum(attend_scale.astype(jnp.bfloat16), "rep").astype(jnp.float32),
        lax.psum(attend_offset.astype(jnp.bfloat16), "rep").astype(jnp.float32),
        lax.psum(feed_scale.astype(jnp.bfloat16), "rep").astype(jnp.float32),
        lax.psum(feed_offset.astype(jnp.bfloat16), "rep").astype(jnp.float32),
    )
    return (
        block_output,
        input_gradient,
        projector_part,
        mixed_bias,
        combiner_part,
        output_bias,
        expander_part,
        hidden_bias,
        contractor_part,
        output_bias,
        attend_scale,
        attend_offset,
        feed_scale,
        feed_offset,
    )


def lane_half(shape):
    return lax.broadcasted_iota(jnp.int32, shape, 1) < ROT // 2


def turn(front, signed):
    moved = jnp.where(
        lane_half(front.shape),
        pltpu.roll(front, LANES - ROT // 2, 1),
        pltpu.roll(front, ROT // 2, 1),
    )
    return moved * signed


def rotated(values, cosine, signed):
    front = values[:, :LANES]
    return jnp.concatenate([front * cosine + turn(front, signed), values[:, LANES:]], axis=1)


def unrotated(grads, cosine, signed):
    front = grads[:, :LANES]
    return jnp.concatenate([front * cosine - turn(front, signed), grads[:, LANES:]], axis=1)


def block_allowed(ends_ref, block, count):
    row = lax.broadcasted_iota(jnp.int32, (count, 1), 0)
    column = lax.broadcasted_iota(jnp.int32, (1, count), 1)
    row_doc = jnp.zeros((count, 1), jnp.int32)
    column_doc = jnp.zeros((1, count), jnp.int32)
    for i in range(DOCS):
        end = ends_ref[block, i]
        row_doc += (row >= end).astype(jnp.int32)
        column_doc += (column >= end).astype(jnp.int32)
    return (row_doc == column_doc) & (column <= row)


def dot(left, right):
    return jnp.dot(left, right, preferred_element_type=f32)


def softmax(q, k, allowed):
    scores = right_trans(q, k) * (1.0 / math.sqrt(q.shape[1]))
    scores = jnp.where(allowed, scores, masked_value)
    raised = jnp.exp(scores - jnp.max(scores, axis=1, keepdims=True))
    return raised / jnp.sum(raised, axis=1, keepdims=True)


def forward_kernel(
    ends_ref, x_ref, cos_ref, sin_ref, norms_ref, pbias_ref, ebias_ref,
    proj_ref, exp_ref, comb_ref, cont_ref,
    h1_ref, h2_ref, qkv_ref, ca_ref, slope_ref, part_ref,
):
    block = pl.program_id(0)
    count, width = x_ref.shape
    head = comb_ref.shape[0]
    units = exp_ref.shape[1]
    normed, _ = normalize(x_ref[...].astype(f32))
    first = (normed * norms_ref[0:1, :] + norms_ref[1:2, :]).astype(bf16)
    h1_ref[...] = first
    second = (normed * norms_ref[2:3, :] + norms_ref[3:4, :]).astype(bf16)
    h2_ref[...] = second
    cosine, signed = cos_ref[...], sin_ref[...]
    mixed = dot(first, proj_ref[...]) + pbias_ref[...]
    q = rotated(mixed[:, :head], cosine, signed).astype(bf16)
    k = rotated(mixed[:, head : 2 * head], cosine, signed).astype(bf16)
    v = mixed[:, 2 * head :].astype(bf16)
    qkv_ref[:, :head] = q
    qkv_ref[:, head : 2 * head] = k
    qkv_ref[:, 2 * head :] = v
    probs = softmax(q, k, block_allowed(ends_ref, block, count)).astype(bf16)
    ca_ref[:, :head] = dot(probs, v).astype(bf16)
    tile = min(256, units)
    for start in range(0, units, tile):
        hidden = dot(second, exp_ref[:, start : start + tile]) + ebias_ref[:, start : start + tile]
        below = 0.5 + 0.5 * lax.erf(hidden * math.sqrt(0.5))
        ca_ref[:, head + start : head + start + tile] = (hidden * below).astype(bf16)
        density = jnp.exp(hidden * hidden * -0.5) * (1.0 / math.sqrt(2.0 * math.pi))
        slope_ref[:, start : start + tile] = (below + hidden * density).astype(bf16)
    tile = min(512, width)
    for start in range(0, width, tile):
        cut = slice(start, start + tile)
        part = dot(ca_ref[:, :head], comb_ref[:, cut]) + dot(ca_ref[:, head:], cont_ref[:, cut])
        part_ref[:, cut] = part.astype(bf16)


def backward_kernel(
    ends_ref, x_ref, up_ref, cos_ref, sin_ref, norms_ref, qkv_ref, slope_ref,
    proj_ref, exp_ref, comb_ref, cont_ref,
    dh_ref, dm_ref, dn_ref, sums_ref, hbias_ref, mbias_ref,
):
    block = pl.program_id(0)
    count, width = x_ref.shape
    head = comb_ref.shape[0]
    units = exp_ref.shape[1]
    up = up_ref[...]

    @pl.when(block == 0)
    def _():
        sums_ref[...] = jnp.zeros_like(sums_ref)
        hbias_ref[...] = jnp.zeros_like(hbias_ref)
        mbias_ref[...] = jnp.zeros_like(mbias_ref)

    d_context = right_trans(up, comb_ref[...]).astype(bf16)
    q, k, v = qkv_ref[:, :head], qkv_ref[:, head : 2 * head], qkv_ref[:, 2 * head :]
    probs = softmax(q, k, block_allowed(ends_ref, block, count))
    d_probs = right_trans(d_context, v)
    d_v = left_trans(probs.astype(bf16), d_context)
    d_s = probs * (d_probs - jnp.sum(d_probs * probs, axis=1, keepdims=True))
    d_s = d_s.astype(bf16)
    factor = 1.0 / math.sqrt(head)
    cosine, signed = cos_ref[...], sin_ref[...]
    d_q = unrotated(dot(d_s, k) * factor, cosine, signed).astype(bf16)
    d_k = unrotated(left_trans(d_s, q) * factor, cosine, signed).astype(bf16)
    dm_ref[:, :head] = d_q
    dm_ref[:, head : 2 * head] = d_k
    dm_ref[:, 2 * head :] = d_v.astype(bf16)
    mbias_ref[...] += jnp.sum(dm_ref[...].astype(f32), axis=0, keepdims=True)
    tile = min(256, units)
    for start in range(0, units, tile):
        cut = slice(start, start + tile)
        d_hidden = (right_trans(up, cont_ref[cut, :]) * slope_ref[:, cut].astype(f32)).astype(bf16)
        dh_ref[:, cut] = d_hidden
        hbias_ref[:, cut] += jnp.sum(d_hidden.astype(f32), axis=0, keepdims=True)
    x = x_ref[...].astype(f32)
    centre = jnp.mean(x, axis=1, keepdims=True)
    spread = jnp.mean((x - centre) * (x - centre), axis=1, keepdims=True)
    inverse = lax.rsqrt(spread + epsilon)
    tile = min(256, width)
    for start in range(0, width, tile):
        cut = slice(start, start + tile)
        normed = (x_ref[:, cut].astype(f32) - centre) * inverse
        d_first = right_trans(dm_ref[...], proj_ref[cut, :])
        d_second = right_trans(dh_ref[...], exp_ref[cut, :])
        dn_ref[:, cut] = (
            d_first * norms_ref[0:1, cut] + d_second * norms_ref[2:3, cut]
        ).astype(bf16)
        sums_ref[0:1, cut] += jnp.sum(d_first * normed, axis=0, keepdims=True)
        sums_ref[1:2, cut] += jnp.sum(d_first, axis=0, keepdims=True)
        sums_ref[2:3, cut] += jnp.sum(d_second * normed, axis=0, keepdims=True)
        sums_ref[3:4, cut] += jnp.sum(d_second, axis=0, keepdims=True)


def rows_spec(count, columns):
    return pl.BlockSpec((count, columns), lambda i, *_: (i, 0))


def whole_spec(array):
    return pl.BlockSpec(array.shape, lambda i, *_: (0, 0), pipeline_mode=pl.Buffered(1))


def acc_spec(rows, columns):
    return pl.BlockSpec((rows, columns), lambda i, *_: (0, 0))


def forward_block(count, ends, x, cosine, signed, norms, pbias, ebias, proj, exp, comb, cont):
    slots, width = x.shape
    units, mix, head = exp.shape[1], proj.shape[1], comb.shape[0]
    flops = 2 * slots * width * (mix + 2 * units + head)
    wide = [width, width, mix, head + units, units, width]
    return pl.pallas_call(
        forward_kernel,
        grid_spec=pltpu.PrefetchScalarGridSpec(
            num_scalar_prefetch=1,
            grid=(slots // count,),
            in_specs=[
                rows_spec(count, width), rows_spec(count, LANES), rows_spec(count, LANES),
            ] + [whole_spec(a) for a in (norms, pbias, ebias, proj, exp, comb, cont)],
            out_specs=[rows_spec(count, w) for w in wide],
        ),
        out_shape=[jax.ShapeDtypeStruct((slots, w), bf16) for w in wide],
        compiler_params=pltpu.CompilerParams(vmem_limit_bytes=VMEM_LIMIT),
        cost_estimate=pl.CostEstimate(
            flops=flops, bytes_accessed=2 * slots * sum(wide), transcendentals=0
        ),
    )(ends, x, cosine, signed, norms, pbias, ebias, proj, exp, comb, cont)


def backward_block(count, ends, x, up, cosine, signed, norms, qkv, slope, proj, exp, comb, cont):
    slots, width = x.shape
    units, mix, head = exp.shape[1], proj.shape[1], comb.shape[0]
    flops = 2 * slots * width * (mix + 2 * units + head)
    return pl.pallas_call(
        backward_kernel,
        grid_spec=pltpu.PrefetchScalarGridSpec(
            num_scalar_prefetch=1,
            grid=(slots // count,),
            in_specs=[
                rows_spec(count, width), rows_spec(count, width),
                rows_spec(count, LANES), rows_spec(count, LANES), whole_spec(norms),
                rows_spec(count, mix), rows_spec(count, units),
            ] + [whole_spec(a) for a in (proj, exp, comb, cont)],
            out_specs=[rows_spec(count, w) for w in (units, mix, width)]
            + [acc_spec(4, width), acc_spec(1, units), acc_spec(1, mix)],
        ),
        out_shape=[jax.ShapeDtypeStruct((slots, w), bf16) for w in (units, mix, width)]
        + [jax.ShapeDtypeStruct(s, f32) for s in ((4, width), (1, units), (1, mix))],
        compiler_params=pltpu.CompilerParams(vmem_limit_bytes=VMEM_LIMIT),
        cost_estimate=pl.CostEstimate(
            flops=flops, bytes_accessed=2 * slots * (3 * width + 2 * units), transcendentals=0
        ),
    )(ends, x, up, cosine, signed, norms, qkv, slope, proj, exp, comb, cont)


def links(move):
    pairs = []
    for y in range(2):
        for x in range(2):
            for z in range(4):
                for c in range(2):
                    ty, tx, tz, tc = move(y, x, z, c)
                    pairs.append((((y * 2 + x) * 4 + z) * 2 + c, ((ty * 2 + tx) * 4 + tz % 4) * 2 + tc))
    return pairs


def send(value, move):
    return lax.ppermute(value, ("rep", "shard"), links(move))


def by_core(value):
    return send(value, lambda y, x, z, c: (y, x, z, 1 - c))


def by_x(value):
    return send(value, lambda y, x, z, c: (y, 1 - x, z, c))


def by_y(value):
    return send(value, lambda y, x, z, c: (1 - y, x, z, c))


def by_z(value, step):
    return send(value, lambda y, x, z, c: (y, x, z + step, c))


def pick(value, index, axis):
    return lax.dynamic_index_in_dim(value, index, axis=axis, keepdims=False)


def put(buffer, value, *index):
    start = index + (0,) * (buffer.ndim - len(index))
    return lax.dynamic_update_slice(
        buffer, value.reshape((1,) * len(index) + buffer.shape[len(index):]).astype(buffer.dtype), start
    )


def added(a, b):
    return (a.astype(f32) + b.astype(f32)).astype(bf16)


def plane_sums(value, y, x):
    a, b = value[:, :, 0], value[:, :, 1]
    got = by_x(pick(a, 1 - x, 1))
    a = added(pick(a, x, 1), got)
    got = by_y(pick(b, 1 - y, 0))
    b = added(pick(b, y, 0), got)
    got = by_y(pick(a, 1 - y, 0))
    a = added(pick(a, y, 0), got)
    got = by_x(pick(b, 1 - x, 0))
    b = added(pick(b, x, 0), got)
    return a, b


def plane_gather(a, b, y, x, place):
    other_x, other_y = 1 - x, 1 - y
    ay = by_y(a)
    bx = by_x(b)
    ax = by_x(jnp.stack([a, ay]))
    by = by_y(jnp.stack([b, bx]))
    place(y, x, 0, a)
    place(y, x, 1, b)
    place(other_y, x, 0, ay)
    place(y, other_x, 1, bx)
    place(y, other_x, 0, ax[0])
    place(other_y, other_x, 0, ax[1])
    place(other_y, x, 1, by[0])
    place(other_y, other_x, 1, by[1])


def sharded_heads(
    tokens, document_ends, projector, projbias, combiner, combbias, expander, expbias,
    contractor, contbias, attendgain, attendshift, feedgain, feedshift, cotangent,
):
    count, width = tokens.shape
    n = lax.axis_size("shard")
    rep = lax.axis_index("rep")
    me = lax.axis_index("shard")
    y, x, z, c = rep // 2, rep % 2, me // 2, me % 2
    head = width // H
    mix = 3 * head
    rows = width // n
    quarter = rows // 4
    units = expbias.shape[0]
    wide = projbias.shape[0]
    both = units + mix

    mine = lax.dynamic_slice_in_dim(expander, rep * quarter, quarter, 0).reshape(quarter, n, units)
    mine_p = lax.dynamic_slice_in_dim(projector, rep * quarter, quarter, 0)
    mine_p = mine_p.reshape(quarter, 3, n, head).transpose(0, 2, 1, 3).reshape(quarter, n, mix)
    cols = jnp.concatenate([mine, mine_p], axis=2).transpose(1, 0, 2).reshape(4, 2, quarter, both)
    far = [by_z(pick(cols, (z + step) % 4, 0), step) for step in (1, 2, 3)]
    far = jnp.stack(far)
    kept = pick(far, c, 1)
    near = jnp.concatenate(
        [
            lax.dynamic_slice_in_dim(expander, (2 * z + 1 - c) * units, units, 1),
            lax.dynamic_slice_in_dim(
                projector.reshape(rows, 3, width), (2 * z + 1 - c) * head, head, 2
            ).reshape(rows, mix),
        ],
        axis=1,
    )
    near = by_core(near)
    passed = by_core(pick(far, 1 - c, 1))
    exp_cols = jnp.zeros((4, 2, 2, 2, quarter, units), bf16)
    proj_cols = jnp.zeros((4, 2, 2, 2, quarter, mix), bf16)
    own = lax.dynamic_slice_in_dim(expander, me * units, units, 1)
    own_p = lax.dynamic_slice_in_dim(projector.reshape(rows, 3, width), me * head, head, 2)
    exp_cols = put(exp_cols, own, z, c)
    exp_cols = put(exp_cols, near[:, :units], z, 1 - c)
    proj_cols = put(proj_cols, own_p.reshape(rows, mix), z, c)
    proj_cols = put(proj_cols, near[:, units:], z, 1 - c)

    def place(py, px, half, value):
        nonlocal exp_cols, proj_cols
        core = c if half == 0 else 1 - c
        for i, step in enumerate((1, 2, 3)):
            source = (z - step) % 4
            exp_cols = put(exp_cols, value[i, :, :units], source, core, py, px)
            proj_cols = put(proj_cols, value[i, :, units:], source, core, py, px)

    plane_gather(kept, passed, y, x, place)
    exp_cols = exp_cols.reshape(width, units)
    proj_cols = proj_cols.reshape(width, mix)

    vectors = jnp.concatenate(
        [projbias, combbias, contbias, attendgain, attendshift, feedgain, feedshift,
         document_ends[0].astype(bf16)]
    )
    extra = 16
    vectors = jnp.pad(vectors, (0, extra * width - vectors.shape[0])).reshape(extra, width)
    chain = [jnp.concatenate([tokens, vectors], axis=0)]
    for _ in range(3):
        chain.append(by_z(chain[-1], 1))
    mine = jnp.stack(chain)
    others = by_core(mine)
    slots = jnp.stack([mine, others], axis=1).reshape(n, count + extra, width)
    x_all = slots[:, :count].reshape(n * count, width)
    vectors = slots[:, count:].reshape(n, extra * width)
    order = ((z - jnp.arange(4)) % 4)[:, None] * 2 + jnp.stack([c, 1 - c])[None, :]
    order = order.reshape(-1)
    ends = vectors[:, wide + 6 * rows : wide + 6 * rows + DOCS].astype(jnp.int32)
    placed = jnp.zeros((n, wide + 6 * rows), bf16).at[order].set(vectors[:, : wide + 6 * rows])
    full_projbias = placed[:, :wide].reshape(3, n, head)
    my_projbias = pick(full_projbias, me, 1).reshape(1, mix).astype(f32)
    gains = placed[:, wide:].reshape(n, 6, rows).transpose(1, 0, 2).reshape(6, width).astype(f32)
    norms = gains[2:]

    _, _, live = layout(document_ends[0], count)
    upstream = jnp.where(live[:, None], cotangent, jnp.zeros_like(cotangent))
    upstream, _ = lax.optimization_barrier((upstream, chain[-1]))
    chain = [upstream]
    for _ in range(3):
        chain.append(by_z(chain[-1], 1))
    mine = jnp.stack(chain)
    others = by_core(mine)
    up_all = jnp.stack([mine, others], axis=1).reshape(n * count, width)

    position = jax.vmap(lambda e: layout(e, count)[0])(ends).reshape(-1)
    half = ROT // 2
    freqs = jnp.exp(-jnp.arange(half, dtype=f32) * (2.0 / ROT) * math.log(10000.0))
    angles = position[:, None] * freqs[None, :]
    sine, cosine = jnp.sin(angles), jnp.cos(angles)
    still = jnp.ones((n * count, LANES - ROT), f32)
    cosine = jnp.concatenate([cosine, cosine, still], axis=1)
    signed = jnp.concatenate([-sine, sine, 0.0 * still], axis=1)

    h1, h2, qkv, ca, slope, part = forward_block(
        count, ends, x_all, cosine, signed, norms, my_projbias, expbias.astype(f32)[None],
        proj_cols, exp_cols, combiner, contractor,
    )

    def group_sums(part):
        part = part.reshape(4, 2, count, width)
        acc = added(part[:, 0], by_core(part[:, 1]))
        total = acc[3]
        for slot in (2, 1, 0):
            total = added(acc[slot], by_z(total, -1)) if slot else (
                acc[0].astype(f32) + by_z(total, -1).astype(f32)
            )
        return total

    summed = group_sums(part)
    floated = tokens.astype(f32)
    block_output = floated + jnp.where(
        live[:, None], summed + (gains[0] + gains[1]), 0.0
    )
    block_output = block_output.astype(bf16)

    low = left_trans(ca, up_all).astype(bf16)
    low = low.reshape(2, 2, 2, (head + units) // 8, width)
    low_a, low_b = plane_sums(low, y, x)
    out_bias = jnp.sum(up_all, axis=0, dtype=f32)

    dh, dm, dn, sums, hidden_bias, mixed_bias = backward_block(
        count, ends, x_all, up_all, cosine, signed, norms, qkv, slope,
        proj_cols, exp_cols, combiner, contractor,
    )
    high = jnp.concatenate(
        [left_trans(h2, dh).astype(bf16), left_trans(h1, dm).astype(bf16)], axis=1
    )
    high = high.reshape(n, 2, 2, 2, quarter // 2, both).transpose(1, 2, 3, 0, 4, 5)
    high_a, high_b = plane_sums(high, y, x)

    low_out = jnp.zeros((2, 2, 2, (head + units) // 8, width), f32)

    def place_low(py, px, half, value):
        nonlocal low_out
        low_out = put(low_out, value, py, px, half)

    plane_gather(low_a, low_b, y, x, place_low)
    low_out = low_out.reshape(head + units, width)

    turned = jnp.stack([high_a, high_b], axis=1).reshape(4, 2, quarter, both)
    far = [pick(turned, z, 0)] + [by_z(pick(turned, (z + step) % 4, 0), step) for step in (1, 2, 3)]
    far = jnp.stack(far)
    kept = pick(far, c, 1)
    passed = by_core(pick(far, 1 - c, 1))
    exp_rows = jnp.zeros((4, 2, quarter, units), bf16)
    proj_rows = jnp.zeros((4, 2, quarter, mix), bf16)
    for i in range(4):
        source = (z - i) % 4
        for core, value in ((c, kept[i]), (1 - c, passed[i])):
            exp_rows = put(exp_rows, value[:, :units], source, core)
            proj_rows = put(proj_rows, value[:, units:], source, core)
    exp_rows = exp_rows.reshape(n, quarter, units).transpose(1, 0, 2).reshape(quarter, n * units)
    proj_rows = (
        proj_rows.reshape(n, quarter, 3, head).transpose(1, 2, 0, 3).reshape(quarter, 3 * width)
    )
    turned = jnp.concatenate([exp_rows, proj_rows], axis=1)
    exp_out = jnp.zeros((2, 2, 2, quarter // 2, n * units), f32)
    proj_out = jnp.zeros((2, 2, 2, quarter // 2, 3 * width), f32)

    def place_high(py, px, half, value):
        nonlocal exp_out, proj_out
        exp_out = put(exp_out, value[:, : n * units], py, px, half)
        proj_out = put(proj_out, value[:, n * units :], py, px, half)

    plane_gather(turned[: quarter // 2], turned[quarter // 2 :], y, x, place_high)
    exp_out = exp_out.reshape(rows, n * units)
    proj_out = proj_out.reshape(rows, 3 * width)

    d_normed = group_sums(dn)
    own_normed, own_inverse = normalize(floated)
    grad = cotangent.astype(f32) + own_inverse * (
        d_normed
        - jnp.mean(d_normed, axis=1, keepdims=True)
        - own_normed * jnp.mean(d_normed * own_normed, axis=1, keepdims=True)
    )
    input_gradient = grad.astype(bf16)

    mixed_full = jnp.zeros((3, n, head), f32)
    mixed_full = lax.dynamic_update_slice(mixed_full, mixed_bias.reshape(3, 1, head), (0, me, 0))
    vector = jnp.concatenate(
        [
            mixed_full.reshape(n, wide),
            sums.reshape(4, n, rows).transpose(1, 0, 2).reshape(n, 4 * rows),
        ],
        axis=1,
    )
    vector = lax.psum_scatter(vector, "shard", scatter_dimension=0, tiled=True)[0]
    own_out = lax.dynamic_slice(out_bias, (me * rows,), (rows,))
    vector = lax.psum(jnp.concatenate([vector, own_out, hidden_bias[0]]), "rep")
    mixed_bias = vector[:wide]
    s0, s1, s2, s3, out_bias = (vector[wide + i * rows : wide + (i + 1) * rows] for i in range(5))
    hidden_bias = vector[wide + 5 * rows :]
    return (
        block_output, input_gradient, proj_out, mixed_bias, low_out[:head], out_bias,
        exp_out, hidden_bias, low_out[head:], out_bias, s0, s1, s2, s3,
    )


def solution(mesh):
    placed = (
        P(("rep", "shard"), None),
        P(("rep", "shard"), None),
        P("shard", None),
        P("shard"),
        P("shard", None),
        P("shard"),
        P("shard", None),
        P("shard"),
        P("shard", None),
        P("shard"),
        P("shard"),
        P("shard"),
        P("shard"),
        P("shard"),
        P(("rep", "shard"), None),
    )
    return jax.shard_map(
        sharded_heads if dict(mesh.shape) == {"rep": 4, "shard": H} else local,
        mesh=mesh,
        in_specs=placed,
        out_specs=(
            P(("rep", "shard"), None),
            P(("rep", "shard"), None),
            P("shard", None),
            P("shard"),
            P("shard", None),
            P("shard"),
            P("shard", None),
            P("shard"),
            P("shard", None),
            P("shard"),
            P("shard"),
            P("shard"),
            P("shard"),
            P("shard"),
        ),
        check_vma=False,
    )
```

```python
from functools import partial
import math

import jax
import jax.numpy as jnp
from jax import lax
from jax.experimental import pallas as pl
from jax.experimental.pallas import tpu as pltpu
from jax.sharding import PartitionSpec as P

H = 8
ROT = 64
DOCS = 4
LANES = 128
VMEM_LIMIT = 60 * 1024 * 1024

epsilon = 1e-05
masked_value = -1e30
f32 = jnp.float32
bf16 = jnp.bfloat16


def normalize(values):
    centre = jnp.mean(values, axis=1, keepdims=True)
    centred = values - centre
    spread = jnp.mean(centred * centred, axis=1, keepdims=True)
    inverse = lax.rsqrt(spread + epsilon)
    return (centred * inverse, inverse)


def layout(ends, count):
    index = jnp.arange(count, dtype=jnp.int32)
    passed = index[:, None] >= ends[None, :]
    document = jnp.sum(passed.astype(jnp.int32), axis=1)
    begin = jnp.max(jnp.where(passed, ends[None, :], 0), axis=1)
    position = (index - begin).astype(f32)
    allowed = (document[:, None] == document[None, :]) & (index[None, :] <= index[:, None])
    return (position, allowed, index < ends[-1])


def rotary_tables(position, rotary):
    half = rotary // 2
    freqs = jnp.exp(-jnp.arange(half, dtype=f32) * (2.0 / rotary) * math.log(10000.0))
    angles = position[..., None] * freqs
    angles = jnp.concatenate([angles, angles], axis=-1)
    return (jnp.cos(angles), jnp.sin(angles))


def rotate(values, cosine, sine, rotary):
    half = rotary // 2
    front = values[..., :rotary]
    turned = jnp.concatenate([-front[..., half:], front[..., :half]], axis=-1)
    return jnp.concatenate([front * cosine + turned * sine, values[..., rotary:]], axis=-1)


def unrotate(grads, cosine, sine, rotary):
    half = rotary // 2
    front = grads[..., :rotary]
    scaled = front * sine
    backward = jnp.concatenate([scaled[..., half:], -scaled[..., :half]], axis=-1)
    return jnp.concatenate([front * cosine + backward, grads[..., rotary:]], axis=-1)


def right_trans(left, right):
    return lax.dot_general(left, right, (((1,), (1,)), ((), ())), preferred_element_type=f32)


def left_trans(left, right):
    return lax.dot_general(left, right, (((0,), (0,)), ((), ())), preferred_element_type=f32)


def masked_scores(query_low, keys_low, allowed, factor):
    scores = (
        jnp.einsum("qhd,khd->hqk", query_low, keys_low, preferred_element_type=jnp.float32) * factor
    )
    return jnp.where(allowed[None], scores, masked_value)


def weight_sums(left, right):
    piece = lax.slice_in_dim(
        left, 0, left.shape[1] // lax.axis_size("shard") * lax.axis_size("shard"), axis=1
    )
    return lax.psum_scatter(
        left_trans(piece, right).astype(jnp.bfloat16), "shard", scatter_dimension=0, tiled=True
    ).astype(jnp.float32)


def local(
    tokens,
    document_ends,
    projector,
    projbias,
    combiner,
    combbias,
    expander,
    expbias,
    contractor,
    contbias,
    attendgain,
    attendshift,
    feedgain,
    feedshift,
    cotangent,
):
    count, width = tokens.shape
    headsize = width // H
    factor = 1.0 / math.sqrt(headsize)
    position, allowed, live = layout(document_ends[0], count)
    cosine, sine = rotary_tables(position, ROT)
    cosine, sine = cosine[:, None, :], sine[:, None, :]
    (
        full_projector,
        full_combiner,
        full_projbias,
        full_combbias,
        gain_attend,
        shift_attend,
        gain_feed,
        shift_feed,
    ) = (
        lax.all_gather(projector, "shard", axis=0, tiled=True),
        lax.all_gather(combiner, "shard", axis=0, tiled=True),
        lax.all_gather(projbias, "shard", axis=0, tiled=True),
        lax.all_gather(combbias, "shard", axis=0, tiled=True),
        lax.all_gather(attendgain, "shard", axis=0, tiled=True),
        lax.all_gather(attendshift, "shard", axis=0, tiled=True),
        lax.all_gather(feedgain, "shard", axis=0, tiled=True),
        lax.all_gather(feedshift, "shard", axis=0, tiled=True),
    )
    floated = tokens.astype(jnp.float32)
    normed, inverse = normalize(floated)
    first_input = (normed * gain_attend + shift_attend).astype(jnp.bfloat16)
    second_input = (normed * gain_feed + shift_feed).astype(jnp.bfloat16)
    mixed = jnp.dot(first_input, full_projector, preferred_element_type=jnp.float32) + full_projbias
    query_low = rotate(mixed[:, :width].reshape(count, H, headsize), cosine, sine, ROT).astype(
        jnp.bfloat16
    )
    keys_low = rotate(
        mixed[:, width : 2 * width].reshape(count, H, headsize), cosine, sine, ROT
    ).astype(jnp.bfloat16)
    values_low = mixed[:, 2 * width :].reshape(count, H, headsize).astype(jnp.bfloat16)
    scores = masked_scores(query_low, keys_low, allowed, factor)
    peak = jnp.max(scores, axis=2, keepdims=True)
    raised = jnp.exp(scores - peak)
    total = jnp.sum(raised, axis=2, keepdims=True)
    probs_low = (raised / total).astype(jnp.bfloat16)
    logsum = peak + jnp.log(total)
    context = jnp.einsum("hqk,khd->qhd", probs_low, values_low, preferred_element_type=jnp.float32)
    context = context.reshape(count, width).astype(jnp.bfloat16)
    attended = jnp.dot(context, full_combiner, preferred_element_type=jnp.float32) + full_combbias
    full_expander, full_contractor, full_expbias, full_contbias = (
        lax.all_gather(expander, "shard", axis=0, tiled=True),
        lax.all_gather(contractor, "shard", axis=0, tiled=True),
        lax.all_gather(expbias, "shard", axis=0, tiled=True),
        lax.all_gather(contbias, "shard", axis=0, tiled=True),
    )
    hidden = jnp.dot(second_input, full_expander, preferred_element_type=jnp.float32) + full_expbias
    activated, gelu_back = jax.vjp(partial(jax.nn.gelu, approximate=False), hidden)
    active_low = activated.astype(jnp.bfloat16)
    feedout = (
        jnp.dot(active_low, full_contractor, preferred_element_type=jnp.float32) + full_contbias
    )
    block_output = (floated + jnp.where(live[:, None], attended + feedout, 0.0)).astype(
        jnp.bfloat16
    )
    (
        back_projector,
        back_combiner,
        back_expander,
        back_contractor,
        back_gain_attend,
        back_gain_feed,
    ) = (
        lax.all_gather(projector, "shard", axis=0, tiled=True),
        lax.all_gather(combiner, "shard", axis=0, tiled=True),
        lax.all_gather(expander, "shard", axis=0, tiled=True),
        lax.all_gather(contractor, "shard", axis=0, tiled=True),
        lax.all_gather(attendgain, "shard", axis=0, tiled=True),
        lax.all_gather(feedgain, "shard", axis=0, tiled=True),
    )
    upstream = jnp.where(live[:, None], cotangent, jnp.zeros_like(cotangent))
    contractor_part = weight_sums(active_low, upstream)
    combiner_part = weight_sums(context, upstream)
    output_bias = jnp.sum(upstream, axis=0, dtype=jnp.float32)
    d_active = right_trans(upstream, back_contractor)
    d_hidden = gelu_back(d_active)[0].astype(jnp.bfloat16)
    expander_part = weight_sums(second_input, d_hidden)
    hidden_bias = jnp.sum(d_hidden, axis=0, dtype=jnp.float32)
    d_second = right_trans(d_hidden, back_expander)
    d_context = (
        right_trans(upstream, back_combiner).reshape(count, H, headsize).astype(jnp.bfloat16)
    )
    scores_again = masked_scores(query_low, keys_low, allowed, factor)
    probs = jnp.exp(scores_again - logsum)
    d_probs = jnp.einsum("qhd,khd->hqk", d_context, values_low, preferred_element_type=jnp.float32)
    d_values = jnp.einsum("hqk,qhd->khd", probs_low, d_context, preferred_element_type=jnp.float32)
    d_scores = (probs * (d_probs - jnp.sum(d_probs * probs, axis=2, keepdims=True))).astype(
        jnp.bfloat16
    )
    d_query = (
        jnp.einsum("hqk,khd->qhd", d_scores, keys_low, preferred_element_type=jnp.float32) * factor
    )
    d_keys = (
        jnp.einsum("hqk,qhd->khd", d_scores, query_low, preferred_element_type=jnp.float32) * factor
    )
    d_mixed = jnp.concatenate(
        [
            unrotate(d_query, cosine, sine, ROT).reshape(count, width),
            unrotate(d_keys, cosine, sine, ROT).reshape(count, width),
            d_values.reshape(count, width),
        ],
        axis=1,
    ).astype(jnp.bfloat16)
    projector_part = weight_sums(first_input, d_mixed)
    mixed_bias = jnp.sum(d_mixed, axis=0, dtype=jnp.float32)
    d_first = right_trans(d_mixed, back_projector)
    attend_scale = jnp.sum(d_first * normed, axis=0)
    attend_offset = jnp.sum(d_first, axis=0)
    feed_scale = jnp.sum(d_second * normed, axis=0)
    feed_offset = jnp.sum(d_second, axis=0)
    d_normed = d_first * back_gain_attend + d_second * back_gain_feed
    grad_float = cotangent.astype(jnp.float32) + inverse * (
        d_normed
        - jnp.mean(d_normed, axis=1, keepdims=True)
        - normed * jnp.mean(d_normed * normed, axis=1, keepdims=True)
    )
    input_gradient = grad_float.astype(jnp.bfloat16)
    mixed_bias, output_bias, hidden_bias, attend_scale, attend_offset, feed_scale, feed_offset = (
        lax.psum_scatter(
            mixed_bias.astype(jnp.bfloat16), "shard", scatter_dimension=0, tiled=True
        ).astype(jnp.float32),
        lax.psum_scatter(
            output_bias.astype(jnp.bfloat16), "shard", scatter_dimension=0, tiled=True
        ).astype(jnp.float32),
        lax.psum_scatter(
            hidden_bias.astype(jnp.bfloat16), "shard", scatter_dimension=0, tiled=True
        ).astype(jnp.float32),
        lax.psum_scatter(
            attend_scale.astype(jnp.bfloat16), "shard", scatter_dimension=0, tiled=True
        ).astype(jnp.float32),
        lax.psum_scatter(
            attend_offset.astype(jnp.bfloat16), "shard", scatter_dimension=0, tiled=True
        ).astype(jnp.float32),
        lax.psum_scatter(
            feed_scale.astype(jnp.bfloat16), "shard", scatter_dimension=0, tiled=True
        ).astype(jnp.float32),
        lax.psum_scatter(
            feed_offset.astype(jnp.bfloat16), "shard", scatter_dimension=0, tiled=True
        ).astype(jnp.float32),
    )
    (
        projector_part,
        mixed_bias,
        combiner_part,
        output_bias,
        expander_part,
        hidden_bias,
        contractor_part,
        attend_scale,
        attend_offset,
        feed_scale,
        feed_offset,
    ) = (
        lax.psum(projector_part.astype(jnp.bfloat16), "rep").astype(jnp.float32),
        lax.psum(mixed_bias.astype(jnp.bfloat16), "rep").astype(jnp.float32),
        lax.psum(combiner_part.astype(jnp.bfloat16), "rep").astype(jnp.float32),
        lax.psum(output_bias.astype(jnp.bfloat16), "rep").astype(jnp.float32),
        lax.psum(expander_part.astype(jnp.bfloat16), "rep").astype(jnp.float32),
        lax.psum(hidden_bias.astype(jnp.bfloat16), "rep").astype(jnp.float32),
        lax.psum(contractor_part.astype(jnp.bfloat16), "rep").astype(jnp.float32),
        lax.psum(attend_scale.astype(jnp.bfloat16), "rep").astype(jnp.float32),
        lax.psum(attend_offset.astype(jnp.bfloat16), "rep").astype(jnp.float32),
        lax.psum(feed_scale.astype(jnp.bfloat16), "rep").astype(jnp.float32),
        lax.psum(feed_offset.astype(jnp.bfloat16), "rep").astype(jnp.float32),
    )
    return (
        block_output,
        input_gradient,
        projector_part,
        mixed_bias,
        combiner_part,
        output_bias,
        expander_part,
        hidden_bias,
        contractor_part,
        output_bias,
        attend_scale,
        attend_offset,
        feed_scale,
        feed_offset,
    )


def lane_half(shape):
    return lax.broadcasted_iota(jnp.int32, shape, 1) < ROT // 2


def turn(front, signed):
    moved = jnp.where(
        lane_half(front.shape),
        pltpu.roll(front, LANES - ROT // 2, 1),
        pltpu.roll(front, ROT // 2, 1),
    )
    return moved * signed


def rotated(values, cosine, signed):
    front = values[:, :LANES]
    return jnp.concatenate([front * cosine + turn(front, signed), values[:, LANES:]], axis=1)


def unrotated(grads, cosine, signed):
    front = grads[:, :LANES]
    return jnp.concatenate([front * cosine - turn(front, signed), grads[:, LANES:]], axis=1)


def block_allowed(ends_ref, block, count):
    row = lax.broadcasted_iota(jnp.int32, (count, 1), 0)
    column = lax.broadcasted_iota(jnp.int32, (1, count), 1)
    row_doc = jnp.zeros((count, 1), jnp.int32)
    column_doc = jnp.zeros((1, count), jnp.int32)
    for i in range(DOCS):
        end = ends_ref[block, i]
        row_doc += (row >= end).astype(jnp.int32)
        column_doc += (column >= end).astype(jnp.int32)
    return (row_doc == column_doc) & (column <= row)


def dot(left, right):
    return jnp.dot(left, right, preferred_element_type=f32)


def softmax(q, k, allowed):
    scores = right_trans(q, k) * (1.0 / math.sqrt(q.shape[1]))
    scores = jnp.where(allowed, scores, masked_value)
    raised = jnp.exp(scores - jnp.max(scores, axis=1, keepdims=True))
    return raised / jnp.sum(raised, axis=1, keepdims=True)


def forward_kernel(
    ends_ref, x_ref, cos_ref, sin_ref, norms_ref, pbias_ref, ebias_ref,
    proj_ref, exp_ref, comb_ref, cont_ref,
    h1_ref, h2_ref, qkv_ref, ca_ref, slope_ref, part_ref,
):
    block = pl.program_id(0)
    count, width = x_ref.shape
    head = comb_ref.shape[0]
    units = exp_ref.shape[1]
    normed, _ = normalize(x_ref[...].astype(f32))
    first = (normed * norms_ref[0:1, :] + norms_ref[1:2, :]).astype(bf16)
    h1_ref[...] = first
    second = (normed * norms_ref[2:3, :] + norms_ref[3:4, :]).astype(bf16)
    h2_ref[...] = second
    cosine, signed = cos_ref[...], sin_ref[...]
    mixed = dot(first, proj_ref[...]) + pbias_ref[...]
    q = rotated(mixed[:, :head], cosine, signed).astype(bf16)
    k = rotated(mixed[:, head : 2 * head], cosine, signed).astype(bf16)
    v = mixed[:, 2 * head :].astype(bf16)
    qkv_ref[:, :head] = q
    qkv_ref[:, head : 2 * head] = k
    qkv_ref[:, 2 * head :] = v
    probs = softmax(q, k, block_allowed(ends_ref, block, count)).astype(bf16)
    ca_ref[:, :head] = dot(probs, v).astype(bf16)
    tile = min(256, units)
    for start in range(0, units, tile):
        hidden = dot(second, exp_ref[:, start : start + tile]) + ebias_ref[:, start : start + tile]
        below = 0.5 + 0.5 * lax.erf(hidden * math.sqrt(0.5))
        ca_ref[:, head + start : head + start + tile] = (hidden * below).astype(bf16)
        density = jnp.exp(hidden * hidden * -0.5) * (1.0 / math.sqrt(2.0 * math.pi))
        slope_ref[:, start : start + tile] = (below + hidden * density).astype(bf16)
    tile = min(512, width)
    for start in range(0, width, tile):
        cut = slice(start, start + tile)
        part = dot(ca_ref[:, :head], comb_ref[:, cut]) + dot(ca_ref[:, head:], cont_ref[:, cut])
        part_ref[:, cut] = part.astype(bf16)


def backward_kernel(
    ends_ref, x_ref, up_ref, cos_ref, sin_ref, norms_ref, qkv_ref, slope_ref,
    proj_ref, exp_ref, comb_ref, cont_ref,
    dh_ref, dm_ref, dn_ref, sums_ref, hbias_ref, mbias_ref,
):
    block = pl.program_id(0)
    count, width = x_ref.shape
    head = comb_ref.shape[0]
    units = exp_ref.shape[1]
    up = up_ref[...]

    @pl.when(block == 0)
    def _():
        sums_ref[...] = jnp.zeros_like(sums_ref)
        hbias_ref[...] = jnp.zeros_like(hbias_ref)
        mbias_ref[...] = jnp.zeros_like(mbias_ref)

    d_context = right_trans(up, comb_ref[...]).astype(bf16)
    q, k, v = qkv_ref[:, :head], qkv_ref[:, head : 2 * head], qkv_ref[:, 2 * head :]
    probs = softmax(q, k, block_allowed(ends_ref, block, count))
    d_probs = right_trans(d_context, v)
    d_v = left_trans(probs.astype(bf16), d_context)
    d_s = probs * (d_probs - jnp.sum(d_probs * probs, axis=1, keepdims=True))
    d_s = d_s.astype(bf16)
    factor = 1.0 / math.sqrt(head)
    cosine, signed = cos_ref[...], sin_ref[...]
    d_q = unrotated(dot(d_s, k) * factor, cosine, signed).astype(bf16)
    d_k = unrotated(left_trans(d_s, q) * factor, cosine, signed).astype(bf16)
    dm_ref[:, :head] = d_q
    dm_ref[:, head : 2 * head] = d_k
    dm_ref[:, 2 * head :] = d_v.astype(bf16)
    mbias_ref[...] += jnp.sum(dm_ref[...].astype(f32), axis=0, keepdims=True)
    tile = min(256, units)
    for start in range(0, units, tile):
        cut = slice(start, start + tile)
        d_hidden = (right_trans(up, cont_ref[cut, :]) * slope_ref[:, cut].astype(f32)).astype(bf16)
        dh_ref[:, cut] = d_hidden
        hbias_ref[:, cut] += jnp.sum(d_hidden.astype(f32), axis=0, keepdims=True)
    x = x_ref[...].astype(f32)
    centre = jnp.mean(x, axis=1, keepdims=True)
    spread = jnp.mean((x - centre) * (x - centre), axis=1, keepdims=True)
    inverse = lax.rsqrt(spread + epsilon)
    tile = min(256, width)
    for start in range(0, width, tile):
        cut = slice(start, start + tile)
        normed = (x_ref[:, cut].astype(f32) - centre) * inverse
        d_first = right_trans(dm_ref[...], proj_ref[cut, :])
        d_second = right_trans(dh_ref[...], exp_ref[cut, :])
        dn_ref[:, cut] = (
            d_first * norms_ref[0:1, cut] + d_second * norms_ref[2:3, cut]
        ).astype(bf16)
        sums_ref[0:1, cut] += jnp.sum(d_first * normed, axis=0, keepdims=True)
        sums_ref[1:2, cut] += jnp.sum(d_first, axis=0, keepdims=True)
        sums_ref[2:3, cut] += jnp.sum(d_second * normed, axis=0, keepdims=True)
        sums_ref[3:4, cut] += jnp.sum(d_second, axis=0, keepdims=True)


def rows_spec(count, columns):
    return pl.BlockSpec((count, columns), lambda i, *_: (i, 0))


def whole_spec(array):
    return pl.BlockSpec(array.shape, lambda i, *_: (0, 0), pipeline_mode=pl.Buffered(1))


def acc_spec(rows, columns):
    return pl.BlockSpec((rows, columns), lambda i, *_: (0, 0))


def forward_block(count, ends, x, cosine, signed, norms, pbias, ebias, proj, exp, comb, cont):
    slots, width = x.shape
    units, mix, head = exp.shape[1], proj.shape[1], comb.shape[0]
    flops = 2 * slots * width * (mix + 2 * units + head)
    wide = [width, width, mix, head + units, units, width]
    return pl.pallas_call(
        forward_kernel,
        grid_spec=pltpu.PrefetchScalarGridSpec(
            num_scalar_prefetch=1,
            grid=(slots // count,),
            in_specs=[
                rows_spec(count, width), rows_spec(count, LANES), rows_spec(count, LANES),
            ] + [whole_spec(a) for a in (norms, pbias, ebias, proj, exp, comb, cont)],
            out_specs=[rows_spec(count, w) for w in wide],
        ),
        out_shape=[jax.ShapeDtypeStruct((slots, w), bf16) for w in wide],
        compiler_params=pltpu.CompilerParams(vmem_limit_bytes=VMEM_LIMIT),
        cost_estimate=pl.CostEstimate(
            flops=flops, bytes_accessed=2 * slots * sum(wide), transcendentals=0
        ),
    )(ends, x, cosine, signed, norms, pbias, ebias, proj, exp, comb, cont)


def backward_block(count, ends, x, up, cosine, signed, norms, qkv, slope, proj, exp, comb, cont):
    slots, width = x.shape
    units, mix, head = exp.shape[1], proj.shape[1], comb.shape[0]
    flops = 2 * slots * width * (mix + 2 * units + head)
    return pl.pallas_call(
        backward_kernel,
        grid_spec=pltpu.PrefetchScalarGridSpec(
            num_scalar_prefetch=1,
            grid=(slots // count,),
            in_specs=[
                rows_spec(count, width), rows_spec(count, width),
                rows_spec(count, LANES), rows_spec(count, LANES), whole_spec(norms),
                rows_spec(count, mix), rows_spec(count, units),
            ] + [whole_spec(a) for a in (proj, exp, comb, cont)],
            out_specs=[rows_spec(count, w) for w in (units, mix, width)]
            + [acc_spec(4, width), acc_spec(1, units), acc_spec(1, mix)],
        ),
        out_shape=[jax.ShapeDtypeStruct((slots, w), bf16) for w in (units, mix, width)]
        + [jax.ShapeDtypeStruct(s, f32) for s in ((4, width), (1, units), (1, mix))],
        compiler_params=pltpu.CompilerParams(vmem_limit_bytes=VMEM_LIMIT),
        cost_estimate=pl.CostEstimate(
            flops=flops, bytes_accessed=2 * slots * (3 * width + 2 * units), transcendentals=0
        ),
    )(ends, x, up, cosine, signed, norms, qkv, slope, proj, exp, comb, cont)
MESH = pl.DeviceIdType.MESH


def position_of():
    rep, me = lax.axis_index("rep"), lax.axis_index("shard")
    return rep, me, lax.div(rep, 2), lax.rem(rep, 2), lax.div(me, 2), lax.rem(me, 2)


def meet(peers):
    barrier = pltpu.get_barrier_semaphore()
    for peer in peers:
        pl.semaphore_signal(barrier, inc=1, device_id=peer, device_id_type=MESH)
    pl.semaphore_wait(barrier, len(peers))


def rows_at(start, size):
    return pl.ds(pl.multiple_of(start, size), size)


class Net:
    def __init__(self, send_sem, recv_sem, local_sem):
        self.send_sem, self.recv_sem, self.local_sem = send_sem, recv_sem, local_sem
        self.sends, self.locals, self.started, self.sent = 0, 0, 0, []

    def slots(self, count):
        first = self.started
        self.started += count
        return first

    def send(self, src, dst, peer, slot, when=None):
        index = self.sends
        self.sends += 1
        copy = pltpu.make_async_remote_copy(
            src_ref=src, dst_ref=dst, send_sem=self.send_sem.at[index],
            recv_sem=self.recv_sem.at[slot], device_id=peer, device_id_type=MESH,
        )
        if when is None:
            copy.start()
        else:
            pl.when(when)(lambda: copy.start())
        self.sent.append((copy, when))

    def arrived(self, dst, peer, slot):
        pltpu.make_async_remote_copy(
            src_ref=dst, dst_ref=dst, send_sem=self.send_sem.at[0],
            recv_sem=self.recv_sem.at[slot], device_id=peer, device_id_type=MESH,
        ).wait_recv()

    def local(self, src, dst):
        copy = pltpu.make_async_copy(src, dst, self.local_sem.at[self.locals])
        self.locals += 1
        copy.start()
        return copy

    def finish(self):
        for copy, when in self.sent:
            if when is None:
                copy.wait_send()
            else:
                pl.when(when)(lambda copy=copy: copy.wait_send())


def gather_kernel(
    tok_ref, vec_ref, up_ref, exp_ref, proj_ref,
    x_out, vec_out, up_out, exp_out, proj_out, send_sem, recv_sem, local_sem,
):
    rep, me, y, x, z, c = position_of()
    count, width = tok_ref.shape
    rows, quarter = exp_ref.shape[0], exp_ref.shape[0] // 4
    units, mix = exp_out.shape[1], proj_out.shape[1]
    head = mix // 3
    sibling = (rep, me + 1 - 2 * c)
    by_x, by_y = (rep + 1 - 2 * x, me), (rep + 2 - 4 * y, me)
    ring = [(rep, lax.rem(me + k, 8)) for k in range(1, 8)]
    meet(ring + [by_x, by_y])
    net = Net(send_sem, recv_sem, local_sem)
    waits = []

    def weight_copies(go, first, size, source_rows, t):
        source = rows_at(source_rows, size)
        target = rows_at(first, size)
        go(exp_ref.at[source, rows_at(t * units, units)], exp_out.at[target, :])
        for j in range(3):
            go(
                proj_ref.at[source, rows_at(j * width + t * head, head)],
                proj_out.at[target, pl.ds(j * head, head)],
            )

    remote = net.slots(24)
    for step in (1, 2, 3):
        tz = lax.rem(z + step, 4)
        for core in (0, 1):
            part = [0]

            def go(src, dst):
                net.send(
                    src, dst, (rep, tz * 2 + core), remote + ((step - 1) * 2 + c) * 4 + part[0]
                )
                part[0] += 1

            weight_copies(go, me * rows + rep * quarter, quarter, rep * quarter, tz * 2 + core)
    near = net.slots(4)
    part = [0]

    def go_near(src, dst):
        net.send(src, dst, sibling, near + part[0])
        part[0] += 1

    weight_copies(go_near, me * rows, rows, 0, sibling[1])
    copies = []
    weight_copies(lambda s, d: copies.append(net.local(s, d)), me * rows, rows, 0, me)

    mine = rows_at(me * count, count)
    small = net.slots(7)
    for k, peer in enumerate(ring):
        net.send(vec_ref, vec_out.at[me], peer, small + k)
    copies.append(net.local(vec_ref, vec_out.at[me]))

    def begin(source, out):
        left, right, across = net.slots(3), net.slots(3), net.slots(7)
        copies.append(net.local(source, out.at[mine]))
        net.send(source, out.at[mine], (rep, me + 2), left, z < 3)
        net.send(source, out.at[mine], (rep, me - 2), right, z > 0)
        net.send(source, out.at[mine], sibling, across)
        return out, left, right, across

    def step_on(state, step):
        out, left, right, across = state
        for side, first, here, on in ((-1, left, z >= step, z < 3), (1, right, z + step <= 3, z > 0)):
            block = out.at[rows_at((me + side * 2 * step) * count, count)]
            pl.when(here)(lambda: net.arrived(block, sibling, first + step - 1))
            if step < 3:
                net.send(block, block, (rep, me - side * 2), first + step, here & on)
            slot = across + step * 2 - (1 if side < 0 else 0)
            net.send(block, block, sibling, slot, here)

            def take(side=side, step=step, slot=slot, here=here):
                block = out.at[rows_at((sibling[1] + side * 2 * step) * count, count)]
                pl.when(here)(lambda: net.arrived(block, sibling, slot))

            waits.append(take)

    tokens = begin(tok_ref, x_out)

    def shard_rows(step, core):
        return (lax.rem(z + 4 - step, 4) * 2 + core) * rows

    first_hop = net.slots(12)
    for step in (1, 2, 3):
        for core in (0, 1):
            base = shard_rows(step, core)
            at = rows_at(base + rep * quarter, quarter)
            slot = remote + ((step - 1) * 2 + core) * 4
            net.arrived(exp_out.at[at, :], sibling, slot)
            for j in range(3):
                net.arrived(proj_out.at[at, pl.ds(j * head, head)], sibling, slot + 1 + j)
            peer = by_x if core == 0 else by_y
            hop = first_hop + ((step - 1) * 2 + core) * 2
            net.send(exp_out.at[at, :], exp_out.at[at, :], peer, hop)
            net.send(proj_out.at[at, :], proj_out.at[at, :], peer, hop + 1)
    step_on(tokens, 1)
    cotangents = begin(up_ref, up_out)
    second_hop = net.slots(18)
    ends = []
    for step in (1, 2, 3):
        for core in (0, 1):
            base = shard_rows(step, core)
            hop = first_hop + ((step - 1) * 2 + core) * 2
            if core == 0:
                other = rows_at(base + (rep + 1 - 2 * x) * quarter, quarter)
            else:
                other = rows_at(base + (rep + 2 - 4 * y) * quarter, quarter)
            net.arrived(exp_out.at[other, :], sibling, hop)
            net.arrived(proj_out.at[other, :], sibling, hop + 1)
            hop = second_hop + (step - 1) * 6
            if core == 0:
                pieces = [(rows_at(base + y * 2 * quarter, 2 * quarter), by_y, hop)]
                gone = [(rows_at(base + (1 - y) * 2 * quarter, 2 * quarter), hop)]
            else:
                here = rows_at(base + rep * quarter, quarter)
                pieces = [(here, by_x, hop + 2), (other, by_x, hop + 4)]
                gone = [
                    (rows_at(base + (rep + 1 - 2 * x) * quarter, quarter), hop + 2),
                    (rows_at(base + (3 - rep) * quarter, quarter), hop + 4),
                ]
            for at, peer, slot in pieces:
                net.send(exp_out.at[at, :], exp_out.at[at, :], peer, slot)
                net.send(proj_out.at[at, :], proj_out.at[at, :], peer, slot + 1)
            ends += gone
    step_on(tokens, 2)
    step_on(tokens, 3)
    for step in (1, 2, 3):
        step_on(cotangents, step)
    for at, slot in ends:
        net.arrived(exp_out.at[at, :], sibling, slot)
        net.arrived(proj_out.at[at, :], sibling, slot + 1)
    at = rows_at(sibling[1] * rows, rows)
    net.arrived(exp_out.at[at, :], sibling, near)
    for j in range(3):
        net.arrived(proj_out.at[at, pl.ds(j * head, head)], sibling, near + 1 + j)
    for k in range(1, 8):
        net.arrived(vec_out.at[lax.rem(me + 8 - k, 8)], sibling, small + k - 1)
    for out, _, _, across in (tokens, cotangents):
        net.arrived(out.at[rows_at(sibling[1] * count, count)], sibling, across)
    for take in waits:
        take()
    for copy in copies:
        copy.wait()
    net.finish()
    assert net.sends <= GATHER_SEMS and net.started <= GATHER_SEMS and net.locals <= 16


GATHER_SEMS = 128


def gather(tokens, vectors, upstream, expander, projector):
    count, width = tokens.shape
    n = lax.axis_size("shard")
    units, mix = expander.shape[1] // n, projector.shape[1] // n
    shapes = [
        (n * count, width), (n,) + vectors.shape, (n * count, width), (width, units), (width, mix)
    ]
    return pl.pallas_call(
        gather_kernel,
        out_shape=[jax.ShapeDtypeStruct(s, bf16) for s in shapes],
        in_specs=[pl.BlockSpec(memory_space=pl.ANY)] * 5,
        out_specs=[pl.BlockSpec(memory_space=pl.ANY)] * 5,
        scratch_shapes=[
            pltpu.SemaphoreType.DMA((GATHER_SEMS,)),
            pltpu.SemaphoreType.DMA((GATHER_SEMS,)),
            pltpu.SemaphoreType.DMA((16,)),
        ],
        compiler_params=pltpu.CompilerParams(
            collective_id=0, has_side_effects=True, vmem_limit_bytes=VMEM_LIMIT
        ),
    )(tokens, vectors, upstream, expander, projector)


def add_into(target, other):
    rows = target.shape[-2]
    step = min(32, rows)

    @pl.loop(0, rows // step)
    def _(i):
        at = (Ellipsis, pl.ds(pl.multiple_of(i * step, step), step), slice(None))
        lead = (slice(None),) * (len(target.shape) - 2)
        at = lead + at[1:]
        target[at] = (target[at].astype(f32) + other[at].astype(f32)).astype(target.dtype)


def settle_kernel(
    low_ref, he_ref, hp_ref, part_ref, dn_ref, vec_ref, own_ref,
    low_out, exp_out, proj_out, osum_out, dsum_out, vec_out,
    low_a, low_a1, low_a2, low_b, low_b1, low_b2,
    he_a, he_a1, he_a2, he_b, he_b1, he_b2,
    hp_a, hp_a1, hp_a2, hp_b, hp_b1, hp_b2,
    o_in, o_sum, o_right, o_left, d_in, d_sum, d_right, d_left,
    vec_in, vec_mix, vec_all, send_sem, recv_sem, local_sem,
):
    rep, me, y, x, z, c = position_of()
    width = low_ref.shape[-1]
    units, mix = he_ref.shape[-1], hp_ref.shape[-1]
    head = mix // 3
    sibling = (rep, me + 1 - 2 * c)
    x_rep, y_rep, d_rep = rep + 1 - 2 * x, rep + 2 - 4 * y, 3 - rep
    by_x, by_y, across = (x_rep, me), (y_rep, me), (d_rep, me)
    ring = [(rep, lax.rem(me + k, 8)) for k in range(1, 8)]
    meet(ring + [by_x, by_y, across])
    net = Net(send_sem, recv_sem, local_sem)

    class Sum:
        def __init__(self, ref, at, a, a1, a2, b, b1, b2):
            self.a, self.a1, self.a2, self.b, self.b1, self.b2 = a, a1, a2, b, b1, b2
            self.loads = []
            self.slot = net.slots(6)
            for i in range(2):
                net.send(at(ref, i * 2 + 1 - x, 0), a1.at[i], by_x, self.slot + i)
                net.send(at(ref, (1 - y) * 2 + i, 1), b1.at[i], by_y, self.slot + 2 + i)
                self.loads.append(net.local(at(ref, i * 2 + x, 0), a.at[i]))
                self.loads.append(net.local(at(ref, y * 2 + i, 1), b.at[i]))

        def second(self):
            for load in self.loads:
                load.wait()
            for i in range(2):
                net.arrived(self.a1.at[i], sibling, self.slot + i)
                add_into(self.a.at[i], self.a1.at[i])
            net.send(self.a.at[1 - y], self.a2, by_y, self.slot + 4)
            for i in range(2):
                net.arrived(self.b1.at[i], sibling, self.slot + 2 + i)
                add_into(self.b.at[i], self.b1.at[i])
            net.send(self.b.at[1 - x], self.b2, by_x, self.slot + 5)

        def third(self):
            net.arrived(self.a2, sibling, self.slot + 4)
            add_into(self.a.at[y], self.a2)
            net.arrived(self.b2, sibling, self.slot + 5)
            add_into(self.b.at[x], self.b2)
            return self.a.at[y], self.b.at[x]

    def deep(ref, quarter, half):
        return ref.at[:, quarter, half]

    he = Sum(he_ref, deep, he_a, he_a1, he_a2, he_b, he_b1, he_b2)
    hp = Sum(hp_ref, deep, hp_a, hp_a1, hp_a2, hp_b, hp_b1, hp_b2)
    low = Sum(
        low_ref, lambda ref, quarter, half: ref.at[quarter, half],
        low_a, low_a1, low_a2, low_b, low_b1, low_b2,
    )

    class Line:
        def __init__(self, ref, inward, total, right, left):
            self.inward, self.total, self.right, self.left = inward, total, right, left
            self.slot = net.slots(10)
            self.loads = []
            for i in range(4):
                net.send(ref.at[i, 1 - c], inward.at[i], sibling, self.slot + i)
                self.loads.append(net.local(ref.at[i, c], total.at[i]))

        def push(self, block, step, side, when):
            into = self.right if side > 0 else self.left
            slot = self.slot + 4 + (step - 1) + (0 if side > 0 else 3)
            net.send(self.total.at[block], into.at[step - 1], (rep, me + 2 * side), slot, when)

        def begin(self):
            for i in range(4):
                self.loads[i].wait()
                net.arrived(self.inward.at[i], sibling, self.slot + i)
                add_into(self.total.at[i], self.inward.at[i])
            for step in (3, 2, 1):
                self.push(step, step, 1, z == 0)
                self.push(3 - step, step, -1, z == 3)

        def step_on(self, step):
            for side, into, first in ((1, self.right, 4), (-1, self.left, 7)):
                block = z + side * (step - 1)
                here = (z >= 1) & (block <= 3) if side > 0 else (z <= 2) & (block >= 0)

                @pl.when(here)
                def _():
                    net.arrived(into.at[step - 1], sibling, self.slot + first + step - 1)
                    add_into(self.total.at[block], into.at[step - 1])

                if step > 1:
                    self.push(block, step - 1, side, here)

    out = Line(part_ref, o_in, o_sum, o_right, o_left)
    back = Line(dn_ref, d_in, d_sum, d_right, d_left)

    small = net.slots(7)
    for k in range(1, 8):
        t = lax.rem(me + k, 8)
        net.send(vec_ref.at[t], vec_in.at[me], (rep, t), small + k - 1)
    vec_load = net.local(vec_ref.at[me], vec_in.at[me])
    own_load = net.local(own_ref, vec_mix.at[pl.ds(56, 16)])

    out.begin()
    back.begin()
    he.second()
    hp.second()
    for k in range(1, 8):
        net.arrived(vec_in.at[lax.rem(me + 8 - k, 8)], sibling, small + k - 1)
    vec_load.wait()
    own_load.wait()
    total = vec_in[0, 0:8]
    for s in range(1, 8):
        total += vec_in[s, 0:8]
    vec_mix[0:8] = total
    for s in range(8):
        vec_mix[8 + 6 * s : 14 + 6 * s] = vec_in[s, 8:14]
    wide = net.slots(4)
    net.send(vec_mix, vec_all.at[rep], by_x, wide + 1)
    net.send(vec_mix, vec_all.at[rep], by_y, wide + 2)
    net.send(vec_mix, vec_all.at[rep], across, wide + 3)
    vec_copy = net.local(vec_mix, vec_all.at[rep])
    out.step_on(3)
    back.step_on(3)
    low.second()

    class Turn:
        def __init__(self, source, half, place):
            self.half, self.place = half, place
            self.slot = net.slots(21)
            self.copies = []
            for k in range(1, 8):
                t = lax.rem(me + k, 8)
                for j, (src, dst) in enumerate(place(source, t, me)):
                    net.send(src, dst, (rep, t), self.slot + (k - 1) * 3 + j)
            for src, dst in place(source, me, me):
                self.copies.append(net.local(src, dst))

        def wait(self):
            for k in range(1, 8):
                s = lax.rem(me + 8 - k, 8)
                for j, (_, dst) in enumerate(self.place(None, me, s)):
                    net.arrived(dst, sibling, self.slot + (k - 1) * 3 + j)
            for copy in self.copies:
                copy.wait()

    def place_exp(half):
        return lambda source, t, s: [(
            None if source is None else source.at[t],
            exp_out.at[rep, half, :, rows_at(s * units, units)],
        )]

    def place_proj(half):
        return lambda source, t, s: [
            (
                None if source is None else source.at[t, :, pl.ds(j * head, head)],
                proj_out.at[rep, half, :, rows_at(j * width + s * head, head)],
            )
            for j in range(3)
        ]

    he_done = he.third()
    he_turns = [Turn(he_done[h], h, place_exp(h)) for h in range(2)]
    hp_done = hp.third()
    hp_turns = [Turn(hp_done[h], h, place_proj(h)) for h in range(2)]
    out.step_on(2)
    back.step_on(2)

    class Spread:
        def __init__(self, target, sources):
            self.target, self.slot = target, net.slots(6)
            for h, source in enumerate(sources):
                for k, peer in enumerate((by_x, by_y)):
                    net.send(source, target.at[rep, h], peer, self.slot + h * 3 + k)

        def on(self):
            for h, (k, got, peer) in enumerate(((1, y_rep, by_x), (0, x_rep, by_y))):
                net.arrived(self.target.at[got, h], sibling, self.slot + h * 3 + k)
                net.send(self.target.at[got, h], self.target.at[got, h], peer, self.slot + h * 3 + 2)

        def wait(self):
            for h, (k, got) in enumerate(((0, x_rep), (1, y_rep))):
                net.arrived(self.target.at[got, h], sibling, self.slot + h * 3 + k)
                net.arrived(self.target.at[d_rep, h], sibling, self.slot + h * 3 + 2)

    low_done = low.third()
    low_copies = [net.local(low_done[h], low_out.at[rep, h]) for h in range(2)]
    low_spread = Spread(low_out, low_done)
    out.step_on(1)
    back.step_on(1)
    for turn in he_turns:
        turn.wait()
    he_spread = Spread(exp_out, [exp_out.at[rep, h] for h in range(2)])
    for turn in hp_turns:
        turn.wait()
    hp_spread = Spread(proj_out, [proj_out.at[rep, h] for h in range(2)])
    low_spread.on()
    osum_copy = net.local(o_sum.at[z], osum_out)
    dsum_copy = net.local(d_sum.at[z], dsum_out)
    for k, r in ((1, x_rep), (2, y_rep), (3, d_rep)):
        net.arrived(vec_all.at[r], sibling, wide + k)
    vec_copy.wait()
    vec_out[...] = (vec_all[0] + vec_all[1]) + (vec_all[2] + vec_all[3])
    he_spread.on()
    hp_spread.on()
    low_spread.wait()
    he_spread.wait()
    hp_spread.wait()
    for copy in low_copies + [osum_copy, dsum_copy]:
        copy.wait()
    net.finish()
    assert net.sends <= SETTLE_SEMS and net.started <= SETTLE_SEMS and net.locals <= 64, (
        net.sends, net.started, net.locals)


SETTLE_SEMS = 224


def settle(low, he, hp, part, dn, vec, own):
    n = lax.axis_size("shard")
    low_rows, width = low.shape
    units, mix = he.shape[1], hp.shape[1]
    rows, eighth, count = width // n, width // n // 8, part.shape[0] // n
    low = low.reshape(4, 2, low_rows // 8, width)
    he = he.reshape(n, 4, 2, eighth, units)
    hp = hp.reshape(n, 4, 2, eighth, mix)
    part = part.reshape(4, 2, count, width)
    dn = dn.reshape(4, 2, count, width)
    vmem = pltpu.VMEM

    def pieces(*shape):
        return [vmem((2,) + shape, bf16), vmem((2,) + shape, bf16), vmem(shape, bf16)] * 2

    block = (count, width)
    line = [vmem((k,) + block, bf16) for k in (4, 4, 3, 3)]
    anywhere = pl.BlockSpec(memory_space=pl.ANY)
    result = pl.pallas_call(
        settle_kernel,
        out_shape=[
            jax.ShapeDtypeStruct((4, 2, low_rows // 8, width), bf16),
            jax.ShapeDtypeStruct((4, 2, eighth, n * units), bf16),
            jax.ShapeDtypeStruct((4, 2, eighth, n * mix), bf16),
            jax.ShapeDtypeStruct(block, bf16),
            jax.ShapeDtypeStruct(block, bf16),
            jax.ShapeDtypeStruct((72, LANES), f32),
        ],
        in_specs=[anywhere] * 7,
        out_specs=[anywhere] * 5 + [pl.BlockSpec(memory_space=vmem)],
        scratch_shapes=pieces(low_rows // 8, width)
        + pieces(n, eighth, units) + pieces(n, eighth, mix) + line + line + [
            vmem((8, 16, LANES), f32), vmem((72, LANES), f32), vmem((4, 72, LANES), f32),
            pltpu.SemaphoreType.DMA((SETTLE_SEMS,)),
            pltpu.SemaphoreType.DMA((SETTLE_SEMS,)),
            pltpu.SemaphoreType.DMA((64,)),
        ],
        compiler_params=pltpu.CompilerParams(
            collective_id=1, has_side_effects=True, vmem_limit_bytes=VMEM_LIMIT
        ),
    )(low, he, hp, part, dn, vec, own)
    low, exp, proj, osum, dsum, vec = result
    return (
        low.reshape(low_rows, width), exp.reshape(rows, n * units), proj.reshape(rows, n * mix),
        osum, dsum, vec,
    )


def sharded_heads(
    tokens, document_ends, projector, projbias, combiner, combbias, expander, expbias,
    contractor, contbias, attendgain, attendshift, feedgain, feedshift, cotangent,
):
    count, width = tokens.shape
    n = lax.axis_size("shard")
    me = lax.axis_index("shard")
    head = width // H
    mix = 3 * head
    rows = width // n
    units = expbias.shape[0]
    wide = projbias.shape[0]

    vectors = jnp.concatenate(
        [projbias, combbias, contbias, attendgain, attendshift, feedgain, feedshift,
         document_ends[0].astype(bf16)]
    )
    extra = 16
    vectors = jnp.pad(vectors, (0, extra * width - vectors.shape[0])).reshape(extra, width)
    _, _, live = layout(document_ends[0], count)
    upstream = jnp.where(live[:, None], cotangent, jnp.zeros_like(cotangent))
    x_all, vectors, up_all, exp_cols, proj_cols = gather(
        tokens, vectors, upstream, expander, projector
    )

    vectors = vectors.reshape(n, extra * width)
    ends = vectors[:, wide + 6 * rows : wide + 6 * rows + DOCS].astype(jnp.int32)
    full_projbias = vectors[:, :wide].reshape(3, n, head)
    my_projbias = lax.dynamic_index_in_dim(full_projbias, me, 1, keepdims=False)
    my_projbias = my_projbias.reshape(1, mix).astype(f32)
    gains = vectors[:, wide : wide + 6 * rows].reshape(n, 6, rows).transpose(1, 0, 2)
    gains = gains.reshape(6, width).astype(f32)
    norms = gains[2:]

    position = jax.vmap(lambda e: layout(e, count)[0])(ends).reshape(-1)
    half = ROT // 2
    freqs = jnp.exp(-jnp.arange(half, dtype=f32) * (2.0 / ROT) * math.log(10000.0))
    angles = position[:, None] * freqs[None, :]
    sine, cosine = jnp.sin(angles), jnp.cos(angles)
    still = jnp.ones((n * count, LANES - ROT), f32)
    cosine = jnp.concatenate([cosine, cosine, still], axis=1)
    signed = jnp.concatenate([-sine, sine, 0.0 * still], axis=1)

    h1, h2, qkv, ca, slope, part = forward_block(
        count, ends, x_all, cosine, signed, norms, my_projbias, expbias.astype(f32)[None],
        proj_cols, exp_cols, combiner, contractor,
    )
    low = left_trans(ca, up_all).astype(bf16)
    out_bias = jnp.sum(up_all, axis=0, dtype=f32)
    dh, dm, dn, sums, hidden_bias, mixed_bias = backward_block(
        count, ends, x_all, up_all, cosine, signed, norms, qkv, slope,
        proj_cols, exp_cols, combiner, contractor,
    )
    he = left_trans(h2, dh).astype(bf16)
    hp = left_trans(h1, dm).astype(bf16)

    vec = jnp.concatenate(
        [
            sums.reshape(4, n, rows).transpose(1, 0, 2).reshape(n, 4 * rows // LANES, LANES),
            jnp.broadcast_to(mixed_bias.reshape(1, mix // LANES, LANES), (n, mix // LANES, LANES)),
            jnp.zeros((n, 2, LANES), f32),
        ],
        axis=1,
    )
    own_out = lax.dynamic_slice(out_bias, (me * rows,), (rows,))
    own = jnp.concatenate([hidden_bias[0], own_out])
    own = jnp.pad(own, (0, 16 * LANES - own.shape[0])).reshape(16, LANES)
    low, exp_out, proj_out, osum, dsum, vec = settle(low, he, hp, part, dn, vec, own)

    floated = tokens.astype(f32)
    block_output = floated + jnp.where(
        live[:, None], osum.astype(f32) + (gains[0] + gains[1]), 0.0
    )
    block_output = block_output.astype(bf16)
    d_normed = dsum.astype(f32)
    normed, inverse = normalize(floated)
    grad = cotangent.astype(f32) + inverse * (
        d_normed
        - jnp.mean(d_normed, axis=1, keepdims=True)
        - normed * jnp.mean(d_normed * normed, axis=1, keepdims=True)
    )
    input_gradient = grad.astype(bf16)

    vec = vec.reshape(-1)
    norm_sums = vec[: 4 * rows].reshape(4, rows)
    mixed_bias = vec[4 * rows : 4 * rows + n * mix].reshape(n, 3, head).transpose(1, 0, 2)
    mixed_bias = lax.dynamic_slice(mixed_bias.reshape(-1), (me * wide,), (wide,))
    rest = vec[4 * rows + n * mix :]
    hidden_bias, out_bias = rest[:units], rest[units : units + rows]
    low = low.astype(f32)
    return (
        block_output, input_gradient, proj_out.astype(f32), mixed_bias, low[:head], out_bias,
        exp_out.astype(f32), hidden_bias, low[head:], out_bias,
        norm_sums[0], norm_sums[1], norm_sums[2], norm_sums[3],
    )


def solution(mesh):
    placed = (
        P(("rep", "shard"), None),
        P(("rep", "shard"), None),
        P("shard", None),
        P("shard"),
        P("shard", None),
        P("shard"),
        P("shard", None),
        P("shard"),
        P("shard", None),
        P("shard"),
        P("shard"),
        P("shard"),
        P("shard"),
        P("shard"),
        P(("rep", "shard"), None),
    )
    return jax.shard_map(
        sharded_heads if dict(mesh.shape) == {"rep": 4, "shard": H} else local,
        mesh=mesh,
        in_specs=placed,
        out_specs=(
            P(("rep", "shard"), None),
            P(("rep", "shard"), None),
            P("shard", None),
            P("shard"),
            P("shard", None),
            P("shard"),
            P("shard", None),
            P("shard"),
            P("shard", None),
            P("shard"),
            P("shard"),
            P("shard"),
            P("shard"),
            P("shard"),
        ),
        check_vma=False,
    )
```

```python
from functools import partial
import math

import jax
import jax.numpy as jnp
from jax import lax
from jax.experimental import pallas as pl
from jax.experimental.pallas import tpu as pltpu
from jax.sharding import PartitionSpec as P

H = 8
ROT = 64
DOCS = 4
LANES = 128
VMEM_LIMIT = 60 * 1024 * 1024

epsilon = 1e-05
masked_value = -1e30
f32 = jnp.float32
bf16 = jnp.bfloat16


def normalize(values):
    centre = jnp.mean(values, axis=1, keepdims=True)
    centred = values - centre
    spread = jnp.mean(centred * centred, axis=1, keepdims=True)
    inverse = lax.rsqrt(spread + epsilon)
    return (centred * inverse, inverse)


def layout(ends, count):
    index = jnp.arange(count, dtype=jnp.int32)
    passed = index[:, None] >= ends[None, :]
    document = jnp.sum(passed.astype(jnp.int32), axis=1)
    begin = jnp.max(jnp.where(passed, ends[None, :], 0), axis=1)
    position = (index - begin).astype(f32)
    allowed = (document[:, None] == document[None, :]) & (index[None, :] <= index[:, None])
    return (position, allowed, index < ends[-1])


def rotary_tables(position, rotary):
    half = rotary // 2
    freqs = jnp.exp(-jnp.arange(half, dtype=f32) * (2.0 / rotary) * math.log(10000.0))
    angles = position[..., None] * freqs
    angles = jnp.concatenate([angles, angles], axis=-1)
    return (jnp.cos(angles), jnp.sin(angles))


def rotate(values, cosine, sine, rotary):
    half = rotary // 2
    front = values[..., :rotary]
    turned = jnp.concatenate([-front[..., half:], front[..., :half]], axis=-1)
    return jnp.concatenate([front * cosine + turned * sine, values[..., rotary:]], axis=-1)


def unrotate(grads, cosine, sine, rotary):
    half = rotary // 2
    front = grads[..., :rotary]
    scaled = front * sine
    backward = jnp.concatenate([scaled[..., half:], -scaled[..., :half]], axis=-1)
    return jnp.concatenate([front * cosine + backward, grads[..., rotary:]], axis=-1)


def right_trans(left, right):
    return lax.dot_general(left, right, (((1,), (1,)), ((), ())), preferred_element_type=f32)


def left_trans(left, right):
    return lax.dot_general(left, right, (((0,), (0,)), ((), ())), preferred_element_type=f32)


def masked_scores(query_low, keys_low, allowed, factor):
    scores = (
        jnp.einsum("qhd,khd->hqk", query_low, keys_low, preferred_element_type=jnp.float32) * factor
    )
    return jnp.where(allowed[None], scores, masked_value)


def weight_sums(left, right):
    piece = lax.slice_in_dim(
        left, 0, left.shape[1] // lax.axis_size("shard") * lax.axis_size("shard"), axis=1
    )
    return lax.psum_scatter(
        left_trans(piece, right).astype(jnp.bfloat16), "shard", scatter_dimension=0, tiled=True
    ).astype(jnp.float32)


def local(
    tokens,
    document_ends,
    projector,
    projbias,
    combiner,
    combbias,
    expander,
    expbias,
    contractor,
    contbias,
    attendgain,
    attendshift,
    feedgain,
    feedshift,
    cotangent,
):
    count, width = tokens.shape
    headsize = width // H
    factor = 1.0 / math.sqrt(headsize)
    position, allowed, live = layout(document_ends[0], count)
    cosine, sine = rotary_tables(position, ROT)
    cosine, sine = cosine[:, None, :], sine[:, None, :]
    (
        full_projector,
        full_combiner,
        full_projbias,
        full_combbias,
        gain_attend,
        shift_attend,
        gain_feed,
        shift_feed,
    ) = (
        lax.all_gather(projector, "shard", axis=0, tiled=True),
        lax.all_gather(combiner, "shard", axis=0, tiled=True),
        lax.all_gather(projbias, "shard", axis=0, tiled=True),
        lax.all_gather(combbias, "shard", axis=0, tiled=True),
        lax.all_gather(attendgain, "shard", axis=0, tiled=True),
        lax.all_gather(attendshift, "shard", axis=0, tiled=True),
        lax.all_gather(feedgain, "shard", axis=0, tiled=True),
        lax.all_gather(feedshift, "shard", axis=0, tiled=True),
    )
    floated = tokens.astype(jnp.float32)
    normed, inverse = normalize(floated)
    first_input = (normed * gain_attend + shift_attend).astype(jnp.bfloat16)
    second_input = (normed * gain_feed + shift_feed).astype(jnp.bfloat16)
    mixed = jnp.dot(first_input, full_projector, preferred_element_type=jnp.float32) + full_projbias
    query_low = rotate(mixed[:, :width].reshape(count, H, headsize), cosine, sine, ROT).astype(
        jnp.bfloat16
    )
    keys_low = rotate(
        mixed[:, width : 2 * width].reshape(count, H, headsize), cosine, sine, ROT
    ).astype(jnp.bfloat16)
    values_low = mixed[:, 2 * width :].reshape(count, H, headsize).astype(jnp.bfloat16)
    scores = masked_scores(query_low, keys_low, allowed, factor)
    peak = jnp.max(scores, axis=2, keepdims=True)
    raised = jnp.exp(scores - peak)
    total = jnp.sum(raised, axis=2, keepdims=True)
    probs_low = (raised / total).astype(jnp.bfloat16)
    logsum = peak + jnp.log(total)
    context = jnp.einsum("hqk,khd->qhd", probs_low, values_low, preferred_element_type=jnp.float32)
    context = context.reshape(count, width).astype(jnp.bfloat16)
    attended = jnp.dot(context, full_combiner, preferred_element_type=jnp.float32) + full_combbias
    full_expander, full_contractor, full_expbias, full_contbias = (
        lax.all_gather(expander, "shard", axis=0, tiled=True),
        lax.all_gather(contractor, "shard", axis=0, tiled=True),
        lax.all_gather(expbias, "shard", axis=0, tiled=True),
        lax.all_gather(contbias, "shard", axis=0, tiled=True),
    )
    hidden = jnp.dot(second_input, full_expander, preferred_element_type=jnp.float32) + full_expbias
    activated, gelu_back = jax.vjp(partial(jax.nn.gelu, approximate=False), hidden)
    active_low = activated.astype(jnp.bfloat16)
    feedout = (
        jnp.dot(active_low, full_contractor, preferred_element_type=jnp.float32) + full_contbias
    )
    block_output = (floated + jnp.where(live[:, None], attended + feedout, 0.0)).astype(
        jnp.bfloat16
    )
    (
        back_projector,
        back_combiner,
        back_expander,
        back_contractor,
        back_gain_attend,
        back_gain_feed,
    ) = (
        lax.all_gather(projector, "shard", axis=0, tiled=True),
        lax.all_gather(combiner, "shard", axis=0, tiled=True),
        lax.all_gather(expander, "shard", axis=0, tiled=True),
        lax.all_gather(contractor, "shard", axis=0, tiled=True),
        lax.all_gather(attendgain, "shard", axis=0, tiled=True),
        lax.all_gather(feedgain, "shard", axis=0, tiled=True),
    )
    upstream = jnp.where(live[:, None], cotangent, jnp.zeros_like(cotangent))
    contractor_part = weight_sums(active_low, upstream)
    combiner_part = weight_sums(context, upstream)
    output_bias = jnp.sum(upstream, axis=0, dtype=jnp.float32)
    d_active = right_trans(upstream, back_contractor)
    d_hidden = gelu_back(d_active)[0].astype(jnp.bfloat16)
    expander_part = weight_sums(second_input, d_hidden)
    hidden_bias = jnp.sum(d_hidden, axis=0, dtype=jnp.float32)
    d_second = right_trans(d_hidden, back_expander)
    d_context = (
        right_trans(upstream, back_combiner).reshape(count, H, headsize).astype(jnp.bfloat16)
    )
    scores_again = masked_scores(query_low, keys_low, allowed, factor)
    probs = jnp.exp(scores_again - logsum)
    d_probs = jnp.einsum("qhd,khd->hqk", d_context, values_low, preferred_element_type=jnp.float32)
    d_values = jnp.einsum("hqk,qhd->khd", probs_low, d_context, preferred_element_type=jnp.float32)
    d_scores = (probs * (d_probs - jnp.sum(d_probs * probs, axis=2, keepdims=True))).astype(
        jnp.bfloat16
    )
    d_query = (
        jnp.einsum("hqk,khd->qhd", d_scores, keys_low, preferred_element_type=jnp.float32) * factor
    )
    d_keys = (
        jnp.einsum("hqk,qhd->khd", d_scores, query_low, preferred_element_type=jnp.float32) * factor
    )
    d_mixed = jnp.concatenate(
        [
            unrotate(d_query, cosine, sine, ROT).reshape(count, width),
            unrotate(d_keys, cosine, sine, ROT).reshape(count, width),
            d_values.reshape(count, width),
        ],
        axis=1,
    ).astype(jnp.bfloat16)
    projector_part = weight_sums(first_input, d_mixed)
    mixed_bias = jnp.sum(d_mixed, axis=0, dtype=jnp.float32)
    d_first = right_trans(d_mixed, back_projector)
    attend_scale = jnp.sum(d_first * normed, axis=0)
    attend_offset = jnp.sum(d_first, axis=0)
    feed_scale = jnp.sum(d_second * normed, axis=0)
    feed_offset = jnp.sum(d_second, axis=0)
    d_normed = d_first * back_gain_attend + d_second * back_gain_feed
    grad_float = cotangent.astype(jnp.float32) + inverse * (
        d_normed
        - jnp.mean(d_normed, axis=1, keepdims=True)
        - normed * jnp.mean(d_normed * normed, axis=1, keepdims=True)
    )
    input_gradient = grad_float.astype(jnp.bfloat16)
    mixed_bias, output_bias, hidden_bias, attend_scale, attend_offset, feed_scale, feed_offset = (
        lax.psum_scatter(
            mixed_bias.astype(jnp.bfloat16), "shard", scatter_dimension=0, tiled=True
        ).astype(jnp.float32),
        lax.psum_scatter(
            output_bias.astype(jnp.bfloat16), "shard", scatter_dimension=0, tiled=True
        ).astype(jnp.float32),
        lax.psum_scatter(
            hidden_bias.astype(jnp.bfloat16), "shard", scatter_dimension=0, tiled=True
        ).astype(jnp.float32),
        lax.psum_scatter(
            attend_scale.astype(jnp.bfloat16), "shard", scatter_dimension=0, tiled=True
        ).astype(jnp.float32),
        lax.psum_scatter(
            attend_offset.astype(jnp.bfloat16), "shard", scatter_dimension=0, tiled=True
        ).astype(jnp.float32),
        lax.psum_scatter(
            feed_scale.astype(jnp.bfloat16), "shard", scatter_dimension=0, tiled=True
        ).astype(jnp.float32),
        lax.psum_scatter(
            feed_offset.astype(jnp.bfloat16), "shard", scatter_dimension=0, tiled=True
        ).astype(jnp.float32),
    )
    (
        projector_part,
        mixed_bias,
        combiner_part,
        output_bias,
        expander_part,
        hidden_bias,
        contractor_part,
        attend_scale,
        attend_offset,
        feed_scale,
        feed_offset,
    ) = (
        lax.psum(projector_part.astype(jnp.bfloat16), "rep").astype(jnp.float32),
        lax.psum(mixed_bias.astype(jnp.bfloat16), "rep").astype(jnp.float32),
        lax.psum(combiner_part.astype(jnp.bfloat16), "rep").astype(jnp.float32),
        lax.psum(output_bias.astype(jnp.bfloat16), "rep").astype(jnp.float32),
        lax.psum(expander_part.astype(jnp.bfloat16), "rep").astype(jnp.float32),
        lax.psum(hidden_bias.astype(jnp.bfloat16), "rep").astype(jnp.float32),
        lax.psum(contractor_part.astype(jnp.bfloat16), "rep").astype(jnp.float32),
        lax.psum(attend_scale.astype(jnp.bfloat16), "rep").astype(jnp.float32),
        lax.psum(attend_offset.astype(jnp.bfloat16), "rep").astype(jnp.float32),
        lax.psum(feed_scale.astype(jnp.bfloat16), "rep").astype(jnp.float32),
        lax.psum(feed_offset.astype(jnp.bfloat16), "rep").astype(jnp.float32),
    )
    return (
        block_output,
        input_gradient,
        projector_part,
        mixed_bias,
        combiner_part,
        output_bias,
        expander_part,
        hidden_bias,
        contractor_part,
        output_bias,
        attend_scale,
        attend_offset,
        feed_scale,
        feed_offset,
    )


def lane_half(shape):
    return lax.broadcasted_iota(jnp.int32, shape, 1) < ROT // 2


def turn(front, signed):
    moved = jnp.where(
        lane_half(front.shape),
        pltpu.roll(front, LANES - ROT // 2, 1),
        pltpu.roll(front, ROT // 2, 1),
    )
    return moved * signed


def rotated(values, cosine, signed):
    front = values[:, :LANES]
    return jnp.concatenate([front * cosine + turn(front, signed), values[:, LANES:]], axis=1)


def unrotated(grads, cosine, signed):
    front = grads[:, :LANES]
    return jnp.concatenate([front * cosine - turn(front, signed), grads[:, LANES:]], axis=1)


def block_layout(ends, count):
    row = lax.broadcasted_iota(jnp.int32, (count, 1), 0).astype(f32)
    column = lax.broadcasted_iota(jnp.int32, (1, count), 1).astype(f32)
    row_doc = jnp.zeros((count, 1), f32)
    column_doc = jnp.zeros((1, count), f32)
    begin = jnp.zeros((count, 1), f32)
    for i in range(DOCS):
        end = ends[:, i : i + 1]
        row_doc += jnp.where(row >= end, 1.0, 0.0)
        column_doc += jnp.where(column >= end, 1.0, 0.0)
        begin = jnp.maximum(begin, jnp.where(row >= end, end, 0.0))
    return (row_doc == column_doc) & (column <= row), row - begin


def dot(left, right):
    return jnp.dot(left, right, preferred_element_type=f32)


def softmax(q, k, allowed):
    scores = right_trans(q, k) * (1.0 / math.sqrt(q.shape[1]))
    scores = jnp.where(allowed, scores, masked_value)
    raised = jnp.exp(scores - jnp.max(scores, axis=1, keepdims=True))
    return raised / jnp.sum(raised, axis=1, keepdims=True)


def forward_block(
    x_ref, ends, angles_ref, norms_ref, pbias_ref, ebias_ref, proj_ref, exp_ref, comb_ref,
    cont_ref, h1_ref, h2_ref, qkv_ref, ca_ref, slope_ref, part_ref,
):
    count, width = x_ref.shape
    head = comb_ref.shape[0]
    units = exp_ref.shape[1]
    allowed, place = block_layout(ends, count)
    angles = place * angles_ref[0:1, :]
    cosine, signed = jnp.cos(angles), jnp.sin(angles) * angles_ref[1:2, :]
    normed, _ = normalize(x_ref[...].astype(f32))
    h1_ref[...] = (normed * norms_ref[0:1, :] + norms_ref[1:2, :]).astype(bf16)
    h2_ref[...] = (normed * norms_ref[2:3, :] + norms_ref[3:4, :]).astype(bf16)
    mixed = dot(h1_ref[...], proj_ref[...]) + pbias_ref[...]
    q = rotated(mixed[:, :head], cosine, signed).astype(bf16)
    k = rotated(mixed[:, head : 2 * head], cosine, signed).astype(bf16)
    v = mixed[:, 2 * head :].astype(bf16)
    qkv_ref[:, :head] = q
    qkv_ref[:, head : 2 * head] = k
    qkv_ref[:, 2 * head :] = v
    probs = softmax(q, k, allowed).astype(bf16)
    ca_ref[:, :head] = dot(probs, v).astype(bf16)
    tile = min(256, units)
    for start in range(0, units, tile):
        hidden = dot(h2_ref[...], exp_ref[:, start : start + tile])
        hidden += ebias_ref[:, start : start + tile]
        below = 0.5 + 0.5 * lax.erf(hidden * math.sqrt(0.5))
        ca_ref[:, head + start : head + start + tile] = (hidden * below).astype(bf16)
        density = jnp.exp(hidden * hidden * -0.5) * (1.0 / math.sqrt(2.0 * math.pi))
        slope_ref[:, start : start + tile] = (below + hidden * density).astype(bf16)
    tile = min(512, width)
    for start in range(0, width, tile):
        cut = slice(start, start + tile)
        part = dot(ca_ref[:, :head], comb_ref[:, cut]) + dot(ca_ref[:, head:], cont_ref[:, cut])
        part_ref[:, cut] = part.astype(bf16)


def backward_block(
    x_ref, up_ref, ends, angles_ref, norms_ref, qkv_ref, slope_ref, proj_ref, exp_ref, comb_ref,
    cont_ref, dh_ref, dm_ref, dn_ref, sums_ref, hbias_ref, mbias_ref, obias_ref,
):
    count, width = x_ref.shape
    head = comb_ref.shape[0]
    units = exp_ref.shape[1]
    allowed, place = block_layout(ends, count)
    angles = place * angles_ref[0:1, :]
    cosine, signed = jnp.cos(angles), jnp.sin(angles) * angles_ref[1:2, :]
    d_context = right_trans(up_ref[...], comb_ref[...]).astype(bf16)
    q, k, v = qkv_ref[:, :head], qkv_ref[:, head : 2 * head], qkv_ref[:, 2 * head :]
    probs = softmax(q, k, allowed)
    d_probs = right_trans(d_context, v)
    d_v = left_trans(probs.astype(bf16), d_context)
    d_s = probs * (d_probs - jnp.sum(d_probs * probs, axis=1, keepdims=True))
    d_s = d_s.astype(bf16)
    factor = 1.0 / math.sqrt(head)
    dm_ref[:, :head] = unrotated(dot(d_s, k) * factor, cosine, signed).astype(bf16)
    d_k = unrotated(left_trans(d_s, q) * factor, cosine, signed).astype(bf16)
    dm_ref[:, head : 2 * head] = d_k
    dm_ref[:, 2 * head :] = d_v.astype(bf16)
    mbias_ref[...] += jnp.sum(dm_ref[...].astype(f32), axis=0, keepdims=True)
    obias_ref[...] += jnp.sum(up_ref[...].astype(f32), axis=0, keepdims=True)
    tile = min(256, units)
    for start in range(0, units, tile):
        cut = slice(start, start + tile)
        d_active = right_trans(up_ref[...], cont_ref[cut, :])
        d_hidden = (d_active * slope_ref[:, cut].astype(f32)).astype(bf16)
        dh_ref[:, cut] = d_hidden
        hbias_ref[:, cut] += jnp.sum(d_hidden.astype(f32), axis=0, keepdims=True)
    x = x_ref[...].astype(f32)
    centre = jnp.mean(x, axis=1, keepdims=True)
    spread = jnp.mean((x - centre) * (x - centre), axis=1, keepdims=True)
    inverse = lax.rsqrt(spread + epsilon)
    tile = min(256, width)
    for start in range(0, width, tile):
        cut = slice(start, start + tile)
        normed = (x_ref[:, cut].astype(f32) - centre) * inverse
        d_first = right_trans(dm_ref[...], proj_ref[cut, :])
        d_second = right_trans(dh_ref[...], exp_ref[cut, :])
        dn_ref[:, cut] = (
            d_first * norms_ref[0:1, cut] + d_second * norms_ref[2:3, cut]
        ).astype(bf16)
        sums_ref[0:1, cut] += jnp.sum(d_first * normed, axis=0, keepdims=True)
        sums_ref[1:2, cut] += jnp.sum(d_first, axis=0, keepdims=True)
        sums_ref[2:3, cut] += jnp.sum(d_second * normed, axis=0, keepdims=True)
        sums_ref[3:4, cut] += jnp.sum(d_second, axis=0, keepdims=True)


def accumulate(total, left, right):
    tile = min(256, left.shape[1])

    @pl.loop(0, left.shape[1] // tile)
    def _(i):
        at = pl.ds(pl.multiple_of(i * tile, tile), tile)
        total[at, :] += left_trans(left[:, at], right[...])


MESH = pl.DeviceIdType.MESH
GATHER_SEMS = 96


def position_of():
    rep, me = lax.axis_index("rep"), lax.axis_index("shard")
    return rep, me, lax.div(rep, 2), lax.rem(rep, 2), lax.div(me, 2), lax.rem(me, 2)


def meet(peers):
    barrier = pltpu.get_barrier_semaphore()
    for peer in peers:
        pl.semaphore_signal(barrier, inc=1, device_id=peer, device_id_type=MESH)
    pl.semaphore_wait(barrier, len(peers))


def rows_at(start, size):
    return pl.ds(pl.multiple_of(start, size), size)


class Net:
    def __init__(self, send_sem, recv_sem, local_sem):
        self.send_sem, self.recv_sem, self.local_sem = send_sem, recv_sem, local_sem
        self.sends, self.locals, self.started, self.sent = 0, 0, 0, []

    def slots(self, count):
        first = self.started
        self.started += count
        return first

    def send(self, src, dst, peer, slot, when=None):
        index = self.sends
        self.sends += 1
        copy = pltpu.make_async_remote_copy(
            src_ref=src, dst_ref=dst, send_sem=self.send_sem.at[index],
            recv_sem=self.recv_sem.at[slot], device_id=peer, device_id_type=MESH,
        )
        if when is None:
            copy.start()
        else:
            pl.when(when)(lambda: copy.start())
        self.sent.append((copy, when))

    def arrived(self, dst, peer, slot):
        pltpu.make_async_remote_copy(
            src_ref=dst, dst_ref=dst, send_sem=self.send_sem.at[0],
            recv_sem=self.recv_sem.at[slot], device_id=peer, device_id_type=MESH,
        ).wait_recv()

    def local(self, src, dst):
        copy = pltpu.make_async_copy(src, dst, self.local_sem.at[self.locals])
        self.locals += 1
        copy.start()
        return copy

    def finish(self):
        for copy, when in self.sent:
            if when is None:
                copy.wait_send()
            else:
                pl.when(when)(lambda copy=copy: copy.wait_send())


class Chain:
    def __init__(self, source, out, count, where, sems):
        self.source, self.out, self.count = source, out, count
        self.rep, self.me, self.z, self.c = where
        self.side_send, self.side_recv, self.core_send, self.core_recv, self.local_sem = sems
        self.sibling = self.me + 1 - 2 * self.c

    def block(self, shard):
        return self.out.at[rows_at(shard * self.count, self.count)]

    def side(self, side, step):
        block = self.block(self.me - side * 2 * step)
        peer = (self.rep, self.me + side * 2)
        index = (0 if side > 0 else 4) + step
        return pltpu.make_async_remote_copy(
            src_ref=block, dst_ref=block, send_sem=self.side_send.at[index],
            recv_sem=self.side_recv.at[index], device_id=peer, device_id_type=MESH,
        )

    def cross(self, side, step):
        block = self.block(self.me - side * 2 * step)
        index = (0 if side > 0 else 4) + step
        return pltpu.make_async_remote_copy(
            src_ref=block, dst_ref=block, send_sem=self.core_send.at[index],
            recv_sem=self.core_recv.at[index], device_id=(self.rep, self.sibling),
            device_id_type=MESH,
        )

    def taken(self, side, step):
        block = self.block(self.sibling - side * 2 * step)
        index = (0 if side > 0 else 4) + step
        return pltpu.make_async_remote_copy(
            src_ref=block, dst_ref=block, send_sem=self.core_send.at[index],
            recv_sem=self.core_recv.at[index], device_id=(self.rep, self.sibling),
            device_id_type=MESH,
        )

    def here(self, side, step):
        return self.z >= step if side > 0 else self.z + step <= 3

    def on(self, side):
        return self.z < 3 if side > 0 else self.z > 0

    def first(self, side):
        mine = self.block(self.me)
        index = 0 if side > 0 else 4
        return pltpu.make_async_remote_copy(
            src_ref=self.source, dst_ref=mine, send_sem=self.side_send.at[index],
            recv_sem=self.side_recv.at[index], device_id=(self.rep, self.me + side * 2),
            device_id_type=MESH,
        )

    def first_cross(self):
        mine = self.block(self.me)
        return pltpu.make_async_remote_copy(
            src_ref=self.source, dst_ref=mine, send_sem=self.core_send.at[0],
            recv_sem=self.core_recv.at[0], device_id=(self.rep, self.sibling),
            device_id_type=MESH,
        )

    def begin(self):
        for side in (1, -1):
            pl.when(self.on(side))(lambda: self.first(side).start())
        self.first_cross().start()
        pltpu.make_async_copy(self.source, self.block(self.me), self.local_sem).start()

    def wait_own(self):
        pltpu.make_async_copy(self.source, self.block(self.me), self.local_sem).wait()
        self.taken(1, 0).wait_recv()

    def step(self, step):
        for side in (1, -1):
            here = self.here(side, step)

            @pl.when(here)
            def _():
                block = self.block(self.me - side * 2 * step)
                index = (0 if side > 0 else 4) + step - 1
                pltpu.make_async_remote_copy(
                    src_ref=block, dst_ref=block, send_sem=self.side_send.at[index],
                    recv_sem=self.side_recv.at[index], device_id=(self.rep, self.sibling),
                    device_id_type=MESH,
                ).wait_recv()
                self.cross(side, step).start()

            pl.when(here & self.on(side) & (step < 3))(lambda: self.side(side, step).start())

    def take(self, step):
        for side in (1, -1):
            pl.when(self.here(side, step))(lambda: self.taken(side, step).wait_recv())

    def finish(self):
        self.first_cross().wait_send()
        for side in (1, -1):
            pl.when(self.on(side))(lambda: self.first(side).wait_send())
            for step in (1, 2, 3):
                here = self.here(side, step)
                pl.when(here)(lambda: self.cross(side, step).wait_send())
                if step < 3:
                    pl.when(here & self.on(side))(lambda: self.side(side, step).wait_send())


def block_kernel(
    tok_ref, vec_ref, up_ref, expander_ref, projector_ref, comb_hbm, cont_hbm, ebias_ref,
    angles_ref,
    x_out, up_out, low_out, he_out, hp_out, part_out, dn_out, vec_out, own_out, norms_ref,
    exp_ref, proj_ref, comb_ref, cont_ref, low_sum, he_sum, hp_sum,
    xs, us, h1s, h2s, ca, slope, qkv, dh, dm, parts, dns,
    vecs, bias_all, ends_all, pbias, sums, hbias, mbias, obias,
    send_sem, recv_sem, local_sem, load_sem, store_sem,
    xs_send, xs_recv, xc_send, xc_recv, us_send, us_recv, uc_send, uc_recv, own_sem,
):
    rep, me, y, x, z, c = position_of()
    count, width = tok_ref.shape
    rows, quarter = expander_ref.shape[0], expander_ref.shape[0] // 4
    units, mix = exp_ref.shape[1], proj_ref.shape[1]
    head = mix // 3
    sibling = (rep, me + 1 - 2 * c)
    by_x, by_y = (rep + 1 - 2 * x, me), (rep + 2 - 4 * y, me)
    ring = [(rep, lax.rem(me + k, 8)) for k in range(1, 8)]
    meet(ring + [by_x, by_y])
    net = Net(send_sem, recv_sem, local_sem)

    def weight_copies(go, first, size, source_rows, t):
        source = rows_at(source_rows, size)
        target = rows_at(first, size)
        go(expander_ref.at[source, rows_at(t * units, units)], exp_ref.at[target, :])
        for j in range(3):
            go(
                projector_ref.at[source, rows_at(j * width + t * head, head)],
                proj_ref.at[target, pl.ds(j * head, head)],
            )

    remote = net.slots(24)
    for step in (1, 2, 3):
        tz = lax.rem(z + step, 4)
        for core in (0, 1):
            part = [0]

            def go(src, dst):
                net.send(
                    src, dst, (rep, tz * 2 + core), remote + ((step - 1) * 2 + c) * 4 + part[0]
                )
                part[0] += 1

            weight_copies(go, me * rows + rep * quarter, quarter, rep * quarter, tz * 2 + core)
    small = net.slots(7)
    for k, peer in enumerate(ring):
        net.send(vec_ref, vecs.at[me], peer, small + k)
    where = (rep, me, z, c)
    tokens = Chain(
        tok_ref, x_out, count, where, (xs_send, xs_recv, xc_send, xc_recv, own_sem.at[0])
    )
    cotangents = Chain(
        up_ref, up_out, count, where, (us_send, us_recv, uc_send, uc_recv, own_sem.at[1])
    )
    tokens.begin()
    near = net.slots(4)
    part = [0]

    def go_near(src, dst):
        net.send(src, dst, sibling, near + part[0])
        part[0] += 1

    weight_copies(go_near, me * rows, rows, 0, sibling[1])
    copies = []
    weight_copies(lambda s, d: copies.append(net.local(s, d)), me * rows, rows, 0, me)
    copies.append(net.local(vec_ref, vecs.at[me]))
    copies.append(net.local(comb_hbm, comb_ref))
    copies.append(net.local(cont_hbm, cont_ref))
    cotangents.begin()
    for ref in (low_sum, he_sum, hp_sum, sums, hbias, mbias, obias):
        if ref.shape[0] <= 8:
            ref[...] = jnp.zeros_like(ref)
        else:

            @pl.loop(0, ref.shape[0] // 64)
            def _(i):
                ref[rows_at(i * 64, 64), :] = jnp.zeros((64, ref.shape[1]), f32)

    def shard_rows(step, core):
        return (lax.rem(z + 4 - step, 4) * 2 + core) * rows

    first_hop = net.slots(12)
    for step in (1, 2, 3):
        for core in (0, 1):
            base = shard_rows(step, core)
            at = rows_at(base + rep * quarter, quarter)
            slot = remote + ((step - 1) * 2 + core) * 4
            net.arrived(exp_ref.at[at, :], sibling, slot)
            for j in range(3):
                net.arrived(proj_ref.at[at, pl.ds(j * head, head)], sibling, slot + 1 + j)
            peer = by_x if core == 0 else by_y
            hop = first_hop + ((step - 1) * 2 + core) * 2
            net.send(exp_ref.at[at, :], exp_ref.at[at, :], peer, hop)
            net.send(proj_ref.at[at, :], proj_ref.at[at, :], peer, hop + 1)
    tokens.step(1)
    second_hop = net.slots(18)
    gone = []
    for step in (1, 2, 3):
        for core in (0, 1):
            base = shard_rows(step, core)
            hop = first_hop + ((step - 1) * 2 + core) * 2
            if core == 0:
                other = rows_at(base + (rep + 1 - 2 * x) * quarter, quarter)
            else:
                other = rows_at(base + (rep + 2 - 4 * y) * quarter, quarter)
            net.arrived(exp_ref.at[other, :], sibling, hop)
            net.arrived(proj_ref.at[other, :], sibling, hop + 1)
            hop = second_hop + (step - 1) * 6
            if core == 0:
                pieces = [(rows_at(base + y * 2 * quarter, 2 * quarter), by_y, hop)]
                gone += [(rows_at(base + (1 - y) * 2 * quarter, 2 * quarter), hop)]
            else:
                here = rows_at(base + rep * quarter, quarter)
                pieces = [(here, by_x, hop + 2), (other, by_x, hop + 4)]
                gone += [
                    (rows_at(base + (rep + 1 - 2 * x) * quarter, quarter), hop + 2),
                    (rows_at(base + (3 - rep) * quarter, quarter), hop + 4),
                ]
            for at, peer, slot in pieces:
                net.send(exp_ref.at[at, :], exp_ref.at[at, :], peer, slot)
                net.send(proj_ref.at[at, :], proj_ref.at[at, :], peer, slot + 1)

    for k in range(1, 8):
        net.arrived(vecs.at[lax.rem(me + 8 - k, 8)], sibling, small + k - 1)
    for copy in copies:
        copy.wait()
    for s in range(8):
        values = vecs[s].astype(f32)
        for j in range(3):
            bias_all[3 * s + j] = values[6 + j : 7 + j, :]
        ends_all[s] = values[9:10, :LANES]
        norms_ref[:, s * rows : s * rows + rows] = values[:8, :]
    for j in range(3):
        pbias[:, j * head : j * head + head] = bias_all[8 * j + me]

    at = rows_at(sibling[1] * rows, rows)
    net.arrived(exp_ref.at[at, :], sibling, near)
    for j in range(3):
        net.arrived(proj_ref.at[at, pl.ds(j * head, head)], sibling, near + 1 + j)
    for at, slot in gone:
        net.arrived(exp_ref.at[at, :], sibling, slot)
        net.arrived(proj_ref.at[at, :], sibling, slot + 1)
    tokens.wait_own()
    cotangents.wait_own()

    @pl.loop(0, 4)
    def _(slot):
        second = jnp.where(z == 0, 2, jnp.where(z == 1, 0, 1))
        last = jnp.where(z < 2, 3, 0)
        after = jnp.where(z < 3, z + 1, 2)
        chip = jnp.where(
            slot == 0, z, jnp.where(slot == 1, after, jnp.where(slot == 2, second, last))
        )

        def loads(source, into, sems):
            return [
                pltpu.make_async_copy(
                    source.at[rows_at((chip * 2 + b) * count, count)], into[b],
                    load_sem.at[sems + b],
                )
                for b in range(2)
            ]

        def stores(source, into, sems):
            return [
                pltpu.make_async_copy(source.at[b], into.at[chip, b], store_sem.at[sems + b])
                for b in range(2)
            ]

        def ends_of(b):
            return ends_all[chip * 2 + b]

        pl.when(slot > 0)(lambda: tokens.take(slot))
        x_loads = loads(x_out, [xs.at[b] for b in range(2)], 0)
        for load in x_loads:
            load.start()
        for load in x_loads:
            load.wait()

        @pl.loop(0, 2)
        def _(b):
            at = rows_at(b * count, count)
            forward_block(
                xs.at[b], ends_of(b), angles_ref, norms_ref, pbias, ebias_ref, proj_ref, exp_ref,
                comb_ref, cont_ref, h1s.at[at], h2s.at[at], qkv.at[at], ca.at[at], slope.at[at],
                parts.at[b],
            )

        for store in stores(parts, part_out, 0):
            store.start()
        pl.when(slot == 2)(lambda: tokens.step(3))
        pl.when(slot > 0)(lambda: cotangents.take(slot))
        up_loads = loads(up_out, [us.at[rows_at(b * count, count)] for b in range(2)], 2)
        for load in up_loads:
            load.start()
        for load in up_loads:
            load.wait()

        @pl.loop(0, 2)
        def _(b):
            at = rows_at(b * count, count)
            backward_block(
                xs.at[b], us.at[at], ends_of(b), angles_ref, norms_ref, qkv.at[at], slope.at[at],
                proj_ref, exp_ref, comb_ref, cont_ref, dh.at[at], dm.at[at], dns.at[b], sums,
                hbias, mbias, obias,
            )

        for store in stores(dns, dn_out, 2):
            store.start()
        accumulate(low_sum, ca, us)
        accumulate(he_sum, h2s, dh)
        accumulate(hp_sum, h1s, dm)
        for store in stores(parts, part_out, 0) + stores(dns, dn_out, 2):
            store.wait()
        pl.when(slot < 3)(lambda: cotangents.step(slot + 1))
        pl.when(slot == 0)(lambda: tokens.step(2))

    for total, out, stage in (
        (low_sum, low_out, h1s), (he_sum, he_out, dh), (hp_sum, hp_out, dm)
    ):
        step = count

        @pl.loop(0, total.shape[0] // step)
        def _(i):
            at = rows_at(lax.rem(i, 2) * step, step)
            move = pltpu.make_async_copy(
                stage.at[at], out.at[rows_at(i * step, step)], store_sem.at[lax.rem(i, 2)]
            )
            pl.when(i >= 2)(lambda: move.wait())
            stage[at, :] = total[rows_at(i * step, step), :].astype(bf16)
            move.start()

        for i in range(2):
            pltpu.make_async_copy(
                stage.at[rows_at(i * step, step)], out.at[rows_at(i * step, step)], store_sem.at[i]
            ).wait()
    vec_out[...] = jnp.zeros_like(vec_out)
    own_out[...] = jnp.zeros_like(own_out)
    per = rows // LANES
    for t in range(8):
        for j in range(4):
            for i in range(per):
                at = t * rows + i * LANES
                vec_out[t, j * per + i : j * per + i + 1, :] = sums[j : j + 1, at : at + LANES]
        for i in range(mix // LANES):
            at = 4 * per + i
            vec_out[t, at : at + 1, :] = mbias[:, i * LANES : (i + 1) * LANES]
    for i in range(units // LANES):
        own_out[i : i + 1, :] = hbias[:, i * LANES : (i + 1) * LANES]
    for i in range(per):
        own_out[units // LANES + i : units // LANES + i + 1, :] = obias[
            :, rows_at(me * rows + i * LANES, LANES)
        ]
    tokens.finish()
    cotangents.finish()
    net.finish()
    assert net.sends <= GATHER_SEMS and net.started <= GATHER_SEMS and net.locals <= 8


def block_passes(tokens, vectors, upstream, expander, projector, combiner, contractor, ebias, angles):
    count, width = tokens.shape
    n = lax.axis_size("shard")
    units, mix, head = expander.shape[1] // n, projector.shape[1] // n, combiner.shape[0]
    low = head + units
    vmem, dma = pltpu.VMEM, pltpu.SemaphoreType.DMA
    shapes = [
        (n * count, width), (n * count, width), (low, width), (width, units), (width, mix),
        (n // 2, 2, count, width), (n // 2, 2, count, width),
    ]
    two = 2 * count
    return pl.pallas_call(
        block_kernel,
        out_shape=[jax.ShapeDtypeStruct(s, bf16) for s in shapes] + [
            jax.ShapeDtypeStruct((n, 16, LANES), f32),
            jax.ShapeDtypeStruct((16, LANES), f32),
            jax.ShapeDtypeStruct((8, width), f32),
        ],
        in_specs=[pl.BlockSpec(memory_space=pl.ANY)] * 7 + [pl.BlockSpec(memory_space=vmem)] * 2,
        out_specs=[pl.BlockSpec(memory_space=pl.ANY)] * 7 + [pl.BlockSpec(memory_space=vmem)] * 3,
        scratch_shapes=[
            vmem((width, units), bf16), vmem((width, mix), bf16), vmem((head, width), bf16),
            vmem((units, width), bf16), vmem((low, width), f32), vmem((width, units), f32),
            vmem((width, mix), f32),
            vmem((2, count, width), bf16), vmem((two, width), bf16),
            vmem((two, width), bf16), vmem((two, width), bf16), vmem((two, low), bf16),
            vmem((two, units), bf16), vmem((two, mix), bf16), vmem((two, units), bf16),
            vmem((two, mix), bf16), vmem((2, count, width), bf16), vmem((2, count, width), bf16),
            vmem((n,) + vectors.shape, bf16), vmem((3 * n, 1, vectors.shape[1]), f32),
            vmem((n, 1, LANES), f32),
            vmem((1, mix), f32), vmem((4, width), f32), vmem((1, units), f32),
            vmem((1, mix), f32), vmem((1, width), f32),
            dma((GATHER_SEMS,)), dma((GATHER_SEMS,)), dma((8,)), dma((4,)), dma((4,)),
        ] + [dma((8,))] * 8 + [dma((2,))],
        compiler_params=pltpu.CompilerParams(
            collective_id=0, has_side_effects=True, vmem_limit_bytes=VMEM_LIMIT
        ),
    )(tokens, vectors, upstream, expander, projector, combiner, contractor, ebias, angles)


def add_into(target, other):
    rows = target.shape[-2]
    step = min(32, rows)

    @pl.loop(0, rows // step)
    def _(i):
        at = (Ellipsis, pl.ds(pl.multiple_of(i * step, step), step), slice(None))
        lead = (slice(None),) * (len(target.shape) - 2)
        at = lead + at[1:]
        target[at] = (target[at].astype(f32) + other[at].astype(f32)).astype(target.dtype)


def settle_kernel(
    low_ref, he_ref, hp_ref, part_ref, dn_ref, vec_ref, own_ref,
    low_out, exp_out, proj_out, osum_out, dsum_out, vec_out,
    low_a, low_a1, low_a2, low_b, low_b1, low_b2,
    he_a, he_a1, he_a2, he_b, he_b1, he_b2,
    hp_a, hp_a1, hp_a2, hp_b, hp_b1, hp_b2,
    o_in, o_sum, o_right, o_left, d_in, d_sum, d_right, d_left,
    vec_in, vec_mix, vec_all, send_sem, recv_sem, local_sem,
):
    rep, me, y, x, z, c = position_of()
    width = low_ref.shape[-1]
    units, mix = he_ref.shape[-1], hp_ref.shape[-1]
    head = mix // 3
    sibling = (rep, me + 1 - 2 * c)
    x_rep, y_rep, d_rep = rep + 1 - 2 * x, rep + 2 - 4 * y, 3 - rep
    by_x, by_y, across = (x_rep, me), (y_rep, me), (d_rep, me)
    ring = [(rep, lax.rem(me + k, 8)) for k in range(1, 8)]
    meet(ring + [by_x, by_y, across])
    net = Net(send_sem, recv_sem, local_sem)

    class Sum:
        def __init__(self, ref, at, a, a1, a2, b, b1, b2):
            self.ref, self.at = ref, at
            self.a, self.a1, self.a2, self.b, self.b1, self.b2 = a, a1, a2, b, b1, b2
            self.slot = net.slots(6)

        def load(self):
            self.loads = []
            for i in range(2):
                self.loads.append(net.local(self.at(self.ref, i * 2 + x, 0), self.a.at[i]))
                self.loads.append(net.local(self.at(self.ref, y * 2 + i, 1), self.b.at[i]))

        def first(self):
            for i in range(2):
                source = self.at(self.ref, i * 2 + 1 - x, 0)
                net.send(source, self.a1.at[i], by_x, self.slot + i)
                source = self.at(self.ref, (1 - y) * 2 + i, 1)
                net.send(source, self.b1.at[i], by_y, self.slot + 2 + i)

        def second(self):
            for load in self.loads:
                load.wait()
            for i in range(2):
                net.arrived(self.a1.at[i], sibling, self.slot + i)
                add_into(self.a.at[i], self.a1.at[i])
            net.send(self.a.at[1 - y], self.a2, by_y, self.slot + 4)
            for i in range(2):
                net.arrived(self.b1.at[i], sibling, self.slot + 2 + i)
                add_into(self.b.at[i], self.b1.at[i])
            net.send(self.b.at[1 - x], self.b2, by_x, self.slot + 5)

        def third(self):
            net.arrived(self.a2, sibling, self.slot + 4)
            add_into(self.a.at[y], self.a2)
            net.arrived(self.b2, sibling, self.slot + 5)
            add_into(self.b.at[x], self.b2)
            return self.a.at[y], self.b.at[x]

    def deep(ref, quarter, half):
        return ref.at[:, quarter, half]

    he = Sum(he_ref, deep, he_a, he_a1, he_a2, he_b, he_b1, he_b2)
    hp = Sum(hp_ref, deep, hp_a, hp_a1, hp_a2, hp_b, hp_b1, hp_b2)
    low = Sum(
        low_ref, lambda ref, quarter, half: ref.at[quarter, half],
        low_a, low_a1, low_a2, low_b, low_b1, low_b2,
    )

    he.first()
    hp.first()
    he.load()
    hp.load()

    class Line:
        def __init__(self, ref, inward, total, right, left):
            self.inward, self.total, self.right, self.left = inward, total, right, left
            self.slot = net.slots(10)
            self.loads = []
            for i in range(4):
                net.send(ref.at[i, 1 - c], inward.at[i], sibling, self.slot + i)
                self.loads.append(net.local(ref.at[i, c], total.at[i]))

        def push(self, block, step, side, when):
            into = self.right if side > 0 else self.left
            slot = self.slot + 4 + (step - 1) + (0 if side > 0 else 3)
            net.send(self.total.at[block], into.at[step - 1], (rep, me + 2 * side), slot, when)

        def join(self):
            for i in range(4):
                self.loads[i].wait()
                net.arrived(self.inward.at[i], sibling, self.slot + i)
                add_into(self.total.at[i], self.inward.at[i])

        def begin(self):
            for step in (3, 2, 1):
                self.push(step, step, 1, z == 0)
                self.push(3 - step, step, -1, z == 3)

        def step_on(self, step):
            for side, into, first in ((1, self.right, 4), (-1, self.left, 7)):
                block = z + side * (step - 1)
                here = (z >= 1) & (block <= 3) if side > 0 else (z <= 2) & (block >= 0)

                @pl.when(here)
                def _():
                    net.arrived(into.at[step - 1], sibling, self.slot + first + step - 1)
                    add_into(self.total.at[block], into.at[step - 1])

                if step > 1:
                    self.push(block, step - 1, side, here)

    out = Line(part_ref, o_in, o_sum, o_right, o_left)
    back = Line(dn_ref, d_in, d_sum, d_right, d_left)

    small = net.slots(7)
    for k in range(1, 8):
        t = lax.rem(me + k, 8)
        net.send(vec_ref.at[t], vec_in.at[me], (rep, t), small + k - 1)
    vec_load = net.local(vec_ref.at[me], vec_in.at[me])
    own_load = net.local(own_ref, vec_mix.at[pl.ds(56, 16)])
    low.load()

    out.join()
    out.begin()
    he.second()
    out.step_on(3)
    back.join()
    hp.second()
    low.first()
    out.step_on(2)

    class Turn:
        def __init__(self, source, half, place):
            self.half, self.place = half, place
            self.slot = net.slots(21)
            self.copies = []
            for k in range(1, 8):
                t = lax.rem(me + k, 8)
                for j, (src, dst) in enumerate(place(source, t, me)):
                    net.send(src, dst, (rep, t), self.slot + (k - 1) * 3 + j)
            for src, dst in place(source, me, me):
                self.copies.append(net.local(src, dst))

        def wait(self):
            for k in range(1, 8):
                s = lax.rem(me + 8 - k, 8)
                for j, (_, dst) in enumerate(self.place(None, me, s)):
                    net.arrived(dst, sibling, self.slot + (k - 1) * 3 + j)
            for copy in self.copies:
                copy.wait()

    def place_exp(half):
        return lambda source, t, s: [(
            None if source is None else source.at[t],
            exp_out.at[rep, half, :, rows_at(s * units, units)],
        )]

    def place_proj(half):
        return lambda source, t, s: [
            (
                None if source is None else source.at[t, :, pl.ds(j * head, head)],
                proj_out.at[rep, half, :, rows_at(j * width + s * head, head)],
            )
            for j in range(3)
        ]

    he_done = he.third()
    he_turns = [Turn(he_done[h], h, place_exp(h)) for h in range(2)]
    hp_done = hp.third()
    hp_turns = [Turn(hp_done[h], h, place_proj(h)) for h in range(2)]
    out.step_on(1)
    back.begin()
    low.second()
    for k in range(1, 8):
        net.arrived(vec_in.at[lax.rem(me + 8 - k, 8)], sibling, small + k - 1)
    vec_load.wait()
    own_load.wait()
    total = vec_in[0, 0:8]
    for s in range(1, 8):
        total += vec_in[s, 0:8]
    vec_mix[0:8] = total
    for s in range(8):
        vec_mix[8 + 6 * s : 14 + 6 * s] = vec_in[s, 8:14]
    wide = net.slots(4)
    net.send(vec_mix, vec_all.at[rep], by_x, wide + 1)
    net.send(vec_mix, vec_all.at[rep], by_y, wide + 2)
    net.send(vec_mix, vec_all.at[rep], across, wide + 3)
    vec_copy = net.local(vec_mix, vec_all.at[rep])

    class Spread:
        def __init__(self, target, sources):
            self.target, self.slot = target, net.slots(6)
            for h, source in enumerate(sources):
                for k, peer in enumerate((by_x, by_y)):
                    net.send(source, target.at[rep, h], peer, self.slot + h * 3 + k)

        def on(self):
            for h, (k, got, peer) in enumerate(((1, y_rep, by_x), (0, x_rep, by_y))):
                net.arrived(self.target.at[got, h], sibling, self.slot + h * 3 + k)
                net.send(self.target.at[got, h], self.target.at[got, h], peer, self.slot + h * 3 + 2)

        def wait(self):
            for h, (k, got) in enumerate(((0, x_rep), (1, y_rep))):
                net.arrived(self.target.at[got, h], sibling, self.slot + h * 3 + k)
                net.arrived(self.target.at[d_rep, h], sibling, self.slot + h * 3 + 2)

    low_done = low.third()
    low_copies = [net.local(low_done[h], low_out.at[rep, h]) for h in range(2)]
    low_spread = Spread(low_out, low_done)
    for turn in he_turns:
        turn.wait()
    he_spread = Spread(exp_out, [exp_out.at[rep, h] for h in range(2)])
    for turn in hp_turns:
        turn.wait()
    hp_spread = Spread(proj_out, [proj_out.at[rep, h] for h in range(2)])
    back.step_on(3)
    low_spread.on()
    back.step_on(2)
    he_spread.on()
    hp_spread.on()
    for k, r in ((1, x_rep), (2, y_rep), (3, d_rep)):
        net.arrived(vec_all.at[r], sibling, wide + k)
    vec_copy.wait()
    vec_out[...] = (vec_all[0] + vec_all[1]) + (vec_all[2] + vec_all[3])
    back.step_on(1)
    osum_copy = net.local(o_sum.at[z], osum_out)
    dsum_copy = net.local(d_sum.at[z], dsum_out)
    low_spread.wait()
    he_spread.wait()
    hp_spread.wait()
    for copy in low_copies + [osum_copy, dsum_copy]:
        copy.wait()
    net.finish()
    assert net.sends <= SETTLE_SEMS and net.started <= SETTLE_SEMS and net.locals <= 64, (
        net.sends, net.started, net.locals)


SETTLE_SEMS = 224


def settle(low, he, hp, part, dn, vec, own):
    n = lax.axis_size("shard")
    low_rows, width = low.shape
    units, mix = he.shape[1], hp.shape[1]
    rows, eighth, count = width // n, width // n // 8, part.shape[2]
    low = low.reshape(4, 2, low_rows // 8, width)
    he = he.reshape(n, 4, 2, eighth, units)
    hp = hp.reshape(n, 4, 2, eighth, mix)
    vmem = pltpu.VMEM

    def pieces(*shape):
        return [vmem((2,) + shape, bf16), vmem((2,) + shape, bf16), vmem(shape, bf16)] * 2

    block = (count, width)
    line = [vmem((k,) + block, bf16) for k in (4, 4, 3, 3)]
    anywhere = pl.BlockSpec(memory_space=pl.ANY)
    result = pl.pallas_call(
        settle_kernel,
        out_shape=[
            jax.ShapeDtypeStruct((4, 2, low_rows // 8, width), bf16),
            jax.ShapeDtypeStruct((4, 2, eighth, n * units), bf16),
            jax.ShapeDtypeStruct((4, 2, eighth, n * mix), bf16),
            jax.ShapeDtypeStruct(block, bf16),
            jax.ShapeDtypeStruct(block, bf16),
            jax.ShapeDtypeStruct((72, LANES), f32),
        ],
        in_specs=[anywhere] * 7,
        out_specs=[anywhere] * 5 + [pl.BlockSpec(memory_space=vmem)],
        scratch_shapes=pieces(low_rows // 8, width)
        + pieces(n, eighth, units) + pieces(n, eighth, mix) + line + line + [
            vmem((8, 16, LANES), f32), vmem((72, LANES), f32), vmem((4, 72, LANES), f32),
            pltpu.SemaphoreType.DMA((SETTLE_SEMS,)),
            pltpu.SemaphoreType.DMA((SETTLE_SEMS,)),
            pltpu.SemaphoreType.DMA((64,)),
        ],
        compiler_params=pltpu.CompilerParams(
            collective_id=1, has_side_effects=True, vmem_limit_bytes=VMEM_LIMIT
        ),
    )(low, he, hp, part, dn, vec, own)
    low, exp, proj, osum, dsum, vec = result
    return (
        low.reshape(low_rows, width), exp.reshape(rows, n * units), proj.reshape(rows, n * mix),
        osum, dsum, vec,
    )


def sharded_heads(
    tokens, document_ends, projector, projbias, combiner, combbias, expander, expbias,
    contractor, contbias, attendgain, attendshift, feedgain, feedshift, cotangent,
):
    count, width = tokens.shape
    n = lax.axis_size("shard")
    me = lax.axis_index("shard")
    head = width // H
    mix = 3 * head
    rows = width // n
    units = expbias.shape[0]
    wide = projbias.shape[0]

    vectors = jnp.concatenate(
        [attendgain, attendshift, feedgain, feedshift, combbias, contbias, projbias,
         document_ends[0].astype(bf16)]
    )
    vectors = jnp.pad(vectors, (0, 16 * rows - vectors.shape[0])).reshape(16, rows)
    _, _, live = layout(document_ends[0], count)
    upstream = jnp.where(live[:, None], cotangent, jnp.zeros_like(cotangent))
    half = ROT // 2
    freqs = jnp.exp(-jnp.arange(half, dtype=f32) * (2.0 / ROT) * math.log(10000.0))
    still = jnp.zeros((LANES - ROT,), f32)
    ones = jnp.ones((half,), f32)
    angles = jnp.stack(
        [jnp.concatenate([freqs, freqs, still]), jnp.concatenate([-ones, ones, still])]
    )
    _, _, low, he, hp, part, dn, vec, own, norms = block_passes(
        tokens, vectors, upstream, expander, projector, combiner, contractor,
        expbias.astype(f32)[None], angles,
    )
    low, exp_out, proj_out, osum, dsum, vec = settle(low, he, hp, part, dn, vec, own)

    floated = tokens.astype(f32)
    block_output = floated + jnp.where(
        live[:, None], osum.astype(f32) + (norms[4] + norms[5]), 0.0
    )
    block_output = block_output.astype(bf16)
    d_normed = dsum.astype(f32)
    normed, inverse = normalize(floated)
    grad = cotangent.astype(f32) + inverse * (
        d_normed
        - jnp.mean(d_normed, axis=1, keepdims=True)
        - normed * jnp.mean(d_normed * normed, axis=1, keepdims=True)
    )
    input_gradient = grad.astype(bf16)

    vec = vec.reshape(-1)
    norm_sums = vec[: 4 * rows].reshape(4, rows)
    mixed_bias = vec[4 * rows : 4 * rows + n * mix].reshape(n, 3, head).transpose(1, 0, 2)
    mixed_bias = lax.dynamic_slice(mixed_bias.reshape(-1), (me * wide,), (wide,))
    rest = vec[4 * rows + n * mix :]
    hidden_bias, out_bias = rest[:units], rest[units : units + rows]
    return (
        block_output, input_gradient, proj_out.astype(f32), mixed_bias, low[:head].astype(f32), out_bias,
        exp_out.astype(f32), hidden_bias, low[head:].astype(f32), out_bias,
        norm_sums[0], norm_sums[1], norm_sums[2], norm_sums[3],
    )


def solution(mesh):
    placed = (
        P(("rep", "shard"), None),
        P(("rep", "shard"), None),
        P("shard", None),
        P("shard"),
        P("shard", None),
        P("shard"),
        P("shard", None),
        P("shard"),
        P("shard", None),
        P("shard"),
        P("shard"),
        P("shard"),
        P("shard"),
        P("shard"),
        P(("rep", "shard"), None),
    )
    return jax.shard_map(
        sharded_heads if dict(mesh.shape) == {"rep": 4, "shard": H} else local,
        mesh=mesh,
        in_specs=placed,
        out_specs=(
            P(("rep", "shard"), None),
            P(("rep", "shard"), None),
            P("shard", None),
            P("shard"),
            P("shard", None),
            P("shard"),
            P("shard", None),
            P("shard"),
            P("shard", None),
            P("shard"),
            P("shard"),
            P("shard"),
            P("shard"),
            P("shard"),
        ),
        check_vma=False,
    )
```

```python
from functools import partial
import math

import jax
import jax.numpy as jnp
from jax import lax
from jax.experimental import pallas as pl
from jax.experimental.pallas import tpu as pltpu
from jax.sharding import PartitionSpec as P

H = 8
ROT = 64
DOCS = 4
LANES = 128
VMEM_LIMIT = 62 * 1024 * 1024

epsilon = 1e-05
masked_value = -1e30
f32 = jnp.float32
bf16 = jnp.bfloat16


def normalize(values):
    centre = jnp.mean(values, axis=1, keepdims=True)
    centred = values - centre
    spread = jnp.mean(centred * centred, axis=1, keepdims=True)
    inverse = lax.rsqrt(spread + epsilon)
    return (centred * inverse, inverse)


def layout(ends, count):
    index = jnp.arange(count, dtype=jnp.int32)
    passed = index[:, None] >= ends[None, :]
    document = jnp.sum(passed.astype(jnp.int32), axis=1)
    begin = jnp.max(jnp.where(passed, ends[None, :], 0), axis=1)
    position = (index - begin).astype(f32)
    allowed = (document[:, None] == document[None, :]) & (index[None, :] <= index[:, None])
    return (position, allowed, index < ends[-1])


def rotary_tables(position, rotary):
    half = rotary // 2
    freqs = jnp.exp(-jnp.arange(half, dtype=f32) * (2.0 / rotary) * math.log(10000.0))
    angles = position[..., None] * freqs
    angles = jnp.concatenate([angles, angles], axis=-1)
    return (jnp.cos(angles), jnp.sin(angles))


def rotate(values, cosine, sine, rotary):
    half = rotary // 2
    front = values[..., :rotary]
    turned = jnp.concatenate([-front[..., half:], front[..., :half]], axis=-1)
    return jnp.concatenate([front * cosine + turned * sine, values[..., rotary:]], axis=-1)


def unrotate(grads, cosine, sine, rotary):
    half = rotary // 2
    front = grads[..., :rotary]
    scaled = front * sine
    backward = jnp.concatenate([scaled[..., half:], -scaled[..., :half]], axis=-1)
    return jnp.concatenate([front * cosine + backward, grads[..., rotary:]], axis=-1)


def right_trans(left, right):
    return lax.dot_general(left, right, (((1,), (1,)), ((), ())), preferred_element_type=f32)


def left_trans(left, right):
    return lax.dot_general(left, right, (((0,), (0,)), ((), ())), preferred_element_type=f32)


def masked_scores(query_low, keys_low, allowed, factor):
    scores = (
        jnp.einsum("qhd,khd->hqk", query_low, keys_low, preferred_element_type=jnp.float32) * factor
    )
    return jnp.where(allowed[None], scores, masked_value)


def weight_sums(left, right):
    piece = lax.slice_in_dim(
        left, 0, left.shape[1] // lax.axis_size("shard") * lax.axis_size("shard"), axis=1
    )
    return lax.psum_scatter(
        left_trans(piece, right).astype(jnp.bfloat16), "shard", scatter_dimension=0, tiled=True
    ).astype(jnp.float32)


def local(
    tokens,
    document_ends,
    projector,
    projbias,
    combiner,
    combbias,
    expander,
    expbias,
    contractor,
    contbias,
    attendgain,
    attendshift,
    feedgain,
    feedshift,
    cotangent,
):
    count, width = tokens.shape
    headsize = width // H
    factor = 1.0 / math.sqrt(headsize)
    position, allowed, live = layout(document_ends[0], count)
    cosine, sine = rotary_tables(position, ROT)
    cosine, sine = cosine[:, None, :], sine[:, None, :]
    (
        full_projector,
        full_combiner,
        full_projbias,
        full_combbias,
        gain_attend,
        shift_attend,
        gain_feed,
        shift_feed,
    ) = (
        lax.all_gather(projector, "shard", axis=0, tiled=True),
        lax.all_gather(combiner, "shard", axis=0, tiled=True),
        lax.all_gather(projbias, "shard", axis=0, tiled=True),
        lax.all_gather(combbias, "shard", axis=0, tiled=True),
        lax.all_gather(attendgain, "shard", axis=0, tiled=True),
        lax.all_gather(attendshift, "shard", axis=0, tiled=True),
        lax.all_gather(feedgain, "shard", axis=0, tiled=True),
        lax.all_gather(feedshift, "shard", axis=0, tiled=True),
    )
    floated = tokens.astype(jnp.float32)
    normed, inverse = normalize(floated)
    first_input = (normed * gain_attend + shift_attend).astype(jnp.bfloat16)
    second_input = (normed * gain_feed + shift_feed).astype(jnp.bfloat16)
    mixed = jnp.dot(first_input, full_projector, preferred_element_type=jnp.float32) + full_projbias
    query_low = rotate(mixed[:, :width].reshape(count, H, headsize), cosine, sine, ROT).astype(
        jnp.bfloat16
    )
    keys_low = rotate(
        mixed[:, width : 2 * width].reshape(count, H, headsize), cosine, sine, ROT
    ).astype(jnp.bfloat16)
    values_low = mixed[:, 2 * width :].reshape(count, H, headsize).astype(jnp.bfloat16)
    scores = masked_scores(query_low, keys_low, allowed, factor)
    peak = jnp.max(scores, axis=2, keepdims=True)
    raised = jnp.exp(scores - peak)
    total = jnp.sum(raised, axis=2, keepdims=True)
    probs_low = (raised / total).astype(jnp.bfloat16)
    logsum = peak + jnp.log(total)
    context = jnp.einsum("hqk,khd->qhd", probs_low, values_low, preferred_element_type=jnp.float32)
    context = context.reshape(count, width).astype(jnp.bfloat16)
    attended = jnp.dot(context, full_combiner, preferred_element_type=jnp.float32) + full_combbias
    full_expander, full_contractor, full_expbias, full_contbias = (
        lax.all_gather(expander, "shard", axis=0, tiled=True),
        lax.all_gather(contractor, "shard", axis=0, tiled=True),
        lax.all_gather(expbias, "shard", axis=0, tiled=True),
        lax.all_gather(contbias, "shard", axis=0, tiled=True),
    )
    hidden = jnp.dot(second_input, full_expander, preferred_element_type=jnp.float32) + full_expbias
    activated, gelu_back = jax.vjp(partial(jax.nn.gelu, approximate=False), hidden)
    active_low = activated.astype(jnp.bfloat16)
    feedout = (
        jnp.dot(active_low, full_contractor, preferred_element_type=jnp.float32) + full_contbias
    )
    block_output = (floated + jnp.where(live[:, None], attended + feedout, 0.0)).astype(
        jnp.bfloat16
    )
    (
        back_projector,
        back_combiner,
        back_expander,
        back_contractor,
        back_gain_attend,
        back_gain_feed,
    ) = (
        lax.all_gather(projector, "shard", axis=0, tiled=True),
        lax.all_gather(combiner, "shard", axis=0, tiled=True),
        lax.all_gather(expander, "shard", axis=0, tiled=True),
        lax.all_gather(contractor, "shard", axis=0, tiled=True),
        lax.all_gather(attendgain, "shard", axis=0, tiled=True),
        lax.all_gather(feedgain, "shard", axis=0, tiled=True),
    )
    upstream = jnp.where(live[:, None], cotangent, jnp.zeros_like(cotangent))
    contractor_part = weight_sums(active_low, upstream)
    combiner_part = weight_sums(context, upstream)
    output_bias = jnp.sum(upstream, axis=0, dtype=jnp.float32)
    d_active = right_trans(upstream, back_contractor)
    d_hidden = gelu_back(d_active)[0].astype(jnp.bfloat16)
    expander_part = weight_sums(second_input, d_hidden)
    hidden_bias = jnp.sum(d_hidden, axis=0, dtype=jnp.float32)
    d_second = right_trans(d_hidden, back_expander)
    d_context = (
        right_trans(upstream, back_combiner).reshape(count, H, headsize).astype(jnp.bfloat16)
    )
    scores_again = masked_scores(query_low, keys_low, allowed, factor)
    probs = jnp.exp(scores_again - logsum)
    d_probs = jnp.einsum("qhd,khd->hqk", d_context, values_low, preferred_element_type=jnp.float32)
    d_values = jnp.einsum("hqk,qhd->khd", probs_low, d_context, preferred_element_type=jnp.float32)
    d_scores = (probs * (d_probs - jnp.sum(d_probs * probs, axis=2, keepdims=True))).astype(
        jnp.bfloat16
    )
    d_query = (
        jnp.einsum("hqk,khd->qhd", d_scores, keys_low, preferred_element_type=jnp.float32) * factor
    )
    d_keys = (
        jnp.einsum("hqk,qhd->khd", d_scores, query_low, preferred_element_type=jnp.float32) * factor
    )
    d_mixed = jnp.concatenate(
        [
            unrotate(d_query, cosine, sine, ROT).reshape(count, width),
            unrotate(d_keys, cosine, sine, ROT).reshape(count, width),
            d_values.reshape(count, width),
        ],
        axis=1,
    ).astype(jnp.bfloat16)
    projector_part = weight_sums(first_input, d_mixed)
    mixed_bias = jnp.sum(d_mixed, axis=0, dtype=jnp.float32)
    d_first = right_trans(d_mixed, back_projector)
    attend_scale = jnp.sum(d_first * normed, axis=0)
    attend_offset = jnp.sum(d_first, axis=0)
    feed_scale = jnp.sum(d_second * normed, axis=0)
    feed_offset = jnp.sum(d_second, axis=0)
    d_normed = d_first * back_gain_attend + d_second * back_gain_feed
    grad_float = cotangent.astype(jnp.float32) + inverse * (
        d_normed
        - jnp.mean(d_normed, axis=1, keepdims=True)
        - normed * jnp.mean(d_normed * normed, axis=1, keepdims=True)
    )
    input_gradient = grad_float.astype(jnp.bfloat16)
    mixed_bias, output_bias, hidden_bias, attend_scale, attend_offset, feed_scale, feed_offset = (
        lax.psum_scatter(
            mixed_bias.astype(jnp.bfloat16), "shard", scatter_dimension=0, tiled=True
        ).astype(jnp.float32),
        lax.psum_scatter(
            output_bias.astype(jnp.bfloat16), "shard", scatter_dimension=0, tiled=True
        ).astype(jnp.float32),
        lax.psum_scatter(
            hidden_bias.astype(jnp.bfloat16), "shard", scatter_dimension=0, tiled=True
        ).astype(jnp.float32),
        lax.psum_scatter(
            attend_scale.astype(jnp.bfloat16), "shard", scatter_dimension=0, tiled=True
        ).astype(jnp.float32),
        lax.psum_scatter(
            attend_offset.astype(jnp.bfloat16), "shard", scatter_dimension=0, tiled=True
        ).astype(jnp.float32),
        lax.psum_scatter(
            feed_scale.astype(jnp.bfloat16), "shard", scatter_dimension=0, tiled=True
        ).astype(jnp.float32),
        lax.psum_scatter(
            feed_offset.astype(jnp.bfloat16), "shard", scatter_dimension=0, tiled=True
        ).astype(jnp.float32),
    )
    (
        projector_part,
        mixed_bias,
        combiner_part,
        output_bias,
        expander_part,
        hidden_bias,
        contractor_part,
        attend_scale,
        attend_offset,
        feed_scale,
        feed_offset,
    ) = (
        lax.psum(projector_part.astype(jnp.bfloat16), "rep").astype(jnp.float32),
        lax.psum(mixed_bias.astype(jnp.bfloat16), "rep").astype(jnp.float32),
        lax.psum(combiner_part.astype(jnp.bfloat16), "rep").astype(jnp.float32),
        lax.psum(output_bias.astype(jnp.bfloat16), "rep").astype(jnp.float32),
        lax.psum(expander_part.astype(jnp.bfloat16), "rep").astype(jnp.float32),
        lax.psum(hidden_bias.astype(jnp.bfloat16), "rep").astype(jnp.float32),
        lax.psum(contractor_part.astype(jnp.bfloat16), "rep").astype(jnp.float32),
        lax.psum(attend_scale.astype(jnp.bfloat16), "rep").astype(jnp.float32),
        lax.psum(attend_offset.astype(jnp.bfloat16), "rep").astype(jnp.float32),
        lax.psum(feed_scale.astype(jnp.bfloat16), "rep").astype(jnp.float32),
        lax.psum(feed_offset.astype(jnp.bfloat16), "rep").astype(jnp.float32),
    )
    return (
        block_output,
        input_gradient,
        projector_part,
        mixed_bias,
        combiner_part,
        output_bias,
        expander_part,
        hidden_bias,
        contractor_part,
        output_bias,
        attend_scale,
        attend_offset,
        feed_scale,
        feed_offset,
    )


def lane_half(shape):
    return lax.broadcasted_iota(jnp.int32, shape, 1) < ROT // 2


def turn(front, signed):
    moved = jnp.where(
        lane_half(front.shape),
        pltpu.roll(front, LANES - ROT // 2, 1),
        pltpu.roll(front, ROT // 2, 1),
    )
    return moved * signed


def rotated(values, cosine, signed):
    front = values[:, :LANES]
    return jnp.concatenate([front * cosine + turn(front, signed), values[:, LANES:]], axis=1)


def unrotated(grads, cosine, signed):
    front = grads[:, :LANES]
    return jnp.concatenate([front * cosine - turn(front, signed), grads[:, LANES:]], axis=1)


def block_layout(ends, count):
    row = lax.broadcasted_iota(jnp.int32, (count, 1), 0).astype(f32)
    column = lax.broadcasted_iota(jnp.int32, (1, count), 1).astype(f32)
    row_doc = jnp.zeros((count, 1), f32)
    column_doc = jnp.zeros((1, count), f32)
    begin = jnp.zeros((count, 1), f32)
    for i in range(DOCS):
        end = ends[:, i : i + 1]
        row_doc += jnp.where(row >= end, 1.0, 0.0)
        column_doc += jnp.where(column >= end, 1.0, 0.0)
        begin = jnp.maximum(begin, jnp.where(row >= end, end, 0.0))
    return (row_doc == column_doc) & (column <= row), row - begin


def dot(left, right):
    return jnp.dot(left, right, preferred_element_type=f32)


def softmax(q, k, allowed):
    scores = right_trans(q, k) * (1.0 / math.sqrt(q.shape[1]))
    scores = jnp.where(allowed, scores, masked_value)
    raised = jnp.exp(scores - jnp.max(scores, axis=1, keepdims=True))
    return raised / jnp.sum(raised, axis=1, keepdims=True)


def norm_parts(x_ref, at):
    x = x_ref[at, :].astype(f32)
    centre = jnp.mean(x, axis=1, keepdims=True)
    centred = x - centre
    inverse = lax.rsqrt(jnp.mean(centred * centred, axis=1, keepdims=True) + epsilon)
    return centred, centre, inverse


def tables(ends, count, angles_ref):
    allowed, place = block_layout(ends, count)
    angles = place * angles_ref[0:1, :]
    return allowed, jnp.cos(angles), jnp.sin(angles) * angles_ref[1:2, :]


def forward_pass(
    x_ref, ends, count, angles_ref, norms_ref, pbias_ref, ebias_ref, proj_ref, exp_ref, comb_ref,
    cont_ref, h1_ref, h2_ref, qkv_ref, ca_ref, slope_ref, stats_ref, part_ref,
):
    slots, width = x_ref.shape
    head = comb_ref.shape[0]
    units = exp_ref.shape[1]
    step = min(64, count)

    @pl.loop(0, slots // step)
    def _(i):
        at = rows_at(i * step, step)
        centred, centre, inverse = norm_parts(x_ref, at)
        normed = centred * inverse
        h1_ref[at, :] = (normed * norms_ref[0:1, :] + norms_ref[1:2, :]).astype(bf16)
        h2_ref[at, :] = (normed * norms_ref[2:3, :] + norms_ref[3:4, :]).astype(bf16)
        stats_ref[at, 0:1] = centre
        stats_ref[at, 1:2] = inverse

    for j in range(3):
        cut = slice(j * head, j * head + head)
        mixed = dot(h1_ref[...], proj_ref[:, cut]) + pbias_ref[:, cut]
        for b in range(slots // count):
            at = slice(b * count, b * count + count)
            value = mixed[at]
            if j < 2:
                _, cosine, signed = tables(ends[b], count, angles_ref)
                value = rotated(value, cosine, signed)
            qkv_ref[at, cut] = value.astype(bf16)
    tile = min(256, units)
    for start in range(0, units, tile):
        hidden = dot(h2_ref[...], exp_ref[:, start : start + tile])
        hidden += ebias_ref[:, start : start + tile]
        below = 0.5 + 0.5 * lax.erf(hidden * math.sqrt(0.5))
        ca_ref[:, head + start : head + start + tile] = (hidden * below).astype(bf16)
        density = jnp.exp(hidden * hidden * -0.5) * (1.0 / math.sqrt(2.0 * math.pi))
        slope_ref[:, start : start + tile] = (below + hidden * density).astype(bf16)
    for b in range(slots // count):
        at = slice(b * count, b * count + count)
        allowed, _ = block_layout(ends[b], count)
        probs = softmax(qkv_ref[at, :head], qkv_ref[at, head : 2 * head], allowed).astype(bf16)
        ca_ref[at, :head] = dot(probs, qkv_ref[at, 2 * head :]).astype(bf16)
    tile = min(512, width)
    for start in range(0, width, tile):
        cut = slice(start, start + tile)
        part = dot(ca_ref[:, :head], comb_ref[:, cut]) + dot(ca_ref[:, head:], cont_ref[:, cut])
        part_ref[:, cut] = part.astype(bf16)


def backward_pass(
    x_ref, up_ref, ends, count, angles_ref, norms_ref, qkv_ref, slope_ref, stats_ref, proj_ref,
    exp_ref, comb_ref, cont_ref, dh_ref, dm_ref, dn_ref, sums_ref, hbias_ref, mbias_ref, obias_ref,
):
    slots, width = x_ref.shape
    head = comb_ref.shape[0]
    units = exp_ref.shape[1]
    tile = min(256, units)
    d_context = right_trans(up_ref[...], comb_ref[...]).astype(bf16)
    for start in range(0, units, tile):
        cut = slice(start, start + tile)
        d_active = right_trans(up_ref[...], cont_ref[cut, :])
        d_hidden = (d_active * slope_ref[:, cut].astype(f32)).astype(bf16)
        dh_ref[:, cut] = d_hidden
        hbias_ref[:, cut] += jnp.sum(d_hidden.astype(f32), axis=0, keepdims=True)
    factor = 1.0 / math.sqrt(head)
    for b in range(slots // count):
        at = slice(b * count, b * count + count)
        allowed, cosine, signed = tables(ends[b], count, angles_ref)
        q, k = qkv_ref[at, :head], qkv_ref[at, head : 2 * head]
        v = qkv_ref[at, 2 * head :]
        d_ctx = d_context[at]
        probs = softmax(q, k, allowed)
        d_probs = right_trans(d_ctx, v)
        d_v = left_trans(probs.astype(bf16), d_ctx)
        d_s = probs * (d_probs - jnp.sum(d_probs * probs, axis=1, keepdims=True))
        d_s = d_s.astype(bf16)
        dm_ref[at, :head] = unrotated(dot(d_s, k) * factor, cosine, signed).astype(bf16)
        d_k = unrotated(left_trans(d_s, q) * factor, cosine, signed).astype(bf16)
        dm_ref[at, head : 2 * head] = d_k
        dm_ref[at, 2 * head :] = d_v.astype(bf16)
    mbias_ref[...] += jnp.sum(dm_ref[...].astype(f32), axis=0, keepdims=True)
    obias_ref[...] += jnp.sum(up_ref[...].astype(f32), axis=0, keepdims=True)
    centre, inverse = stats_ref[:, 0:1], stats_ref[:, 1:2]
    tile = min(256, width)

    @pl.loop(0, width // tile, unroll=2)
    def _(i):
        cut = rows_at(i * tile, tile)
        normed = (x_ref[:, cut].astype(f32) - centre) * inverse
        d_first = right_trans(dm_ref[...], proj_ref[cut, :])
        d_second = right_trans(dh_ref[...], exp_ref[cut, :])
        dn_ref[:, cut] = (
            d_first * norms_ref[0:1, cut] + d_second * norms_ref[2:3, cut]
        ).astype(bf16)
        sums_ref[0:1, cut] += jnp.sum(d_first * normed, axis=0, keepdims=True)
        sums_ref[1:2, cut] += jnp.sum(d_first, axis=0, keepdims=True)
        sums_ref[2:3, cut] += jnp.sum(d_second * normed, axis=0, keepdims=True)
        sums_ref[3:4, cut] += jnp.sum(d_second, axis=0, keepdims=True)


def accumulate(total, left, right, tall):
    wide = min(256, right.shape[1])

    @pl.loop(0, left.shape[1] // tall)
    def _(i):
        at = pl.ds(pl.multiple_of(i * tall, LANES), tall)
        for start in range(0, right.shape[1], wide):
            cut = slice(start, start + wide)
            total[at, cut] += left_trans(left[:, at], right[:, cut])


MESH = pl.DeviceIdType.MESH
GATHER_SEMS = 96


def position_of():
    rep, me = lax.axis_index("rep"), lax.axis_index("shard")
    return rep, me, lax.div(rep, 2), lax.rem(rep, 2), lax.div(me, 2), lax.rem(me, 2)


def meet(peers):
    barrier = pltpu.get_barrier_semaphore()
    for peer in peers:
        pl.semaphore_signal(barrier, inc=1, device_id=peer, device_id_type=MESH)
    pl.semaphore_wait(barrier, len(peers))


def rows_at(start, size):
    return pl.ds(pl.multiple_of(start, size), size)


class Net:
    def __init__(self, send_sem, recv_sem, local_sem):
        self.send_sem, self.recv_sem, self.local_sem = send_sem, recv_sem, local_sem
        self.sends, self.locals, self.started, self.sent = 0, 0, 0, []

    def slots(self, count):
        first = self.started
        self.started += count
        return first

    def send(self, src, dst, peer, slot, when=None):
        index = self.sends
        self.sends += 1
        copy = pltpu.make_async_remote_copy(
            src_ref=src, dst_ref=dst, send_sem=self.send_sem.at[index],
            recv_sem=self.recv_sem.at[slot], device_id=peer, device_id_type=MESH,
        )
        if when is None:
            copy.start()
        else:
            pl.when(when)(lambda: copy.start())
        self.sent.append((copy, when))

    def arrived(self, dst, peer, slot):
        pltpu.make_async_remote_copy(
            src_ref=dst, dst_ref=dst, send_sem=self.send_sem.at[0],
            recv_sem=self.recv_sem.at[slot], device_id=peer, device_id_type=MESH,
        ).wait_recv()

    def local(self, src, dst):
        copy = pltpu.make_async_copy(src, dst, self.local_sem.at[self.locals])
        self.locals += 1
        copy.start()
        return copy

    def finish(self):
        for copy, when in self.sent:
            if when is None:
                copy.wait_send()
            else:
                pl.when(when)(lambda copy=copy: copy.wait_send())


class Chain:
    def __init__(self, source, out, count, where, sems):
        self.source, self.out, self.count = source, out, count
        self.rep, self.me, self.z, self.c = where
        self.side_send, self.side_recv, self.core_send, self.core_recv = sems
        self.sibling = self.me + 1 - 2 * self.c

    def block(self, shard):
        return self.out.at[rows_at(shard * self.count, self.count)]

    def side(self, side, step):
        block = self.block(self.me - side * 2 * step)
        peer = (self.rep, self.me + side * 2)
        index = (0 if side > 0 else 4) + step
        return pltpu.make_async_remote_copy(
            src_ref=block, dst_ref=block, send_sem=self.side_send.at[index],
            recv_sem=self.side_recv.at[index], device_id=peer, device_id_type=MESH,
        )

    def cross(self, side, step):
        block = self.block(self.me - side * 2 * step)
        index = (0 if side > 0 else 4) + step
        return pltpu.make_async_remote_copy(
            src_ref=block, dst_ref=block, send_sem=self.core_send.at[index],
            recv_sem=self.core_recv.at[index], device_id=(self.rep, self.sibling),
            device_id_type=MESH,
        )

    def taken(self, side, step):
        block = self.block(self.sibling - side * 2 * step)
        index = (0 if side > 0 else 4) + step
        return pltpu.make_async_remote_copy(
            src_ref=block, dst_ref=block, send_sem=self.core_send.at[index],
            recv_sem=self.core_recv.at[index], device_id=(self.rep, self.sibling),
            device_id_type=MESH,
        )

    def here(self, side, step):
        return self.z >= step if side > 0 else self.z + step <= 3

    def on(self, side):
        return self.z < 3 if side > 0 else self.z > 0

    def first(self, side):
        mine = self.block(self.me)
        index = 0 if side > 0 else 4
        return pltpu.make_async_remote_copy(
            src_ref=self.source, dst_ref=mine, send_sem=self.side_send.at[index],
            recv_sem=self.side_recv.at[index], device_id=(self.rep, self.me + side * 2),
            device_id_type=MESH,
        )

    def first_cross(self):
        mine = self.block(self.me)
        return pltpu.make_async_remote_copy(
            src_ref=self.source, dst_ref=mine, send_sem=self.core_send.at[0],
            recv_sem=self.core_recv.at[0], device_id=(self.rep, self.sibling),
            device_id_type=MESH,
        )

    def begin(self):
        for side in (1, -1):
            pl.when(self.on(side))(lambda: self.first(side).start())
        self.first_cross().start()
    def wait_own(self):
        self.taken(1, 0).wait_recv()

    def step(self, step):
        for side in (1, -1):
            here = self.here(side, step)

            @pl.when(here)
            def _():
                block = self.block(self.me - side * 2 * step)
                index = (0 if side > 0 else 4) + step - 1
                pltpu.make_async_remote_copy(
                    src_ref=block, dst_ref=block, send_sem=self.side_send.at[index],
                    recv_sem=self.side_recv.at[index], device_id=(self.rep, self.sibling),
                    device_id_type=MESH,
                ).wait_recv()
                self.cross(side, step).start()

            pl.when(here & self.on(side) & (step < 3))(lambda: self.side(side, step).start())

    def take(self, step):
        for side in (1, -1):
            pl.when(self.here(side, step))(lambda: self.taken(side, step).wait_recv())

    def finish(self):
        self.first_cross().wait_send()
        for side in (1, -1):
            pl.when(self.on(side))(lambda: self.first(side).wait_send())
            for step in (1, 2, 3):
                here = self.here(side, step)
                pl.when(here)(lambda: self.cross(side, step).wait_send())
                if step < 3:
                    pl.when(here & self.on(side))(lambda: self.side(side, step).wait_send())


def block_kernel(
    tok_ref, vec_ref, up_ref, expander_ref, projector_ref, comb_hbm, cont_hbm, ebias_ref,
    angles_ref,
    x_out, up_out, low_out, he_out, hp_out, part_out, dn_out, vec_out, own_out, norms_ref,
    exp_ref, proj_ref, comb_ref, cont_ref, low_sum, he_sum, hp_sum,
    xs, us, h1s, h2s, ca, slope, qkv, dh, dm, parts, dns, stats,
    vecs, bias_all, ends_all, pbias, sums, hbias, mbias, obias,
    send_sem, recv_sem, local_sem, load_sem, store_sem,
    xs_send, xs_recv, xc_send, xc_recv, us_send, us_recv, uc_send, uc_recv,
):
    rep, me, y, x, z, c = position_of()
    count, width = tok_ref.shape
    rows, quarter = expander_ref.shape[0], expander_ref.shape[0] // 4
    units, mix = exp_ref.shape[1], proj_ref.shape[1]
    head = mix // 3
    sibling = (rep, me + 1 - 2 * c)
    by_x, by_y = (rep + 1 - 2 * x, me), (rep + 2 - 4 * y, me)
    ring = [(rep, lax.rem(me + k, 8)) for k in range(1, 8)]
    meet(ring + [by_x, by_y])
    net = Net(send_sem, recv_sem, local_sem)

    def weight_copies(go, first, size, source_rows, t):
        source = rows_at(source_rows, size)
        target = rows_at(first, size)
        go(expander_ref.at[source, rows_at(t * units, units)], exp_ref.at[target, :])
        for j in range(3):
            go(
                projector_ref.at[source, rows_at(j * width + t * head, head)],
                proj_ref.at[target, pl.ds(j * head, head)],
            )

    remote = net.slots(24)
    for step in (1, 2, 3):
        tz = lax.rem(z + step, 4)
        for core in (0, 1):
            part = [0]

            def go(src, dst):
                net.send(
                    src, dst, (rep, tz * 2 + core), remote + ((step - 1) * 2 + c) * 4 + part[0]
                )
                part[0] += 1

            weight_copies(go, me * rows + rep * quarter, quarter, rep * quarter, tz * 2 + core)
    small = net.slots(7)
    for k, peer in enumerate(ring):
        net.send(vec_ref, vecs.at[me], peer, small + k)
    where = (rep, me, z, c)
    tokens = Chain(
        tok_ref, x_out, count, where, (xs_send, xs_recv, xc_send, xc_recv)
    )
    cotangents = Chain(
        up_ref, up_out, count, where, (us_send, us_recv, uc_send, uc_recv)
    )
    tokens.begin()
    near = net.slots(4)
    part = [0]

    def go_near(src, dst):
        net.send(src, dst, sibling, near + part[0])
        part[0] += 1

    weight_copies(go_near, me * rows, rows, 0, sibling[1])
    copies = []
    weight_copies(lambda s, d: copies.append(net.local(s, d)), me * rows, rows, 0, me)
    copies.append(net.local(vec_ref, vecs.at[me]))
    copies.append(net.local(comb_hbm, comb_ref))
    copies.append(net.local(cont_hbm, cont_ref))
    cotangents.begin()
    for ref in (low_sum, he_sum, hp_sum, sums, hbias, mbias, obias):
        if ref.shape[0] <= 8:
            ref[...] = jnp.zeros_like(ref)
        else:

            @pl.loop(0, ref.shape[0] // 64)
            def _(i):
                ref[rows_at(i * 64, 64), :] = jnp.zeros((64, ref.shape[1]), f32)

    def shard_rows(step, core):
        return (lax.rem(z + 4 - step, 4) * 2 + core) * rows

    first_hop = net.slots(12)
    for step in (1, 2, 3):
        for core in (0, 1):
            base = shard_rows(step, core)
            at = rows_at(base + rep * quarter, quarter)
            slot = remote + ((step - 1) * 2 + core) * 4
            net.arrived(exp_ref.at[at, :], sibling, slot)
            for j in range(3):
                net.arrived(proj_ref.at[at, pl.ds(j * head, head)], sibling, slot + 1 + j)
            peer = by_x if core == 0 else by_y
            hop = first_hop + ((step - 1) * 2 + core) * 2
            net.send(exp_ref.at[at, :], exp_ref.at[at, :], peer, hop)
            net.send(proj_ref.at[at, :], proj_ref.at[at, :], peer, hop + 1)
    tokens.step(1)
    second_hop = net.slots(18)
    gone = []
    for step in (1, 2, 3):
        for core in (0, 1):
            base = shard_rows(step, core)
            hop = first_hop + ((step - 1) * 2 + core) * 2
            if core == 0:
                other = rows_at(base + (rep + 1 - 2 * x) * quarter, quarter)
            else:
                other = rows_at(base + (rep + 2 - 4 * y) * quarter, quarter)
            net.arrived(exp_ref.at[other, :], sibling, hop)
            net.arrived(proj_ref.at[other, :], sibling, hop + 1)
            hop = second_hop + (step - 1) * 6
            if core == 0:
                pieces = [(rows_at(base + y * 2 * quarter, 2 * quarter), by_y, hop)]
                gone += [(rows_at(base + (1 - y) * 2 * quarter, 2 * quarter), hop)]
            else:
                here = rows_at(base + rep * quarter, quarter)
                pieces = [(here, by_x, hop + 2), (other, by_x, hop + 4)]
                gone += [
                    (rows_at(base + (rep + 1 - 2 * x) * quarter, quarter), hop + 2),
                    (rows_at(base + (3 - rep) * quarter, quarter), hop + 4),
                ]
            for at, peer, slot in pieces:
                net.send(exp_ref.at[at, :], exp_ref.at[at, :], peer, slot)
                net.send(proj_ref.at[at, :], proj_ref.at[at, :], peer, slot + 1)

    for k in range(1, 8):
        net.arrived(vecs.at[lax.rem(me + 8 - k, 8)], sibling, small + k - 1)
    for copy in copies:
        copy.wait()
    for s in range(8):
        values = vecs[s].astype(f32)
        for j in range(3):
            bias_all[3 * s + j] = values[6 + j : 7 + j, :]
        ends_all[s] = values[9:10, :LANES]
        norms_ref[:, s * rows : s * rows + rows] = values[:8, :]
    for j in range(3):
        pbias[:, j * head : j * head + head] = bias_all[8 * j + me]

    at = rows_at(sibling[1] * rows, rows)
    net.arrived(exp_ref.at[at, :], sibling, near)
    for j in range(3):
        net.arrived(proj_ref.at[at, pl.ds(j * head, head)], sibling, near + 1 + j)
    for at, slot in gone:
        net.arrived(exp_ref.at[at, :], sibling, slot)
        net.arrived(proj_ref.at[at, :], sibling, slot + 1)
    tokens.wait_own()
    cotangents.wait_own()
    cotangents.step(1)

    def chip_of(slot):
        second = jnp.where(z == 0, 2, jnp.where(z == 1, 0, 1))
        last = jnp.where(z < 2, 3, 0)
        after = jnp.where(z < 3, z + 1, 2)
        return jnp.where(
            slot == 0, z, jnp.where(slot == 1, after, jnp.where(slot == 2, second, last))
        )

    class Loads:
        def __init__(self, own, source, into, first):
            self.own, self.source, self.into, self.first = own, source, into, first

        def start_own(self):
            theirs = self.source.at[rows_at(sibling[1] * count, count)]
            for source, b in ((self.own, c), (theirs, 1 - c)):
                pltpu.make_async_copy(
                    source, self.into.at[rows_at(b * count, count)], load_sem.at[self.first + b]
                ).start()

        def copies(self, slot):
            return [
                pltpu.make_async_copy(
                    self.source.at[rows_at((chip_of(slot) * 2 + b) * count, count)],
                    self.into.at[rows_at(b * count, count)], load_sem.at[self.first + b],
                )
                for b in range(2)
            ]

        def start(self, slot):
            for copy in self.copies(slot):
                copy.start()

        def wait(self, slot):
            for copy in self.copies(slot):
                copy.wait()

    x_loads, up_loads = Loads(tok_ref, x_out, xs, 0), Loads(up_ref, up_out, us, 2)
    x_loads.start_own()
    up_loads.start_own()

    @pl.loop(0, 4)
    def _(slot):
        chip = chip_of(slot)
        ends = [ends_all[chip * 2 + b] for b in range(2)]

        def stores(source, into, first):
            return [
                pltpu.make_async_copy(
                    source.at[rows_at(b * count, count)], into.at[chip, b],
                    store_sem.at[first + b],
                )
                for b in range(2)
            ]

        x_loads.wait(slot)
        forward_pass(
            xs, ends, count, angles_ref, norms_ref, pbias, ebias_ref, proj_ref, exp_ref, comb_ref,
            cont_ref, h1s, h2s, qkv, ca, slope, stats, parts,
        )
        for store in stores(parts, part_out, 0):
            store.start()
        pl.when(slot == 2)(lambda: tokens.step(3))

        @pl.when(slot == 3)
        def _():
            cotangents.take(slot)
            up_loads.start(slot)

        up_loads.wait(slot)
        backward_pass(
            xs, us, ends, count, angles_ref, norms_ref, qkv, slope, stats, proj_ref, exp_ref,
            comb_ref, cont_ref, dh, dm, dns, sums, hbias, mbias, obias,
        )
        for store in stores(dns, dn_out, 2):
            store.start()
        pl.when(slot == 0)(lambda: tokens.step(2))
        pl.when(slot == 1)(lambda: cotangents.step(2))

        @pl.when(slot < 3)
        def _():
            tokens.take(slot + 1)
            x_loads.start(slot + 1)

        accumulate(low_sum, ca, us, ca.shape[1])

        @pl.when(slot < 2)
        def _():
            cotangents.take(slot + 1)
            up_loads.start(slot + 1)

        accumulate(he_sum, h2s, dh, width // 2)
        accumulate(hp_sum, h1s, dm, width // 2)
        for store in stores(parts, part_out, 0) + stores(dns, dn_out, 2):
            store.wait()
        pl.when(slot == 2)(lambda: cotangents.step(3))

    for total, out, stage in (
        (low_sum, low_out, h1s), (he_sum, he_out, dh), (hp_sum, hp_out, dm)
    ):
        step = count

        @pl.loop(0, total.shape[0] // step)
        def _(i):
            at = rows_at(lax.rem(i, 2) * step, step)
            move = pltpu.make_async_copy(
                stage.at[at], out.at[rows_at(i * step, step)], store_sem.at[lax.rem(i, 2)]
            )
            pl.when(i >= 2)(lambda: move.wait())
            stage[at, :] = total[rows_at(i * step, step), :].astype(bf16)
            move.start()

        for i in range(2):
            pltpu.make_async_copy(
                stage.at[rows_at(i * step, step)], out.at[rows_at(i * step, step)], store_sem.at[i]
            ).wait()
    vec_out[...] = jnp.zeros_like(vec_out)
    own_out[...] = jnp.zeros_like(own_out)
    per = rows // LANES
    for t in range(8):
        for j in range(4):
            for i in range(per):
                at = t * rows + i * LANES
                vec_out[t, j * per + i : j * per + i + 1, :] = sums[j : j + 1, at : at + LANES]
        for i in range(mix // LANES):
            at = 4 * per + i
            vec_out[t, at : at + 1, :] = mbias[:, i * LANES : (i + 1) * LANES]
    for i in range(units // LANES):
        own_out[i : i + 1, :] = hbias[:, i * LANES : (i + 1) * LANES]
    for i in range(per):
        own_out[units // LANES + i : units // LANES + i + 1, :] = obias[
            :, rows_at(me * rows + i * LANES, LANES)
        ]
    tokens.finish()
    cotangents.finish()
    net.finish()
    assert net.sends <= GATHER_SEMS and net.started <= GATHER_SEMS and net.locals <= 8


def block_passes(tokens, vectors, upstream, expander, projector, combiner, contractor, ebias, angles):
    count, width = tokens.shape
    n = lax.axis_size("shard")
    units, mix, head = expander.shape[1] // n, projector.shape[1] // n, combiner.shape[0]
    low = head + units
    vmem, dma = pltpu.VMEM, pltpu.SemaphoreType.DMA
    shapes = [
        (n * count, width), (n * count, width), (low, width), (width, units), (width, mix),
        (n // 2, 2, count, width), (n // 2, 2, count, width),
    ]
    two = 2 * count
    return pl.pallas_call(
        block_kernel,
        out_shape=[jax.ShapeDtypeStruct(s, bf16) for s in shapes] + [
            jax.ShapeDtypeStruct((n, 16, LANES), f32),
            jax.ShapeDtypeStruct((16, LANES), f32),
            jax.ShapeDtypeStruct((8, width), f32),
        ],
        in_specs=[pl.BlockSpec(memory_space=pl.ANY)] * 7 + [pl.BlockSpec(memory_space=vmem)] * 2,
        out_specs=[pl.BlockSpec(memory_space=pl.ANY)] * 7 + [pl.BlockSpec(memory_space=vmem)] * 3,
        scratch_shapes=[
            vmem((width, units), bf16), vmem((width, mix), bf16), vmem((head, width), bf16),
            vmem((units, width), bf16), vmem((low, width), f32), vmem((width, units), f32),
            vmem((width, mix), f32),
            vmem((two, width), bf16), vmem((two, width), bf16),
            vmem((two, width), bf16), vmem((two, width), bf16), vmem((two, low), bf16),
            vmem((two, units), bf16), vmem((two, mix), bf16), vmem((two, units), bf16),
            vmem((two, mix), bf16), vmem((two, width), bf16), vmem((two, width), bf16),
            vmem((two, LANES), f32),
            vmem((n,) + vectors.shape, bf16), vmem((3 * n, 1, vectors.shape[1]), f32),
            vmem((n, 1, LANES), f32),
            vmem((1, mix), f32), vmem((4, width), f32), vmem((1, units), f32),
            vmem((1, mix), f32), vmem((1, width), f32),
            dma((GATHER_SEMS,)), dma((GATHER_SEMS,)), dma((8,)), dma((4,)), dma((4,)),
        ] + [dma((8,))] * 8,
        compiler_params=pltpu.CompilerParams(
            collective_id=0, has_side_effects=True, vmem_limit_bytes=VMEM_LIMIT
        ),
    )(tokens, vectors, upstream, expander, projector, combiner, contractor, ebias, angles)


def add_into(target, other):
    rows = target.shape[-2]
    step = min(32, rows)

    @pl.loop(0, rows // step)
    def _(i):
        at = (Ellipsis, pl.ds(pl.multiple_of(i * step, step), step), slice(None))
        lead = (slice(None),) * (len(target.shape) - 2)
        at = lead + at[1:]
        target[at] = (target[at].astype(f32) + other[at].astype(f32)).astype(target.dtype)


def settle_kernel(
    low_ref, he_ref, hp_ref, part_ref, dn_ref, vec_ref, own_ref,
    low_out, exp_out, proj_out, osum_out, dsum_out, vec_out,
    low_a, low_a1, low_a2, low_b, low_b1, low_b2,
    he_a, he_a1, he_a2, he_b, he_b1, he_b2,
    hp_a, hp_a1, hp_a2, hp_b, hp_b1, hp_b2,
    o_in, o_sum, o_right, o_left, d_in, d_sum, d_right, d_left,
    vec_in, vec_mix, vec_all, send_sem, recv_sem, local_sem,
):
    rep, me, y, x, z, c = position_of()
    width = low_ref.shape[-1]
    units, mix = he_ref.shape[-1], hp_ref.shape[-1]
    head = mix // 3
    sibling = (rep, me + 1 - 2 * c)
    x_rep, y_rep, d_rep = rep + 1 - 2 * x, rep + 2 - 4 * y, 3 - rep
    by_x, by_y, across = (x_rep, me), (y_rep, me), (d_rep, me)
    ring = [(rep, lax.rem(me + k, 8)) for k in range(1, 8)]
    meet(ring + [by_x, by_y, across])
    net = Net(send_sem, recv_sem, local_sem)

    class Sum:
        def __init__(self, ref, at, a, a1, a2, b, b1, b2):
            self.ref, self.at = ref, at
            self.a, self.a1, self.a2, self.b, self.b1, self.b2 = a, a1, a2, b, b1, b2
            self.slot = net.slots(6)

        def load(self):
            self.loads = []
            for i in range(2):
                self.loads.append(net.local(self.at(self.ref, i * 2 + x, 0), self.a.at[i]))
                self.loads.append(net.local(self.at(self.ref, y * 2 + i, 1), self.b.at[i]))

        def first(self):
            for i in range(2):
                source = self.at(self.ref, i * 2 + 1 - x, 0)
                net.send(source, self.a1.at[i], by_x, self.slot + i)
                source = self.at(self.ref, (1 - y) * 2 + i, 1)
                net.send(source, self.b1.at[i], by_y, self.slot + 2 + i)

        def second(self):
            for load in self.loads:
                load.wait()
            for i in range(2):
                net.arrived(self.a1.at[i], sibling, self.slot + i)
                add_into(self.a.at[i], self.a1.at[i])
            net.send(self.a.at[1 - y], self.a2, by_y, self.slot + 4)
            for i in range(2):
                net.arrived(self.b1.at[i], sibling, self.slot + 2 + i)
                add_into(self.b.at[i], self.b1.at[i])
            net.send(self.b.at[1 - x], self.b2, by_x, self.slot + 5)

        def third(self):
            net.arrived(self.a2, sibling, self.slot + 4)
            add_into(self.a.at[y], self.a2)
            net.arrived(self.b2, sibling, self.slot + 5)
            add_into(self.b.at[x], self.b2)
            return self.a.at[y], self.b.at[x]

    def deep(ref, quarter, half):
        return ref.at[:, quarter, half]

    he = Sum(he_ref, deep, he_a, he_a1, he_a2, he_b, he_b1, he_b2)
    hp = Sum(hp_ref, deep, hp_a, hp_a1, hp_a2, hp_b, hp_b1, hp_b2)
    low = Sum(
        low_ref, lambda ref, quarter, half: ref.at[quarter, half],
        low_a, low_a1, low_a2, low_b, low_b1, low_b2,
    )

    he.first()
    hp.first()
    he.load()
    hp.load()

    class Line:
        def __init__(self, ref, inward, total, right, left):
            self.inward, self.total, self.right, self.left = inward, total, right, left
            self.slot = net.slots(10)
            self.loads = []
            for i in range(4):
                net.send(ref.at[i, 1 - c], inward.at[i], sibling, self.slot + i)
                self.loads.append(net.local(ref.at[i, c], total.at[i]))

        def push(self, block, step, side, when):
            into = self.right if side > 0 else self.left
            slot = self.slot + 4 + (step - 1) + (0 if side > 0 else 3)
            net.send(self.total.at[block], into.at[step - 1], (rep, me + 2 * side), slot, when)

        def join(self):
            for i in range(4):
                self.loads[i].wait()
                net.arrived(self.inward.at[i], sibling, self.slot + i)
                add_into(self.total.at[i], self.inward.at[i])

        def begin(self):
            for step in (3, 2, 1):
                self.push(step, step, 1, z == 0)
                self.push(3 - step, step, -1, z == 3)

        def step_on(self, step):
            for side, into, first in ((1, self.right, 4), (-1, self.left, 7)):
                block = z + side * (step - 1)
                here = (z >= 1) & (block <= 3) if side > 0 else (z <= 2) & (block >= 0)

                @pl.when(here)
                def _():
                    net.arrived(into.at[step - 1], sibling, self.slot + first + step - 1)
                    add_into(self.total.at[block], into.at[step - 1])

                if step > 1:
                    self.push(block, step - 1, side, here)

    out = Line(part_ref, o_in, o_sum, o_right, o_left)
    back = Line(dn_ref, d_in, d_sum, d_right, d_left)

    small = net.slots(7)
    for k in range(1, 8):
        t = lax.rem(me + k, 8)
        net.send(vec_ref.at[t], vec_in.at[me], (rep, t), small + k - 1)
    vec_load = net.local(vec_ref.at[me], vec_in.at[me])
    own_load = net.local(own_ref, vec_mix.at[pl.ds(56, 16)])
    low.load()

    out.join()
    out.begin()
    he.second()
    out.step_on(3)
    back.join()
    hp.second()
    low.first()
    out.step_on(2)

    class Turn:
        def __init__(self, source, half, place):
            self.half, self.place = half, place
            self.slot = net.slots(21)
            self.copies = []
            for k in range(1, 8):
                t = lax.rem(me + k, 8)
                for j, (src, dst) in enumerate(place(source, t, me)):
                    net.send(src, dst, (rep, t), self.slot + (k - 1) * 3 + j)
            for src, dst in place(source, me, me):
                self.copies.append(net.local(src, dst))

        def wait(self):
            for k in range(1, 8):
                s = lax.rem(me + 8 - k, 8)
                for j, (_, dst) in enumerate(self.place(None, me, s)):
                    net.arrived(dst, sibling, self.slot + (k - 1) * 3 + j)
            for copy in self.copies:
                copy.wait()

    def place_exp(half):
        return lambda source, t, s: [(
            None if source is None else source.at[t],
            exp_out.at[rep, half, :, rows_at(s * units, units)],
        )]

    def place_proj(half):
        return lambda source, t, s: [
            (
                None if source is None else source.at[t, :, pl.ds(j * head, head)],
                proj_out.at[rep, half, :, rows_at(j * width + s * head, head)],
            )
            for j in range(3)
        ]

    he_done = he.third()
    he_turns = [Turn(he_done[h], h, place_exp(h)) for h in range(2)]
    hp_done = hp.third()
    hp_turns = [Turn(hp_done[h], h, place_proj(h)) for h in range(2)]
    out.step_on(1)
    back.begin()
    low.second()
    for k in range(1, 8):
        net.arrived(vec_in.at[lax.rem(me + 8 - k, 8)], sibling, small + k - 1)
    vec_load.wait()
    own_load.wait()
    total = vec_in[0, 0:8]
    for s in range(1, 8):
        total += vec_in[s, 0:8]
    vec_mix[0:8] = total
    for s in range(8):
        vec_mix[8 + 6 * s : 14 + 6 * s] = vec_in[s, 8:14]
    wide = net.slots(4)
    net.send(vec_mix, vec_all.at[rep], by_x, wide + 1)
    net.send(vec_mix, vec_all.at[rep], by_y, wide + 2)
    net.send(vec_mix, vec_all.at[rep], across, wide + 3)
    vec_copy = net.local(vec_mix, vec_all.at[rep])

    class Spread:
        def __init__(self, target, sources):
            self.target, self.slot = target, net.slots(6)
            for h, source in enumerate(sources):
                for k, peer in enumerate((by_x, by_y)):
                    net.send(source, target.at[rep, h], peer, self.slot + h * 3 + k)

        def on(self):
            for h, (k, got, peer) in enumerate(((1, y_rep, by_x), (0, x_rep, by_y))):
                net.arrived(self.target.at[got, h], sibling, self.slot + h * 3 + k)
                net.send(self.target.at[got, h], self.target.at[got, h], peer, self.slot + h * 3 + 2)

        def wait(self):
            for h, (k, got) in enumerate(((0, x_rep), (1, y_rep))):
                net.arrived(self.target.at[got, h], sibling, self.slot + h * 3 + k)
                net.arrived(self.target.at[d_rep, h], sibling, self.slot + h * 3 + 2)

    low_done = low.third()
    low_copies = [net.local(low_done[h], low_out.at[rep, h]) for h in range(2)]
    low_spread = Spread(low_out, low_done)
    for turn in he_turns:
        turn.wait()
    he_spread = Spread(exp_out, [exp_out.at[rep, h] for h in range(2)])
    for turn in hp_turns:
        turn.wait()
    hp_spread = Spread(proj_out, [proj_out.at[rep, h] for h in range(2)])
    back.step_on(3)
    low_spread.on()
    back.step_on(2)
    he_spread.on()
    hp_spread.on()
    for k, r in ((1, x_rep), (2, y_rep), (3, d_rep)):
        net.arrived(vec_all.at[r], sibling, wide + k)
    vec_copy.wait()
    vec_out[...] = (vec_all[0] + vec_all[1]) + (vec_all[2] + vec_all[3])
    back.step_on(1)
    osum_copy = net.local(o_sum.at[z], osum_out)
    dsum_copy = net.local(d_sum.at[z], dsum_out)
    low_spread.wait()
    he_spread.wait()
    hp_spread.wait()
    for copy in low_copies + [osum_copy, dsum_copy]:
        copy.wait()
    net.finish()
    assert net.sends <= SETTLE_SEMS and net.started <= SETTLE_SEMS and net.locals <= 64, (
        net.sends, net.started, net.locals)


SETTLE_SEMS = 224


def settle(low, he, hp, part, dn, vec, own):
    n = lax.axis_size("shard")
    low_rows, width = low.shape
    units, mix = he.shape[1], hp.shape[1]
    rows, eighth, count = width // n, width // n // 8, part.shape[2]
    low = low.reshape(4, 2, low_rows // 8, width)
    he = he.reshape(n, 4, 2, eighth, units)
    hp = hp.reshape(n, 4, 2, eighth, mix)
    vmem = pltpu.VMEM

    def pieces(*shape):
        return [vmem((2,) + shape, bf16), vmem((2,) + shape, bf16), vmem(shape, bf16)] * 2

    block = (count, width)
    line = [vmem((k,) + block, bf16) for k in (4, 4, 3, 3)]
    anywhere = pl.BlockSpec(memory_space=pl.ANY)
    result = pl.pallas_call(
        settle_kernel,
        out_shape=[
            jax.ShapeDtypeStruct((4, 2, low_rows // 8, width), bf16),
            jax.ShapeDtypeStruct((4, 2, eighth, n * units), bf16),
            jax.ShapeDtypeStruct((4, 2, eighth, n * mix), bf16),
            jax.ShapeDtypeStruct(block, bf16),
            jax.ShapeDtypeStruct(block, bf16),
            jax.ShapeDtypeStruct((72, LANES), f32),
        ],
        in_specs=[anywhere] * 7,
        out_specs=[anywhere] * 5 + [pl.BlockSpec(memory_space=vmem)],
        scratch_shapes=pieces(low_rows // 8, width)
        + pieces(n, eighth, units) + pieces(n, eighth, mix) + line + line + [
            vmem((8, 16, LANES), f32), vmem((72, LANES), f32), vmem((4, 72, LANES), f32),
            pltpu.SemaphoreType.DMA((SETTLE_SEMS,)),
            pltpu.SemaphoreType.DMA((SETTLE_SEMS,)),
            pltpu.SemaphoreType.DMA((64,)),
        ],
        compiler_params=pltpu.CompilerParams(
            collective_id=1, has_side_effects=True, vmem_limit_bytes=VMEM_LIMIT
        ),
    )(low, he, hp, part, dn, vec, own)
    low, exp, proj, osum, dsum, vec = result
    return (
        low.reshape(low_rows, width), exp.reshape(rows, n * units), proj.reshape(rows, n * mix),
        osum, dsum, vec,
    )


def sharded_heads(
    tokens, document_ends, projector, projbias, combiner, combbias, expander, expbias,
    contractor, contbias, attendgain, attendshift, feedgain, feedshift, cotangent,
):
    count, width = tokens.shape
    n = lax.axis_size("shard")
    me = lax.axis_index("shard")
    head = width // H
    mix = 3 * head
    rows = width // n
    units = expbias.shape[0]
    wide = projbias.shape[0]

    vectors = jnp.concatenate(
        [attendgain, attendshift, feedgain, feedshift, combbias, contbias, projbias,
         document_ends[0].astype(bf16)]
    )
    vectors = jnp.pad(vectors, (0, 16 * rows - vectors.shape[0])).reshape(16, rows)
    _, _, live = layout(document_ends[0], count)
    upstream = jnp.where(live[:, None], cotangent, jnp.zeros_like(cotangent))
    half = ROT // 2
    freqs = jnp.exp(-jnp.arange(half, dtype=f32) * (2.0 / ROT) * math.log(10000.0))
    still = jnp.zeros((LANES - ROT,), f32)
    ones = jnp.ones((half,), f32)
    angles = jnp.stack(
        [jnp.concatenate([freqs, freqs, still]), jnp.concatenate([-ones, ones, still])]
    )
    _, _, low, he, hp, part, dn, vec, own, norms = block_passes(
        tokens, vectors, upstream, expander, projector, combiner, contractor,
        expbias.astype(f32)[None], angles,
    )
    low, exp_out, proj_out, osum, dsum, vec = settle(low, he, hp, part, dn, vec, own)

    floated = tokens.astype(f32)
    block_output = floated + jnp.where(
        live[:, None], osum.astype(f32) + (norms[4] + norms[5]), 0.0
    )
    block_output = block_output.astype(bf16)
    d_normed = dsum.astype(f32)
    normed, inverse = normalize(floated)
    grad = cotangent.astype(f32) + inverse * (
        d_normed
        - jnp.mean(d_normed, axis=1, keepdims=True)
        - normed * jnp.mean(d_normed * normed, axis=1, keepdims=True)
    )
    input_gradient = grad.astype(bf16)

    vec = vec.reshape(-1)
    norm_sums = vec[: 4 * rows].reshape(4, rows)
    mixed_bias = vec[4 * rows : 4 * rows + n * mix].reshape(n, 3, head).transpose(1, 0, 2)
    mixed_bias = lax.dynamic_slice(mixed_bias.reshape(-1), (me * wide,), (wide,))
    rest = vec[4 * rows + n * mix :]
    hidden_bias, out_bias = rest[:units], rest[units : units + rows]
    return (
        block_output, input_gradient, proj_out.astype(f32), mixed_bias, low[:head].astype(f32), out_bias,
        exp_out.astype(f32), hidden_bias, low[head:].astype(f32), out_bias,
        norm_sums[0], norm_sums[1], norm_sums[2], norm_sums[3],
    )


def solution(mesh):
    placed = (
        P(("rep", "shard"), None),
        P(("rep", "shard"), None),
        P("shard", None),
        P("shard"),
        P("shard", None),
        P("shard"),
        P("shard", None),
        P("shard"),
        P("shard", None),
        P("shard"),
        P("shard"),
        P("shard"),
        P("shard"),
        P("shard"),
        P(("rep", "shard"), None),
    )
    return jax.shard_map(
        sharded_heads if dict(mesh.shape) == {"rep": 4, "shard": H} else local,
        mesh=mesh,
        in_specs=placed,
        out_specs=(
            P(("rep", "shard"), None),
            P(("rep", "shard"), None),
            P("shard", None),
            P("shard"),
            P("shard", None),
            P("shard"),
            P("shard", None),
            P("shard"),
            P("shard", None),
            P("shard"),
            P("shard"),
            P("shard"),
            P("shard"),
            P("shard"),
        ),
        check_vma=False,
    )
```

```python
from functools import partial
import math

import jax
import jax.numpy as jnp
from jax import lax
from jax.experimental import pallas as pl
from jax.experimental.pallas import tpu as pltpu
from jax.sharding import PartitionSpec as P

H = 8
ROT = 64
DOCS = 4
LANES = 128
VMEM_LIMIT = 62 * 1024 * 1024

epsilon = 1e-05
masked_value = -1e30
f32 = jnp.float32
bf16 = jnp.bfloat16


def normalize(values):
    centre = jnp.mean(values, axis=1, keepdims=True)
    centred = values - centre
    spread = jnp.mean(centred * centred, axis=1, keepdims=True)
    inverse = lax.rsqrt(spread + epsilon)
    return (centred * inverse, inverse)


def layout(ends, count):
    index = jnp.arange(count, dtype=jnp.int32)
    passed = index[:, None] >= ends[None, :]
    document = jnp.sum(passed.astype(jnp.int32), axis=1)
    begin = jnp.max(jnp.where(passed, ends[None, :], 0), axis=1)
    position = (index - begin).astype(f32)
    allowed = (document[:, None] == document[None, :]) & (index[None, :] <= index[:, None])
    return (position, allowed, index < ends[-1])


def rotary_tables(position, rotary):
    half = rotary // 2
    freqs = jnp.exp(-jnp.arange(half, dtype=f32) * (2.0 / rotary) * math.log(10000.0))
    angles = position[..., None] * freqs
    angles = jnp.concatenate([angles, angles], axis=-1)
    return (jnp.cos(angles), jnp.sin(angles))


def rotate(values, cosine, sine, rotary):
    half = rotary // 2
    front = values[..., :rotary]
    turned = jnp.concatenate([-front[..., half:], front[..., :half]], axis=-1)
    return jnp.concatenate([front * cosine + turned * sine, values[..., rotary:]], axis=-1)


def unrotate(grads, cosine, sine, rotary):
    half = rotary // 2
    front = grads[..., :rotary]
    scaled = front * sine
    backward = jnp.concatenate([scaled[..., half:], -scaled[..., :half]], axis=-1)
    return jnp.concatenate([front * cosine + backward, grads[..., rotary:]], axis=-1)


def right_trans(left, right):
    return lax.dot_general(left, right, (((1,), (1,)), ((), ())), preferred_element_type=f32)


def left_trans(left, right):
    return lax.dot_general(left, right, (((0,), (0,)), ((), ())), preferred_element_type=f32)


def masked_scores(query_low, keys_low, allowed, factor):
    scores = (
        jnp.einsum("qhd,khd->hqk", query_low, keys_low, preferred_element_type=jnp.float32) * factor
    )
    return jnp.where(allowed[None], scores, masked_value)


def weight_sums(left, right):
    piece = lax.slice_in_dim(
        left, 0, left.shape[1] // lax.axis_size("shard") * lax.axis_size("shard"), axis=1
    )
    return lax.psum_scatter(
        left_trans(piece, right).astype(jnp.bfloat16), "shard", scatter_dimension=0, tiled=True
    ).astype(jnp.float32)


def local(
    tokens,
    document_ends,
    projector,
    projbias,
    combiner,
    combbias,
    expander,
    expbias,
    contractor,
    contbias,
    attendgain,
    attendshift,
    feedgain,
    feedshift,
    cotangent,
):
    count, width = tokens.shape
    headsize = width // H
    factor = 1.0 / math.sqrt(headsize)
    position, allowed, live = layout(document_ends[0], count)
    cosine, sine = rotary_tables(position, ROT)
    cosine, sine = cosine[:, None, :], sine[:, None, :]
    (
        full_projector,
        full_combiner,
        full_projbias,
        full_combbias,
        gain_attend,
        shift_attend,
        gain_feed,
        shift_feed,
    ) = (
        lax.all_gather(projector, "shard", axis=0, tiled=True),
        lax.all_gather(combiner, "shard", axis=0, tiled=True),
        lax.all_gather(projbias, "shard", axis=0, tiled=True),
        lax.all_gather(combbias, "shard", axis=0, tiled=True),
        lax.all_gather(attendgain, "shard", axis=0, tiled=True),
        lax.all_gather(attendshift, "shard", axis=0, tiled=True),
        lax.all_gather(feedgain, "shard", axis=0, tiled=True),
        lax.all_gather(feedshift, "shard", axis=0, tiled=True),
    )
    floated = tokens.astype(jnp.float32)
    normed, inverse = normalize(floated)
    first_input = (normed * gain_attend + shift_attend).astype(jnp.bfloat16)
    second_input = (normed * gain_feed + shift_feed).astype(jnp.bfloat16)
    mixed = jnp.dot(first_input, full_projector, preferred_element_type=jnp.float32) + full_projbias
    query_low = rotate(mixed[:, :width].reshape(count, H, headsize), cosine, sine, ROT).astype(
        jnp.bfloat16
    )
    keys_low = rotate(
        mixed[:, width : 2 * width].reshape(count, H, headsize), cosine, sine, ROT
    ).astype(jnp.bfloat16)
    values_low = mixed[:, 2 * width :].reshape(count, H, headsize).astype(jnp.bfloat16)
    scores = masked_scores(query_low, keys_low, allowed, factor)
    peak = jnp.max(scores, axis=2, keepdims=True)
    raised = jnp.exp(scores - peak)
    total = jnp.sum(raised, axis=2, keepdims=True)
    probs_low = (raised / total).astype(jnp.bfloat16)
    logsum = peak + jnp.log(total)
    context = jnp.einsum("hqk,khd->qhd", probs_low, values_low, preferred_element_type=jnp.float32)
    context = context.reshape(count, width).astype(jnp.bfloat16)
    attended = jnp.dot(context, full_combiner, preferred_element_type=jnp.float32) + full_combbias
    full_expander, full_contractor, full_expbias, full_contbias = (
        lax.all_gather(expander, "shard", axis=0, tiled=True),
        lax.all_gather(contractor, "shard", axis=0, tiled=True),
        lax.all_gather(expbias, "shard", axis=0, tiled=True),
        lax.all_gather(contbias, "shard", axis=0, tiled=True),
    )
    hidden = jnp.dot(second_input, full_expander, preferred_element_type=jnp.float32) + full_expbias
    activated, gelu_back = jax.vjp(partial(jax.nn.gelu, approximate=False), hidden)
    active_low = activated.astype(jnp.bfloat16)
    feedout = (
        jnp.dot(active_low, full_contractor, preferred_element_type=jnp.float32) + full_contbias
    )
    block_output = (floated + jnp.where(live[:, None], attended + feedout, 0.0)).astype(
        jnp.bfloat16
    )
    (
        back_projector,
        back_combiner,
        back_expander,
        back_contractor,
        back_gain_attend,
        back_gain_feed,
    ) = (
        lax.all_gather(projector, "shard", axis=0, tiled=True),
        lax.all_gather(combiner, "shard", axis=0, tiled=True),
        lax.all_gather(expander, "shard", axis=0, tiled=True),
        lax.all_gather(contractor, "shard", axis=0, tiled=True),
        lax.all_gather(attendgain, "shard", axis=0, tiled=True),
        lax.all_gather(feedgain, "shard", axis=0, tiled=True),
    )
    upstream = jnp.where(live[:, None], cotangent, jnp.zeros_like(cotangent))
    contractor_part = weight_sums(active_low, upstream)
    combiner_part = weight_sums(context, upstream)
    output_bias = jnp.sum(upstream, axis=0, dtype=jnp.float32)
    d_active = right_trans(upstream, back_contractor)
    d_hidden = gelu_back(d_active)[0].astype(jnp.bfloat16)
    expander_part = weight_sums(second_input, d_hidden)
    hidden_bias = jnp.sum(d_hidden, axis=0, dtype=jnp.float32)
    d_second = right_trans(d_hidden, back_expander)
    d_context = (
        right_trans(upstream, back_combiner).reshape(count, H, headsize).astype(jnp.bfloat16)
    )
    scores_again = masked_scores(query_low, keys_low, allowed, factor)
    probs = jnp.exp(scores_again - logsum)
    d_probs = jnp.einsum("qhd,khd->hqk", d_context, values_low, preferred_element_type=jnp.float32)
    d_values = jnp.einsum("hqk,qhd->khd", probs_low, d_context, preferred_element_type=jnp.float32)
    d_scores = (probs * (d_probs - jnp.sum(d_probs * probs, axis=2, keepdims=True))).astype(
        jnp.bfloat16
    )
    d_query = (
        jnp.einsum("hqk,khd->qhd", d_scores, keys_low, preferred_element_type=jnp.float32) * factor
    )
    d_keys = (
        jnp.einsum("hqk,qhd->khd", d_scores, query_low, preferred_element_type=jnp.float32) * factor
    )
    d_mixed = jnp.concatenate(
        [
            unrotate(d_query, cosine, sine, ROT).reshape(count, width),
            unrotate(d_keys, cosine, sine, ROT).reshape(count, width),
            d_values.reshape(count, width),
        ],
        axis=1,
    ).astype(jnp.bfloat16)
    projector_part = weight_sums(first_input, d_mixed)
    mixed_bias = jnp.sum(d_mixed, axis=0, dtype=jnp.float32)
    d_first = right_trans(d_mixed, back_projector)
    attend_scale = jnp.sum(d_first * normed, axis=0)
    attend_offset = jnp.sum(d_first, axis=0)
    feed_scale = jnp.sum(d_second * normed, axis=0)
    feed_offset = jnp.sum(d_second, axis=0)
    d_normed = d_first * back_gain_attend + d_second * back_gain_feed
    grad_float = cotangent.astype(jnp.float32) + inverse * (
        d_normed
        - jnp.mean(d_normed, axis=1, keepdims=True)
        - normed * jnp.mean(d_normed * normed, axis=1, keepdims=True)
    )
    input_gradient = grad_float.astype(jnp.bfloat16)
    mixed_bias, output_bias, hidden_bias, attend_scale, attend_offset, feed_scale, feed_offset = (
        lax.psum_scatter(
            mixed_bias.astype(jnp.bfloat16), "shard", scatter_dimension=0, tiled=True
        ).astype(jnp.float32),
        lax.psum_scatter(
            output_bias.astype(jnp.bfloat16), "shard", scatter_dimension=0, tiled=True
        ).astype(jnp.float32),
        lax.psum_scatter(
            hidden_bias.astype(jnp.bfloat16), "shard", scatter_dimension=0, tiled=True
        ).astype(jnp.float32),
        lax.psum_scatter(
            attend_scale.astype(jnp.bfloat16), "shard", scatter_dimension=0, tiled=True
        ).astype(jnp.float32),
        lax.psum_scatter(
            attend_offset.astype(jnp.bfloat16), "shard", scatter_dimension=0, tiled=True
        ).astype(jnp.float32),
        lax.psum_scatter(
            feed_scale.astype(jnp.bfloat16), "shard", scatter_dimension=0, tiled=True
        ).astype(jnp.float32),
        lax.psum_scatter(
            feed_offset.astype(jnp.bfloat16), "shard", scatter_dimension=0, tiled=True
        ).astype(jnp.float32),
    )
    (
        projector_part,
        mixed_bias,
        combiner_part,
        output_bias,
        expander_part,
        hidden_bias,
        contractor_part,
        attend_scale,
        attend_offset,
        feed_scale,
        feed_offset,
    ) = (
        lax.psum(projector_part.astype(jnp.bfloat16), "rep").astype(jnp.float32),
        lax.psum(mixed_bias.astype(jnp.bfloat16), "rep").astype(jnp.float32),
        lax.psum(combiner_part.astype(jnp.bfloat16), "rep").astype(jnp.float32),
        lax.psum(output_bias.astype(jnp.bfloat16), "rep").astype(jnp.float32),
        lax.psum(expander_part.astype(jnp.bfloat16), "rep").astype(jnp.float32),
        lax.psum(hidden_bias.astype(jnp.bfloat16), "rep").astype(jnp.float32),
        lax.psum(contractor_part.astype(jnp.bfloat16), "rep").astype(jnp.float32),
        lax.psum(attend_scale.astype(jnp.bfloat16), "rep").astype(jnp.float32),
        lax.psum(attend_offset.astype(jnp.bfloat16), "rep").astype(jnp.float32),
        lax.psum(feed_scale.astype(jnp.bfloat16), "rep").astype(jnp.float32),
        lax.psum(feed_offset.astype(jnp.bfloat16), "rep").astype(jnp.float32),
    )
    return (
        block_output,
        input_gradient,
        projector_part,
        mixed_bias,
        combiner_part,
        output_bias,
        expander_part,
        hidden_bias,
        contractor_part,
        output_bias,
        attend_scale,
        attend_offset,
        feed_scale,
        feed_offset,
    )


def lane_half(shape):
    return lax.broadcasted_iota(jnp.int32, shape, 1) < ROT // 2


def turn(front, signed):
    moved = jnp.where(
        lane_half(front.shape),
        pltpu.roll(front, LANES - ROT // 2, 1),
        pltpu.roll(front, ROT // 2, 1),
    )
    return moved * signed


def rotated(values, cosine, signed):
    front = values[:, :LANES]
    return jnp.concatenate([front * cosine + turn(front, signed), values[:, LANES:]], axis=1)


def unrotated(grads, cosine, signed):
    front = grads[:, :LANES]
    return jnp.concatenate([front * cosine - turn(front, signed), grads[:, LANES:]], axis=1)


def block_layout(ends, count):
    row = lax.broadcasted_iota(jnp.int32, (count, 1), 0).astype(f32)
    column = lax.broadcasted_iota(jnp.int32, (1, count), 1).astype(f32)
    row_doc = jnp.zeros((count, 1), f32)
    column_doc = jnp.zeros((1, count), f32)
    begin = jnp.zeros((count, 1), f32)
    for i in range(DOCS):
        end = ends[:, i : i + 1]
        row_doc += jnp.where(row >= end, 1.0, 0.0)
        column_doc += jnp.where(column >= end, 1.0, 0.0)
        begin = jnp.maximum(begin, jnp.where(row >= end, end, 0.0))
    return (row_doc == column_doc) & (column <= row), row - begin


def dot(left, right):
    return jnp.dot(left, right, preferred_element_type=f32)


def softmax(q, k, allowed):
    scores = right_trans(q, k) * (1.0 / math.sqrt(q.shape[1]))
    scores = jnp.where(allowed, scores, masked_value)
    raised = jnp.exp(scores - jnp.max(scores, axis=1, keepdims=True))
    return raised / jnp.sum(raised, axis=1, keepdims=True)


def norm_parts(x_ref, at):
    x = x_ref[at, :].astype(f32)
    centre = jnp.mean(x, axis=1, keepdims=True)
    centred = x - centre
    inverse = lax.rsqrt(jnp.mean(centred * centred, axis=1, keepdims=True) + epsilon)
    return centred, centre, inverse


def tables(ends, count, angles_ref):
    allowed, place = block_layout(ends, count)
    angles = place * angles_ref[0:1, :]
    return allowed, jnp.cos(angles), jnp.sin(angles) * angles_ref[1:2, :]


def forward_pass(
    x_ref, ends, count, angles_ref, norms_ref, pbias_ref, ebias_ref, proj_ref, exp_ref, comb_ref,
    cont_ref, h1_ref, h2_ref, qkv_ref, ca_ref, slope_ref, stats_ref, part_ref,
):
    slots, width = x_ref.shape
    head = comb_ref.shape[0]
    units = exp_ref.shape[1]
    step = min(64, count)

    @pl.loop(0, slots // step)
    def _(i):
        at = rows_at(i * step, step)
        centred, centre, inverse = norm_parts(x_ref, at)
        normed = centred * inverse
        h1_ref[at, :] = (normed * norms_ref[0:1, :] + norms_ref[1:2, :]).astype(bf16)
        h2_ref[at, :] = (normed * norms_ref[2:3, :] + norms_ref[3:4, :]).astype(bf16)
        stats_ref[at, 0:1] = centre
        stats_ref[at, 1:2] = inverse

    for j in range(3):
        cut = slice(j * head, j * head + head)
        mixed = dot(h1_ref[...], proj_ref[:, cut]) + pbias_ref[:, cut]
        for b in range(slots // count):
            at = slice(b * count, b * count + count)
            value = mixed[at]
            if j < 2:
                _, cosine, signed = tables(ends[b], count, angles_ref)
                value = rotated(value, cosine, signed)
            qkv_ref[at, cut] = value.astype(bf16)
    tile = min(256, units)
    for start in range(0, units, tile):
        hidden = dot(h2_ref[...], exp_ref[:, start : start + tile])
        hidden += ebias_ref[:, start : start + tile]
        below = 0.5 + 0.5 * lax.erf(hidden * math.sqrt(0.5))
        ca_ref[:, head + start : head + start + tile] = (hidden * below).astype(bf16)
        density = jnp.exp(hidden * hidden * -0.5) * (1.0 / math.sqrt(2.0 * math.pi))
        slope_ref[:, start : start + tile] = (below + hidden * density).astype(bf16)
    for b in range(slots // count):
        at = slice(b * count, b * count + count)
        allowed, _ = block_layout(ends[b], count)
        probs = softmax(qkv_ref[at, :head], qkv_ref[at, head : 2 * head], allowed).astype(bf16)
        ca_ref[at, :head] = dot(probs, qkv_ref[at, 2 * head :]).astype(bf16)
    tile = min(512, width)
    for start in range(0, width, tile):
        cut = slice(start, start + tile)
        part = dot(ca_ref[:, :head], comb_ref[:, cut]) + dot(ca_ref[:, head:], cont_ref[:, cut])
        part_ref[:, cut] = part.astype(bf16)


def backward_pass(
    x_ref, up_ref, ends, count, angles_ref, norms_ref, qkv_ref, slope_ref, stats_ref, proj_ref,
    exp_ref, comb_ref, cont_ref, dh_ref, dm_ref, dn_ref, sums_ref, hbias_ref, mbias_ref, obias_ref,
):
    slots, width = x_ref.shape
    head = comb_ref.shape[0]
    units = exp_ref.shape[1]
    tile = min(256, units)
    d_context = right_trans(up_ref[...], comb_ref[...]).astype(bf16)
    for start in range(0, units, tile):
        cut = slice(start, start + tile)
        d_active = right_trans(up_ref[...], cont_ref[cut, :])
        d_hidden = (d_active * slope_ref[:, cut].astype(f32)).astype(bf16)
        dh_ref[:, cut] = d_hidden
        hbias_ref[:, cut] += jnp.sum(d_hidden.astype(f32), axis=0, keepdims=True)
    factor = 1.0 / math.sqrt(head)
    for b in range(slots // count):
        at = slice(b * count, b * count + count)
        allowed, cosine, signed = tables(ends[b], count, angles_ref)
        q, k = qkv_ref[at, :head], qkv_ref[at, head : 2 * head]
        v = qkv_ref[at, 2 * head :]
        d_ctx = d_context[at]
        probs = softmax(q, k, allowed)
        d_probs = right_trans(d_ctx, v)
        d_v = left_trans(probs.astype(bf16), d_ctx)
        d_s = probs * (d_probs - jnp.sum(d_probs * probs, axis=1, keepdims=True))
        d_s = d_s.astype(bf16)
        dm_ref[at, :head] = unrotated(dot(d_s, k) * factor, cosine, signed).astype(bf16)
        d_k = unrotated(left_trans(d_s, q) * factor, cosine, signed).astype(bf16)
        dm_ref[at, head : 2 * head] = d_k
        dm_ref[at, 2 * head :] = d_v.astype(bf16)
    mbias_ref[...] += jnp.sum(dm_ref[...].astype(f32), axis=0, keepdims=True)
    obias_ref[...] += jnp.sum(up_ref[...].astype(f32), axis=0, keepdims=True)
    centre, inverse = stats_ref[:, 0:1], stats_ref[:, 1:2]
    tile = min(256, width)

    @pl.loop(0, width // tile, unroll=2)
    def _(i):
        cut = rows_at(i * tile, tile)
        normed = (x_ref[:, cut].astype(f32) - centre) * inverse
        d_first = right_trans(dm_ref[...], proj_ref[cut, :])
        d_second = right_trans(dh_ref[...], exp_ref[cut, :])
        dn_ref[:, cut] = (
            d_first * norms_ref[0:1, cut] + d_second * norms_ref[2:3, cut]
        ).astype(bf16)
        sums_ref[0:1, cut] += jnp.sum(d_first * normed, axis=0, keepdims=True)
        sums_ref[1:2, cut] += jnp.sum(d_first, axis=0, keepdims=True)
        sums_ref[2:3, cut] += jnp.sum(d_second * normed, axis=0, keepdims=True)
        sums_ref[3:4, cut] += jnp.sum(d_second, axis=0, keepdims=True)


def accumulate(total, left, right, tall):
    wide = min(256, right.shape[1])

    @pl.loop(0, left.shape[1] // tall)
    def _(i):
        at = pl.ds(pl.multiple_of(i * tall, LANES), tall)
        for start in range(0, right.shape[1], wide):
            cut = slice(start, start + wide)
            total[at, cut] += left_trans(left[:, at], right[:, cut])


MESH = pl.DeviceIdType.MESH


def position_of():
    rep, me = lax.axis_index("rep"), lax.axis_index("shard")
    return rep, me, lax.div(rep, 2), lax.rem(rep, 2), lax.div(me, 2), lax.rem(me, 2)


def meet(peers):
    barrier = pltpu.get_barrier_semaphore()
    for peer in peers:
        pl.semaphore_signal(barrier, inc=1, device_id=peer, device_id_type=MESH)
    pl.semaphore_wait(barrier, len(peers))


def rows_at(start, size):
    return pl.ds(pl.multiple_of(start, size), size)


class Net:
    def __init__(self, send_sem, recv_sem, local_sem):
        self.send_sem, self.recv_sem, self.local_sem = send_sem, recv_sem, local_sem
        self.sends, self.locals, self.started, self.sent = 0, 0, 0, []

    def slots(self, count):
        first = self.started
        self.started += count
        return first

    def send(self, ends, slot, when=None):
        index = self.sends
        self.sends += 1

        def copy():
            src, dst, peer = ends()
            return pltpu.make_async_remote_copy(
                src_ref=src, dst_ref=dst, send_sem=self.send_sem.at[index],
                recv_sem=self.recv_sem.at[slot], device_id=peer, device_id_type=MESH,
            )

        if when is None:
            copy().start()
        else:
            pl.when(when)(lambda: copy().start())
        self.sent.append((copy, when))

    def arrived(self, dst, peer, slot):
        pltpu.make_async_remote_copy(
            src_ref=dst, dst_ref=dst, send_sem=self.send_sem.at[0],
            recv_sem=self.recv_sem.at[slot], device_id=peer, device_id_type=MESH,
        ).wait_recv()

    def local(self, src, dst):
        copy = pltpu.make_async_copy(src, dst, self.local_sem.at[self.locals])
        self.locals += 1
        copy.start()
        return copy

    def left(self, sent):
        for copy, when in sent:
            if when is None:
                copy().wait_send()
            else:
                pl.when(when)(lambda copy=copy: copy().wait_send())


class Chain:
    def __init__(self, source, out, count, where, sems):
        self.source, self.out, self.count = source, out, count
        self.rep, self.me, self.z, self.c = where
        self.side_send, self.side_recv, self.core_send, self.core_recv = sems
        self.sibling = self.me + 1 - 2 * self.c

    def block(self, shard):
        return self.out.at[rows_at(shard * self.count, self.count)]

    def side(self, side, step):
        block = self.block(self.me - side * 2 * step)
        peer = (self.rep, self.me + side * 2)
        index = (0 if side > 0 else 4) + step
        return pltpu.make_async_remote_copy(
            src_ref=block, dst_ref=block, send_sem=self.side_send.at[index],
            recv_sem=self.side_recv.at[index], device_id=peer, device_id_type=MESH,
        )

    def cross(self, side, step):
        block = self.block(self.me - side * 2 * step)
        index = (0 if side > 0 else 4) + step
        return pltpu.make_async_remote_copy(
            src_ref=block, dst_ref=block, send_sem=self.core_send.at[index],
            recv_sem=self.core_recv.at[index], device_id=(self.rep, self.sibling),
            device_id_type=MESH,
        )

    def taken(self, side, step):
        block = self.block(self.sibling - side * 2 * step)
        index = (0 if side > 0 else 4) + step
        return pltpu.make_async_remote_copy(
            src_ref=block, dst_ref=block, send_sem=self.core_send.at[index],
            recv_sem=self.core_recv.at[index], device_id=(self.rep, self.sibling),
            device_id_type=MESH,
        )

    def here(self, side, step):
        return self.z >= step if side > 0 else self.z + step <= 3

    def on(self, side):
        return self.z < 3 if side > 0 else self.z > 0

    def first(self, side):
        mine = self.block(self.me)
        index = 0 if side > 0 else 4
        return pltpu.make_async_remote_copy(
            src_ref=self.source, dst_ref=mine, send_sem=self.side_send.at[index],
            recv_sem=self.side_recv.at[index], device_id=(self.rep, self.me + side * 2),
            device_id_type=MESH,
        )

    def first_cross(self):
        mine = self.block(self.me)
        return pltpu.make_async_remote_copy(
            src_ref=self.source, dst_ref=mine, send_sem=self.core_send.at[0],
            recv_sem=self.core_recv.at[0], device_id=(self.rep, self.sibling),
            device_id_type=MESH,
        )

    def begin(self):
        for side in (1, -1):
            pl.when(self.on(side))(lambda: self.first(side).start())
        self.first_cross().start()
    def wait_own(self):
        self.taken(1, 0).wait_recv()

    def step(self, step):
        for side in (1, -1):
            here = self.here(side, step)

            @pl.when(here)
            def _():
                block = self.block(self.me - side * 2 * step)
                index = (0 if side > 0 else 4) + step - 1
                pltpu.make_async_remote_copy(
                    src_ref=block, dst_ref=block, send_sem=self.side_send.at[index],
                    recv_sem=self.side_recv.at[index], device_id=(self.rep, self.sibling),
                    device_id_type=MESH,
                ).wait_recv()
                self.cross(side, step).start()

            pl.when(here & self.on(side) & (step < 3))(lambda: self.side(side, step).start())

    def take(self, step):
        for side in (1, -1):
            pl.when(self.here(side, step))(lambda: self.taken(side, step).wait_recv())

    def finish(self):
        self.first_cross().wait_send()
        for side in (1, -1):
            pl.when(self.on(side))(lambda: self.first(side).wait_send())
            for step in (1, 2, 3):
                here = self.here(side, step)
                pl.when(here)(lambda: self.cross(side, step).wait_send())
                if step < 3:
                    pl.when(here & self.on(side))(lambda: self.side(side, step).wait_send())


def add_into(target, other):
    rows = target.shape[-2]
    step = min(32, rows)

    @pl.loop(0, rows // step)
    def _(i):
        at = (Ellipsis, pl.ds(pl.multiple_of(i * step, step), step), slice(None))
        lead = (slice(None),) * (len(target.shape) - 2)
        at = lead + at[1:]
        target[at] = (target[at].astype(f32) + other[at].astype(f32)).astype(target.dtype)


def block_kernel(
    tok_ref, vec_ref, up_ref, expander_ref, projector_ref, comb_hbm, cont_hbm, ebias_ref,
    angles_ref,
    low_out, exp_out, proj_out, osum_out, dsum_out, vec_out, norms_ref,
    x_out, up_out, part_own, dn_own, o_in, d_in, o_land, d_land, low_land, he_land, hp_land,
    h_save, qkv_save, slope_save, stats_save,
    exp_ref, proj_ref, comb_ref, cont_ref, low_sum, he_sum, hp_sum,
    xs, us, hs, pd, ca, slope, qkv, dh, dm, spare, stats,
    vecs, bias_all, ends_all, pbias, sums, hbias, mbias, obias,
    vec_msg, vec_in, vec_mix, vec_all,
    send_sem, recv_sem, local_sem, load_sem, store_sem, cross_send, cross_recv,
    xs_send, xs_recv, xc_send, xc_recv, us_send, us_recv, uc_send, uc_recv,
):
    rep, me, y, x, z, c = position_of()
    count, width = tok_ref.shape
    rows, quarter = expander_ref.shape[0], expander_ref.shape[0] // 4
    units, mix = exp_ref.shape[1], proj_ref.shape[1]
    head = mix // 3
    sibling = (rep, me + 1 - 2 * c)
    x_rep, y_rep, d_rep = rep + 1 - 2 * x, rep + 2 - 4 * y, 3 - rep
    by_x, by_y, across = (x_rep, me), (y_rep, me), (d_rep, me)
    ring = [(rep, lax.rem(me + k, 8)) for k in range(1, 8)]
    meet(ring + [by_x, by_y, across])
    slots = hs.shape[0] // 2
    h1s, h2s = hs.at[pl.ds(0, slots)], hs.at[pl.ds(slots, slots)]
    parts, dns = pd.at[pl.ds(0, slots)], pd.at[pl.ds(slots, slots)]
    net = Net(send_sem, recv_sem, local_sem)

    def weight_copies(go, first, size, source_rows, t):
        source = rows_at(source_rows, size)
        target = rows_at(first, size)
        go(expander_ref.at[source, rows_at(t * units, units)], exp_ref.at[target, :])
        for j in range(3):
            go(
                projector_ref.at[source, rows_at(j * width + t * head, head)],
                proj_ref.at[target, pl.ds(j * head, head)],
            )

    remote = net.slots(32)
    chips = []
    for i in range(3):
        down, up = 3 - i, i
        chips.append(jnp.where(
            z < 2, jnp.where(down <= z, down - 1, down), jnp.where(up >= z, up + 1, up)
        ))
    for chip in chips:
        for core in (0, 1):
            part = [0]

            def go(src, dst):
                net.send(
                    lambda: (src, dst, (rep, chip * 2 + core)), remote + me * 4 + part[0]
                )
                part[0] += 1

            weight_copies(go, me * rows + rep * quarter, quarter, rep * quarter, chip * 2 + core)
    small = net.slots(7)
    for k, peer in enumerate(ring):
        net.send(lambda peer=peer: (vec_ref, vecs.at[me], peer), small + k)
    where = (rep, me, z, c)
    tokens = Chain(
        tok_ref, x_out, count, where, (xs_send, xs_recv, xc_send, xc_recv)
    )
    cotangents = Chain(
        up_ref, up_out, count, where, (us_send, us_recv, uc_send, uc_recv)
    )
    tokens.begin()
    near = net.slots(4)
    part = [0]

    def go_near(src, dst):
        net.send(lambda: (src, dst, sibling), near + part[0])
        part[0] += 1

    weight_copies(go_near, me * rows, rows, 0, sibling[1])
    copies = []
    weight_copies(lambda s, d: copies.append(net.local(s, d)), me * rows, rows, 0, me)
    copies.append(net.local(vec_ref, vecs.at[me]))
    copies.append(net.local(comb_hbm, comb_ref))
    copies.append(net.local(cont_hbm, cont_ref))
    cotangents.begin()
    for ref in (low_sum, he_sum, hp_sum, sums, hbias, mbias, obias):
        if ref.shape[0] <= 8:
            ref[...] = jnp.zeros_like(ref)
        else:

            @pl.loop(0, ref.shape[0] // 64)
            def _(i):
                ref[rows_at(i * 64, 64), :] = jnp.zeros((64, ref.shape[1]), f32)

    def shard_rows(step, core):
        return (chips[step - 1] * 2 + core) * rows

    first_hop, second_hop = net.slots(12), net.slots(18)
    gone = []

    def pass_on(ref_at, peer, slot):
        for ref, more in ((exp_ref, 0), (proj_ref, 1)):
            net.send(lambda ref=ref: (ref.at[ref_at, :], ref.at[ref_at, :], peer), slot + more)

    def landed(step):
        for core in (0, 1):
            at = rows_at(shard_rows(step, core) + rep * quarter, quarter)
            slot = remote + (chips[step - 1] * 2 + core) * 4
            net.arrived(exp_ref.at[at, :], sibling, slot)
            for j in range(3):
                net.arrived(proj_ref.at[at, pl.ds(j * head, head)], sibling, slot + 1 + j)
            peer = by_x if core == 0 else by_y
            pass_on(at, peer, first_hop + ((step - 1) * 2 + core) * 2)

    def crossed(step):
        for core in (0, 1):
            base = shard_rows(step, core)
            hop = first_hop + ((step - 1) * 2 + core) * 2
            other = rows_at(base + (x_rep if core == 0 else y_rep) * quarter, quarter)
            net.arrived(exp_ref.at[other, :], sibling, hop)
            net.arrived(proj_ref.at[other, :], sibling, hop + 1)
            hop = second_hop + (step - 1) * 6
            if core == 0:
                pass_on(rows_at(base + y * 2 * quarter, 2 * quarter), by_y, hop)
                gone.append((rows_at(base + (1 - y) * 2 * quarter, 2 * quarter), hop))
            else:
                pass_on(rows_at(base + rep * quarter, quarter), by_x, hop + 2)
                pass_on(other, by_x, hop + 4)
                gone.append((rows_at(base + x_rep * quarter, quarter), hop + 2))
                gone.append((rows_at(base + d_rep * quarter, quarter), hop + 4))

    landed(1)
    landed(2)
    crossed(1)
    landed(3)
    crossed(2)
    crossed(3)
    tokens.step(1)
    opening, net.sent = net.sent, []

    for k in range(1, 8):
        net.arrived(vecs.at[lax.rem(me + 8 - k, 8)], sibling, small + k - 1)
    for copy in copies:
        copy.wait()
    for s in range(8):
        values = vecs[s].astype(f32)
        for j in range(3):
            bias_all[3 * s + j] = values[6 + j : 7 + j, :]
        ends_all[s] = values[9:10, :LANES]
        norms_ref[:, s * rows : s * rows + rows] = values[:8, :]
    for j in range(3):
        pbias[:, j * head : j * head + head] = bias_all[8 * j + me]

    at = rows_at(sibling[1] * rows, rows)
    net.arrived(exp_ref.at[at, :], sibling, near)
    for j in range(3):
        net.arrived(proj_ref.at[at, pl.ds(j * head, head)], sibling, near + 1 + j)
    for at, slot in gone:
        net.arrived(exp_ref.at[at, :], sibling, slot)
        net.arrived(proj_ref.at[at, :], sibling, slot + 1)
    tokens.wait_own()
    cotangents.wait_own()
    cotangents.step(1)

    def chip_of(slot):
        second = jnp.where(z == 0, 2, jnp.where(z == 1, 0, 1))
        last = jnp.where(z < 2, 3, 0)
        after = jnp.where(z < 3, z + 1, 2)
        return jnp.where(
            slot == 0, z, jnp.where(slot == 1, after, jnp.where(slot == 2, second, last))
        )

    class Loads:
        def __init__(self, own, source, into, first):
            self.own, self.source, self.into, self.first = own, source, into, first

        def start_own(self):
            theirs = self.source.at[rows_at(sibling[1] * count, count)]
            for source, b in ((self.own, c), (theirs, 1 - c)):
                pltpu.make_async_copy(
                    source, self.into.at[rows_at(b * count, count)], load_sem.at[self.first + b]
                ).start()

        def copies(self, slot):
            return [
                pltpu.make_async_copy(
                    self.source.at[rows_at((chip_of(slot) * 2 + b) * count, count)],
                    self.into.at[rows_at(b * count, count)], load_sem.at[self.first + b],
                )
                for b in range(2)
            ]

        def start(self, slot):
            for copy in self.copies(slot):
                copy.start()

        def wait(self, slot):
            for copy in self.copies(slot):
                copy.wait()

    x_loads, up_loads = Loads(tok_ref, x_out, xs, 0), Loads(up_ref, up_out, us, 2)
    x_loads.start_own()
    up_loads.start_own()

    def stores(source, own, theirs, first, chip):
        mine = pltpu.make_async_copy(
            source.at[rows_at(c * count, count)], own.at[chip], store_sem.at[first]
        )
        other = pltpu.make_async_remote_copy(
            src_ref=source.at[rows_at((1 - c) * count, count)], dst_ref=theirs.at[chip],
            send_sem=cross_send.at[first], recv_sem=cross_recv.at[first * 4 + chip],
            device_id=sibling, device_id_type=MESH,
        )
        return mine, other

    def store(source, own, theirs, first, chip):
        mine, other = stores(source, own, theirs, first, chip)
        mine.start()
        other.start()

    def stored(source, own, theirs, first, chip):
        mine, other = stores(source, own, theirs, first, chip)
        mine.wait()
        other.wait_send()

    def saves():
        pairs = [(hs, h_save), (qkv, qkv_save), (slope, slope_save), (stats, stats_save)]
        return [(pair, store_sem.at[2 + i]) for i, pair in enumerate(pairs)]

    class Piece:
        def __init__(self, total, land, start, step, stage, tmp):
            self.total, self.land, self.start, self.step = total, land, start, step
            self.stage, self.tmp = stage, tmp
            self.size = land.shape[1]
            self.slot = net.slots(6)

        def each(self, quarter, half, work):
            @pl.loop(0, self.size // self.step)
            def _(i):
                work(
                    rows_at(self.start(quarter, half, i), self.step),
                    rows_at(i * self.step, self.step),
                )

        def lower(self, quarter, half, target):
            def work(at, to):
                target[to, :] = self.total[at, :].astype(bf16)

            self.each(quarter, half, work)

        def add(self, quarter, half, source):
            def work(at, to):
                self.total[at, :] += source[to, :].astype(f32)

            self.each(quarter, half, work)

        def room(self, first):
            return self.tmp.at[pl.ds(first, self.size)]

        def first(self):
            before = len(net.sent)
            for i in range(2):
                for half, quarter, peer in (
                    (0, i * 2 + 1 - x, by_x), (1, (1 - y) * 2 + i, by_y)
                ):
                    place = half * 2 + i
                    self.lower(quarter, half, self.stage[place])
                    net.send(
                        lambda place=place, peer=peer: (
                            self.stage[place], self.land.at[place], peer
                        ),
                        self.slot + place,
                    )
            self.sent, net.sent = net.sent[before:], net.sent[:before]

        def fetch(self, place):
            net.arrived(self.land.at[place], sibling, self.slot + place)
            return net.local(self.land.at[place], self.room(place * self.size))

        def second(self):
            loads = [self.fetch(place) for place in range(4)]
            for half, other, peer in ((0, 1 - y, by_y), (1, 1 - x, by_x)):
                for i in range(2):
                    loads[half * 2 + i].wait()
                    quarter = i * 2 + x if half == 0 else y * 2 + i
                    self.add(quarter, half, self.room((half * 2 + i) * self.size))
                quarter = other * 2 + x if half == 0 else y * 2 + other
                stage = self.later(half)
                self.lower(quarter, half, stage)
                net.send(
                    lambda stage=stage, half=half, peer=peer: (
                        stage, self.land.at[4 + half], peer
                    ),
                    self.slot + 4 + half,
                )

        def later(self, half):
            first = 6 + half if self.tmp.shape[0] >= 8 * self.size else half
            return self.room(first * self.size)

        def third(self):
            loads = [self.fetch(4 + half) for half in range(2)]
            for half in range(2):
                loads[half].wait()
                self.add(rep, half, self.room((4 + half) * self.size))
                self.lower(rep, half, self.room((2 + half) * self.size))
            return [self.room((2 + half) * self.size) for half in range(2)]

    def low_start(quarter, half, i):
        return quarter * (low_sum.shape[0] // 4) + half * (low_sum.shape[0] // 8) + i * 32

    def high_start(quarter, half, i):
        return i * rows + quarter * (rows // 4) + half * (rows // 8)

    low_size, high_size = low_land.shape[1], he_land.shape[1]

    def halves(ref):
        return [ref.at[pl.ds(i * high_size, high_size)] for i in range(2)]

    low_stage = [parts.at[pl.ds(i * low_size, low_size)] for i in range(3)] + [spare]
    low = Piece(low_sum, low_land, low_start, 32, low_stage, cont_ref)
    he = Piece(he_sum, he_land, high_start, rows // 8, halves(dh) + halves(slope), exp_ref)
    hp = Piece(hp_sum, hp_land, high_start, rows // 8, halves(dm) + halves(qkv), proj_ref)

    @pl.loop(0, 5)
    def _(turn_index):
        slot = jnp.minimum(turn_index, 3)

        @pl.when(turn_index < 4)
        def _():
            chip = chip_of(slot)
            ends = [ends_all[chip * 2 + b] for b in range(2)]
            x_loads.wait(slot)
            forward_pass(
                xs, ends, count, angles_ref, norms_ref, pbias, ebias_ref, proj_ref, exp_ref,
                comb_ref, cont_ref, h1s, h2s, qkv, ca, slope, stats, parts,
            )
            store(parts, part_own, o_in, 0, chip)
            pl.when(slot == 2)(lambda: tokens.step(3))

            @pl.when(slot == 3)
            def _():
                cotangents.step(3)
                cotangents.take(3)
                up_loads.start(3)

            up_loads.wait(slot)
            accumulate(low_sum, ca, us, ca.shape[1])
            stored(parts, part_own, o_in, 0, chip)

        @pl.when(turn_index == 2)
        def _():
            for (here, there), sem in saves():
                pltpu.make_async_copy(here, there, sem).start()
            tokens.take(3)
            x_loads.start(3)
            for (here, there), sem in saves():
                pltpu.make_async_copy(here, there, sem).wait()

        pl.when(turn_index == 3)(lambda: low.first())

        @pl.when(turn_index == 4)
        def _():
            for (here, there), sem in saves():
                pltpu.make_async_copy(there, here, sem).start()
            x_loads.start(2)
            up_loads.start(2)
            for (here, there), sem in saves():
                pltpu.make_async_copy(there, here, sem).wait()
            x_loads.wait(2)
            up_loads.wait(2)

        @pl.when(turn_index != 2)
        def _():
            slot = jnp.where(turn_index == 4, 2, turn_index)
            chip = chip_of(slot)
            ends = [ends_all[chip * 2 + b] for b in range(2)]
            backward_pass(
                xs, us, ends, count, angles_ref, norms_ref, qkv, slope, stats, proj_ref, exp_ref,
                comb_ref, cont_ref, dh, dm, dns, sums, hbias, mbias, obias,
            )
            store(dns, dn_own, d_in, 1, chip)
            pl.when(slot == 0)(lambda: tokens.step(2))
            pl.when(slot == 1)(lambda: cotangents.step(2))

            @pl.when(turn_index < 2)
            def _():
                tokens.take(slot + 1)
                x_loads.start(slot + 1)
                cotangents.take(slot + 1)
                up_loads.start(slot + 1)

            accumulate(he_sum, h2s, dh, width // 2)
            accumulate(hp_sum, h1s, dm, width // 2)
            stored(dns, dn_own, d_in, 1, chip)

    he.first()
    low.second()
    hp.first()
    net.left(opening)

    class Line:
        def __init__(self, own, inward, land, total, first):
            self.own, self.inward, self.land, self.total = own, inward, land, total
            self.first = first
            self.slot = net.slots(6)

        def block(self, index):
            return self.total.at[rows_at(index * count, count)]

        def join(self):
            room = [xs.at[pl.ds(i * count, count)] for i in range(2)]
            room += [us.at[pl.ds(i * count, count)] for i in range(2)]
            loads = []
            for i in range(4):
                loads.append(net.local(self.own.at[i], self.block(i)))
                pltpu.make_async_remote_copy(
                    src_ref=self.inward.at[i], dst_ref=self.inward.at[i],
                    send_sem=cross_send.at[self.first],
                    recv_sem=cross_recv.at[self.first * 4 + i],
                    device_id=sibling, device_id_type=MESH,
                ).wait_recv()
                loads.append(net.local(self.inward.at[i], room[i]))
            for i in range(4):
                loads[2 * i].wait()
                loads[2 * i + 1].wait()
                add_into(self.block(i), room[i])

        def push(self, block, step, side, when):
            place = (step - 1) + (0 if side > 0 else 3)
            net.send(
                lambda: (self.block(block), self.land.at[place], (rep, me + 2 * side)),
                self.slot + place, when,
            )

        def begin(self, steps):
            for step in steps:
                self.push(step, step, 1, z == 0)
                self.push(3 - step, step, -1, z == 3)

        def step_on(self, step):
            for side in (1, -1):
                place = (step - 1) + (0 if side > 0 else 3)
                block = z + side * (step - 1)
                here = (z >= 1) & (block <= 3) if side > 0 else (z <= 2) & (block >= 0)
                index = net.locals
                net.locals += 1

                @pl.when(here)
                def _():
                    net.arrived(self.land.at[place], sibling, self.slot + place)
                    load = pltpu.make_async_copy(
                        self.land.at[place], comb_ref, local_sem.at[index]
                    )
                    load.start()
                    load.wait()
                    add_into(self.block(block), comb_ref)

                if step > 1:
                    self.push(block, step - 1, side, here)

    out = Line(part_own, o_in, o_land, hs, 0)
    back = Line(dn_own, d_in, d_land, pd, 1)
    out.join()
    out.begin((3, 2, 1))

    vec_msg[...] = jnp.zeros_like(vec_msg)
    vec_mix[...] = jnp.zeros_like(vec_mix)
    per = rows // LANES
    for t in range(8):
        for j in range(4):
            for i in range(per):
                at = t * rows + i * LANES
                vec_msg[t, j * per + i : j * per + i + 1, :] = sums[j : j + 1, at : at + LANES]
        for i in range(mix // LANES):
            at = 4 * per + i
            vec_msg[t, at : at + 1, :] = mbias[:, i * LANES : (i + 1) * LANES]
    for i in range(units // LANES):
        vec_mix[56 + i : 57 + i, :] = hbias[:, i * LANES : (i + 1) * LANES]
    for i in range(per):
        vec_mix[64 + i : 65 + i, :] = obias[:, rows_at(me * rows + i * LANES, LANES)]
    small = net.slots(7)
    for k in range(1, 8):
        t = lax.rem(me + k, 8)
        net.send(lambda t=t: (vec_msg.at[t], vec_in.at[me], (rep, t)), small + k - 1)
    vec_load = net.local(vec_msg.at[me], vec_in.at[me])

    he.second()
    out.step_on(3)
    net.left(low.sent)
    back.join()
    hp.second()
    out.step_on(2)
    low_done = low.third()

    class Turn:
        def __init__(self, source, half, place):
            self.half, self.place = half, place
            self.slot = net.slots(21)
            self.copies = []
            for k in range(1, 8):
                t = lax.rem(me + k, 8)
                for j, (src, dst) in enumerate(place(source, t, me)):
                    net.send(
                        lambda src=src, dst=dst, t=t: (src, dst, (rep, t)),
                        self.slot + (k - 1) * 3 + j,
                    )
            for src, dst in place(source, me, me):
                self.copies.append(net.local(src, dst))

        def wait(self):
            for k in range(1, 8):
                s = lax.rem(me + 8 - k, 8)
                for j, (_, dst) in enumerate(self.place(None, me, s)):
                    net.arrived(dst, sibling, self.slot + (k - 1) * 3 + j)
            for copy in self.copies:
                copy.wait()

    eighth = rows // 8

    def place_exp(half):
        return lambda source, t, s: [(
            None if source is None else source.at[rows_at(t * eighth, eighth)],
            exp_out.at[rep, half, :, rows_at(s * units, units)],
        )]

    def place_proj(half):
        return lambda source, t, s: [
            (
                None if source is None
                else source.at[rows_at(t * eighth, eighth), pl.ds(j * head, head)],
                proj_out.at[rep, half, :, rows_at(j * width + s * head, head)],
            )
            for j in range(3)
        ]

    he_done = he.third()
    he_turns = [Turn(he_done[h], h, place_exp(h)) for h in range(2)]
    hp_done = hp.third()
    hp_turns = [Turn(hp_done[h], h, place_proj(h)) for h in range(2)]

    class Spread:
        def __init__(self, target, sources):
            self.target, self.slot = target, net.slots(6)
            for h, source in enumerate(sources):
                for k, peer in enumerate((by_x, by_y)):
                    net.send(
                        lambda source=source, h=h, peer=peer: (source, target.at[rep, h], peer),
                        self.slot + h * 3 + k,
                    )

        def on(self):
            for h, (k, got, peer) in enumerate(((1, y_rep, by_x), (0, x_rep, by_y))):
                net.arrived(self.target.at[got, h], sibling, self.slot + h * 3 + k)
                net.send(
                    lambda h=h, got=got, peer=peer: (
                        self.target.at[got, h], self.target.at[got, h], peer
                    ),
                    self.slot + h * 3 + 2,
                )

        def wait(self):
            for h, (k, got) in enumerate(((0, x_rep), (1, y_rep))):
                net.arrived(self.target.at[got, h], sibling, self.slot + h * 3 + k)
                net.arrived(self.target.at[d_rep, h], sibling, self.slot + h * 3 + 2)

    low_copies = [net.local(low_done[h], low_out.at[rep, h]) for h in range(2)]
    low_spread = Spread(low_out, low_done)
    out.step_on(1)
    back.begin((3, 2, 1))

    for k in range(1, 8):
        net.arrived(vec_in.at[lax.rem(me + 8 - k, 8)], sibling, small + k - 1)
    vec_load.wait()
    total = vec_in[0, 0:8]
    for s in range(1, 8):
        total += vec_in[s, 0:8]
    vec_mix[0:8] = total
    for s in range(8):
        vec_mix[8 + 6 * s : 14 + 6 * s] = vec_in[s, 8:14]
    wide = net.slots(4)
    for k, peer in ((1, by_x), (2, by_y), (3, across)):
        net.send(lambda peer=peer: (vec_mix, vec_all.at[rep], peer), wide + k)
    vec_copy = net.local(vec_mix, vec_all.at[rep])

    for turn_of in he_turns:
        turn_of.wait()
    he_spread = Spread(exp_out, [exp_out.at[rep, h] for h in range(2)])
    for turn_of in hp_turns:
        turn_of.wait()
    hp_spread = Spread(proj_out, [proj_out.at[rep, h] for h in range(2)])
    low_spread.on()
    back.step_on(3)
    back.step_on(2)
    he_spread.on()
    hp_spread.on()
    for k, r in ((1, x_rep), (2, y_rep), (3, d_rep)):
        net.arrived(vec_all.at[r], sibling, wide + k)
    vec_copy.wait()
    vec_out[...] = (vec_all[0] + vec_all[1]) + (vec_all[2] + vec_all[3])
    back.step_on(1)
    osum_copy = net.local(out.block(z), osum_out)
    dsum_copy = net.local(back.block(z), dsum_out)
    low_spread.wait()
    he_spread.wait()
    hp_spread.wait()
    for copy in low_copies + [osum_copy, dsum_copy]:
        copy.wait()
    tokens.finish()
    cotangents.finish()
    net.left(net.sent + he.sent + hp.sent)
    assert net.sends <= SENDS and net.started <= SENDS and net.locals <= LOCALS, (
        net.sends, net.started, net.locals)


SENDS = 320
LOCALS = 80


def block_passes(tokens, vectors, upstream, expander, projector, combiner, contractor, ebias, angles):
    count, width = tokens.shape
    n = lax.axis_size("shard")
    units, mix, head = expander.shape[1] // n, projector.shape[1] // n, combiner.shape[0]
    low, rows, two = head + units, width // n, 2 * count
    eighth = rows // 8
    vmem, dma = pltpu.VMEM, pltpu.SemaphoreType.DMA
    anywhere = pl.BlockSpec(memory_space=pl.ANY)
    block = (n // 2, count, width)
    results = [
        (4, 2, low // 8, width), (4, 2, eighth, n * units), (4, 2, eighth, n * mix),
        (count, width), (count, width),
    ]
    passing = [
        (n * count, width), (n * count, width), block, block, block, block,
        (6, count, width), (6, count, width),
        (6, low // 8, width), (6, n * eighth, units), (6, n * eighth, mix),
        (2 * two, width), (two, mix), (two, units),
    ]
    result = pl.pallas_call(
        block_kernel,
        out_shape=[jax.ShapeDtypeStruct(s, bf16) for s in results] + [
            jax.ShapeDtypeStruct((72, LANES), f32), jax.ShapeDtypeStruct((8, width), f32),
        ] + [jax.ShapeDtypeStruct(s, bf16) for s in passing] + [
            jax.ShapeDtypeStruct((two, LANES), f32)
        ],
        in_specs=[anywhere] * 7 + [pl.BlockSpec(memory_space=vmem)] * 2,
        out_specs=[anywhere] * 5 + [pl.BlockSpec(memory_space=vmem)] * 2
        + [anywhere] * (len(passing) + 1),
        scratch_shapes=[
            vmem((width, units), bf16), vmem((width, mix), bf16), vmem((head, width), bf16),
            vmem((units, width), bf16), vmem((low, width), f32), vmem((width, units), f32),
            vmem((width, mix), f32),
            vmem((two, width), bf16), vmem((two, width), bf16), vmem((2 * two, width), bf16),
            vmem((2 * two, width), bf16), vmem((two, low), bf16),
            vmem((two, units), bf16), vmem((two, mix), bf16), vmem((two, units), bf16),
            vmem((two, mix), bf16), vmem((low // 8, width), bf16), vmem((two, LANES), f32),
            vmem((n,) + vectors.shape, bf16), vmem((3 * n, 1, vectors.shape[1]), f32),
            vmem((n, 1, LANES), f32),
            vmem((1, mix), f32), vmem((4, width), f32), vmem((1, units), f32),
            vmem((1, mix), f32), vmem((1, width), f32),
            vmem((n, 16, LANES), f32), vmem((n, 16, LANES), f32), vmem((72, LANES), f32),
            vmem((4, 72, LANES), f32),
            dma((SENDS,)), dma((SENDS,)), dma((LOCALS,)), dma((4,)), dma((6,)), dma((2,)), dma((8,)),
        ] + [dma((8,))] * 8,
        compiler_params=pltpu.CompilerParams(
            collective_id=0, has_side_effects=True, vmem_limit_bytes=VMEM_LIMIT
        ),
    )(tokens, vectors, upstream, expander, projector, combiner, contractor, ebias, angles)
    low_sum, exp_sum, proj_sum, osum, dsum, vec, norms = result[:7]
    return (
        low_sum.reshape(low, width), exp_sum.reshape(rows, n * units),
        proj_sum.reshape(rows, n * mix), osum, dsum, vec, norms,
    )


def sharded_heads(
    tokens, document_ends, projector, projbias, combiner, combbias, expander, expbias,
    contractor, contbias, attendgain, attendshift, feedgain, feedshift, cotangent,
):
    count, width = tokens.shape
    n = lax.axis_size("shard")
    me = lax.axis_index("shard")
    head = width // H
    mix = 3 * head
    rows = width // n
    units = expbias.shape[0]
    wide = projbias.shape[0]

    vectors = jnp.concatenate(
        [attendgain, attendshift, feedgain, feedshift, combbias, contbias, projbias,
         document_ends[0].astype(bf16)]
    )
    vectors = jnp.pad(vectors, (0, 16 * rows - vectors.shape[0])).reshape(16, rows)
    _, _, live = layout(document_ends[0], count)
    upstream = jnp.where(live[:, None], cotangent, jnp.zeros_like(cotangent))
    half = ROT // 2
    freqs = jnp.exp(-jnp.arange(half, dtype=f32) * (2.0 / ROT) * math.log(10000.0))
    still = jnp.zeros((LANES - ROT,), f32)
    ones = jnp.ones((half,), f32)
    angles = jnp.stack(
        [jnp.concatenate([freqs, freqs, still]), jnp.concatenate([-ones, ones, still])]
    )
    low, exp_out, proj_out, osum, dsum, vec, norms = block_passes(
        tokens, vectors, upstream, expander, projector, combiner, contractor,
        expbias.astype(f32)[None], angles,
    )

    floated = tokens.astype(f32)
    block_output = floated + jnp.where(
        live[:, None], osum.astype(f32) + (norms[4] + norms[5]), 0.0
    )
    block_output = block_output.astype(bf16)
    d_normed = dsum.astype(f32)
    normed, inverse = normalize(floated)
    grad = cotangent.astype(f32) + inverse * (
        d_normed
        - jnp.mean(d_normed, axis=1, keepdims=True)
        - normed * jnp.mean(d_normed * normed, axis=1, keepdims=True)
    )
    input_gradient = grad.astype(bf16)

    vec = vec.reshape(-1)
    norm_sums = vec[: 4 * rows].reshape(4, rows)
    mixed_bias = vec[4 * rows : 4 * rows + n * mix].reshape(n, 3, head).transpose(1, 0, 2)
    mixed_bias = lax.dynamic_slice(mixed_bias.reshape(-1), (me * wide,), (wide,))
    rest = vec[4 * rows + n * mix :]
    hidden_bias, out_bias = rest[:units], rest[units : units + rows]
    return (
        block_output, input_gradient, proj_out.astype(f32), mixed_bias, low[:head].astype(f32), out_bias,
        exp_out.astype(f32), hidden_bias, low[head:].astype(f32), out_bias,
        norm_sums[0], norm_sums[1], norm_sums[2], norm_sums[3],
    )


def solution(mesh):
    placed = (
        P(("rep", "shard"), None),
        P(("rep", "shard"), None),
        P("shard", None),
        P("shard"),
        P("shard", None),
        P("shard"),
        P("shard", None),
        P("shard"),
        P("shard", None),
        P("shard"),
        P("shard"),
        P("shard"),
        P("shard"),
        P("shard"),
        P(("rep", "shard"), None),
    )
    return jax.shard_map(
        sharded_heads if dict(mesh.shape) == {"rep": 4, "shard": H} else local,
        mesh=mesh,
        in_specs=placed,
        out_specs=(
            P(("rep", "shard"), None),
            P(("rep", "shard"), None),
            P("shard", None),
            P("shard"),
            P("shard", None),
            P("shard"),
            P("shard", None),
            P("shard"),
            P("shard", None),
            P("shard"),
            P("shard"),
            P("shard"),
            P("shard"),
            P("shard"),
        ),
        check_vma=False,
    )
```

```python
from functools import partial
import math

import jax
import jax.numpy as jnp
from jax import lax
from jax.experimental import pallas as pl
from jax.experimental.pallas import tpu as pltpu
from jax.sharding import PartitionSpec as P

H = 8
ROT = 64
DOCS = 4
LANES = 128
VMEM_LIMIT = 62 * 1024 * 1024

epsilon = 1e-05
masked_value = -1e30
f32 = jnp.float32
bf16 = jnp.bfloat16


def normalize(values):
    centre = jnp.mean(values, axis=1, keepdims=True)
    centred = values - centre
    spread = jnp.mean(centred * centred, axis=1, keepdims=True)
    inverse = lax.rsqrt(spread + epsilon)
    return (centred * inverse, inverse)


def layout(ends, count):
    index = jnp.arange(count, dtype=jnp.int32)
    passed = index[:, None] >= ends[None, :]
    document = jnp.sum(passed.astype(jnp.int32), axis=1)
    begin = jnp.max(jnp.where(passed, ends[None, :], 0), axis=1)
    position = (index - begin).astype(f32)
    allowed = (document[:, None] == document[None, :]) & (index[None, :] <= index[:, None])
    return (position, allowed, index < ends[-1])


def rotary_tables(position, rotary):
    half = rotary // 2
    freqs = jnp.exp(-jnp.arange(half, dtype=f32) * (2.0 / rotary) * math.log(10000.0))
    angles = position[..., None] * freqs
    angles = jnp.concatenate([angles, angles], axis=-1)
    return (jnp.cos(angles), jnp.sin(angles))


def rotate(values, cosine, sine, rotary):
    half = rotary // 2
    front = values[..., :rotary]
    turned = jnp.concatenate([-front[..., half:], front[..., :half]], axis=-1)
    return jnp.concatenate([front * cosine + turned * sine, values[..., rotary:]], axis=-1)


def unrotate(grads, cosine, sine, rotary):
    half = rotary // 2
    front = grads[..., :rotary]
    scaled = front * sine
    backward = jnp.concatenate([scaled[..., half:], -scaled[..., :half]], axis=-1)
    return jnp.concatenate([front * cosine + backward, grads[..., rotary:]], axis=-1)


def right_trans(left, right):
    return lax.dot_general(left, right, (((1,), (1,)), ((), ())), preferred_element_type=f32)


def left_trans(left, right):
    return lax.dot_general(left, right, (((0,), (0,)), ((), ())), preferred_element_type=f32)


def masked_scores(query_low, keys_low, allowed, factor):
    scores = (
        jnp.einsum("qhd,khd->hqk", query_low, keys_low, preferred_element_type=jnp.float32) * factor
    )
    return jnp.where(allowed[None], scores, masked_value)


def weight_sums(left, right):
    piece = lax.slice_in_dim(
        left, 0, left.shape[1] // lax.axis_size("shard") * lax.axis_size("shard"), axis=1
    )
    return lax.psum_scatter(
        left_trans(piece, right).astype(jnp.bfloat16), "shard", scatter_dimension=0, tiled=True
    ).astype(jnp.float32)


def local(
    tokens,
    document_ends,
    projector,
    projbias,
    combiner,
    combbias,
    expander,
    expbias,
    contractor,
    contbias,
    attendgain,
    attendshift,
    feedgain,
    feedshift,
    cotangent,
):
    count, width = tokens.shape
    headsize = width // H
    factor = 1.0 / math.sqrt(headsize)
    position, allowed, live = layout(document_ends[0], count)
    cosine, sine = rotary_tables(position, ROT)
    cosine, sine = cosine[:, None, :], sine[:, None, :]
    (
        full_projector,
        full_combiner,
        full_projbias,
        full_combbias,
        gain_attend,
        shift_attend,
        gain_feed,
        shift_feed,
    ) = (
        lax.all_gather(projector, "shard", axis=0, tiled=True),
        lax.all_gather(combiner, "shard", axis=0, tiled=True),
        lax.all_gather(projbias, "shard", axis=0, tiled=True),
        lax.all_gather(combbias, "shard", axis=0, tiled=True),
        lax.all_gather(attendgain, "shard", axis=0, tiled=True),
        lax.all_gather(attendshift, "shard", axis=0, tiled=True),
        lax.all_gather(feedgain, "shard", axis=0, tiled=True),
        lax.all_gather(feedshift, "shard", axis=0, tiled=True),
    )
    floated = tokens.astype(jnp.float32)
    normed, inverse = normalize(floated)
    first_input = (normed * gain_attend + shift_attend).astype(jnp.bfloat16)
    second_input = (normed * gain_feed + shift_feed).astype(jnp.bfloat16)
    mixed = jnp.dot(first_input, full_projector, preferred_element_type=jnp.float32) + full_projbias
    query_low = rotate(mixed[:, :width].reshape(count, H, headsize), cosine, sine, ROT).astype(
        jnp.bfloat16
    )
    keys_low = rotate(
        mixed[:, width : 2 * width].reshape(count, H, headsize), cosine, sine, ROT
    ).astype(jnp.bfloat16)
    values_low = mixed[:, 2 * width :].reshape(count, H, headsize).astype(jnp.bfloat16)
    scores = masked_scores(query_low, keys_low, allowed, factor)
    peak = jnp.max(scores, axis=2, keepdims=True)
    raised = jnp.exp(scores - peak)
    total = jnp.sum(raised, axis=2, keepdims=True)
    probs_low = (raised / total).astype(jnp.bfloat16)
    logsum = peak + jnp.log(total)
    context = jnp.einsum("hqk,khd->qhd", probs_low, values_low, preferred_element_type=jnp.float32)
    context = context.reshape(count, width).astype(jnp.bfloat16)
    attended = jnp.dot(context, full_combiner, preferred_element_type=jnp.float32) + full_combbias
    full_expander, full_contractor, full_expbias, full_contbias = (
        lax.all_gather(expander, "shard", axis=0, tiled=True),
        lax.all_gather(contractor, "shard", axis=0, tiled=True),
        lax.all_gather(expbias, "shard", axis=0, tiled=True),
        lax.all_gather(contbias, "shard", axis=0, tiled=True),
    )
    hidden = jnp.dot(second_input, full_expander, preferred_element_type=jnp.float32) + full_expbias
    activated, gelu_back = jax.vjp(partial(jax.nn.gelu, approximate=False), hidden)
    active_low = activated.astype(jnp.bfloat16)
    feedout = (
        jnp.dot(active_low, full_contractor, preferred_element_type=jnp.float32) + full_contbias
    )
    block_output = (floated + jnp.where(live[:, None], attended + feedout, 0.0)).astype(
        jnp.bfloat16
    )
    (
        back_projector,
        back_combiner,
        back_expander,
        back_contractor,
        back_gain_attend,
        back_gain_feed,
    ) = (
        lax.all_gather(projector, "shard", axis=0, tiled=True),
        lax.all_gather(combiner, "shard", axis=0, tiled=True),
        lax.all_gather(expander, "shard", axis=0, tiled=True),
        lax.all_gather(contractor, "shard", axis=0, tiled=True),
        lax.all_gather(attendgain, "shard", axis=0, tiled=True),
        lax.all_gather(feedgain, "shard", axis=0, tiled=True),
    )
    upstream = jnp.where(live[:, None], cotangent, jnp.zeros_like(cotangent))
    contractor_part = weight_sums(active_low, upstream)
    combiner_part = weight_sums(context, upstream)
    output_bias = jnp.sum(upstream, axis=0, dtype=jnp.float32)
    d_active = right_trans(upstream, back_contractor)
    d_hidden = gelu_back(d_active)[0].astype(jnp.bfloat16)
    expander_part = weight_sums(second_input, d_hidden)
    hidden_bias = jnp.sum(d_hidden, axis=0, dtype=jnp.float32)
    d_second = right_trans(d_hidden, back_expander)
    d_context = (
        right_trans(upstream, back_combiner).reshape(count, H, headsize).astype(jnp.bfloat16)
    )
    scores_again = masked_scores(query_low, keys_low, allowed, factor)
    probs = jnp.exp(scores_again - logsum)
    d_probs = jnp.einsum("qhd,khd->hqk", d_context, values_low, preferred_element_type=jnp.float32)
    d_values = jnp.einsum("hqk,qhd->khd", probs_low, d_context, preferred_element_type=jnp.float32)
    d_scores = (probs * (d_probs - jnp.sum(d_probs * probs, axis=2, keepdims=True))).astype(
        jnp.bfloat16
    )
    d_query = (
        jnp.einsum("hqk,khd->qhd", d_scores, keys_low, preferred_element_type=jnp.float32) * factor
    )
    d_keys = (
        jnp.einsum("hqk,qhd->khd", d_scores, query_low, preferred_element_type=jnp.float32) * factor
    )
    d_mixed = jnp.concatenate(
        [
            unrotate(d_query, cosine, sine, ROT).reshape(count, width),
            unrotate(d_keys, cosine, sine, ROT).reshape(count, width),
            d_values.reshape(count, width),
        ],
        axis=1,
    ).astype(jnp.bfloat16)
    projector_part = weight_sums(first_input, d_mixed)
    mixed_bias = jnp.sum(d_mixed, axis=0, dtype=jnp.float32)
    d_first = right_trans(d_mixed, back_projector)
    attend_scale = jnp.sum(d_first * normed, axis=0)
    attend_offset = jnp.sum(d_first, axis=0)
    feed_scale = jnp.sum(d_second * normed, axis=0)
    feed_offset = jnp.sum(d_second, axis=0)
    d_normed = d_first * back_gain_attend + d_second * back_gain_feed
    grad_float = cotangent.astype(jnp.float32) + inverse * (
        d_normed
        - jnp.mean(d_normed, axis=1, keepdims=True)
        - normed * jnp.mean(d_normed * normed, axis=1, keepdims=True)
    )
    input_gradient = grad_float.astype(jnp.bfloat16)
    mixed_bias, output_bias, hidden_bias, attend_scale, attend_offset, feed_scale, feed_offset = (
        lax.psum_scatter(
            mixed_bias.astype(jnp.bfloat16), "shard", scatter_dimension=0, tiled=True
        ).astype(jnp.float32),
        lax.psum_scatter(
            output_bias.astype(jnp.bfloat16), "shard", scatter_dimension=0, tiled=True
        ).astype(jnp.float32),
        lax.psum_scatter(
            hidden_bias.astype(jnp.bfloat16), "shard", scatter_dimension=0, tiled=True
        ).astype(jnp.float32),
        lax.psum_scatter(
            attend_scale.astype(jnp.bfloat16), "shard", scatter_dimension=0, tiled=True
        ).astype(jnp.float32),
        lax.psum_scatter(
            attend_offset.astype(jnp.bfloat16), "shard", scatter_dimension=0, tiled=True
        ).astype(jnp.float32),
        lax.psum_scatter(
            feed_scale.astype(jnp.bfloat16), "shard", scatter_dimension=0, tiled=True
        ).astype(jnp.float32),
        lax.psum_scatter(
            feed_offset.astype(jnp.bfloat16), "shard", scatter_dimension=0, tiled=True
        ).astype(jnp.float32),
    )
    (
        projector_part,
        mixed_bias,
        combiner_part,
        output_bias,
        expander_part,
        hidden_bias,
        contractor_part,
        attend_scale,
        attend_offset,
        feed_scale,
        feed_offset,
    ) = (
        lax.psum(projector_part.astype(jnp.bfloat16), "rep").astype(jnp.float32),
        lax.psum(mixed_bias.astype(jnp.bfloat16), "rep").astype(jnp.float32),
        lax.psum(combiner_part.astype(jnp.bfloat16), "rep").astype(jnp.float32),
        lax.psum(output_bias.astype(jnp.bfloat16), "rep").astype(jnp.float32),
        lax.psum(expander_part.astype(jnp.bfloat16), "rep").astype(jnp.float32),
        lax.psum(hidden_bias.astype(jnp.bfloat16), "rep").astype(jnp.float32),
        lax.psum(contractor_part.astype(jnp.bfloat16), "rep").astype(jnp.float32),
        lax.psum(attend_scale.astype(jnp.bfloat16), "rep").astype(jnp.float32),
        lax.psum(attend_offset.astype(jnp.bfloat16), "rep").astype(jnp.float32),
        lax.psum(feed_scale.astype(jnp.bfloat16), "rep").astype(jnp.float32),
        lax.psum(feed_offset.astype(jnp.bfloat16), "rep").astype(jnp.float32),
    )
    return (
        block_output,
        input_gradient,
        projector_part,
        mixed_bias,
        combiner_part,
        output_bias,
        expander_part,
        hidden_bias,
        contractor_part,
        output_bias,
        attend_scale,
        attend_offset,
        feed_scale,
        feed_offset,
    )


def lane_half(shape):
    return lax.broadcasted_iota(jnp.int32, shape, 1) < ROT // 2


def turn(front, signed):
    moved = jnp.where(
        lane_half(front.shape),
        pltpu.roll(front, LANES - ROT // 2, 1),
        pltpu.roll(front, ROT // 2, 1),
    )
    return moved * signed


def rotated(values, cosine, signed):
    front = values[:, :LANES]
    return jnp.concatenate([front * cosine + turn(front, signed), values[:, LANES:]], axis=1)


def unrotated(grads, cosine, signed):
    front = grads[:, :LANES]
    return jnp.concatenate([front * cosine - turn(front, signed), grads[:, LANES:]], axis=1)


def block_layout(ends, count):
    row = lax.broadcasted_iota(jnp.int32, (count, 1), 0).astype(f32)
    column = lax.broadcasted_iota(jnp.int32, (1, count), 1).astype(f32)
    row_doc = jnp.zeros((count, 1), f32)
    column_doc = jnp.zeros((1, count), f32)
    begin = jnp.zeros((count, 1), f32)
    for i in range(DOCS):
        end = ends[:, i : i + 1]
        row_doc += jnp.where(row >= end, 1.0, 0.0)
        column_doc += jnp.where(column >= end, 1.0, 0.0)
        begin = jnp.maximum(begin, jnp.where(row >= end, end, 0.0))
    return (row_doc == column_doc) & (column <= row), row - begin


def dot(left, right):
    return jnp.dot(left, right, preferred_element_type=f32)


def softmax(q, k, allowed):
    scores = right_trans(q, k) * (1.0 / math.sqrt(q.shape[1]))
    scores = jnp.where(allowed, scores, masked_value)
    raised = jnp.exp(scores - jnp.max(scores, axis=1, keepdims=True))
    return raised / jnp.sum(raised, axis=1, keepdims=True)


def norm_parts(x_ref, at):
    x = x_ref[at, :].astype(f32)
    centre = jnp.mean(x, axis=1, keepdims=True)
    centred = x - centre
    inverse = lax.rsqrt(jnp.mean(centred * centred, axis=1, keepdims=True) + epsilon)
    return centred, centre, inverse


def tables(ends, count, angles_ref):
    allowed, place = block_layout(ends, count)
    angles = place * angles_ref[0:1, :]
    return allowed, jnp.cos(angles), jnp.sin(angles) * angles_ref[1:2, :]


def forward_pass(
    x_ref, ends, count, angles_ref, norms_ref, pbias_ref, ebias_ref, proj_ref, exp_ref, comb_ref,
    cont_ref, h1_ref, h2_ref, qkv_ref, ca_ref, slope_ref, stats_ref, part_ref,
):
    slots, width = x_ref.shape
    head = comb_ref.shape[0]
    units = exp_ref.shape[1]
    step = min(64, count)

    @pl.loop(0, slots // step)
    def _(i):
        at = rows_at(i * step, step)
        centred, centre, inverse = norm_parts(x_ref, at)
        normed = centred * inverse
        h1_ref[at, :] = (normed * norms_ref[0:1, :] + norms_ref[1:2, :]).astype(bf16)
        h2_ref[at, :] = (normed * norms_ref[2:3, :] + norms_ref[3:4, :]).astype(bf16)
        stats_ref[at, 0:1] = centre
        stats_ref[at, 1:2] = inverse

    for j in range(3):
        cut = slice(j * head, j * head + head)
        mixed = dot(h1_ref[...], proj_ref[:, cut]) + pbias_ref[:, cut]
        for b in range(slots // count):
            at = slice(b * count, b * count + count)
            value = mixed[at]
            if j < 2:
                _, cosine, signed = tables(ends[b], count, angles_ref)
                value = rotated(value, cosine, signed)
            qkv_ref[at, cut] = value.astype(bf16)
    tile = min(256, units)
    for start in range(0, units, tile):
        hidden = dot(h2_ref[...], exp_ref[:, start : start + tile])
        hidden += ebias_ref[:, start : start + tile]
        below = 0.5 + 0.5 * lax.erf(hidden * math.sqrt(0.5))
        ca_ref[:, head + start : head + start + tile] = (hidden * below).astype(bf16)
        density = jnp.exp(hidden * hidden * -0.5) * (1.0 / math.sqrt(2.0 * math.pi))
        slope_ref[:, start : start + tile] = (below + hidden * density).astype(bf16)
    for b in range(slots // count):
        at = slice(b * count, b * count + count)
        allowed, _ = block_layout(ends[b], count)
        probs = softmax(qkv_ref[at, :head], qkv_ref[at, head : 2 * head], allowed).astype(bf16)
        ca_ref[at, :head] = dot(probs, qkv_ref[at, 2 * head :]).astype(bf16)
    tile = min(512, width)
    for start in range(0, width, tile):
        cut = slice(start, start + tile)
        part = dot(ca_ref[:, :head], comb_ref[:, cut]) + dot(ca_ref[:, head:], cont_ref[:, cut])
        part_ref[:, cut] = part.astype(bf16)


def backward_pass(
    x_ref, up_ref, ends, count, angles_ref, norms_ref, qkv_ref, slope_ref, stats_ref, proj_ref,
    exp_ref, comb_ref, cont_ref, dh_ref, dm_ref, dn_ref, sums_ref, hbias_ref, mbias_ref, obias_ref,
):
    slots, width = x_ref.shape
    head = comb_ref.shape[0]
    units = exp_ref.shape[1]
    tile = min(256, units)
    d_context = right_trans(up_ref[...], comb_ref[...]).astype(bf16)
    for start in range(0, units, tile):
        cut = slice(start, start + tile)
        d_active = right_trans(up_ref[...], cont_ref[cut, :])
        d_hidden = (d_active * slope_ref[:, cut].astype(f32)).astype(bf16)
        dh_ref[:, cut] = d_hidden
        hbias_ref[:, cut] += jnp.sum(d_hidden.astype(f32), axis=0, keepdims=True)
    factor = 1.0 / math.sqrt(head)
    for b in range(slots // count):
        at = slice(b * count, b * count + count)
        allowed, cosine, signed = tables(ends[b], count, angles_ref)
        q, k = qkv_ref[at, :head], qkv_ref[at, head : 2 * head]
        v = qkv_ref[at, 2 * head :]
        d_ctx = d_context[at]
        probs = softmax(q, k, allowed)
        d_probs = right_trans(d_ctx, v)
        d_v = left_trans(probs.astype(bf16), d_ctx)
        d_s = probs * (d_probs - jnp.sum(d_probs * probs, axis=1, keepdims=True))
        d_s = d_s.astype(bf16)
        dm_ref[at, :head] = unrotated(dot(d_s, k) * factor, cosine, signed).astype(bf16)
        d_k = unrotated(left_trans(d_s, q) * factor, cosine, signed).astype(bf16)
        dm_ref[at, head : 2 * head] = d_k
        dm_ref[at, 2 * head :] = d_v.astype(bf16)
    mbias_ref[...] += jnp.sum(dm_ref[...].astype(f32), axis=0, keepdims=True)
    obias_ref[...] += jnp.sum(up_ref[...].astype(f32), axis=0, keepdims=True)
    centre, inverse = stats_ref[:, 0:1], stats_ref[:, 1:2]
    tile = min(256, width)

    @pl.loop(0, width // tile, unroll=2)
    def _(i):
        cut = rows_at(i * tile, tile)
        normed = (x_ref[:, cut].astype(f32) - centre) * inverse
        d_first = right_trans(dm_ref[...], proj_ref[cut, :])
        d_second = right_trans(dh_ref[...], exp_ref[cut, :])
        dn_ref[:, cut] = (
            d_first * norms_ref[0:1, cut] + d_second * norms_ref[2:3, cut]
        ).astype(bf16)
        sums_ref[0:1, cut] += jnp.sum(d_first * normed, axis=0, keepdims=True)
        sums_ref[1:2, cut] += jnp.sum(d_first, axis=0, keepdims=True)
        sums_ref[2:3, cut] += jnp.sum(d_second * normed, axis=0, keepdims=True)
        sums_ref[3:4, cut] += jnp.sum(d_second, axis=0, keepdims=True)


def accumulate(total, left, right, tall):
    wide = min(256, right.shape[1])

    @pl.loop(0, left.shape[1] // tall)
    def _(i):
        at = pl.ds(pl.multiple_of(i * tall, LANES), tall)
        for start in range(0, right.shape[1], wide):
            cut = slice(start, start + wide)
            total[at, cut] += left_trans(left[:, at], right[:, cut])


MESH = pl.DeviceIdType.MESH


def position_of():
    rep, me = lax.axis_index("rep"), lax.axis_index("shard")
    return rep, me, lax.div(rep, 2), lax.rem(rep, 2), lax.div(me, 2), lax.rem(me, 2)


def meet(peers):
    barrier = pltpu.get_barrier_semaphore()
    for peer in peers:
        pl.semaphore_signal(barrier, inc=1, device_id=peer, device_id_type=MESH)
    pl.semaphore_wait(barrier, len(peers))


def rows_at(start, size):
    return pl.ds(pl.multiple_of(start, size), size)


class Net:
    def __init__(self, send_sem, recv_sem, local_sem):
        self.send_sem, self.recv_sem, self.local_sem = send_sem, recv_sem, local_sem
        self.sends, self.locals, self.started, self.sent = 0, 0, 0, []

    def slots(self, count):
        first = self.started
        self.started += count
        return first

    def send(self, ends, slot, when=None):
        index = self.sends
        self.sends += 1

        def copy():
            src, dst, peer = ends()
            return pltpu.make_async_remote_copy(
                src_ref=src, dst_ref=dst, send_sem=self.send_sem.at[index],
                recv_sem=self.recv_sem.at[slot], device_id=peer, device_id_type=MESH,
            )

        if when is None:
            copy().start()
        else:
            pl.when(when)(lambda: copy().start())
        self.sent.append((copy, when))

    def arrived(self, dst, peer, slot):
        pltpu.make_async_remote_copy(
            src_ref=dst, dst_ref=dst, send_sem=self.send_sem.at[0],
            recv_sem=self.recv_sem.at[slot], device_id=peer, device_id_type=MESH,
        ).wait_recv()

    def local(self, src, dst):
        copy = pltpu.make_async_copy(src, dst, self.local_sem.at[self.locals])
        self.locals += 1
        copy.start()
        return copy

    def left(self, sent):
        for copy, when in sent:
            if when is None:
                copy().wait_send()
            else:
                pl.when(when)(lambda copy=copy: copy().wait_send())


class Chain:
    def __init__(self, source, out, count, where, sems):
        self.source, self.out, self.count = source, out, count
        self.rep, self.me, self.z, self.c = where
        self.side_send, self.side_recv, self.core_send, self.core_recv = sems
        self.sibling = self.me + 1 - 2 * self.c

    def block(self, shard):
        return self.out.at[rows_at(shard * self.count, self.count)]

    def side(self, side, step):
        block = self.block(self.me - side * 2 * step)
        peer = (self.rep, self.me + side * 2)
        index = (0 if side > 0 else 4) + step
        return pltpu.make_async_remote_copy(
            src_ref=block, dst_ref=block, send_sem=self.side_send.at[index],
            recv_sem=self.side_recv.at[index], device_id=peer, device_id_type=MESH,
        )

    def cross(self, side, step):
        block = self.block(self.me - side * 2 * step)
        index = (0 if side > 0 else 4) + step
        return pltpu.make_async_remote_copy(
            src_ref=block, dst_ref=block, send_sem=self.core_send.at[index],
            recv_sem=self.core_recv.at[index], device_id=(self.rep, self.sibling),
            device_id_type=MESH,
        )

    def taken(self, side, step):
        block = self.block(self.sibling - side * 2 * step)
        index = (0 if side > 0 else 4) + step
        return pltpu.make_async_remote_copy(
            src_ref=block, dst_ref=block, send_sem=self.core_send.at[index],
            recv_sem=self.core_recv.at[index], device_id=(self.rep, self.sibling),
            device_id_type=MESH,
        )

    def here(self, side, step):
        return self.z >= step if side > 0 else self.z + step <= 3

    def on(self, side):
        return self.z < 3 if side > 0 else self.z > 0

    def first(self, side):
        mine = self.block(self.me)
        index = 0 if side > 0 else 4
        return pltpu.make_async_remote_copy(
            src_ref=self.source, dst_ref=mine, send_sem=self.side_send.at[index],
            recv_sem=self.side_recv.at[index], device_id=(self.rep, self.me + side * 2),
            device_id_type=MESH,
        )

    def first_cross(self):
        mine = self.block(self.me)
        return pltpu.make_async_remote_copy(
            src_ref=self.source, dst_ref=mine, send_sem=self.core_send.at[0],
            recv_sem=self.core_recv.at[0], device_id=(self.rep, self.sibling),
            device_id_type=MESH,
        )

    def begin(self):
        for side in (1, -1):
            pl.when(self.on(side))(lambda: self.first(side).start())
        self.first_cross().start()
    def wait_own(self):
        self.taken(1, 0).wait_recv()

    def step(self, step):
        for side in (1, -1):
            here = self.here(side, step)

            @pl.when(here)
            def _():
                block = self.block(self.me - side * 2 * step)
                index = (0 if side > 0 else 4) + step - 1
                pltpu.make_async_remote_copy(
                    src_ref=block, dst_ref=block, send_sem=self.side_send.at[index],
                    recv_sem=self.side_recv.at[index], device_id=(self.rep, self.sibling),
                    device_id_type=MESH,
                ).wait_recv()
                self.cross(side, step).start()

            pl.when(here & self.on(side) & (step < 3))(lambda: self.side(side, step).start())

    def take(self, step):
        for side in (1, -1):
            pl.when(self.here(side, step))(lambda: self.taken(side, step).wait_recv())

    def finish(self):
        self.first_cross().wait_send()
        for side in (1, -1):
            pl.when(self.on(side))(lambda: self.first(side).wait_send())
            for step in (1, 2, 3):
                here = self.here(side, step)
                pl.when(here)(lambda: self.cross(side, step).wait_send())
                if step < 3:
                    pl.when(here & self.on(side))(lambda: self.side(side, step).wait_send())


def add_into(target, other):
    rows = target.shape[-2]
    step = min(32, rows)

    @pl.loop(0, rows // step)
    def _(i):
        at = (Ellipsis, pl.ds(pl.multiple_of(i * step, step), step), slice(None))
        lead = (slice(None),) * (len(target.shape) - 2)
        at = lead + at[1:]
        target[at] = (target[at].astype(f32) + other[at].astype(f32)).astype(target.dtype)


def block_kernel(
    tok_ref, vec_ref, up_ref, expander_ref, projector_ref, comb_hbm, cont_hbm, ebias_ref,
    angles_ref,
    comb_out, cont_out, exp_out, proj_out, osum_out, dsum_out, vec_out, norms_ref,
    x_out, up_out, part_own, dn_own, o_in, d_in, o_land, d_land, low_land, he_land, hp_land,
    h_save, qkv_save, slope_save, stats_save,
    exp_ref, proj_ref, comb_ref, cont_ref, low_sum, he_sum, hp_sum,
    xs, us, hs, pd, ca, slope, qkv, dh, dm, spare, stats,
    vecs, bias_all, ends_all, pbias, sums, hbias, mbias, obias,
    vec_msg, vec_in, vec_mix, vec_all,
    send_sem, recv_sem, local_sem, load_sem, store_sem, cross_send, cross_recv,
    xs_send, xs_recv, xc_send, xc_recv, us_send, us_recv, uc_send, uc_recv,
):
    rep, me, y, x, z, c = position_of()
    count, width = tok_ref.shape
    rows, quarter = expander_ref.shape[0], expander_ref.shape[0] // 4
    units, mix = exp_ref.shape[1], proj_ref.shape[1]
    head = mix // 3
    sibling = (rep, me + 1 - 2 * c)
    x_rep, y_rep, d_rep = rep + 1 - 2 * x, rep + 2 - 4 * y, 3 - rep
    by_x, by_y, across = (x_rep, me), (y_rep, me), (d_rep, me)
    ring = [(rep, lax.rem(me + k, 8)) for k in range(1, 8)]
    meet(ring + [by_x, by_y, across])
    slots = hs.shape[0] // 2
    h1s, h2s = hs.at[pl.ds(0, slots)], hs.at[pl.ds(slots, slots)]
    parts, dns = pd.at[pl.ds(0, slots)], pd.at[pl.ds(slots, slots)]
    net = Net(send_sem, recv_sem, local_sem)

    def weight_copies(go, first, size, source_rows, t):
        source = rows_at(source_rows, size)
        target = rows_at(first, size)
        go(expander_ref.at[source, rows_at(t * units, units)], exp_ref.at[target, :])
        for j in range(3):
            go(
                projector_ref.at[source, rows_at(j * width + t * head, head)],
                proj_ref.at[target, pl.ds(j * head, head)],
            )

    remote = net.slots(32)
    chips = []
    for i in range(3):
        down, up = 3 - i, i
        chips.append(jnp.where(
            z < 2, jnp.where(up >= z, up + 1, up), jnp.where(down <= z, down - 1, down)
        ))
    for chip in chips:
        for core in (0, 1):
            part = [0]

            def go(src, dst):
                net.send(
                    lambda: (src, dst, (rep, chip * 2 + core)), remote + me * 4 + part[0]
                )
                part[0] += 1

            weight_copies(go, me * rows + rep * quarter, quarter, rep * quarter, chip * 2 + core)
    small = net.slots(7)
    for k, peer in enumerate(ring):
        net.send(lambda peer=peer: (vec_ref, vecs.at[me], peer), small + k)
    where = (rep, me, z, c)
    tokens = Chain(
        tok_ref, x_out, count, where, (xs_send, xs_recv, xc_send, xc_recv)
    )
    cotangents = Chain(
        up_ref, up_out, count, where, (us_send, us_recv, uc_send, uc_recv)
    )
    tokens.begin()
    near = net.slots(4)
    part = [0]

    def go_near(src, dst):
        net.send(lambda: (src, dst, sibling), near + part[0])
        part[0] += 1

    weight_copies(go_near, me * rows, rows, 0, sibling[1])
    copies = []
    weight_copies(lambda s, d: copies.append(net.local(s, d)), me * rows, rows, 0, me)
    copies.append(net.local(vec_ref, vecs.at[me]))
    copies.append(net.local(comb_hbm, comb_ref))
    copies.append(net.local(cont_hbm, cont_ref))
    cotangents.begin()
    for ref in (low_sum, he_sum, hp_sum, sums, hbias, mbias, obias):
        if ref.shape[0] <= 8:
            ref[...] = jnp.zeros_like(ref)
        else:

            @pl.loop(0, ref.shape[0] // 64)
            def _(i):
                ref[rows_at(i * 64, 64), :] = jnp.zeros((64, ref.shape[1]), f32)

    def shard_rows(step, core):
        return (chips[step - 1] * 2 + core) * rows

    first_hop, second_hop = net.slots(12), net.slots(18)
    gone = []

    def pass_on(ref_at, peer, slot):
        for ref, more in ((exp_ref, 0), (proj_ref, 1)):
            net.send(lambda ref=ref: (ref.at[ref_at, :], ref.at[ref_at, :], peer), slot + more)

    def landed(step):
        for core in (0, 1):
            at = rows_at(shard_rows(step, core) + rep * quarter, quarter)
            slot = remote + (chips[step - 1] * 2 + core) * 4
            net.arrived(exp_ref.at[at, :], sibling, slot)
            for j in range(3):
                net.arrived(proj_ref.at[at, pl.ds(j * head, head)], sibling, slot + 1 + j)
            peer = by_x if core == 0 else by_y
            pass_on(at, peer, first_hop + ((step - 1) * 2 + core) * 2)

    def crossed(step):
        for core in (0, 1):
            base = shard_rows(step, core)
            hop = first_hop + ((step - 1) * 2 + core) * 2
            other = rows_at(base + (x_rep if core == 0 else y_rep) * quarter, quarter)
            net.arrived(exp_ref.at[other, :], sibling, hop)
            net.arrived(proj_ref.at[other, :], sibling, hop + 1)
            hop = second_hop + (step - 1) * 6
            if core == 0:
                pass_on(rows_at(base + y * 2 * quarter, 2 * quarter), by_y, hop)
                gone.append((rows_at(base + (1 - y) * 2 * quarter, 2 * quarter), hop))
            else:
                pass_on(rows_at(base + rep * quarter, quarter), by_x, hop + 2)
                pass_on(other, by_x, hop + 4)
                gone.append((rows_at(base + x_rep * quarter, quarter), hop + 2))
                gone.append((rows_at(base + d_rep * quarter, quarter), hop + 4))

    landed(1)
    landed(2)
    crossed(1)
    landed(3)
    crossed(2)
    crossed(3)
    tokens.step(1)
    opening, net.sent = net.sent, []

    for k in range(1, 8):
        net.arrived(vecs.at[lax.rem(me + 8 - k, 8)], sibling, small + k - 1)
    for copy in copies:
        copy.wait()
    for s in range(8):
        values = vecs[s].astype(f32)
        for j in range(3):
            bias_all[3 * s + j] = values[6 + j : 7 + j, :]
        ends_all[s] = values[9:10, :LANES]
        norms_ref[:, s * rows : s * rows + rows] = values[:8, :]
    for j in range(3):
        pbias[:, j * head : j * head + head] = bias_all[8 * j + me]

    at = rows_at(sibling[1] * rows, rows)
    net.arrived(exp_ref.at[at, :], sibling, near)
    for j in range(3):
        net.arrived(proj_ref.at[at, pl.ds(j * head, head)], sibling, near + 1 + j)
    for at, slot in gone:
        net.arrived(exp_ref.at[at, :], sibling, slot)
        net.arrived(proj_ref.at[at, :], sibling, slot + 1)
    tokens.wait_own()
    cotangents.wait_own()
    cotangents.step(1)

    def chip_of(slot):
        second = jnp.where(z == 0, 2, jnp.where(z == 1, 0, 1))
        last = jnp.where(z < 2, 3, 0)
        after = jnp.where(z < 3, z + 1, 2)
        return jnp.where(
            slot == 0, z, jnp.where(slot == 1, after, jnp.where(slot == 2, second, last))
        )

    class Loads:
        def __init__(self, own, source, into, first):
            self.own, self.source, self.into, self.first = own, source, into, first

        def start_own(self):
            theirs = self.source.at[rows_at(sibling[1] * count, count)]
            for source, b in ((self.own, c), (theirs, 1 - c)):
                pltpu.make_async_copy(
                    source, self.into.at[rows_at(b * count, count)], load_sem.at[self.first + b]
                ).start()

        def copies(self, slot):
            return [
                pltpu.make_async_copy(
                    self.source.at[rows_at((chip_of(slot) * 2 + b) * count, count)],
                    self.into.at[rows_at(b * count, count)], load_sem.at[self.first + b],
                )
                for b in range(2)
            ]

        def start(self, slot):
            for copy in self.copies(slot):
                copy.start()

        def wait(self, slot):
            for copy in self.copies(slot):
                copy.wait()

    x_loads, up_loads = Loads(tok_ref, x_out, xs, 0), Loads(up_ref, up_out, us, 2)
    x_loads.start_own()
    up_loads.start_own()

    def stores(source, own, theirs, first, chip):
        mine = pltpu.make_async_copy(
            source.at[rows_at(c * count, count)], own.at[chip], store_sem.at[first]
        )
        other = pltpu.make_async_remote_copy(
            src_ref=source.at[rows_at((1 - c) * count, count)], dst_ref=theirs.at[chip],
            send_sem=cross_send.at[first], recv_sem=cross_recv.at[first * 4 + chip],
            device_id=sibling, device_id_type=MESH,
        )
        return mine, other

    def store(source, own, theirs, first, chip):
        mine, other = stores(source, own, theirs, first, chip)
        mine.start()
        other.start()

    def stored(source, own, theirs, first, chip):
        mine, other = stores(source, own, theirs, first, chip)
        mine.wait()
        other.wait_send()

    def saves():
        pairs = [(hs, h_save), (qkv, qkv_save), (slope, slope_save), (stats, stats_save)]
        return [(pair, store_sem.at[2 + i]) for i, pair in enumerate(pairs)]

    restores = [pltpu.make_async_copy(there, here, sem) for (here, there), sem in saves()]

    class Piece:
        def __init__(self, total, land, start, step, stage, tmp):
            self.total, self.land, self.start, self.step = total, land, start, step
            self.stage, self.tmp = stage, tmp
            self.size = land.shape[1]
            self.slot = net.slots(6)

        def each(self, quarter, half, work):
            @pl.loop(0, self.size // self.step)
            def _(i):
                work(
                    rows_at(self.start(quarter, half, i), self.step),
                    rows_at(i * self.step, self.step),
                )

        def lower(self, quarter, half, target):
            def work(at, to):
                target[to, :] = self.total[at, :].astype(bf16)

            self.each(quarter, half, work)

        def add(self, quarter, half, source):
            def work(at, to):
                self.total[at, :] += source[to, :].astype(f32)

            self.each(quarter, half, work)

        def room(self, first):
            return self.tmp.at[pl.ds(first, self.size)]

        def first(self):
            before = len(net.sent)
            for i in range(2):
                for half, quarter, peer in (
                    (0, i * 2 + 1 - x, by_x), (1, (1 - y) * 2 + i, by_y)
                ):
                    place = half * 2 + i
                    self.lower(quarter, half, self.stage[place])
                    net.send(
                        lambda place=place, peer=peer: (
                            self.stage[place], self.land.at[place], peer
                        ),
                        self.slot + place,
                    )
            self.sent, net.sent = net.sent[before:], net.sent[:before]

        def fetch(self, place):
            net.arrived(self.land.at[place], sibling, self.slot + place)
            return net.local(self.land.at[place], self.room(place * self.size))

        def second(self):
            loads = [self.fetch(place) for place in range(4)]
            for half, other, peer in ((0, 1 - y, by_y), (1, 1 - x, by_x)):
                for i in range(2):
                    loads[half * 2 + i].wait()
                    quarter = i * 2 + x if half == 0 else y * 2 + i
                    self.add(quarter, half, self.room((half * 2 + i) * self.size))
                quarter = other * 2 + x if half == 0 else y * 2 + other
                stage = self.later(half)
                self.lower(quarter, half, stage)
                net.send(
                    lambda stage=stage, half=half, peer=peer: (
                        stage, self.land.at[4 + half], peer
                    ),
                    self.slot + 4 + half,
                )

        def later(self, half):
            first = 6 + half if self.tmp.shape[0] >= 8 * self.size else half
            return self.room(first * self.size)

        def third(self):
            loads = [self.fetch(4 + half) for half in range(2)]
            for half in range(2):
                loads[half].wait()
                self.add(rep, half, self.room((4 + half) * self.size))
                self.lower(rep, half, self.room((2 + half) * self.size))
            return [self.room((2 + half) * self.size) for half in range(2)]

    def low_start(quarter, half, i):
        first = quarter * (head // 4) + half * (head // 8)
        rest = head + quarter * (units // 4) + half * (units // 8) + (i - 1) * 32
        return jnp.where(i == 0, first, rest)

    def high_start(quarter, half, i):
        return i * rows + quarter * (rows // 4) + half * (rows // 8)

    low_size, high_size = low_land.shape[1], he_land.shape[1]

    def halves(ref):
        return [ref.at[pl.ds(i * high_size, high_size)] for i in range(2)]

    low_stage = [parts.at[pl.ds(i * low_size, low_size)] for i in range(3)] + [spare]
    low = Piece(low_sum, low_land, low_start, 32, low_stage, cont_ref)
    he = Piece(he_sum, he_land, high_start, rows // 8, halves(dh) + halves(slope), exp_ref)
    hp = Piece(hp_sum, hp_land, high_start, rows // 8, halves(dm) + halves(qkv), proj_ref)

    @pl.loop(0, 5)
    def _(turn_index):
        slot = jnp.minimum(turn_index, 3)

        @pl.when(turn_index < 4)
        def _():
            chip = chip_of(slot)
            ends = [ends_all[chip * 2 + b] for b in range(2)]
            x_loads.wait(slot)
            forward_pass(
                xs, ends, count, angles_ref, norms_ref, pbias, ebias_ref, proj_ref, exp_ref,
                comb_ref, cont_ref, h1s, h2s, qkv, ca, slope, stats, parts,
            )
            store(parts, part_own, o_in, 0, chip)
            pl.when(slot == 2)(lambda: tokens.step(3))

            @pl.when(slot == 3)
            def _():
                cotangents.step(3)
                cotangents.take(3)
                up_loads.start(3)

            up_loads.wait(slot)
            accumulate(low_sum, ca, us, ca.shape[1])
            stored(parts, part_own, o_in, 0, chip)

        @pl.when(turn_index == 2)
        def _():
            for (here, there), sem in saves():
                pltpu.make_async_copy(here, there, sem).start()
            tokens.take(3)
            x_loads.start(3)
            for (here, there), sem in saves():
                pltpu.make_async_copy(here, there, sem).wait()

        pl.when(turn_index == 3)(lambda: low.first())

        @pl.when(turn_index == 4)
        def _():
            restores[0].start()
            for restore in restores[1:]:
                restore.wait()
            x_loads.wait(2)
            up_loads.wait(2)

        @pl.when(turn_index != 2)
        def _():
            slot = jnp.where(turn_index == 4, 2, turn_index)
            chip = chip_of(slot)
            ends = [ends_all[chip * 2 + b] for b in range(2)]
            backward_pass(
                xs, us, ends, count, angles_ref, norms_ref, qkv, slope, stats, proj_ref, exp_ref,
                comb_ref, cont_ref, dh, dm, dns, sums, hbias, mbias, obias,
            )
            store(dns, dn_own, d_in, 1, chip)
            pl.when(slot == 0)(lambda: tokens.step(2))
            pl.when(slot == 1)(lambda: cotangents.step(2))

            @pl.when(turn_index < 2)
            def _():
                tokens.take(slot + 1)
                x_loads.start(slot + 1)
                cotangents.take(slot + 1)
                up_loads.start(slot + 1)

            @pl.when(turn_index == 3)
            def _():
                for restore in restores[1:]:
                    restore.start()
                x_loads.start(2)
                up_loads.start(2)

            pl.when(turn_index == 4)(lambda: restores[0].wait())
            accumulate(he_sum, h2s, dh, width // 2)
            accumulate(hp_sum, h1s, dm, width // 2)
            stored(dns, dn_own, d_in, 1, chip)

    net.left(opening)
    he.first()

    class Line:
        def __init__(self, own, inward, land, total, first):
            self.own, self.inward, self.land, self.total = own, inward, land, total
            self.first = first
            self.slot = net.slots(6)

        def block(self, index):
            return self.total.at[rows_at(index * count, count)]

        def join(self):
            room = [xs.at[pl.ds(i * count, count)] for i in range(2)]
            room += [us.at[pl.ds(i * count, count)] for i in range(2)]
            loads = []
            for i in range(4):
                loads.append(net.local(self.own.at[i], self.block(i)))
                pltpu.make_async_remote_copy(
                    src_ref=self.inward.at[i], dst_ref=self.inward.at[i],
                    send_sem=cross_send.at[self.first],
                    recv_sem=cross_recv.at[self.first * 4 + i],
                    device_id=sibling, device_id_type=MESH,
                ).wait_recv()
                loads.append(net.local(self.inward.at[i], room[i]))
            for i in range(4):
                loads[2 * i].wait()
                loads[2 * i + 1].wait()
                add_into(self.block(i), room[i])

        def push(self, block, step, side, when):
            place = (step - 1) + (0 if side > 0 else 3)
            net.send(
                lambda: (self.block(block), self.land.at[place], (rep, me + 2 * side)),
                self.slot + place, when,
            )

        def begin(self, steps):
            for step in steps:
                self.push(step, step, 1, z == 0)
                self.push(3 - step, step, -1, z == 3)

        def step_on(self, step):
            for side in (1, -1):
                place = (step - 1) + (0 if side > 0 else 3)
                block = z + side * (step - 1)
                here = (z >= 1) & (block <= 3) if side > 0 else (z <= 2) & (block >= 0)
                index = net.locals
                net.locals += 1

                @pl.when(here)
                def _():
                    net.arrived(self.land.at[place], sibling, self.slot + place)
                    load = pltpu.make_async_copy(
                        self.land.at[place], comb_ref, local_sem.at[index]
                    )
                    load.start()
                    load.wait()
                    add_into(self.block(block), comb_ref)

                if step > 1:
                    self.push(block, step - 1, side, here)

    out = Line(part_own, o_in, o_land, hs, 0)
    back = Line(dn_own, d_in, d_land, pd, 1)
    out.join()
    out.begin((3, 2, 1))
    hp.first()
    low.second()

    vec_msg[...] = jnp.zeros_like(vec_msg)
    vec_mix[...] = jnp.zeros_like(vec_mix)
    per = rows // LANES
    for t in range(8):
        for j in range(4):
            for i in range(per):
                at = t * rows + i * LANES
                vec_msg[t, j * per + i : j * per + i + 1, :] = sums[j : j + 1, at : at + LANES]
        for i in range(mix // LANES):
            at = 4 * per + i
            vec_msg[t, at : at + 1, :] = mbias[:, i * LANES : (i + 1) * LANES]
    for i in range(units // LANES):
        vec_mix[56 + i : 57 + i, :] = hbias[:, i * LANES : (i + 1) * LANES]
    for i in range(per):
        vec_mix[64 + i : 65 + i, :] = obias[:, rows_at(me * rows + i * LANES, LANES)]
    small = net.slots(7)
    for k in range(1, 8):
        t = lax.rem(me + k, 8)
        net.send(lambda t=t: (vec_msg.at[t], vec_in.at[me], (rep, t)), small + k - 1)
    vec_load = net.local(vec_msg.at[me], vec_in.at[me])

    he.second()
    out.step_on(3)
    net.left(low.sent)
    back.join()
    hp.second()
    out.step_on(2)
    low_done = low.third()

    class Spread:
        def __init__(self, target, sources):
            self.target, self.slot = target, net.slots(6)
            for h, source in enumerate(sources):
                for k, peer in enumerate((by_x, by_y)):
                    net.send(
                        lambda source=source, h=h, peer=peer: (source, target.at[rep, h], peer),
                        self.slot + h * 3 + k,
                    )

        def on(self):
            for h, (k, got, peer) in enumerate(((1, y_rep, by_x), (0, x_rep, by_y))):
                net.arrived(self.target.at[got, h], sibling, self.slot + h * 3 + k)
                net.send(
                    lambda h=h, got=got, peer=peer: (
                        self.target.at[got, h], self.target.at[got, h], peer
                    ),
                    self.slot + h * 3 + 2,
                )

        def wait(self):
            for h, (k, got) in enumerate(((0, x_rep), (1, y_rep))):
                net.arrived(self.target.at[got, h], sibling, self.slot + h * 3 + k)
                net.arrived(self.target.at[d_rep, h], sibling, self.slot + h * 3 + 2)

    low_copies, low_spreads = [], []
    for target, first in ((cont_out, head // 8), (comb_out, 0)):
        pieces = [done.at[pl.ds(first, target.shape[2])] for done in low_done]
        low_copies += [net.local(pieces[h], target.at[rep, h]) for h in range(2)]
        low_spreads.append(Spread(target, pieces))
    class Turn:
        def __init__(self, source, half, place):
            self.half, self.place = half, place
            self.slot = net.slots(21)
            self.copies = []
            for k in range(1, 8):
                t = lax.rem(me + k, 8)
                for j, (src, dst) in enumerate(place(source, t, me)):
                    net.send(
                        lambda src=src, dst=dst, t=t: (src, dst, (rep, t)),
                        self.slot + (k - 1) * 3 + j,
                    )
            for src, dst in place(source, me, me):
                self.copies.append(net.local(src, dst))

        def wait(self):
            for k in range(1, 8):
                s = lax.rem(me + 8 - k, 8)
                for j, (_, dst) in enumerate(self.place(None, me, s)):
                    net.arrived(dst, sibling, self.slot + (k - 1) * 3 + j)
            for copy in self.copies:
                copy.wait()

    eighth = rows // 8

    def place_exp(half):
        return lambda source, t, s: [(
            None if source is None else source.at[rows_at(t * eighth, eighth)],
            exp_out.at[rep, half, :, rows_at(s * units, units)],
        )]

    def place_proj(half):
        return lambda source, t, s: [
            (
                None if source is None
                else source.at[rows_at(t * eighth, eighth), pl.ds(j * head, head)],
                proj_out.at[rep, half, :, rows_at(j * width + s * head, head)],
            )
            for j in range(3)
        ]

    he_done = he.third()
    he_turns = [Turn(he_done[h], h, place_exp(h)) for h in range(2)]
    hp_done = hp.third()
    hp_turns = [Turn(hp_done[h], h, place_proj(h)) for h in range(2)]

    out.step_on(1)
    back.begin((3, 2, 1))

    for k in range(1, 8):
        net.arrived(vec_in.at[lax.rem(me + 8 - k, 8)], sibling, small + k - 1)
    vec_load.wait()
    total = vec_in[0, 0:8]
    for s in range(1, 8):
        total += vec_in[s, 0:8]
    vec_mix[0:8] = total
    for s in range(8):
        vec_mix[8 + 6 * s : 14 + 6 * s] = vec_in[s, 8:14]
    wide = net.slots(4)
    for k, peer in ((1, by_x), (2, by_y), (3, across)):
        net.send(lambda peer=peer: (vec_mix, vec_all.at[rep], peer), wide + k)
    vec_copy = net.local(vec_mix, vec_all.at[rep])

    for turn_of in he_turns:
        turn_of.wait()
    he_spread = Spread(exp_out, [exp_out.at[rep, h] for h in range(2)])
    for turn_of in hp_turns:
        turn_of.wait()
    hp_spread = Spread(proj_out, [proj_out.at[rep, h] for h in range(2)])
    for spread in low_spreads:
        spread.on()
    he_spread.on()
    back.step_on(3)
    hp_spread.on()
    back.step_on(2)
    for k, r in ((1, x_rep), (2, y_rep), (3, d_rep)):
        net.arrived(vec_all.at[r], sibling, wide + k)
    vec_copy.wait()
    vec_out[...] = (vec_all[0] + vec_all[1]) + (vec_all[2] + vec_all[3])
    back.step_on(1)
    osum_copy = net.local(out.block(z), osum_out)
    dsum_copy = net.local(back.block(z), dsum_out)
    for spread in low_spreads:
        spread.wait()
    he_spread.wait()
    hp_spread.wait()
    for copy in low_copies + [osum_copy, dsum_copy]:
        copy.wait()
    tokens.finish()
    cotangents.finish()
    net.left(net.sent + he.sent + hp.sent)
    assert net.sends <= SENDS and net.started <= SENDS and net.locals <= LOCALS, (
        net.sends, net.started, net.locals)


SENDS = 320
LOCALS = 80


def block_passes(tokens, vectors, upstream, expander, projector, combiner, contractor, ebias, angles):
    count, width = tokens.shape
    n = lax.axis_size("shard")
    units, mix, head = expander.shape[1] // n, projector.shape[1] // n, combiner.shape[0]
    low, rows, two = head + units, width // n, 2 * count
    eighth = rows // 8
    vmem, dma = pltpu.VMEM, pltpu.SemaphoreType.DMA
    anywhere = pl.BlockSpec(memory_space=pl.ANY)
    block = (n // 2, count, width)
    results = [
        (4, 2, head // 8, width), (4, 2, units // 8, width),
        (4, 2, eighth, n * units), (4, 2, eighth, n * mix),
        (count, width), (count, width),
    ]
    passing = [
        (n * count, width), (n * count, width), block, block, block, block,
        (6, count, width), (6, count, width),
        (6, low // 8, width), (6, n * eighth, units), (6, n * eighth, mix),
        (2 * two, width), (two, mix), (two, units),
    ]
    result = pl.pallas_call(
        block_kernel,
        out_shape=[jax.ShapeDtypeStruct(s, bf16) for s in results] + [
            jax.ShapeDtypeStruct((72, LANES), f32), jax.ShapeDtypeStruct((8, width), f32),
        ] + [jax.ShapeDtypeStruct(s, bf16) for s in passing] + [
            jax.ShapeDtypeStruct((two, LANES), f32)
        ],
        in_specs=[anywhere] * 7 + [pl.BlockSpec(memory_space=vmem)] * 2,
        out_specs=[anywhere] * 6 + [pl.BlockSpec(memory_space=vmem)] * 2
        + [anywhere] * (len(passing) + 1),
        scratch_shapes=[
            vmem((width, units), bf16), vmem((width, mix), bf16), vmem((head, width), bf16),
            vmem((units, width), bf16), vmem((low, width), f32), vmem((width, units), f32),
            vmem((width, mix), f32),
            vmem((two, width), bf16), vmem((two, width), bf16), vmem((2 * two, width), bf16),
            vmem((2 * two, width), bf16), vmem((two, low), bf16),
            vmem((two, units), bf16), vmem((two, mix), bf16), vmem((two, units), bf16),
            vmem((two, mix), bf16), vmem((low // 8, width), bf16), vmem((two, LANES), f32),
            vmem((n,) + vectors.shape, bf16), vmem((3 * n, 1, vectors.shape[1]), f32),
            vmem((n, 1, LANES), f32),
            vmem((1, mix), f32), vmem((4, width), f32), vmem((1, units), f32),
            vmem((1, mix), f32), vmem((1, width), f32),
            vmem((n, 16, LANES), f32), vmem((n, 16, LANES), f32), vmem((72, LANES), f32),
            vmem((4, 72, LANES), f32),
            dma((SENDS,)), dma((SENDS,)), dma((LOCALS,)), dma((4,)), dma((6,)), dma((2,)), dma((8,)),
        ] + [dma((8,))] * 8,
        compiler_params=pltpu.CompilerParams(
            collective_id=0, has_side_effects=True, vmem_limit_bytes=VMEM_LIMIT
        ),
    )(tokens, vectors, upstream, expander, projector, combiner, contractor, ebias, angles)
    comb_sum, cont_sum, exp_sum, proj_sum, osum, dsum, vec, norms = result[:8]
    return (
        comb_sum.reshape(head, width), cont_sum.reshape(units, width), exp_sum.reshape(rows, n * units),
        proj_sum.reshape(rows, n * mix), osum, dsum, vec, norms,
    )


def sharded_heads(
    tokens, document_ends, projector, projbias, combiner, combbias, expander, expbias,
    contractor, contbias, attendgain, attendshift, feedgain, feedshift, cotangent,
):
    count, width = tokens.shape
    n = lax.axis_size("shard")
    me = lax.axis_index("shard")
    head = width // H
    mix = 3 * head
    rows = width // n
    units = expbias.shape[0]
    wide = projbias.shape[0]

    vectors = jnp.concatenate(
        [attendgain, attendshift, feedgain, feedshift, combbias, contbias, projbias,
         document_ends[0].astype(bf16)]
    )
    vectors = jnp.pad(vectors, (0, 16 * rows - vectors.shape[0])).reshape(16, rows)
    _, _, live = layout(document_ends[0], count)
    upstream = jnp.where(live[:, None], cotangent, jnp.zeros_like(cotangent))
    half = ROT // 2
    freqs = jnp.exp(-jnp.arange(half, dtype=f32) * (2.0 / ROT) * math.log(10000.0))
    still = jnp.zeros((LANES - ROT,), f32)
    ones = jnp.ones((half,), f32)
    angles = jnp.stack(
        [jnp.concatenate([freqs, freqs, still]), jnp.concatenate([-ones, ones, still])]
    )
    comb_out, cont_out, exp_out, proj_out, osum, dsum, vec, norms = block_passes(
        tokens, vectors, upstream, expander, projector, combiner, contractor,
        expbias.astype(f32)[None], angles,
    )

    floated = tokens.astype(f32)
    block_output = floated + jnp.where(
        live[:, None], osum.astype(f32) + (norms[4] + norms[5]), 0.0
    )
    block_output = block_output.astype(bf16)
    d_normed = dsum.astype(f32)
    normed, inverse = normalize(floated)
    grad = cotangent.astype(f32) + inverse * (
        d_normed
        - jnp.mean(d_normed, axis=1, keepdims=True)
        - normed * jnp.mean(d_normed * normed, axis=1, keepdims=True)
    )
    input_gradient = grad.astype(bf16)

    vec = vec.reshape(-1)
    norm_sums = vec[: 4 * rows].reshape(4, rows)
    mixed_bias = vec[4 * rows : 4 * rows + n * mix].reshape(n, 3, head).transpose(1, 0, 2)
    mixed_bias = lax.dynamic_slice(mixed_bias.reshape(-1), (me * wide,), (wide,))
    rest = vec[4 * rows + n * mix :]
    hidden_bias, out_bias = rest[:units], rest[units : units + rows]
    return (
        block_output, input_gradient, proj_out.astype(f32), mixed_bias, comb_out.astype(f32), out_bias,
        exp_out.astype(f32), hidden_bias, cont_out.astype(f32), out_bias,
        norm_sums[0], norm_sums[1], norm_sums[2], norm_sums[3],
    )


def solution(mesh):
    placed = (
        P(("rep", "shard"), None),
        P(("rep", "shard"), None),
        P("shard", None),
        P("shard"),
        P("shard", None),
        P("shard"),
        P("shard", None),
        P("shard"),
        P("shard", None),
        P("shard"),
        P("shard"),
        P("shard"),
        P("shard"),
        P("shard"),
        P(("rep", "shard"), None),
    )
    return jax.shard_map(
        sharded_heads if dict(mesh.shape) == {"rep": 4, "shard": H} else local,
        mesh=mesh,
        in_specs=placed,
        out_specs=(
            P(("rep", "shard"), None),
            P(("rep", "shard"), None),
            P("shard", None),
            P("shard"),
            P("shard", None),
            P("shard"),
            P("shard", None),
            P("shard"),
            P("shard", None),
            P("shard"),
            P("shard"),
            P("shard"),
            P("shard"),
            P("shard"),
        ),
        check_vma=False,
    )
```

```python
from functools import partial
import math

import jax
import jax.numpy as jnp
import numpy as np
from jax import lax
from jax.experimental import pallas as pl
from jax.experimental.pallas import tpu as pltpu
from jax.sharding import PartitionSpec as P

H = 8
ROT = 64
DOCS = 4
LANES = 128
VMEM_LIMIT = 62 * 1024 * 1024

epsilon = 1e-05
masked_value = -1e30
f32 = jnp.float32
bf16 = jnp.bfloat16


def normalize(values):
    centre = jnp.mean(values, axis=1, keepdims=True)
    centred = values - centre
    spread = jnp.mean(centred * centred, axis=1, keepdims=True)
    inverse = lax.rsqrt(spread + epsilon)
    return (centred * inverse, inverse)


def layout(ends, count):
    index = jnp.arange(count, dtype=jnp.int32)
    passed = index[:, None] >= ends[None, :]
    document = jnp.sum(passed.astype(jnp.int32), axis=1)
    begin = jnp.max(jnp.where(passed, ends[None, :], 0), axis=1)
    position = (index - begin).astype(f32)
    allowed = (document[:, None] == document[None, :]) & (index[None, :] <= index[:, None])
    return (position, allowed, index < ends[-1])


def rotary_tables(position, rotary):
    half = rotary // 2
    freqs = jnp.exp(-jnp.arange(half, dtype=f32) * (2.0 / rotary) * math.log(10000.0))
    angles = position[..., None] * freqs
    angles = jnp.concatenate([angles, angles], axis=-1)
    return (jnp.cos(angles), jnp.sin(angles))


def rotate(values, cosine, sine, rotary):
    half = rotary // 2
    front = values[..., :rotary]
    turned = jnp.concatenate([-front[..., half:], front[..., :half]], axis=-1)
    return jnp.concatenate([front * cosine + turned * sine, values[..., rotary:]], axis=-1)


def unrotate(grads, cosine, sine, rotary):
    half = rotary // 2
    front = grads[..., :rotary]
    scaled = front * sine
    backward = jnp.concatenate([scaled[..., half:], -scaled[..., :half]], axis=-1)
    return jnp.concatenate([front * cosine + backward, grads[..., rotary:]], axis=-1)


def right_trans(left, right):
    return lax.dot_general(left, right, (((1,), (1,)), ((), ())), preferred_element_type=f32)


def left_trans(left, right):
    return lax.dot_general(left, right, (((0,), (0,)), ((), ())), preferred_element_type=f32)


def masked_scores(query_low, keys_low, allowed, factor):
    scores = (
        jnp.einsum("qhd,khd->hqk", query_low, keys_low, preferred_element_type=jnp.float32) * factor
    )
    return jnp.where(allowed[None], scores, masked_value)


def weight_sums(left, right):
    piece = lax.slice_in_dim(
        left, 0, left.shape[1] // lax.axis_size("shard") * lax.axis_size("shard"), axis=1
    )
    return lax.psum_scatter(
        left_trans(piece, right).astype(jnp.bfloat16), "shard", scatter_dimension=0, tiled=True
    ).astype(jnp.float32)


def local(
    tokens,
    document_ends,
    projector,
    projbias,
    combiner,
    combbias,
    expander,
    expbias,
    contractor,
    contbias,
    attendgain,
    attendshift,
    feedgain,
    feedshift,
    cotangent,
):
    count, width = tokens.shape
    headsize = width // H
    factor = 1.0 / math.sqrt(headsize)
    position, allowed, live = layout(document_ends[0], count)
    cosine, sine = rotary_tables(position, ROT)
    cosine, sine = cosine[:, None, :], sine[:, None, :]
    (
        full_projector,
        full_combiner,
        full_projbias,
        full_combbias,
        gain_attend,
        shift_attend,
        gain_feed,
        shift_feed,
    ) = (
        lax.all_gather(projector, "shard", axis=0, tiled=True),
        lax.all_gather(combiner, "shard", axis=0, tiled=True),
        lax.all_gather(projbias, "shard", axis=0, tiled=True),
        lax.all_gather(combbias, "shard", axis=0, tiled=True),
        lax.all_gather(attendgain, "shard", axis=0, tiled=True),
        lax.all_gather(attendshift, "shard", axis=0, tiled=True),
        lax.all_gather(feedgain, "shard", axis=0, tiled=True),
        lax.all_gather(feedshift, "shard", axis=0, tiled=True),
    )
    floated = tokens.astype(jnp.float32)
    normed, inverse = normalize(floated)
    first_input = (normed * gain_attend + shift_attend).astype(jnp.bfloat16)
    second_input = (normed * gain_feed + shift_feed).astype(jnp.bfloat16)
    mixed = jnp.dot(first_input, full_projector, preferred_element_type=jnp.float32) + full_projbias
    query_low = rotate(mixed[:, :width].reshape(count, H, headsize), cosine, sine, ROT).astype(
        jnp.bfloat16
    )
    keys_low = rotate(
        mixed[:, width : 2 * width].reshape(count, H, headsize), cosine, sine, ROT
    ).astype(jnp.bfloat16)
    values_low = mixed[:, 2 * width :].reshape(count, H, headsize).astype(jnp.bfloat16)
    scores = masked_scores(query_low, keys_low, allowed, factor)
    peak = jnp.max(scores, axis=2, keepdims=True)
    raised = jnp.exp(scores - peak)
    total = jnp.sum(raised, axis=2, keepdims=True)
    probs_low = (raised / total).astype(jnp.bfloat16)
    logsum = peak + jnp.log(total)
    context = jnp.einsum("hqk,khd->qhd", probs_low, values_low, preferred_element_type=jnp.float32)
    context = context.reshape(count, width).astype(jnp.bfloat16)
    attended = jnp.dot(context, full_combiner, preferred_element_type=jnp.float32) + full_combbias
    full_expander, full_contractor, full_expbias, full_contbias = (
        lax.all_gather(expander, "shard", axis=0, tiled=True),
        lax.all_gather(contractor, "shard", axis=0, tiled=True),
        lax.all_gather(expbias, "shard", axis=0, tiled=True),
        lax.all_gather(contbias, "shard", axis=0, tiled=True),
    )
    hidden = jnp.dot(second_input, full_expander, preferred_element_type=jnp.float32) + full_expbias
    activated, gelu_back = jax.vjp(partial(jax.nn.gelu, approximate=False), hidden)
    active_low = activated.astype(jnp.bfloat16)
    feedout = (
        jnp.dot(active_low, full_contractor, preferred_element_type=jnp.float32) + full_contbias
    )
    block_output = (floated + jnp.where(live[:, None], attended + feedout, 0.0)).astype(
        jnp.bfloat16
    )
    (
        back_projector,
        back_combiner,
        back_expander,
        back_contractor,
        back_gain_attend,
        back_gain_feed,
    ) = (
        lax.all_gather(projector, "shard", axis=0, tiled=True),
        lax.all_gather(combiner, "shard", axis=0, tiled=True),
        lax.all_gather(expander, "shard", axis=0, tiled=True),
        lax.all_gather(contractor, "shard", axis=0, tiled=True),
        lax.all_gather(attendgain, "shard", axis=0, tiled=True),
        lax.all_gather(feedgain, "shard", axis=0, tiled=True),
    )
    upstream = jnp.where(live[:, None], cotangent, jnp.zeros_like(cotangent))
    contractor_part = weight_sums(active_low, upstream)
    combiner_part = weight_sums(context, upstream)
    output_bias = jnp.sum(upstream, axis=0, dtype=jnp.float32)
    d_active = right_trans(upstream, back_contractor)
    d_hidden = gelu_back(d_active)[0].astype(jnp.bfloat16)
    expander_part = weight_sums(second_input, d_hidden)
    hidden_bias = jnp.sum(d_hidden, axis=0, dtype=jnp.float32)
    d_second = right_trans(d_hidden, back_expander)
    d_context = (
        right_trans(upstream, back_combiner).reshape(count, H, headsize).astype(jnp.bfloat16)
    )
    scores_again = masked_scores(query_low, keys_low, allowed, factor)
    probs = jnp.exp(scores_again - logsum)
    d_probs = jnp.einsum("qhd,khd->hqk", d_context, values_low, preferred_element_type=jnp.float32)
    d_values = jnp.einsum("hqk,qhd->khd", probs_low, d_context, preferred_element_type=jnp.float32)
    d_scores = (probs * (d_probs - jnp.sum(d_probs * probs, axis=2, keepdims=True))).astype(
        jnp.bfloat16
    )
    d_query = (
        jnp.einsum("hqk,khd->qhd", d_scores, keys_low, preferred_element_type=jnp.float32) * factor
    )
    d_keys = (
        jnp.einsum("hqk,qhd->khd", d_scores, query_low, preferred_element_type=jnp.float32) * factor
    )
    d_mixed = jnp.concatenate(
        [
            unrotate(d_query, cosine, sine, ROT).reshape(count, width),
            unrotate(d_keys, cosine, sine, ROT).reshape(count, width),
            d_values.reshape(count, width),
        ],
        axis=1,
    ).astype(jnp.bfloat16)
    projector_part = weight_sums(first_input, d_mixed)
    mixed_bias = jnp.sum(d_mixed, axis=0, dtype=jnp.float32)
    d_first = right_trans(d_mixed, back_projector)
    attend_scale = jnp.sum(d_first * normed, axis=0)
    attend_offset = jnp.sum(d_first, axis=0)
    feed_scale = jnp.sum(d_second * normed, axis=0)
    feed_offset = jnp.sum(d_second, axis=0)
    d_normed = d_first * back_gain_attend + d_second * back_gain_feed
    grad_float = cotangent.astype(jnp.float32) + inverse * (
        d_normed
        - jnp.mean(d_normed, axis=1, keepdims=True)
        - normed * jnp.mean(d_normed * normed, axis=1, keepdims=True)
    )
    input_gradient = grad_float.astype(jnp.bfloat16)
    mixed_bias, output_bias, hidden_bias, attend_scale, attend_offset, feed_scale, feed_offset = (
        lax.psum_scatter(
            mixed_bias.astype(jnp.bfloat16), "shard", scatter_dimension=0, tiled=True
        ).astype(jnp.float32),
        lax.psum_scatter(
            output_bias.astype(jnp.bfloat16), "shard", scatter_dimension=0, tiled=True
        ).astype(jnp.float32),
        lax.psum_scatter(
            hidden_bias.astype(jnp.bfloat16), "shard", scatter_dimension=0, tiled=True
        ).astype(jnp.float32),
        lax.psum_scatter(
            attend_scale.astype(jnp.bfloat16), "shard", scatter_dimension=0, tiled=True
        ).astype(jnp.float32),
        lax.psum_scatter(
            attend_offset.astype(jnp.bfloat16), "shard", scatter_dimension=0, tiled=True
        ).astype(jnp.float32),
        lax.psum_scatter(
            feed_scale.astype(jnp.bfloat16), "shard", scatter_dimension=0, tiled=True
        ).astype(jnp.float32),
        lax.psum_scatter(
            feed_offset.astype(jnp.bfloat16), "shard", scatter_dimension=0, tiled=True
        ).astype(jnp.float32),
    )
    (
        projector_part,
        mixed_bias,
        combiner_part,
        output_bias,
        expander_part,
        hidden_bias,
        contractor_part,
        attend_scale,
        attend_offset,
        feed_scale,
        feed_offset,
    ) = (
        lax.psum(projector_part.astype(jnp.bfloat16), "rep").astype(jnp.float32),
        lax.psum(mixed_bias.astype(jnp.bfloat16), "rep").astype(jnp.float32),
        lax.psum(combiner_part.astype(jnp.bfloat16), "rep").astype(jnp.float32),
        lax.psum(output_bias.astype(jnp.bfloat16), "rep").astype(jnp.float32),
        lax.psum(expander_part.astype(jnp.bfloat16), "rep").astype(jnp.float32),
        lax.psum(hidden_bias.astype(jnp.bfloat16), "rep").astype(jnp.float32),
        lax.psum(contractor_part.astype(jnp.bfloat16), "rep").astype(jnp.float32),
        lax.psum(attend_scale.astype(jnp.bfloat16), "rep").astype(jnp.float32),
        lax.psum(attend_offset.astype(jnp.bfloat16), "rep").astype(jnp.float32),
        lax.psum(feed_scale.astype(jnp.bfloat16), "rep").astype(jnp.float32),
        lax.psum(feed_offset.astype(jnp.bfloat16), "rep").astype(jnp.float32),
    )
    return (
        block_output,
        input_gradient,
        projector_part,
        mixed_bias,
        combiner_part,
        output_bias,
        expander_part,
        hidden_bias,
        contractor_part,
        output_bias,
        attend_scale,
        attend_offset,
        feed_scale,
        feed_offset,
    )


def lane_half(shape):
    return lax.broadcasted_iota(jnp.int32, shape, 1) < ROT // 2


def turn(front, signed):
    moved = jnp.where(
        lane_half(front.shape),
        pltpu.roll(front, LANES - ROT // 2, 1),
        pltpu.roll(front, ROT // 2, 1),
    )
    return moved * signed


def rotated(values, cosine, signed):
    front = values[:, :LANES]
    return jnp.concatenate([front * cosine + turn(front, signed), values[:, LANES:]], axis=1)


def unrotated(grads, cosine, signed):
    front = grads[:, :LANES]
    return jnp.concatenate([front * cosine - turn(front, signed), grads[:, LANES:]], axis=1)


def block_layout(ends, count):
    row = lax.broadcasted_iota(jnp.int32, (count, 1), 0).astype(f32)
    column = lax.broadcasted_iota(jnp.int32, (1, count), 1).astype(f32)
    row_doc = jnp.zeros((count, 1), f32)
    column_doc = jnp.zeros((1, count), f32)
    begin = jnp.zeros((count, 1), f32)
    for i in range(DOCS):
        end = ends[:, i : i + 1]
        row_doc += jnp.where(row >= end, 1.0, 0.0)
        column_doc += jnp.where(column >= end, 1.0, 0.0)
        begin = jnp.maximum(begin, jnp.where(row >= end, end, 0.0))
    return (row_doc == column_doc) & (column <= row), row - begin


def dot(left, right):
    return jnp.dot(left, right, preferred_element_type=f32)


def softmax(q, k, allowed):
    scores = right_trans(q, k) * (1.0 / math.sqrt(q.shape[1]))
    scores = jnp.where(allowed, scores, masked_value)
    raised = jnp.exp(scores - jnp.max(scores, axis=1, keepdims=True))
    return raised / jnp.sum(raised, axis=1, keepdims=True)


def norm_parts(x_ref, at):
    x = x_ref[at, :].astype(f32)
    centre = jnp.mean(x, axis=1, keepdims=True)
    centred = x - centre
    inverse = lax.rsqrt(jnp.mean(centred * centred, axis=1, keepdims=True) + epsilon)
    return centred, centre, inverse


def tables(ends, count, angles_ref):
    allowed, place = block_layout(ends, count)
    angles = place * angles_ref[0:1, :]
    return allowed, jnp.cos(angles), jnp.sin(angles) * angles_ref[1:2, :]


def forward_pass(
    x_ref, ends, count, angles_ref, norms_ref, pbias_ref, ebias_ref, proj_ref, exp_ref, comb_ref,
    cont_ref, h1_ref, h2_ref, qkv_ref, ca_ref, slope_ref, stats_ref, part_ref,
):
    slots, width = x_ref.shape
    head = comb_ref.shape[0]
    units = exp_ref.shape[1]
    step = min(64, count)

    @pl.loop(0, slots // step)
    def _(i):
        at = rows_at(i * step, step)
        centred, centre, inverse = norm_parts(x_ref, at)
        normed = centred * inverse
        h1_ref[at, :] = (normed * norms_ref[0:1, :] + norms_ref[1:2, :]).astype(bf16)
        h2_ref[at, :] = (normed * norms_ref[2:3, :] + norms_ref[3:4, :]).astype(bf16)
        stats_ref[at, 0:1] = centre
        stats_ref[at, 1:2] = inverse

    for j in range(3):
        cut = slice(j * head, j * head + head)
        mixed = dot(h1_ref[...], proj_ref[:, cut]) + pbias_ref[:, cut]
        for b in range(slots // count):
            at = slice(b * count, b * count + count)
            value = mixed[at]
            if j < 2:
                _, cosine, signed = tables(ends[b], count, angles_ref)
                value = rotated(value, cosine, signed)
            qkv_ref[at, cut] = value.astype(bf16)
    tile = min(256, units)
    for start in range(0, units, tile):
        hidden = dot(h2_ref[...], exp_ref[:, start : start + tile])
        hidden += ebias_ref[:, start : start + tile]
        below = 0.5 + 0.5 * lax.erf(hidden * math.sqrt(0.5))
        ca_ref[:, head + start : head + start + tile] = (hidden * below).astype(bf16)
        density = jnp.exp(hidden * hidden * -0.5) * (1.0 / math.sqrt(2.0 * math.pi))
        slope_ref[:, start : start + tile] = (below + hidden * density).astype(bf16)
    for b in range(slots // count):
        at = slice(b * count, b * count + count)
        allowed, _ = block_layout(ends[b], count)
        probs = softmax(qkv_ref[at, :head], qkv_ref[at, head : 2 * head], allowed).astype(bf16)
        ca_ref[at, :head] = dot(probs, qkv_ref[at, 2 * head :]).astype(bf16)
    tile = min(512, width)
    for start in range(0, width, tile):
        cut = slice(start, start + tile)
        part = dot(ca_ref[:, :head], comb_ref[:, cut]) + dot(ca_ref[:, head:], cont_ref[:, cut])
        part_ref[:, cut] = part.astype(bf16)


def backward_pass(
    x_ref, up_ref, ends, count, angles_ref, norms_ref, qkv_ref, slope_ref, stats_ref, proj_ref,
    exp_ref, comb_ref, cont_ref, dh_ref, dm_ref, dn_ref, sums_ref, hbias_ref, mbias_ref, obias_ref,
):
    slots, width = x_ref.shape
    head = comb_ref.shape[0]
    units = exp_ref.shape[1]
    tile = min(256, units)
    d_context = right_trans(up_ref[...], comb_ref[...]).astype(bf16)
    for start in range(0, units, tile):
        cut = slice(start, start + tile)
        d_active = right_trans(up_ref[...], cont_ref[cut, :])
        d_hidden = (d_active * slope_ref[:, cut].astype(f32)).astype(bf16)
        dh_ref[:, cut] = d_hidden
        hbias_ref[:, cut] += jnp.sum(d_hidden.astype(f32), axis=0, keepdims=True)
    factor = 1.0 / math.sqrt(head)
    for b in range(slots // count):
        at = slice(b * count, b * count + count)
        allowed, cosine, signed = tables(ends[b], count, angles_ref)
        q, k = qkv_ref[at, :head], qkv_ref[at, head : 2 * head]
        v = qkv_ref[at, 2 * head :]
        d_ctx = d_context[at]
        probs = softmax(q, k, allowed)
        d_probs = right_trans(d_ctx, v)
        d_v = left_trans(probs.astype(bf16), d_ctx)
        d_s = probs * (d_probs - jnp.sum(d_probs * probs, axis=1, keepdims=True))
        d_s = d_s.astype(bf16)
        dm_ref[at, :head] = unrotated(dot(d_s, k) * factor, cosine, signed).astype(bf16)
        d_k = unrotated(left_trans(d_s, q) * factor, cosine, signed).astype(bf16)
        dm_ref[at, head : 2 * head] = d_k
        dm_ref[at, 2 * head :] = d_v.astype(bf16)
    mbias_ref[...] += jnp.sum(dm_ref[...].astype(f32), axis=0, keepdims=True)
    obias_ref[...] += jnp.sum(up_ref[...].astype(f32), axis=0, keepdims=True)
    centre, inverse = stats_ref[:, 0:1], stats_ref[:, 1:2]
    tile = min(256, width)

    @pl.loop(0, width // tile, unroll=2)
    def _(i):
        cut = rows_at(i * tile, tile)
        normed = (x_ref[:, cut].astype(f32) - centre) * inverse
        d_first = right_trans(dm_ref[...], proj_ref[cut, :])
        d_second = right_trans(dh_ref[...], exp_ref[cut, :])
        dn_ref[:, cut] = (
            d_first * norms_ref[0:1, cut] + d_second * norms_ref[2:3, cut]
        ).astype(bf16)
        sums_ref[0:1, cut] += jnp.sum(d_first * normed, axis=0, keepdims=True)
        sums_ref[1:2, cut] += jnp.sum(d_first, axis=0, keepdims=True)
        sums_ref[2:3, cut] += jnp.sum(d_second * normed, axis=0, keepdims=True)
        sums_ref[3:4, cut] += jnp.sum(d_second, axis=0, keepdims=True)


def accumulate(total, left, right, tall):
    wide = min(256, right.shape[1])

    @pl.loop(0, left.shape[1] // tall)
    def _(i):
        at = pl.ds(pl.multiple_of(i * tall, LANES), tall)
        for start in range(0, right.shape[1], wide):
            cut = slice(start, start + wide)
            total[at, cut] += left_trans(left[:, at], right[:, cut])


MESH = pl.DeviceIdType.MESH


def position_of():
    rep, me = lax.axis_index("rep"), lax.axis_index("shard")
    return rep, me, lax.div(rep, 2), lax.rem(rep, 2), lax.div(me, 2), lax.rem(me, 2)


def meet(peers):
    barrier = pltpu.get_barrier_semaphore()
    for peer in peers:
        pl.semaphore_signal(barrier, inc=1, device_id=peer, device_id_type=MESH)
    pl.semaphore_wait(barrier, len(peers))


def rows_at(start, size):
    return pl.ds(pl.multiple_of(start, size), size)


class Net:
    def __init__(self, send_sem, recv_sem, local_sem):
        self.send_sem, self.recv_sem, self.local_sem = send_sem, recv_sem, local_sem
        self.sends, self.locals, self.started, self.sent = 0, 0, 0, []

    def slots(self, count):
        first = self.started
        self.started += count
        return first

    def send(self, ends, slot, when=None):
        index = self.sends
        self.sends += 1

        def copy():
            src, dst, peer = ends()
            return pltpu.make_async_remote_copy(
                src_ref=src, dst_ref=dst, send_sem=self.send_sem.at[index],
                recv_sem=self.recv_sem.at[slot], device_id=peer, device_id_type=MESH,
            )

        if when is None:
            copy().start()
        else:
            pl.when(when)(lambda: copy().start())
        self.sent.append((copy, when))

    def arrived(self, dst, peer, slot):
        pltpu.make_async_remote_copy(
            src_ref=dst, dst_ref=dst, send_sem=self.send_sem.at[0],
            recv_sem=self.recv_sem.at[slot], device_id=peer, device_id_type=MESH,
        ).wait_recv()

    def local(self, src, dst):
        copy = pltpu.make_async_copy(src, dst, self.local_sem.at[self.locals])
        self.locals += 1
        copy.start()
        return copy

    def left(self, sent):
        for copy, when in sent:
            if when is None:
                copy().wait_send()
            else:
                pl.when(when)(lambda copy=copy: copy().wait_send())


class Chain:
    def __init__(self, source, out, count, where, sems):
        self.source, self.out, self.count = source, out, count
        self.rep, self.me, self.z, self.c = where
        self.side_send, self.side_recv, self.core_send, self.core_recv = sems
        self.sibling = self.me + 1 - 2 * self.c

    def block(self, shard):
        return self.out.at[rows_at(shard * self.count, self.count)]

    def side(self, side, step):
        block = self.block(self.me - side * 2 * step)
        peer = (self.rep, self.me + side * 2)
        index = (0 if side > 0 else 4) + step
        return pltpu.make_async_remote_copy(
            src_ref=block, dst_ref=block, send_sem=self.side_send.at[index],
            recv_sem=self.side_recv.at[index], device_id=peer, device_id_type=MESH,
        )

    def cross(self, side, step):
        block = self.block(self.me - side * 2 * step)
        index = (0 if side > 0 else 4) + step
        return pltpu.make_async_remote_copy(
            src_ref=block, dst_ref=block, send_sem=self.core_send.at[index],
            recv_sem=self.core_recv.at[index], device_id=(self.rep, self.sibling),
            device_id_type=MESH,
        )

    def taken(self, side, step):
        block = self.block(self.sibling - side * 2 * step)
        index = (0 if side > 0 else 4) + step
        return pltpu.make_async_remote_copy(
            src_ref=block, dst_ref=block, send_sem=self.core_send.at[index],
            recv_sem=self.core_recv.at[index], device_id=(self.rep, self.sibling),
            device_id_type=MESH,
        )

    def here(self, side, step):
        return self.z >= step if side > 0 else self.z + step <= 3

    def on(self, side):
        return self.z < 3 if side > 0 else self.z > 0

    def first(self, side):
        mine = self.block(self.me)
        index = 0 if side > 0 else 4
        return pltpu.make_async_remote_copy(
            src_ref=self.source, dst_ref=mine, send_sem=self.side_send.at[index],
            recv_sem=self.side_recv.at[index], device_id=(self.rep, self.me + side * 2),
            device_id_type=MESH,
        )

    def first_cross(self):
        mine = self.block(self.me)
        return pltpu.make_async_remote_copy(
            src_ref=self.source, dst_ref=mine, send_sem=self.core_send.at[0],
            recv_sem=self.core_recv.at[0], device_id=(self.rep, self.sibling),
            device_id_type=MESH,
        )

    def begin(self):
        for side in (1, -1):
            pl.when(self.on(side))(lambda: self.first(side).start())
        self.first_cross().start()
    def wait_own(self):
        self.taken(1, 0).wait_recv()

    def step(self, step):
        for side in (1, -1):
            here = self.here(side, step)

            @pl.when(here)
            def _():
                block = self.block(self.me - side * 2 * step)
                index = (0 if side > 0 else 4) + step - 1
                pltpu.make_async_remote_copy(
                    src_ref=block, dst_ref=block, send_sem=self.side_send.at[index],
                    recv_sem=self.side_recv.at[index], device_id=(self.rep, self.sibling),
                    device_id_type=MESH,
                ).wait_recv()
                self.cross(side, step).start()

            pl.when(here & self.on(side) & (step < 3))(lambda: self.side(side, step).start())

    def take(self, step):
        for side in (1, -1):
            pl.when(self.here(side, step))(lambda: self.taken(side, step).wait_recv())

    def finish(self):
        self.first_cross().wait_send()
        for side in (1, -1):
            pl.when(self.on(side))(lambda: self.first(side).wait_send())
            for step in (1, 2, 3):
                here = self.here(side, step)
                pl.when(here)(lambda: self.cross(side, step).wait_send())
                if step < 3:
                    pl.when(here & self.on(side))(lambda: self.side(side, step).wait_send())


def add_into(target, other):
    rows = target.shape[-2]
    step = min(32, rows)

    @pl.loop(0, rows // step)
    def _(i):
        at = (Ellipsis, pl.ds(pl.multiple_of(i * step, step), step), slice(None))
        lead = (slice(None),) * (len(target.shape) - 2)
        at = lead + at[1:]
        target[at] = (target[at].astype(f32) + other[at].astype(f32)).astype(target.dtype)


def block_kernel(
    tok_ref, vec_ref, up_ref, expander_ref, projector_ref, comb_hbm, cont_hbm, ebias_ref,
    angles_ref,
    comb_out, cont_out, exp_out, proj_out, osum_out, dsum_out, vec_out, norms_ref,
    x_out, up_out, part_own, dn_own, o_in, d_in, o_land, d_land, low_land, he_land, hp_land,
    h_save, qkv_save, slope_save, stats_save,
    exp_ref, proj_ref, comb_ref, cont_ref, low_sum, he_sum, hp_sum,
    xs, us, hs, pd, ca, slope, qkv, dh, dm, spare, stats,
    vecs, bias_all, ends_all, pbias, sums, hbias, mbias, obias,
    vec_msg, vec_in, vec_mix, vec_all,
    send_sem, recv_sem, local_sem, load_sem, store_sem, cross_send, cross_recv,
    xs_send, xs_recv, xc_send, xc_recv, us_send, us_recv, uc_send, uc_recv,
):
    rep, me, y, x, z, c = position_of()
    count, width = tok_ref.shape
    rows, quarter = expander_ref.shape[0], expander_ref.shape[0] // 4
    units, mix = exp_ref.shape[1], proj_ref.shape[1]
    head = mix // 3
    sibling = (rep, me + 1 - 2 * c)
    x_rep, y_rep, d_rep = rep + 1 - 2 * x, rep + 2 - 4 * y, 3 - rep
    by_x, by_y, across = (x_rep, me), (y_rep, me), (d_rep, me)
    ring = [(rep, lax.rem(me + k, 8)) for k in range(1, 8)]
    meet(ring + [by_x, by_y, across])
    slots = hs.shape[0] // 2
    h1s, h2s = hs.at[pl.ds(0, slots)], hs.at[pl.ds(slots, slots)]
    parts, dns = pd.at[pl.ds(0, slots)], pd.at[pl.ds(slots, slots)]
    net = Net(send_sem, recv_sem, local_sem)

    def weight_copies(go, first, size, source_rows, t):
        source = rows_at(source_rows, size)
        target = rows_at(first, size)
        go(expander_ref.at[source, rows_at(t * units, units)], exp_ref.at[target, :])
        for j in range(3):
            go(
                projector_ref.at[source, rows_at(j * width + t * head, head)],
                proj_ref.at[target, pl.ds(j * head, head)],
            )

    remote = net.slots(32)
    chips = []
    for i in range(3):
        down, up = 3 - i, i
        chips.append(jnp.where(
            z < 2, jnp.where(up >= z, up + 1, up), jnp.where(down <= z, down - 1, down)
        ))
    for chip in chips:
        for core in (0, 1):
            part = [0]

            def go(src, dst):
                net.send(
                    lambda: (src, dst, (rep, chip * 2 + core)), remote + me * 4 + part[0]
                )
                part[0] += 1

            weight_copies(go, me * rows + rep * quarter, quarter, rep * quarter, chip * 2 + core)
    small = net.slots(7)
    for k, peer in enumerate(ring):
        net.send(lambda peer=peer: (vec_ref, vecs.at[me], peer), small + k)
    where = (rep, me, z, c)
    tokens = Chain(
        tok_ref, x_out, count, where, (xs_send, xs_recv, xc_send, xc_recv)
    )
    cotangents = Chain(
        up_ref, up_out, count, where, (us_send, us_recv, uc_send, uc_recv)
    )
    tokens.begin()
    near = net.slots(4)
    part = [0]

    def go_near(src, dst):
        net.send(lambda: (src, dst, sibling), near + part[0])
        part[0] += 1

    weight_copies(go_near, me * rows, rows, 0, sibling[1])
    copies = []
    weight_copies(lambda s, d: copies.append(net.local(s, d)), me * rows, rows, 0, me)
    copies.append(net.local(vec_ref, vecs.at[me]))
    copies.append(net.local(comb_hbm, comb_ref))
    copies.append(net.local(cont_hbm, cont_ref))
    cotangents.begin()
    for ref in (low_sum, he_sum, hp_sum, sums, hbias, mbias, obias):
        if ref.shape[0] <= 8:
            ref[...] = jnp.zeros_like(ref)
        else:

            @pl.loop(0, ref.shape[0] // 64)
            def _(i):
                ref[rows_at(i * 64, 64), :] = jnp.zeros((64, ref.shape[1]), f32)

    def shard_rows(step, core):
        return (chips[step - 1] * 2 + core) * rows

    first_hop, second_hop = net.slots(12), net.slots(18)
    gone = []

    def pass_on(ref_at, peer, slot):
        for ref, more in ((exp_ref, 0), (proj_ref, 1)):
            net.send(lambda ref=ref: (ref.at[ref_at, :], ref.at[ref_at, :], peer), slot + more)

    def landed(step):
        for core in (0, 1):
            at = rows_at(shard_rows(step, core) + rep * quarter, quarter)
            slot = remote + (chips[step - 1] * 2 + core) * 4
            net.arrived(exp_ref.at[at, :], sibling, slot)
            for j in range(3):
                net.arrived(proj_ref.at[at, pl.ds(j * head, head)], sibling, slot + 1 + j)
            peer = by_x if core == 0 else by_y
            pass_on(at, peer, first_hop + ((step - 1) * 2 + core) * 2)

    def crossed(step):
        for core in (0, 1):
            base = shard_rows(step, core)
            hop = first_hop + ((step - 1) * 2 + core) * 2
            other = rows_at(base + (x_rep if core == 0 else y_rep) * quarter, quarter)
            net.arrived(exp_ref.at[other, :], sibling, hop)
            net.arrived(proj_ref.at[other, :], sibling, hop + 1)
            hop = second_hop + (step - 1) * 6
            if core == 0:
                pass_on(rows_at(base + y * 2 * quarter, 2 * quarter), by_y, hop)
                gone.append((rows_at(base + (1 - y) * 2 * quarter, 2 * quarter), hop))
            else:
                pass_on(rows_at(base + rep * quarter, quarter), by_x, hop + 2)
                pass_on(other, by_x, hop + 4)
                gone.append((rows_at(base + x_rep * quarter, quarter), hop + 2))
                gone.append((rows_at(base + d_rep * quarter, quarter), hop + 4))

    landed(1)
    landed(2)
    crossed(1)
    landed(3)
    crossed(2)
    crossed(3)
    tokens.step(1)
    opening, net.sent = net.sent, []

    for k in range(1, 8):
        net.arrived(vecs.at[lax.rem(me + 8 - k, 8)], sibling, small + k - 1)
    for copy in copies:
        copy.wait()
    for s in range(8):
        values = vecs[s].astype(f32)
        for j in range(3):
            bias_all[3 * s + j] = values[6 + j : 7 + j, :]
        ends_all[s] = values[9:10, :LANES]
        norms_ref[:, s * rows : s * rows + rows] = values[:8, :]
    for j in range(3):
        pbias[:, j * head : j * head + head] = bias_all[8 * j + me]

    at = rows_at(sibling[1] * rows, rows)
    net.arrived(exp_ref.at[at, :], sibling, near)
    for j in range(3):
        net.arrived(proj_ref.at[at, pl.ds(j * head, head)], sibling, near + 1 + j)
    for at, slot in gone:
        net.arrived(exp_ref.at[at, :], sibling, slot)
        net.arrived(proj_ref.at[at, :], sibling, slot + 1)
    tokens.wait_own()
    cotangents.wait_own()
    cotangents.step(1)

    def chip_of(slot):
        second = jnp.where(z == 0, 2, jnp.where(z == 1, 0, 1))
        last = jnp.where(z < 2, 3, 0)
        after = jnp.where(z < 3, z + 1, 2)
        return jnp.where(
            slot == 0, z, jnp.where(slot == 1, after, jnp.where(slot == 2, second, last))
        )

    class Loads:
        def __init__(self, own, source, into, first):
            self.own, self.source, self.into, self.first = own, source, into, first

        def start_own(self):
            theirs = self.source.at[rows_at(sibling[1] * count, count)]
            for source, b in ((self.own, c), (theirs, 1 - c)):
                pltpu.make_async_copy(
                    source, self.into.at[rows_at(b * count, count)], load_sem.at[self.first + b]
                ).start()

        def copies(self, slot):
            return [
                pltpu.make_async_copy(
                    self.source.at[rows_at((chip_of(slot) * 2 + b) * count, count)],
                    self.into.at[rows_at(b * count, count)], load_sem.at[self.first + b],
                )
                for b in range(2)
            ]

        def start(self, slot):
            for copy in self.copies(slot):
                copy.start()

        def wait(self, slot):
            for copy in self.copies(slot):
                copy.wait()

    x_loads, up_loads = Loads(tok_ref, x_out, xs, 0), Loads(up_ref, up_out, us, 2)
    x_loads.start_own()
    up_loads.start_own()

    def stores(source, own, theirs, first, chip):
        mine = pltpu.make_async_copy(
            source.at[rows_at(c * count, count)], own.at[chip], store_sem.at[first]
        )
        other = pltpu.make_async_remote_copy(
            src_ref=source.at[rows_at((1 - c) * count, count)], dst_ref=theirs.at[chip],
            send_sem=cross_send.at[first], recv_sem=cross_recv.at[first * 4 + chip],
            device_id=sibling, device_id_type=MESH,
        )
        return mine, other

    def store(source, own, theirs, first, chip):
        mine, other = stores(source, own, theirs, first, chip)
        mine.start()
        other.start()

    def stored(source, own, theirs, first, chip):
        mine, other = stores(source, own, theirs, first, chip)
        mine.wait()
        other.wait_send()

    def saves():
        pairs = [(hs, h_save), (qkv, qkv_save), (slope, slope_save), (stats, stats_save)]
        return [(pair, store_sem.at[2 + i]) for i, pair in enumerate(pairs)]

    restores = [pltpu.make_async_copy(there, here, sem) for (here, there), sem in saves()]

    class Piece:
        def __init__(self, total, land, start, step, stage, tmp):
            self.total, self.land, self.start, self.step = total, land, start, step
            self.stage, self.tmp = stage, tmp
            self.size = land.shape[1]
            self.slot = net.slots(6)

        def each(self, quarter, half, work):
            @pl.loop(0, self.size // self.step)
            def _(i):
                work(
                    rows_at(self.start(quarter, half, i), self.step),
                    rows_at(i * self.step, self.step),
                )

        def lower(self, quarter, half, target):
            def work(at, to):
                target[to, :] = self.total[at, :].astype(bf16)

            self.each(quarter, half, work)

        def add(self, quarter, half, source):
            def work(at, to):
                self.total[at, :] += source[to, :].astype(f32)

            self.each(quarter, half, work)

        def room(self, first):
            return self.tmp.at[pl.ds(first, self.size)]

        def first(self):
            before = len(net.sent)
            for i in range(2):
                for half, quarter, peer in (
                    (0, i * 2 + 1 - x, by_x), (1, (1 - y) * 2 + i, by_y)
                ):
                    place = half * 2 + i
                    self.lower(quarter, half, self.stage[place])
                    net.send(
                        lambda place=place, peer=peer: (
                            self.stage[place], self.land.at[place], peer
                        ),
                        self.slot + place,
                    )
            self.sent, net.sent = net.sent[before:], net.sent[:before]

        def fetch(self, place):
            net.arrived(self.land.at[place], sibling, self.slot + place)
            return net.local(self.land.at[place], self.room(place * self.size))

        def second(self):
            loads = [self.fetch(place) for place in range(4)]
            for half, other, peer in ((0, 1 - y, by_y), (1, 1 - x, by_x)):
                for i in range(2):
                    loads[half * 2 + i].wait()
                    quarter = i * 2 + x if half == 0 else y * 2 + i
                    self.add(quarter, half, self.room((half * 2 + i) * self.size))
                quarter = other * 2 + x if half == 0 else y * 2 + other
                stage = self.later(half)
                self.lower(quarter, half, stage)
                net.send(
                    lambda stage=stage, half=half, peer=peer: (
                        stage, self.land.at[4 + half], peer
                    ),
                    self.slot + 4 + half,
                )

        def later(self, half):
            first = 6 + half if self.tmp.shape[0] >= 8 * self.size else half
            return self.room(first * self.size)

        def third(self):
            loads = [self.fetch(4 + half) for half in range(2)]
            for half in range(2):
                loads[half].wait()
                self.add(rep, half, self.room((4 + half) * self.size))
                self.lower(rep, half, self.room((2 + half) * self.size))
            return [self.room((2 + half) * self.size) for half in range(2)]

    def low_start(quarter, half, i):
        first = quarter * (head // 4) + half * (head // 8)
        rest = head + quarter * (units // 4) + half * (units // 8) + (i - 1) * 32
        return jnp.where(i == 0, first, rest)

    def high_start(quarter, half, i):
        return i * rows + quarter * (rows // 4) + half * (rows // 8)

    low_size, high_size = low_land.shape[1], he_land.shape[1]

    def halves(ref):
        return [ref.at[pl.ds(i * high_size, high_size)] for i in range(2)]

    low_stage = [parts.at[pl.ds(i * low_size, low_size)] for i in range(3)] + [spare]
    low = Piece(low_sum, low_land, low_start, 32, low_stage, cont_ref)
    he = Piece(he_sum, he_land, high_start, rows // 8, halves(dh) + halves(slope), exp_ref)
    hp = Piece(hp_sum, hp_land, high_start, rows // 8, halves(dm) + halves(qkv), proj_ref)

    @pl.loop(0, 5)
    def _(turn_index):
        slot = jnp.minimum(turn_index, 3)

        @pl.when(turn_index < 4)
        def _():
            chip = chip_of(slot)
            ends = [ends_all[chip * 2 + b] for b in range(2)]
            x_loads.wait(slot)
            forward_pass(
                xs, ends, count, angles_ref, norms_ref, pbias, ebias_ref, proj_ref, exp_ref,
                comb_ref, cont_ref, h1s, h2s, qkv, ca, slope, stats, parts,
            )
            store(parts, part_own, o_in, 0, chip)
            pl.when(slot == 2)(lambda: tokens.step(3))

            @pl.when(slot == 3)
            def _():
                cotangents.step(3)
                cotangents.take(3)
                up_loads.start(3)

            up_loads.wait(slot)
            accumulate(low_sum, ca, us, ca.shape[1])
            stored(parts, part_own, o_in, 0, chip)

        @pl.when(turn_index == 2)
        def _():
            for (here, there), sem in saves():
                pltpu.make_async_copy(here, there, sem).start()
            tokens.take(3)
            x_loads.start(3)
            for (here, there), sem in saves():
                pltpu.make_async_copy(here, there, sem).wait()

        pl.when(turn_index == 3)(lambda: low.first())

        @pl.when(turn_index == 4)
        def _():
            restores[0].start()
            for restore in restores[1:]:
                restore.wait()
            x_loads.wait(2)
            up_loads.wait(2)

        @pl.when(turn_index != 2)
        def _():
            slot = jnp.where(turn_index == 4, 2, turn_index)
            chip = chip_of(slot)
            ends = [ends_all[chip * 2 + b] for b in range(2)]
            backward_pass(
                xs, us, ends, count, angles_ref, norms_ref, qkv, slope, stats, proj_ref, exp_ref,
                comb_ref, cont_ref, dh, dm, dns, sums, hbias, mbias, obias,
            )
            store(dns, dn_own, d_in, 1, chip)
            pl.when(slot == 0)(lambda: tokens.step(2))
            pl.when(slot == 1)(lambda: cotangents.step(2))

            @pl.when(turn_index < 2)
            def _():
                tokens.take(slot + 1)
                x_loads.start(slot + 1)
                cotangents.take(slot + 1)
                up_loads.start(slot + 1)

            @pl.when(turn_index == 3)
            def _():
                for restore in restores[1:]:
                    restore.start()
                x_loads.start(2)
                up_loads.start(2)

            pl.when(turn_index == 4)(lambda: restores[0].wait())
            accumulate(he_sum, h2s, dh, width // 2)
            accumulate(hp_sum, h1s, dm, width // 2)
            stored(dns, dn_own, d_in, 1, chip)

    net.left(opening)
    he.first()

    class Line:
        def __init__(self, own, inward, land, total, first):
            self.own, self.inward, self.land, self.total = own, inward, land, total
            self.first = first
            self.slot = net.slots(6)

        def block(self, index):
            return self.total.at[rows_at(index * count, count)]

        def join(self):
            room = [xs.at[pl.ds(i * count, count)] for i in range(2)]
            room += [us.at[pl.ds(i * count, count)] for i in range(2)]
            loads = []
            for i in range(4):
                loads.append(net.local(self.own.at[i], self.block(i)))
                pltpu.make_async_remote_copy(
                    src_ref=self.inward.at[i], dst_ref=self.inward.at[i],
                    send_sem=cross_send.at[self.first],
                    recv_sem=cross_recv.at[self.first * 4 + i],
                    device_id=sibling, device_id_type=MESH,
                ).wait_recv()
                loads.append(net.local(self.inward.at[i], room[i]))
            for i in range(4):
                loads[2 * i].wait()
                loads[2 * i + 1].wait()
                add_into(self.block(i), room[i])

        def push(self, block, step, side, when):
            place = (step - 1) + (0 if side > 0 else 3)
            net.send(
                lambda: (self.block(block), self.land.at[place], (rep, me + 2 * side)),
                self.slot + place, when,
            )

        def begin(self, steps):
            for step in steps:
                self.push(step, step, 1, z == 0)
                self.push(3 - step, step, -1, z == 3)

        def step_on(self, step):
            for side in (1, -1):
                place = (step - 1) + (0 if side > 0 else 3)
                block = z + side * (step - 1)
                here = (z >= 1) & (block <= 3) if side > 0 else (z <= 2) & (block >= 0)
                index = net.locals
                net.locals += 1

                @pl.when(here)
                def _():
                    net.arrived(self.land.at[place], sibling, self.slot + place)
                    load = pltpu.make_async_copy(
                        self.land.at[place], comb_ref, local_sem.at[index]
                    )
                    load.start()
                    load.wait()
                    add_into(self.block(block), comb_ref)

                if step > 1:
                    self.push(block, step - 1, side, here)

    out = Line(part_own, o_in, o_land, hs, 0)
    back = Line(dn_own, d_in, d_land, pd, 1)
    out.join()
    out.begin((3, 2, 1))
    hp.first()
    low.second()

    vec_msg[...] = jnp.zeros_like(vec_msg)
    vec_mix[...] = jnp.zeros_like(vec_mix)
    per = rows // LANES
    for t in range(8):
        for j in range(4):
            for i in range(per):
                at = t * rows + i * LANES
                vec_msg[t, j * per + i : j * per + i + 1, :] = sums[j : j + 1, at : at + LANES]
        for i in range(mix // LANES):
            at = 4 * per + i
            vec_msg[t, at : at + 1, :] = mbias[:, i * LANES : (i + 1) * LANES]
    for i in range(units // LANES):
        vec_mix[56 + i : 57 + i, :] = hbias[:, i * LANES : (i + 1) * LANES]
    for i in range(per):
        vec_mix[64 + i : 65 + i, :] = obias[:, rows_at(me * rows + i * LANES, LANES)]
    small = net.slots(7)
    for k in range(1, 8):
        t = lax.rem(me + k, 8)
        net.send(lambda t=t: (vec_msg.at[t], vec_in.at[me], (rep, t)), small + k - 1)
    vec_load = net.local(vec_msg.at[me], vec_in.at[me])

    he.second()
    out.step_on(3)
    net.left(low.sent)
    back.join()
    hp.second()
    out.step_on(2)
    low_done = low.third()

    class Spread:
        def __init__(self, target, sources):
            self.target, self.slot = target, net.slots(6)
            for h, source in enumerate(sources):
                for k, peer in enumerate((by_x, by_y)):
                    net.send(
                        lambda source=source, h=h, peer=peer: (source, target.at[rep, h], peer),
                        self.slot + h * 3 + k,
                    )

        def on(self):
            for h, (k, got, peer) in enumerate(((1, y_rep, by_x), (0, x_rep, by_y))):
                net.arrived(self.target.at[got, h], sibling, self.slot + h * 3 + k)
                net.send(
                    lambda h=h, got=got, peer=peer: (
                        self.target.at[got, h], self.target.at[got, h], peer
                    ),
                    self.slot + h * 3 + 2,
                )

        def wait(self):
            for h, (k, got) in enumerate(((0, x_rep), (1, y_rep))):
                net.arrived(self.target.at[got, h], sibling, self.slot + h * 3 + k)
                net.arrived(self.target.at[d_rep, h], sibling, self.slot + h * 3 + 2)

    low_copies, low_spreads = [], []
    for target, first in ((cont_out, head // 8), (comb_out, 0)):
        pieces = [done.at[pl.ds(first, target.shape[2])] for done in low_done]
        low_copies += [net.local(pieces[h], target.at[rep, h]) for h in range(2)]
        low_spreads.append(Spread(target, pieces))
    class Turn:
        def __init__(self, source, half, place):
            self.half, self.place = half, place
            self.slot = net.slots(21)
            self.copies = []
            for k in range(1, 8):
                t = lax.rem(me + k, 8)
                for j, (src, dst) in enumerate(place(source, t, me)):
                    net.send(
                        lambda src=src, dst=dst, t=t: (src, dst, (rep, t)),
                        self.slot + (k - 1) * 3 + j,
                    )
            for src, dst in place(source, me, me):
                self.copies.append(net.local(src, dst))

        def wait(self):
            for k in range(1, 8):
                s = lax.rem(me + 8 - k, 8)
                for j, (_, dst) in enumerate(self.place(None, me, s)):
                    net.arrived(dst, sibling, self.slot + (k - 1) * 3 + j)
            for copy in self.copies:
                copy.wait()

    eighth = rows // 8

    def place_exp(half):
        return lambda source, t, s: [(
            None if source is None else source.at[rows_at(t * eighth, eighth)],
            exp_out.at[rep, half, :, rows_at(s * units, units)],
        )]

    def place_proj(half):
        return lambda source, t, s: [
            (
                None if source is None
                else source.at[rows_at(t * eighth, eighth), pl.ds(j * head, head)],
                proj_out.at[rep, half, :, rows_at(j * width + s * head, head)],
            )
            for j in range(3)
        ]

    he_done = he.third()
    he_turns = [Turn(he_done[h], h, place_exp(h)) for h in range(2)]
    hp_done = hp.third()
    hp_turns = [Turn(hp_done[h], h, place_proj(h)) for h in range(2)]

    out.step_on(1)
    back.begin((3, 2, 1))

    for k in range(1, 8):
        net.arrived(vec_in.at[lax.rem(me + 8 - k, 8)], sibling, small + k - 1)
    vec_load.wait()
    total = vec_in[0, 0:8]
    for s in range(1, 8):
        total += vec_in[s, 0:8]
    vec_mix[0:8] = total
    for s in range(8):
        vec_mix[8 + 6 * s : 14 + 6 * s] = vec_in[s, 8:14]
    wide = net.slots(4)
    for k, peer in ((1, by_x), (2, by_y), (3, across)):
        net.send(lambda peer=peer: (vec_mix, vec_all.at[rep], peer), wide + k)
    vec_copy = net.local(vec_mix, vec_all.at[rep])

    for turn_of in he_turns:
        turn_of.wait()
    he_spread = Spread(exp_out, [exp_out.at[rep, h] for h in range(2)])
    for turn_of in hp_turns:
        turn_of.wait()
    hp_spread = Spread(proj_out, [proj_out.at[rep, h] for h in range(2)])
    for spread in low_spreads:
        spread.on()
    he_spread.on()
    back.step_on(3)
    hp_spread.on()
    back.step_on(2)
    for k, r in ((1, x_rep), (2, y_rep), (3, d_rep)):
        net.arrived(vec_all.at[r], sibling, wide + k)
    vec_copy.wait()
    vec_out[...] = (vec_all[0] + vec_all[1]) + (vec_all[2] + vec_all[3])
    back.step_on(1)
    osum_copy = net.local(out.block(z), osum_out)
    dsum_copy = net.local(back.block(z), dsum_out)
    for spread in low_spreads:
        spread.wait()
    he_spread.wait()
    hp_spread.wait()
    for copy in low_copies + [osum_copy, dsum_copy]:
        copy.wait()
    tokens.finish()
    cotangents.finish()
    net.left(net.sent + he.sent + hp.sent)
    assert net.sends <= SENDS and net.started <= SENDS and net.locals <= LOCALS, (
        net.sends, net.started, net.locals)


SENDS = 320
LOCALS = 80


def block_passes(tokens, vectors, upstream, expander, projector, combiner, contractor, ebias, angles):
    count, width = tokens.shape
    n = lax.axis_size("shard")
    units, mix, head = expander.shape[1] // n, projector.shape[1] // n, combiner.shape[0]
    low, rows, two = head + units, width // n, 2 * count
    eighth = rows // 8
    vmem, dma = pltpu.VMEM, pltpu.SemaphoreType.DMA
    anywhere = pl.BlockSpec(memory_space=pl.ANY)
    block = (n // 2, count, width)
    results = [
        (4, 2, head // 8, width), (4, 2, units // 8, width),
        (4, 2, eighth, n * units), (4, 2, eighth, n * mix),
        (count, width), (count, width),
    ]
    passing = [
        (n * count, width), (n * count, width), block, block, block, block,
        (6, count, width), (6, count, width),
        (6, low // 8, width), (6, n * eighth, units), (6, n * eighth, mix),
        (2 * two, width), (two, mix), (two, units),
    ]
    result = pl.pallas_call(
        block_kernel,
        out_shape=[jax.ShapeDtypeStruct(s, bf16) for s in results] + [
            jax.ShapeDtypeStruct((72, LANES), f32), jax.ShapeDtypeStruct((8, width), f32),
        ] + [jax.ShapeDtypeStruct(s, bf16) for s in passing] + [
            jax.ShapeDtypeStruct((two, LANES), f32)
        ],
        in_specs=[anywhere] * 7 + [pl.BlockSpec(memory_space=vmem)] * 2,
        out_specs=[anywhere] * 6 + [pl.BlockSpec(memory_space=vmem)] * 2
        + [anywhere] * (len(passing) + 1),
        scratch_shapes=[
            vmem((width, units), bf16), vmem((width, mix), bf16), vmem((head, width), bf16),
            vmem((units, width), bf16), vmem((low, width), f32), vmem((width, units), f32),
            vmem((width, mix), f32),
            vmem((two, width), bf16), vmem((two, width), bf16), vmem((2 * two, width), bf16),
            vmem((2 * two, width), bf16), vmem((two, low), bf16),
            vmem((two, units), bf16), vmem((two, mix), bf16), vmem((two, units), bf16),
            vmem((two, mix), bf16), vmem((low // 8, width), bf16), vmem((two, LANES), f32),
            vmem((n,) + vectors.shape, bf16), vmem((3 * n, 1, vectors.shape[1]), f32),
            vmem((n, 1, LANES), f32),
            vmem((1, mix), f32), vmem((4, width), f32), vmem((1, units), f32),
            vmem((1, mix), f32), vmem((1, width), f32),
            vmem((n, 16, LANES), f32), vmem((n, 16, LANES), f32), vmem((72, LANES), f32),
            vmem((4, 72, LANES), f32),
            dma((SENDS,)), dma((SENDS,)), dma((LOCALS,)), dma((4,)), dma((6,)), dma((2,)), dma((8,)),
        ] + [dma((8,))] * 8,
        compiler_params=pltpu.CompilerParams(
            collective_id=0, has_side_effects=True, vmem_limit_bytes=VMEM_LIMIT
        ),
    )(tokens, vectors, upstream, expander, projector, combiner, contractor, ebias, angles)
    comb_sum, cont_sum, exp_sum, proj_sum, osum, dsum, vec, norms = result[:8]
    return (
        comb_sum.reshape(head, width), cont_sum.reshape(units, width), exp_sum.reshape(rows, n * units),
        proj_sum.reshape(rows, n * mix), osum, dsum, vec, norms,
    )


def finish_kernel(
    ends_ref, tok_ref, cot_ref, osum_ref, dsum_ref, norms_ref, comb_ref, cont_ref, exp_ref, proj_ref,
    out_ref, grad_ref, comb_out, cont_out, exp_out, proj_out,
):
    for source, target in (
        (comb_ref, comb_out), (cont_ref, cont_out), (exp_ref, exp_out), (proj_ref, proj_out)
    ):
        target[...] = source[...].astype(f32)
    count = tok_ref.shape[0]
    row = pl.program_id(0) * count + lax.broadcasted_iota(jnp.int32, (count, 1), 0)
    live = row < ends_ref[0, DOCS - 1]
    floated = tok_ref[...].astype(f32)
    added_up = osum_ref[...].astype(f32) + (norms_ref[4:5, :] + norms_ref[5:6, :])
    out_ref[...] = (floated + jnp.where(live, added_up, 0.0)).astype(bf16)
    normed, inverse = normalize(floated)
    d_normed = dsum_ref[...].astype(f32)
    grad = cot_ref[...].astype(f32) + inverse * (
        d_normed
        - jnp.mean(d_normed, axis=1, keepdims=True)
        - normed * jnp.mean(d_normed * normed, axis=1, keepdims=True)
    )
    grad_ref[...] = grad.astype(bf16)


def finish(ends, tokens, cotangent, osum, dsum, norms, sums):
    steps = 2
    thin = [tokens, cotangent, osum, dsum]

    def spec(array):
        return pl.BlockSpec((array.shape[0] // steps, array.shape[1]), lambda i, *_: (i, 0))

    return pl.pallas_call(
        finish_kernel,
        grid_spec=pltpu.PrefetchScalarGridSpec(
            num_scalar_prefetch=1,
            grid=(steps,),
            in_specs=[spec(a) for a in thin]
            + [pl.BlockSpec(norms.shape, lambda i, *_: (0, 0))] + [spec(a) for a in sums],
            out_specs=[spec(a) for a in [tokens, cotangent] + list(sums)],
        ),
        out_shape=[jax.ShapeDtypeStruct(tokens.shape, bf16)] * 2
        + [jax.ShapeDtypeStruct(a.shape, f32) for a in sums],
        compiler_params=pltpu.CompilerParams(vmem_limit_bytes=VMEM_LIMIT),
        cost_estimate=pl.CostEstimate(
            flops=20 * tokens.size, bytes_accessed=6 * sum(a.size for a in sums), transcendentals=0
        ),
    )(ends, *thin, norms, *sums)


def sharded_heads(
    tokens, document_ends, projector, projbias, combiner, combbias, expander, expbias,
    contractor, contbias, attendgain, attendshift, feedgain, feedshift, cotangent,
):
    count, width = tokens.shape
    n = lax.axis_size("shard")
    me = lax.axis_index("shard")
    head = width // H
    mix = 3 * head
    rows = width // n
    units = expbias.shape[0]
    wide = projbias.shape[0]

    parts = [attendgain, attendshift, feedgain, feedshift, combbias, contbias, projbias,
             document_ends[0].astype(bf16)]
    vectors, first = jnp.zeros((16 * rows,), bf16), 0
    for part in parts:
        last = first + part.shape[0]
        vectors += jnp.pad(part, (first, 16 * rows - last))
        first = last
    vectors = vectors.reshape(16, rows)
    _, _, live = layout(document_ends[0], count)
    upstream = jnp.where(live[:, None], cotangent, jnp.zeros_like(cotangent))
    half = ROT // 2
    freqs = np.exp(-np.arange(half) * (2.0 / ROT) * math.log(10000.0))
    still, ones = np.zeros(LANES - ROT), np.ones(half)
    angles = jnp.asarray(
        np.stack([np.concatenate([freqs, freqs, still]), np.concatenate([-ones, ones, still])]), f32
    )
    comb_out, cont_out, exp_out, proj_out, osum, dsum, vec, norms = block_passes(
        tokens, vectors, upstream, expander, projector, combiner, contractor,
        expbias.astype(f32)[None], angles,
    )

    block_output, input_gradient, comb_out, cont_out, exp_out, proj_out = finish(
        document_ends, tokens, cotangent, osum, dsum, norms, (comb_out, cont_out, exp_out, proj_out)
    )

    vec = vec.reshape(-1)
    norm_sums = vec[: 4 * rows].reshape(4, rows)
    mixed_bias = vec[4 * rows : 4 * rows + n * mix].reshape(n, 3, head).transpose(1, 0, 2)
    mixed_bias = lax.dynamic_slice(mixed_bias.reshape(-1), (me * wide,), (wide,))
    rest = vec[4 * rows + n * mix :]
    hidden_bias, out_bias = rest[:units], rest[units : units + rows]
    return (
        block_output, input_gradient, proj_out, mixed_bias, comb_out, out_bias,
        exp_out, hidden_bias, cont_out, out_bias,
        norm_sums[0], norm_sums[1], norm_sums[2], norm_sums[3],
    )


def solution(mesh):
    placed = (
        P(("rep", "shard"), None),
        P(("rep", "shard"), None),
        P("shard", None),
        P("shard"),
        P("shard", None),
        P("shard"),
        P("shard", None),
        P("shard"),
        P("shard", None),
        P("shard"),
        P("shard"),
        P("shard"),
        P("shard"),
        P("shard"),
        P(("rep", "shard"), None),
    )
    return jax.shard_map(
        sharded_heads if dict(mesh.shape) == {"rep": 4, "shard": H} else local,
        mesh=mesh,
        in_specs=placed,
        out_specs=(
            P(("rep", "shard"), None),
            P(("rep", "shard"), None),
            P("shard", None),
            P("shard"),
            P("shard", None),
            P("shard"),
            P("shard", None),
            P("shard"),
            P("shard", None),
            P("shard"),
            P("shard"),
            P("shard"),
            P("shard"),
            P("shard"),
        ),
        check_vma=False,
    )
```
